32 devices in a mesh: dp: 4 (over y, x), row: 2 (over core), col: 4 (over z).
Axes of the slice: x: 2, y: 2, z: 4, core: 2. Of those that a mesh axis runs over, the one named last changes fastest.
Arguments:
- inputs: bfloat16 [8192, 1536], P(('dp', 'row'), 'col'), may hold values from -6 to 6
- seq_lengths: int32 [4, 4], P('dp'), may hold values from 1 to 1982, as said below
- gain_one: float32 [1536], P('col'), may hold values from 0.5 to 1.5
- w_query: bfloat16 [1536, 1536], P('row', 'col'), may hold values from -0.15625 to 0.15625
- b_query: bfloat16 [1536], P('col'), may hold values from -0.59765625 to 0.59765625
- w_key: bfloat16 [1536, 256], P('row', 'col'), may hold values from -0.15625 to 0.15625
- b_key: bfloat16 [256], P('col'), may hold values from -0.59765625 to 0.59765625
- w_value: bfloat16 [1536, 256], P('row', 'col'), may hold values from -0.15625 to 0.15625
- b_value: bfloat16 [256], P('col'), may hold values from -0.59765625 to 0.59765625
- w_out: bfloat16 [1536, 1536], P('col', 'row'), may hold values from -1 to 1
- gain_two: float32 [1536], P('col'), may hold values from 0.5 to 1.5
- w_gate: bfloat16 [1536, 8960], P('row', 'col'), may hold values from -0.15625 to 0.15625
- w_up: bfloat16 [1536, 8960], P('row', 'col'), may hold values from -0.15625 to 0.15625
- w_down: bfloat16 [8960, 1536], P('col', 'row'), may hold values from -0.09375 to 0.09375
- cotangent: bfloat16 [8192, 1536], P(('dp', 'row'), 'col'), may hold values from -6 to 6
Outputs:
- out: bfloat16 [8192, 1536], P(('dp', 'row'), 'col')
- grad_inputs: bfloat16 [8192, 1536], P(('dp', 'row'), 'col')
- grad_gain_one: float32 [1536], P('col')
- grad_w_query: float32 [1536, 1536], P('row', 'col')
- grad_b_query: float32 [1536], P('col')
- grad_w_key: float32 [1536, 256], P('row', 'col')
- grad_b_key: float32 [256], P('col')
- grad_w_value: float32 [1536, 256], P('row', 'col')
- grad_b_value: float32 [256], P('col')
- grad_w_out: float32 [1536, 1536], P('col', 'row')
- grad_gain_two: float32 [1536], P('col')
- grad_w_gate: float32 [1536, 8960], P('row', 'col')
- grad_w_up: float32 [1536, 8960], P('row', 'col')
- grad_w_down: float32 [8960, 1536], P('col', 'row')
The draws below stay inside these ranges and needn't reach their ends.
Inputs may be any that keep to these rules, and one draw needn't show every extreme that they name: `seq_lengths`: each row holds the lengths of 4 documents packed in order into one sequence and sums to 2048; one entry of each row is the largest value, the other entries sum to 66, and one of them is 1.
All inputs are finite; a program needn't handle non-finite values.
Results may differ from the reference program's by a relative error of at most 0.035.
Values may be sent and summed in bfloat16 or wider, within the bound.
A program may use at most 192 MiB of HBM per device.

```python
import jax
import jax.numpy as jnp
from jax import lax

D = 1536
HEAD_WIDTH = 128
QUERY_HEADS = 12
KEY_VALUE_HEADS = 2
FF = 8960
DEVICE_TOKENS = 256
DOCS = 4
QW = 1536
KW = 256
SEQUENCE_TOKENS = 2048
SEQS = 4
TOKENS = 8192


def draw_seq_lengths(key, part):
    key = jax.random.fold_in(key, 7)
    pick_key, size_key, turn_key = jax.random.split(key, 3)
    chosen = jax.random.randint(pick_key, (SEQS, 1), 0, DOCS)
    quarter = DEVICE_TOKENS // 4
    first = jax.random.randint(size_key, (SEQS, 1), 1, quarter + 1)
    turn = jax.random.randint(turn_key, (SEQS, 1), 0, 3)
    short_values = jnp.concatenate([jnp.ones_like(first), first, quarter + 1 - first], axis=1).astype(jnp.int32)
    slot_ids = jnp.arange(DOCS, dtype=jnp.int32)[None, :]
    is_long = slot_ids == chosen
    rank = (jnp.cumsum(jnp.where(is_long, 0, 1), axis=1) - 1).astype(jnp.int32)
    which = ((rank + turn) % 3).astype(jnp.int32)
    pick = which[:, :, None] == jnp.arange(3, dtype=jnp.int32)[None, None, :]
    shorts = jnp.sum(jnp.where(pick, short_values[:, None, :], 0), axis=2).astype(jnp.int32)
    long_length = SEQUENCE_TOKENS - quarter - 2
    return jnp.where(is_long, long_length, shorts).astype(jnp.int32)


def with_spikes(values, rng, source, target, blocks, factor):
    def block_of(position):
        return (jnp.arange(values.shape[position]) // (values.shape[position] // blocks)).reshape((-1,) + (1,) * (values.ndim - 1 - position))

    one_side = jax.random.permutation(rng, blocks)[block_of(target)]
    second = (block_of(target) + blocks // 2) % blocks
    return jnp.where((block_of(source) == one_side) | (block_of(source) == second), factor * values, values)


def shard_levels(stream_key, extent, cuts, low, top_value):
    loudness = 1.0
    for position, blocks in cuts:
        steps = jax.random.uniform(jax.random.fold_in(jax.random.fold_in(stream_key, 6), position), (blocks,), jnp.float32, low / len(cuts), top_value / len(cuts))
        loudness = loudness * jnp.repeat(jnp.exp(steps), extent[position] // blocks).reshape((-1,) + (1,) * (len(extent) - 1 - position))
    return loudness


def gaussian(stream_key, dims, spread, most, shards=(), kind=jnp.bfloat16):
    values = jax.random.normal(stream_key, dims, jnp.float32) * spread
    if len(shards) > 0:
        values = shard_levels(stream_key, dims, shards, -0.22, 0.18) * values
    return jnp.clip(values, min=-most, max=most).astype(kind)


def bell_draw_with(own_key, dims, spread, limit, shards, heavy, held_as=jnp.bfloat16):
    values = spread * jax.random.normal(own_key, dims, jnp.float32)
    if shards:
        values = values * shard_levels(own_key, dims, shards, -0.22, 0.18)
    return jnp.clip(with_spikes(values, jax.random.fold_in(own_key, 3), *heavy), -limit, limit).astype(held_as)


def setup_inputs(seed: int = 0) -> dict:
    seeds = jax.random.split(jax.random.key(seed), 16)
    return {
        "inputs": gaussian(seeds[0], (TOKENS, D), 1.0, 6.0, ((0, 8), (1, 4))),
        "seq_lengths": draw_seq_lengths(jax.random.fold_in(seeds[15], 71), 0),
        "gain_one": jnp.clip(1.0 + 0.1 * jax.random.normal(seeds[2], (D,), jnp.float32), 0.5, 1.5),
        "w_query": gaussian(seeds[3], (D, QW), D ** -0.5, 0.15625, ((0, 2), (1, 4))),
        "b_query": gaussian(seeds[4], (QW,), 0.1, 0.59765625, ((0, 4),)),
        "w_key": gaussian(seeds[5], (D, KW), D ** -0.5, 0.15625, ((0, 2), (1, 4))),
        "b_key": gaussian(seeds[6], (KW,), 0.1, 0.59765625, ((0, 4),)),
        "w_value": gaussian(seeds[7], (D, KW), D ** -0.5, 0.15625, ((0, 2), (1, 4))),
        "b_value": gaussian(seeds[8], (KW,), 0.1, 0.59765625, ((0, 4),)),
        "w_out": bell_draw_with(seeds[9], (QW, D), (HEAD_WIDTH // 2) ** -0.5, 1.0, ((0, 4), (1, 2)), (0, 1, 4, 2.0)),
        "gain_two": jnp.clip(1.0 + 0.1 * jax.random.normal(seeds[10], (D,), jnp.float32), 0.5, 1.5),
        "w_gate": gaussian(seeds[11], (D, FF), D ** -0.5, 0.15625, ((0, 2), (1, 4))),
        "w_up": gaussian(seeds[12], (D, FF), D ** -0.5, 0.15625, ((0, 2), (1, 4))),
        "w_down": bell_draw_with(seeds[13], (FF, D), FF ** -0.5, 0.09375, ((0, 4), (1, 2)), (0, 1, 4, 2.0)),
        "cotangent": gaussian(seeds[14], (TOKENS, D), 1.0, 6.0, ((0, 8), (1, 4))),
    }


theta_base = 1000000.0
eps = 1e-06
highest = lax.Precision.HIGHEST

@jax.custom_vjp
def reduced_precision(v):
    return lax.optimization_barrier(v.astype(jnp.bfloat16)).astype(jnp.float32)

@jax.custom_vjp
def low_back(v):
    return v

def low_keep(v):
    return (reduced_precision(v), None)

def low_pass(kept, grad):
    return (grad,)

def back_keep(v):
    return (v, None)

def back_low(kept, grad):
    return (reduced_precision(grad),)
reduced_precision.defvjp(low_keep, low_pass)
low_back.defvjp(back_keep, back_low)

def documents(lengths, places):
    doc_ends = jnp.cumsum(lengths).astype(jnp.int32)
    doc_starts = (doc_ends - lengths).astype(jnp.int32)
    doc_index = lax.optimization_barrier(jnp.sum((places[:, None] >= doc_ends[None, :]).astype(jnp.int32), axis=1)).astype(jnp.int32)
    chosen = doc_index[:, None] == jnp.arange(lengths.shape[0], dtype=jnp.int32)[None, :]
    offset = lax.optimization_barrier(jnp.sum(jnp.where(chosen, doc_starts[None, :], 0), axis=1)).astype(jnp.int32)
    return (doc_index, (places - offset).astype(jnp.int32))

def rotary_embedding(values, token_position):
    half_size = HEAD_WIDTH // 2
    frequency = theta_base ** (-(jnp.arange(half_size, dtype=jnp.float32) * 2.0) / HEAD_WIDTH)
    angles = token_position.astype(jnp.float32)[:, None] * frequency[None, :]
    cosine = jnp.cos(angles)[:, None, :]
    sine_part = jnp.sin(angles)[:, None, :]
    leading = values[..., :half_size]
    second = values[..., half_size:]
    return jnp.concatenate([leading * cosine - second * sine_part, second * cosine + leading * sine_part], axis=-1)

def rms_norm(values, gain):
    inverse = lax.rsqrt(lax.optimization_barrier(jnp.mean(values * values, axis=-1, keepdims=True)) + eps)
    return values * inverse * gain

def sequence_layer(inputs, lengths, params):
    gain_one, w_query, b_query, w_key, b_key, w_value, b_value, w_out, gain_two, w_gate, w_up, w_down = params
    places = jnp.arange(SEQUENCE_TOKENS, dtype=jnp.int32)
    doc_index, token_position = documents(lengths, places)
    normed_one = reduced_precision(rms_norm(inputs, gain_one))
    query_lin = reduced_precision(low_back(jnp.dot(normed_one, w_query, precision=highest) + b_query))
    projected_keys = reduced_precision(low_back(jnp.dot(normed_one, w_key, precision=highest) + b_key))
    projected_values = reduced_precision(low_back(jnp.dot(normed_one, w_value, precision=highest) + b_value))
    rotated_queries = reduced_precision(rotary_embedding(query_lin.reshape(SEQUENCE_TOKENS, QUERY_HEADS, HEAD_WIDTH), token_position))
    rotated_keys = reduced_precision(rotary_embedding(projected_keys.reshape(SEQUENCE_TOKENS, KEY_VALUE_HEADS, HEAD_WIDTH), token_position))
    heads_of_values = projected_values.reshape(SEQUENCE_TOKENS, KEY_VALUE_HEADS, HEAD_WIDTH)
    query_block_index = min(512, SEQUENCE_TOKENS)
    count_blocks = SEQUENCE_TOKENS // query_block_index
    query_group_width = QUERY_HEADS // KEY_VALUE_HEADS
    blocks_of_queries = rotated_queries.reshape(count_blocks, query_block_index, KEY_VALUE_HEADS, query_group_width, HEAD_WIDTH)
    doc_blocks = doc_index.reshape(count_blocks, query_block_index)
    place_blocks = places.reshape(count_blocks, query_block_index)

    def attend(packed):
        query_blk, doc_blk, place_blk = packed
        scores = jnp.einsum('tkgh,skh->tkgs', query_blk, rotated_keys, precision=highest) * HEAD_WIDTH ** (-0.5)
        scores = low_back(scores)
        allowed = (doc_index[None, :] == doc_blk[:, None]) & (places[None, :] <= place_blk[:, None])
        masked = jnp.where(allowed[:, None, None, :], scores, -1e+30)
        largest = lax.optimization_barrier(jnp.max(masked, axis=-1, keepdims=True))
        raised = jnp.exp(masked - largest)
        probs = reduced_precision(raised / lax.optimization_barrier(jnp.sum(raised, axis=-1, keepdims=True)))
        return jnp.einsum('tkgs,skh->tkgh', probs, heads_of_values, precision=highest)
    attended = lax.map(jax.checkpoint(attend), (blocks_of_queries, doc_blocks, place_blocks))
    attended = reduced_precision(low_back(attended.reshape(SEQUENCE_TOKENS, QW)))
    hidden_mid = inputs + low_back(jnp.dot(attended, w_out, precision=highest))
    normed_two = reduced_precision(rms_norm(hidden_mid, gain_two))
    gate = low_back(jnp.dot(normed_two, w_gate, precision=highest))
    up_proj = low_back(jnp.dot(normed_two, w_up, precision=highest))
    mixed = reduced_precision(jax.nn.silu(gate) * up_proj)
    return hidden_mid + low_back(jnp.dot(mixed, w_down, precision=highest))

def reference(inputs, seq_lengths, gain_one, w_query, b_query, w_key, b_key, w_value, b_value, w_out, gain_two, w_gate, w_up, w_down, cotangent):
    params = (gain_one.astype(jnp.float32), w_query.astype(jnp.float32), b_query.astype(jnp.float32), w_key.astype(jnp.float32), b_key.astype(jnp.float32), w_value.astype(jnp.float32), b_value.astype(jnp.float32), w_out.astype(jnp.float32), gain_two.astype(jnp.float32), w_gate.astype(jnp.float32), w_up.astype(jnp.float32), w_down.astype(jnp.float32))

    def forward(hidden, weights):
        sequences = hidden.reshape(SEQS, SEQUENCE_TOKENS, D)

        def one_sequence(packed):
            return sequence_layer(packed[0], packed[1], weights)
        return lax.map(jax.checkpoint(one_sequence), (sequences, seq_lengths)).reshape(TOKENS, D)
    result, pullback = jax.vjp(forward, inputs.astype(jnp.float32), params)
    grad_inputs, grads = pullback(cotangent.astype(jnp.float32))
    grad_gain_one, grad_w_query, grad_b_query, grad_w_key, grad_b_key, grad_w_value, grad_b_value, grad_w_out, grad_gain_two, grad_w_gate, grad_w_up, grad_w_down = grads
    return (result.astype(jnp.bfloat16), grad_inputs.astype(jnp.bfloat16), grad_gain_one, grad_w_query, grad_b_query, grad_w_key, grad_b_key, grad_w_value, grad_b_value, grad_w_out, grad_gain_two, grad_w_gate, grad_w_up, grad_w_down)
```

```python
import jax
import jax.numpy as jnp
from jax import lax
from jax.sharding import PartitionSpec as P

D = 1536
HEAD_WIDTH = 128
QUERY_HEADS = 12
KEY_VALUE_HEADS = 2
DEVICE_TOKENS = 256
QW = 1536
KW = 256


theta_base = 1000000.0
eps = 1e-06


def matmul(left, right):
    return jnp.dot(left, right, preferred_element_type=jnp.float32)


def matmul_tn(left, right):
    return lax.dot_general(
        left, right, (((0,), (0,)), ((), ())), preferred_element_type=jnp.float32
    )


def matmul_nt(left, right):
    return lax.dot_general(
        left, right, (((1,), (1,)), ((), ())), preferred_element_type=jnp.float32
    )


def row_squares(values):
    return lax.psum(values, "col")


def gather_width(values):
    return lax.all_gather(values, "col", axis=1, tiled=True)


def sum_width(values):
    return lax.psum_scatter(
        values.astype(jnp.bfloat16), "col", scatter_dimension=1, tiled=True
    ).astype(jnp.float32)


def documents(lengths, places):
    doc_ends = jnp.cumsum(lengths)
    doc_starts = doc_ends - lengths
    doc_index = jnp.sum((places[:, None] >= doc_ends[None, :]).astype(jnp.int32), axis=1)
    chosen = doc_index[:, None] == jnp.arange(lengths.shape[0], dtype=jnp.int32)[None, :]
    offset = jnp.sum(jnp.where(chosen, doc_starts[None, :], 0), axis=1)
    return (doc_index, places - offset)


def rotary_embedding(values, token_position, direction):
    half_size = HEAD_WIDTH // 2
    frequency = theta_base ** (-(jnp.arange(half_size, dtype=jnp.float32) * 2.0) / HEAD_WIDTH)
    angles = token_position.astype(jnp.float32)[:, None] * frequency[None, :]
    cosine = jnp.cos(angles)[:, None, :]
    sine_part = direction * jnp.sin(angles)[:, None, :]
    leading = values[..., :half_size]
    second = values[..., half_size:]
    return jnp.concatenate(
        [leading * cosine - second * sine_part, second * cosine + leading * sine_part], axis=-1
    )


def norm_forward(hidden, gain):
    square_total = row_squares(jnp.sum(hidden * hidden, axis=1))
    inverse = lax.rsqrt(square_total / D + eps)
    normed = (hidden * inverse[:, None] * gain[None, :]).astype(jnp.bfloat16)
    return (normed, inverse)


def norm_backward(hidden, gain, inverse, grad_normed):
    scaled = grad_normed * gain[None, :]
    inner = row_squares(jnp.sum(scaled * hidden, axis=1))
    grad_hidden = (
        inverse[:, None] * scaled - hidden * (inverse * inverse * inverse * inner / D)[:, None]
    )
    grad_gain = jnp.sum(grad_normed * hidden * inverse[:, None], axis=0)
    return (grad_hidden, grad_gain)


def key_layout(gathered_keys, gathered_values, doc_all):
    seq_len = gathered_keys.shape[0]
    key_block_index = min(512, seq_len)
    count_blocks = seq_len // key_block_index
    blocks_of_keys = gathered_keys.reshape(
        count_blocks, key_block_index, gathered_keys.shape[1] // HEAD_WIDTH, HEAD_WIDTH
    )
    blocks_of_values = gathered_values.reshape(
        count_blocks, key_block_index, gathered_values.shape[1] // HEAD_WIDTH, HEAD_WIDTH
    )
    doc_blocks = doc_all.reshape(count_blocks, key_block_index)
    place_blocks = jnp.arange(seq_len, dtype=jnp.int32).reshape(count_blocks, key_block_index)
    return (blocks_of_keys, doc_blocks, place_blocks, blocks_of_values)


def block_scores(heads_of_queries, key_blk, doc_blk, place_blk, doc_local, place_local):
    scores = jnp.einsum(
        "tkgh,skh->tkgs", heads_of_queries, key_blk, preferred_element_type=jnp.float32
    ) * HEAD_WIDTH ** (-0.5)
    allowed = (doc_blk[None, :] == doc_local[:, None]) & (
        place_blk[None, :] <= place_local[:, None]
    )
    return (scores, allowed[:, None, None, :])


def attention_forward(heads_of_queries, blocks, doc_local, place_local):
    head_shape = heads_of_queries.shape[:3]

    def first_pass(state_in, packed):
        running_max, running_sum = state_in
        scores, allowed = block_scores(
            heads_of_queries, packed[0], packed[1], packed[2], doc_local, place_local
        )
        masked = jnp.where(allowed, scores, -1e30)
        new_max = jnp.maximum(running_max, jnp.max(masked, axis=-1))
        raised = jnp.where(allowed, jnp.exp(scores - new_max[..., None]), 0.0)
        running_sum = running_sum * jnp.exp(running_max - new_max) + jnp.sum(raised, axis=-1)
        return ((new_max, running_sum), None)

    initial = (jnp.full(head_shape, -1e30, jnp.float32), jnp.zeros(head_shape, jnp.float32))
    (running_max, running_sum), unused = lax.scan(first_pass, initial, blocks)
    log_total = running_max + jnp.log(running_sum)

    def second_pass(acc_out, packed):
        scores, allowed = block_scores(
            heads_of_queries, packed[0], packed[1], packed[2], doc_local, place_local
        )
        probs_low = jnp.where(allowed, jnp.exp(scores - log_total[..., None]), 0.0).astype(
            jnp.bfloat16
        )
        return (
            acc_out
            + jnp.einsum(
                "tkgs,skh->tkgh", probs_low, packed[3], preferred_element_type=jnp.float32
            ),
            None,
        )

    attended, unused = lax.scan(second_pass, jnp.zeros(heads_of_queries.shape, jnp.float32), blocks)
    return (attended, log_total)


def attention_backward(
    heads_of_queries, blocks, doc_local, place_local, log_total, attended, heads_gradient
):
    inner = jnp.sum(heads_gradient.astype(jnp.float32) * attended, axis=-1)
    scale_factor = HEAD_WIDTH ** (-0.5)

    def back_pass(grad_query, packed):
        scores, allowed = block_scores(
            heads_of_queries, packed[0], packed[1], packed[2], doc_local, place_local
        )
        probs = jnp.where(allowed, jnp.exp(scores - log_total[..., None]), 0.0)
        grad_probs = jnp.einsum(
            "tkgh,skh->tkgs", heads_gradient, packed[3], preferred_element_type=jnp.float32
        )
        grad_scores = (probs * (grad_probs - inner[..., None])).astype(jnp.bfloat16)
        grad_query = (
            grad_query
            + jnp.einsum(
                "tkgs,skh->tkgh", grad_scores, packed[0], preferred_element_type=jnp.float32
            )
            * scale_factor
        )
        grad_key = (
            jnp.einsum(
                "tkgs,tkgh->skh", grad_scores, heads_of_queries, preferred_element_type=jnp.float32
            )
            * scale_factor
        )
        grad_value = jnp.einsum(
            "tkgs,tkgh->skh",
            probs.astype(jnp.bfloat16),
            heads_gradient,
            preferred_element_type=jnp.float32,
        )
        return (grad_query, (grad_key, grad_value))

    grad_query, (key_grads, value_grads) = lax.scan(
        back_pass, jnp.zeros(heads_of_queries.shape, jnp.float32), blocks
    )
    seq_len = key_grads.shape[0] * key_grads.shape[1]
    return (grad_query, key_grads.reshape(seq_len, -1), value_grads.reshape(seq_len, -1))


def per_device_any(
    inputs,
    seq_lengths,
    gain_one,
    w_query,
    b_query,
    w_key,
    b_key,
    w_value,
    b_value,
    w_out,
    gain_two,
    w_gate,
    w_up,
    w_down,
    cotangent,
):
    full_query, full_key, full_value, full_out, full_gate, full_up, full_down = (
        lax.all_gather(w_query, "row", axis=0, tiled=True),
        lax.all_gather(w_key, "row", axis=0, tiled=True),
        lax.all_gather(w_value, "row", axis=0, tiled=True),
        lax.all_gather(w_out, "row", axis=1, tiled=True),
        lax.all_gather(w_gate, "row", axis=0, tiled=True),
        lax.all_gather(w_up, "row", axis=0, tiled=True),
        lax.all_gather(w_down, "row", axis=1, tiled=True),
    )
    row_pos = lax.axis_index("row")
    col_pos = lax.axis_index("col")
    row_count = lax.axis_size("row")
    col_count = lax.axis_size("col")
    seq_len = DEVICE_TOKENS * row_count * col_count
    query_group_width = QUERY_HEADS // KEY_VALUE_HEADS
    lengths = seq_lengths[0]
    place_local = (row_pos * col_count + col_pos) * DEVICE_TOKENS + jnp.arange(
        DEVICE_TOKENS, dtype=jnp.int32
    )
    doc_local, local_position = documents(lengths, place_local)
    doc_all = documents(lengths, jnp.arange(seq_len, dtype=jnp.int32))[0]
    hidden_in = inputs.astype(jnp.float32)
    normed_one, inverse_one = norm_forward(hidden_in, gain_one)
    normed_full = gather_width(normed_one)
    query_lin = (matmul(normed_full, full_query) + b_query.astype(jnp.float32)).astype(jnp.bfloat16)
    projected_keys = (matmul(normed_full, full_key) + b_key.astype(jnp.float32)).astype(
        jnp.bfloat16
    )
    projected_values = (matmul(normed_full, full_value) + b_value.astype(jnp.float32)).astype(
        jnp.bfloat16
    )
    query_rows, rows_of_keys, value_rows = (
        lax.all_to_all(query_lin, "col", split_axis=0, concat_axis=1, tiled=True),
        lax.all_to_all(projected_keys, "col", split_axis=0, concat_axis=1, tiled=True),
        lax.all_to_all(projected_values, "col", split_axis=0, concat_axis=1, tiled=True),
    )
    rotated_queries = rotary_embedding(
        query_rows.astype(jnp.float32).reshape(DEVICE_TOKENS, QUERY_HEADS, HEAD_WIDTH),
        local_position,
        1.0,
    ).astype(jnp.bfloat16)
    rotated_keys = rotary_embedding(
        rows_of_keys.astype(jnp.float32).reshape(DEVICE_TOKENS, KEY_VALUE_HEADS, HEAD_WIDTH),
        local_position,
        1.0,
    ).astype(jnp.bfloat16)
    gathered_keys, gathered_values = (
        lax.all_gather(rotated_keys.reshape(DEVICE_TOKENS, KW), ("row", "col"), axis=0, tiled=True),
        lax.all_gather(value_rows, ("row", "col"), axis=0, tiled=True),
    )
    blocks = key_layout(gathered_keys, gathered_values, doc_all)
    heads_of_queries = rotated_queries.reshape(
        DEVICE_TOKENS, KEY_VALUE_HEADS, query_group_width, HEAD_WIDTH
    )
    attended, log_total = attention_forward(heads_of_queries, blocks, doc_local, place_local)
    attended_low = attended.reshape(DEVICE_TOKENS, QW).astype(jnp.bfloat16)
    attended_cols = lax.all_to_all(attended_low, "col", split_axis=1, concat_axis=0, tiled=True)
    hidden_mid = hidden_in + sum_width(matmul(attended_cols, full_out))
    normed_two, inverse_two = norm_forward(hidden_mid, gain_two)
    normed_wide = gather_width(normed_two)
    gate = matmul(normed_wide, full_gate)
    up_proj = matmul(normed_wide, full_up)
    sigmoid_gate = jax.nn.sigmoid(gate)
    silu_gate = gate * sigmoid_gate
    mixed = (silu_gate * up_proj).astype(jnp.bfloat16)
    result = (hidden_mid + sum_width(matmul(mixed, full_down))).astype(jnp.bfloat16)
    grad_full = gather_width(cotangent)
    grad_w_down = matmul_tn(mixed, grad_full)
    grad_mixed = matmul_nt(grad_full, full_down)
    grad_gate = (grad_mixed * up_proj * sigmoid_gate * (1.0 + gate * (1.0 - sigmoid_gate))).astype(
        jnp.bfloat16
    )
    grad_up = (grad_mixed * silu_gate).astype(jnp.bfloat16)
    grad_w_gate = matmul_tn(normed_wide, grad_gate)
    grad_w_up = matmul_tn(normed_wide, grad_up)
    grad_normed_two = sum_width(matmul_nt(grad_gate, full_gate) + matmul_nt(grad_up, full_up))
    grad_back_two, grad_gain_two = norm_backward(hidden_mid, gain_two, inverse_two, grad_normed_two)
    grad_mid = cotangent.astype(jnp.float32) + grad_back_two
    grad_attn_full = gather_width(grad_mid.astype(jnp.bfloat16))
    grad_w_out = matmul_tn(attended_cols, grad_attn_full)
    grad_attended_cols = matmul_nt(grad_attn_full, full_out).astype(jnp.bfloat16)
    attended_gradient = lax.all_to_all(
        grad_attended_cols, "col", split_axis=0, concat_axis=1, tiled=True
    )
    heads_gradient = attended_gradient.reshape(
        DEVICE_TOKENS, KEY_VALUE_HEADS, query_group_width, HEAD_WIDTH
    )
    grad_query_rot, key_grads, value_grads = attention_backward(
        heads_of_queries, blocks, doc_local, place_local, log_total, attended, heads_gradient
    )
    rotated_key_gradient, grad_value = (
        lax.psum_scatter(
            key_grads.astype(jnp.bfloat16), ("row", "col"), scatter_dimension=0, tiled=True
        ).astype(jnp.float32),
        lax.psum_scatter(
            value_grads.astype(jnp.bfloat16), ("row", "col"), scatter_dimension=0, tiled=True
        ).astype(jnp.float32),
    )
    grad_query_lin = (
        rotary_embedding(
            grad_query_rot.reshape(DEVICE_TOKENS, QUERY_HEADS, HEAD_WIDTH), local_position, -1.0
        )
        .reshape(DEVICE_TOKENS, QW)
        .astype(jnp.bfloat16)
    )
    grad_key_lin = (
        rotary_embedding(
            rotated_key_gradient.reshape(DEVICE_TOKENS, KEY_VALUE_HEADS, HEAD_WIDTH),
            local_position,
            -1.0,
        )
        .reshape(DEVICE_TOKENS, KW)
        .astype(jnp.bfloat16)
    )
    grad_value_lin = grad_value.astype(jnp.bfloat16)
    query_grad_cols, key_grad_cols, value_grad_cols = (
        lax.all_to_all(grad_query_lin, "col", split_axis=1, concat_axis=0, tiled=True),
        lax.all_to_all(grad_key_lin, "col", split_axis=1, concat_axis=0, tiled=True),
        lax.all_to_all(grad_value_lin, "col", split_axis=1, concat_axis=0, tiled=True),
    )
    grad_b_query = jnp.sum(query_grad_cols.astype(jnp.float32), axis=0)
    grad_b_key = jnp.sum(key_grad_cols.astype(jnp.float32), axis=0)
    grad_b_value = jnp.sum(value_grad_cols.astype(jnp.float32), axis=0)
    grad_w_query = matmul_tn(normed_full, query_grad_cols)
    grad_w_key = matmul_tn(normed_full, key_grad_cols)
    grad_w_value = matmul_tn(normed_full, value_grad_cols)
    grad_normed_one = sum_width(
        matmul_nt(query_grad_cols, full_query)
        + matmul_nt(key_grad_cols, full_key)
        + matmul_nt(value_grad_cols, full_value)
    )
    grad_back_one, grad_gain_one = norm_backward(hidden_in, gain_one, inverse_one, grad_normed_one)
    grad_inputs = (grad_mid + grad_back_one).astype(jnp.bfloat16)
    summed = (
        lax.psum(grad_w_query.astype(jnp.bfloat16), ("dp", "row")).astype(jnp.float32),
        lax.psum(grad_w_key.astype(jnp.bfloat16), ("dp", "row")).astype(jnp.float32),
        lax.psum(grad_w_value.astype(jnp.bfloat16), ("dp", "row")).astype(jnp.float32),
        lax.psum(grad_w_out.astype(jnp.bfloat16), ("dp", "row")).astype(jnp.float32),
        lax.psum(grad_w_gate.astype(jnp.bfloat16), ("dp", "row")).astype(jnp.float32),
        lax.psum(grad_w_up.astype(jnp.bfloat16), ("dp", "row")).astype(jnp.float32),
        lax.psum(grad_w_down.astype(jnp.bfloat16), ("dp", "row")).astype(jnp.float32),
        lax.psum(grad_gain_one.astype(jnp.bfloat16), ("dp", "row")).astype(jnp.float32),
        lax.psum(grad_b_query.astype(jnp.bfloat16), ("dp", "row")).astype(jnp.float32),
        lax.psum(grad_b_key.astype(jnp.bfloat16), ("dp", "row")).astype(jnp.float32),
        lax.psum(grad_b_value.astype(jnp.bfloat16), ("dp", "row")).astype(jnp.float32),
        lax.psum(grad_gain_two.astype(jnp.bfloat16), ("dp", "row")).astype(jnp.float32),
    )
    rows_each = D // row_count
    split_dims = (0, 0, 0, 1, 0, 0, 1)
    weight_sums = tuple(
        (
            lax.dynamic_slice_in_dim(
                summed[member], row_pos * rows_each, rows_each, split_dims[member]
            )
            for member in range(7)
        )
    )
    small_sums = summed[7:]
    return (
        result,
        grad_inputs,
        small_sums[0],
        weight_sums[0],
        small_sums[1],
        weight_sums[1],
        small_sums[2],
        weight_sums[2],
        small_sums[3],
        weight_sums[3],
        small_sums[4],
        weight_sums[4],
        weight_sums[5],
        weight_sums[6],
    )


def norm_rows(hidden, gain):
    inverse = lax.rsqrt(jnp.mean(hidden * hidden, axis=1, keepdims=True) + eps)
    return ((hidden * inverse * gain[None, :]).astype(jnp.bfloat16), inverse)


def per_device(
    inputs,
    seq_lengths,
    gain_one,
    w_query,
    b_query,
    w_key,
    b_key,
    w_value,
    b_value,
    w_out,
    gain_two,
    w_gate,
    w_up,
    w_down,
    cotangent,
):
    row_pos = lax.axis_index("row")
    col_pos = lax.axis_index("col")
    row_count = lax.axis_size("row")
    col_count = lax.axis_size("col")
    rows = inputs.shape[0]
    part = rows // col_count
    seq_len = rows * row_count
    heads = QUERY_HEADS // col_count
    share = col_count // KEY_VALUE_HEADS
    groups = [[g * share + s for s in range(share)] for g in range(KEY_VALUE_HEADS)]
    f32, bf16 = jnp.float32, jnp.bfloat16

    inputs_full = gather_width(inputs)
    gain_one_full, gain_two_full = lax.all_gather(
        jnp.stack([gain_one, gain_two]), "col", axis=1, tiled=True
    )
    full_query = lax.all_gather(w_query, "row", axis=0, tiled=True)
    key_value = jnp.concatenate(
        [
            jnp.concatenate([w_key, w_value], axis=1),
            jnp.stack([jnp.concatenate([b_key, b_value])] * 16),
        ],
        axis=0,
    )
    key_value = lax.all_gather(key_value, "row", axis=0, tiled=False)
    key_value = lax.all_gather(key_value, "col", axis=0, tiled=False, axis_index_groups=groups)
    kv_cols = key_value.shape[-1] // 2
    kv_w = key_value[:, :, : w_key.shape[0]].reshape(share, D, 2, kv_cols)
    head_weights = kv_w.transpose(1, 2, 0, 3).reshape(D, 2 * HEAD_WIDTH)
    head_bias = key_value[:, 0, w_key.shape[0]].reshape(share, 2, kv_cols)
    head_bias = head_bias.transpose(1, 0, 2).reshape(2 * HEAD_WIDTH)
    own_kv = lax.all_gather(jnp.concatenate([w_key, w_value], axis=1), "row", axis=0, tiled=True)
    cot_full = gather_width(cotangent)
    full_out = lax.all_gather(w_out, "row", axis=1, tiled=True)
    full_gate = lax.all_gather(w_gate, "row", axis=0, tiled=True)
    full_up = lax.all_gather(w_up, "row", axis=0, tiled=True)
    full_down = lax.all_gather(w_down, "row", axis=1, tiled=True)

    lengths = seq_lengths[0]
    place_local = row_pos * rows + jnp.arange(rows, dtype=jnp.int32)
    doc_local, local_position = documents(lengths, place_local)
    doc_all = documents(lengths, jnp.arange(seq_len, dtype=jnp.int32))[0]

    hidden_in = inputs_full.astype(f32)
    normed_one, inverse_one = norm_rows(hidden_in, gain_one_full)
    query_lin = (matmul(normed_one, full_query) + b_query.astype(f32)).astype(bf16)
    kv_lin = (matmul(normed_one, head_weights) + head_bias.astype(f32)).astype(bf16)
    rotated_queries = rotary_embedding(
        query_lin.astype(f32).reshape(rows, heads, HEAD_WIDTH), local_position, 1.0
    ).astype(bf16)
    rotated_keys = rotary_embedding(
        kv_lin[:, None, :HEAD_WIDTH].astype(f32), local_position, 1.0
    ).astype(bf16)
    seq_kv = lax.all_gather(
        jnp.concatenate([rotated_keys.reshape(rows, HEAD_WIDTH), kv_lin[:, HEAD_WIDTH:]], axis=1),
        "row",
        axis=0,
        tiled=True,
    )
    blocks = key_layout(seq_kv[:, :HEAD_WIDTH], seq_kv[:, HEAD_WIDTH:], doc_all)
    heads_of_queries = rotated_queries.reshape(rows, 1, heads, HEAD_WIDTH)
    attended, log_total = attention_forward(heads_of_queries, blocks, doc_local, place_local)
    attended_cols = attended.reshape(rows, heads * HEAD_WIDTH).astype(bf16)
    attn_rows = lax.psum_scatter(
        matmul(attended_cols, full_out).astype(bf16), "col", scatter_dimension=0, tiled=True
    ).astype(f32)
    start = col_pos * part
    hidden_mid = lax.dynamic_slice_in_dim(hidden_in, start, part, 0) + attn_rows
    normed_part, inverse_two = norm_rows(hidden_mid, gain_two_full)
    normed_two = lax.all_gather(normed_part, "col", axis=0, tiled=True)

    gate = matmul(normed_two, full_gate)
    up_proj = matmul(normed_two, full_up)
    sigmoid_gate = jax.nn.sigmoid(gate)
    silu_gate = gate * sigmoid_gate
    mixed = (silu_gate * up_proj).astype(bf16)
    grad_mixed = matmul_nt(cot_full, full_down)
    grad_gate = (grad_mixed * up_proj * sigmoid_gate * (1.0 + gate * (1.0 - sigmoid_gate))).astype(
        bf16
    )
    grad_up = (grad_mixed * silu_gate).astype(bf16)
    grad_normed_two = lax.psum_scatter(
        (matmul_nt(grad_gate, full_gate) + matmul_nt(grad_up, full_up)).astype(bf16),
        "col",
        scatter_dimension=0,
        tiled=True,
    ).astype(f32)

    def row_sum(grad, dim):
        return lax.psum_scatter(grad.astype(bf16), "row", scatter_dimension=dim, tiled=True)

    out_partial = matmul(mixed, full_down)
    out_partial = lax.dynamic_update_slice_in_dim(
        out_partial, lax.dynamic_slice_in_dim(out_partial, start, part, 0) + hidden_mid, start, 0
    )
    result = lax.psum_scatter(out_partial.astype(bf16), "col", scatter_dimension=1, tiled=True)

    wide_sums = lax.psum(
        (
            row_sum(matmul_tn(mixed, cot_full), 1),
            row_sum(matmul_tn(normed_two, grad_gate), 0),
            row_sum(matmul_tn(normed_two, grad_up), 0),
        ),
        "dp",
    )

    scaled = grad_normed_two * gain_two_full[None, :]
    inner = jnp.sum(scaled * hidden_mid, axis=1, keepdims=True)
    grad_gain_two = jnp.sum(grad_normed_two * hidden_mid * inverse_two, axis=0)
    grad_mid = (
        lax.dynamic_slice_in_dim(cot_full, start, part, 0).astype(f32)
        + inverse_two * scaled
        - hidden_mid * (inverse_two * inverse_two * inverse_two * inner / D)
    )
    grad_mid_full = lax.all_gather(grad_mid.astype(bf16), "col", axis=0, tiled=True)
    grad_attended = matmul_nt(grad_mid_full, full_out).astype(bf16)
    grad_query_rot, key_grads, value_grads = attention_backward(
        heads_of_queries,
        blocks,
        doc_local,
        place_local,
        log_total,
        attended,
        grad_attended.reshape(rows, 1, heads, HEAD_WIDTH),
    )
    grad_w_out = row_sum(matmul_tn(attended_cols, grad_mid_full), 1)
    kv_grads = lax.psum_scatter(
        jnp.concatenate([key_grads, value_grads], axis=1).astype(bf16),
        "row",
        scatter_dimension=0,
        tiled=True,
    ).astype(f32)
    grad_key_part = rotary_embedding(kv_grads[:, None, :HEAD_WIDTH], local_position, -1.0)
    kv_part = jnp.stack(
        [grad_key_part.reshape(rows, share, kv_cols), kv_grads[:, HEAD_WIDTH:].reshape(rows, share, kv_cols)],
        axis=2,
    ).reshape(rows, 2 * HEAD_WIDTH)
    kv_grad_cols = lax.psum_scatter(
        kv_part.astype(bf16), "col", scatter_dimension=1, tiled=True, axis_index_groups=groups
    )
    query_grad_cols = (
        rotary_embedding(
            grad_query_rot.reshape(rows, heads, HEAD_WIDTH), local_position, -1.0
        )
        .reshape(rows, heads * HEAD_WIDTH)
        .astype(bf16)
    )
    grad_w_query = row_sum(matmul_tn(normed_one, query_grad_cols), 0)
    grad_w_kv = row_sum(matmul_tn(normed_one, kv_grad_cols), 0)
    (grad_w_out, grad_w_query, grad_w_kv), wide_sums = lax.optimization_barrier(
        ((grad_w_out, grad_w_query, grad_w_kv), wide_sums)
    )
    grad_w_out, grad_w_query, grad_w_kv = (
        g.astype(f32) for g in lax.psum((grad_w_out, grad_w_query, grad_w_kv), "dp")
    )
    grad_w_down, grad_w_gate, grad_w_up = (g.astype(f32) for g in wide_sums)
    grad_b_query = jnp.sum(query_grad_cols.astype(f32), axis=0)
    grad_b_kv = jnp.sum(kv_grad_cols.astype(f32), axis=0)
    grad_normed_one = matmul_nt(query_grad_cols, full_query) + matmul_nt(kv_grad_cols, own_kv)
    scaled_one = grad_normed_one * gain_one_full[None, :]
    inner_one = jnp.sum(scaled_one * hidden_in, axis=1, keepdims=True)
    grad_gain_one = jnp.sum(grad_normed_one * hidden_in * inverse_one, axis=0)
    back_one = inverse_one * scaled_one - hidden_in * (
        inverse_one * inverse_one * inverse_one * inner_one / D
    )
    back_one = lax.dynamic_update_slice_in_dim(
        back_one, lax.dynamic_slice_in_dim(back_one, start, part, 0) + grad_mid, start, 0
    )
    grad_inputs = lax.psum_scatter(back_one.astype(bf16), "col", scatter_dimension=1, tiled=True)
    gains = lax.psum_scatter(
        jnp.stack([grad_gain_one, grad_gain_two]), "col", scatter_dimension=1, tiled=True
    )
    width = gains.shape[1]
    small = jnp.concatenate([gains.reshape(-1), grad_b_query, grad_b_kv])
    small = lax.psum(small, ("dp", "row"))
    biases = small[2 * width :]
    return (
        result,
        grad_inputs,
        small[:width],
        grad_w_query,
        biases[:width],
        grad_w_kv[:, :kv_cols],
        biases[width : width + kv_cols],
        grad_w_kv[:, kv_cols:],
        biases[width + kv_cols :],
        grad_w_out,
        small[width : 2 * width],
        grad_w_gate,
        grad_w_up,
        grad_w_down,
    )


def solution(mesh):
    whole_heads = QUERY_HEADS % mesh.shape["col"] == 0 and mesh.shape["col"] % KEY_VALUE_HEADS == 0
    return jax.shard_map(
        per_device if whole_heads else per_device_any,
        mesh=mesh,
        in_specs=(
            P(("dp", "row"), "col"),
            P("dp", None),
            P("col"),
            P("row", "col"),
            P("col"),
            P("row", "col"),
            P("col"),
            P("row", "col"),
            P("col"),
            P("col", "row"),
            P("col"),
            P("row", "col"),
            P("row", "col"),
            P("col", "row"),
            P(("dp", "row"), "col"),
        ),
        out_specs=(
            P(("dp", "row"), "col"),
            P(("dp", "row"), "col"),
            P("col"),
            P("row", "col"),
            P("col"),
            P("row", "col"),
            P("col"),
            P("row", "col"),
            P("col"),
            P("col", "row"),
            P("col"),
            P("row", "col"),
            P("row", "col"),
            P("col", "row"),
        ),
        check_vma=False,
    )
```

```python
import functools

import jax
import jax.numpy as jnp
from jax import lax
from jax.experimental import pallas as pl
from jax.experimental.pallas import tpu as pltpu
from jax.sharding import PartitionSpec as P

D = 1536
HEAD_WIDTH = 128
QUERY_HEADS = 12
KEY_VALUE_HEADS = 2
DEVICE_TOKENS = 256
QW = 1536
KW = 256


theta_base = 1000000.0
eps = 1e-06


def matmul(left, right):
    return jnp.dot(left, right, preferred_element_type=jnp.float32)


def matmul_tn(left, right):
    return lax.dot_general(
        left, right, (((0,), (0,)), ((), ())), preferred_element_type=jnp.float32
    )


def matmul_nt(left, right):
    return lax.dot_general(
        left, right, (((1,), (1,)), ((), ())), preferred_element_type=jnp.float32
    )


def row_squares(values):
    return lax.psum(values, "col")


def gather_width(values):
    return lax.all_gather(values, "col", axis=1, tiled=True)


def sum_width(values):
    return lax.psum_scatter(
        values.astype(jnp.bfloat16), "col", scatter_dimension=1, tiled=True
    ).astype(jnp.float32)


def documents(lengths, places):
    doc_ends = jnp.cumsum(lengths)
    doc_starts = doc_ends - lengths
    doc_index = jnp.sum((places[:, None] >= doc_ends[None, :]).astype(jnp.int32), axis=1)
    chosen = doc_index[:, None] == jnp.arange(lengths.shape[0], dtype=jnp.int32)[None, :]
    offset = jnp.sum(jnp.where(chosen, doc_starts[None, :], 0), axis=1)
    return (doc_index, places - offset)


def rotary_embedding(values, token_position, direction):
    half_size = HEAD_WIDTH // 2
    frequency = theta_base ** (-(jnp.arange(half_size, dtype=jnp.float32) * 2.0) / HEAD_WIDTH)
    angles = token_position.astype(jnp.float32)[:, None] * frequency[None, :]
    cosine = jnp.cos(angles)[:, None, :]
    sine_part = direction * jnp.sin(angles)[:, None, :]
    leading = values[..., :half_size]
    second = values[..., half_size:]
    return jnp.concatenate(
        [leading * cosine - second * sine_part, second * cosine + leading * sine_part], axis=-1
    )


def norm_forward(hidden, gain):
    square_total = row_squares(jnp.sum(hidden * hidden, axis=1))
    inverse = lax.rsqrt(square_total / D + eps)
    normed = (hidden * inverse[:, None] * gain[None, :]).astype(jnp.bfloat16)
    return (normed, inverse)


def norm_backward(hidden, gain, inverse, grad_normed):
    scaled = grad_normed * gain[None, :]
    inner = row_squares(jnp.sum(scaled * hidden, axis=1))
    grad_hidden = (
        inverse[:, None] * scaled - hidden * (inverse * inverse * inverse * inner / D)[:, None]
    )
    grad_gain = jnp.sum(grad_normed * hidden * inverse[:, None], axis=0)
    return (grad_hidden, grad_gain)


def key_layout(gathered_keys, gathered_values, doc_all):
    seq_len = gathered_keys.shape[0]
    key_block_index = min(512, seq_len)
    count_blocks = seq_len // key_block_index
    blocks_of_keys = gathered_keys.reshape(
        count_blocks, key_block_index, gathered_keys.shape[1] // HEAD_WIDTH, HEAD_WIDTH
    )
    blocks_of_values = gathered_values.reshape(
        count_blocks, key_block_index, gathered_values.shape[1] // HEAD_WIDTH, HEAD_WIDTH
    )
    doc_blocks = doc_all.reshape(count_blocks, key_block_index)
    place_blocks = jnp.arange(seq_len, dtype=jnp.int32).reshape(count_blocks, key_block_index)
    return (blocks_of_keys, doc_blocks, place_blocks, blocks_of_values)


def block_scores(heads_of_queries, key_blk, doc_blk, place_blk, doc_local, place_local):
    scores = jnp.einsum(
        "tkgh,skh->tkgs", heads_of_queries, key_blk, preferred_element_type=jnp.float32
    ) * HEAD_WIDTH ** (-0.5)
    allowed = (doc_blk[None, :] == doc_local[:, None]) & (
        place_blk[None, :] <= place_local[:, None]
    )
    return (scores, allowed[:, None, None, :])


def attention_forward(heads_of_queries, blocks, doc_local, place_local):
    head_shape = heads_of_queries.shape[:3]

    def first_pass(state_in, packed):
        running_max, running_sum = state_in
        scores, allowed = block_scores(
            heads_of_queries, packed[0], packed[1], packed[2], doc_local, place_local
        )
        masked = jnp.where(allowed, scores, -1e30)
        new_max = jnp.maximum(running_max, jnp.max(masked, axis=-1))
        raised = jnp.where(allowed, jnp.exp(scores - new_max[..., None]), 0.0)
        running_sum = running_sum * jnp.exp(running_max - new_max) + jnp.sum(raised, axis=-1)
        return ((new_max, running_sum), None)

    initial = (jnp.full(head_shape, -1e30, jnp.float32), jnp.zeros(head_shape, jnp.float32))
    (running_max, running_sum), unused = lax.scan(first_pass, initial, blocks)
    log_total = running_max + jnp.log(running_sum)

    def second_pass(acc_out, packed):
        scores, allowed = block_scores(
            heads_of_queries, packed[0], packed[1], packed[2], doc_local, place_local
        )
        probs_low = jnp.where(allowed, jnp.exp(scores - log_total[..., None]), 0.0).astype(
            jnp.bfloat16
        )
        return (
            acc_out
            + jnp.einsum(
                "tkgs,skh->tkgh", probs_low, packed[3], preferred_element_type=jnp.float32
            ),
            None,
        )

    attended, unused = lax.scan(second_pass, jnp.zeros(heads_of_queries.shape, jnp.float32), blocks)
    return (attended, log_total)


def attention_backward(
    heads_of_queries, blocks, doc_local, place_local, log_total, attended, heads_gradient
):
    inner = jnp.sum(heads_gradient.astype(jnp.float32) * attended, axis=-1)
    scale_factor = HEAD_WIDTH ** (-0.5)

    def back_pass(grad_query, packed):
        scores, allowed = block_scores(
            heads_of_queries, packed[0], packed[1], packed[2], doc_local, place_local
        )
        probs = jnp.where(allowed, jnp.exp(scores - log_total[..., None]), 0.0)
        grad_probs = jnp.einsum(
            "tkgh,skh->tkgs", heads_gradient, packed[3], preferred_element_type=jnp.float32
        )
        grad_scores = (probs * (grad_probs - inner[..., None])).astype(jnp.bfloat16)
        grad_query = (
            grad_query
            + jnp.einsum(
                "tkgs,skh->tkgh", grad_scores, packed[0], preferred_element_type=jnp.float32
            )
            * scale_factor
        )
        grad_key = (
            jnp.einsum(
                "tkgs,tkgh->skh", grad_scores, heads_of_queries, preferred_element_type=jnp.float32
            )
            * scale_factor
        )
        grad_value = jnp.einsum(
            "tkgs,tkgh->skh",
            probs.astype(jnp.bfloat16),
            heads_gradient,
            preferred_element_type=jnp.float32,
        )
        return (grad_query, (grad_key, grad_value))

    grad_query, (key_grads, value_grads) = lax.scan(
        back_pass, jnp.zeros(heads_of_queries.shape, jnp.float32), blocks
    )
    seq_len = key_grads.shape[0] * key_grads.shape[1]
    return (grad_query, key_grads.reshape(seq_len, -1), value_grads.reshape(seq_len, -1))


def per_device_any(
    inputs,
    seq_lengths,
    gain_one,
    w_query,
    b_query,
    w_key,
    b_key,
    w_value,
    b_value,
    w_out,
    gain_two,
    w_gate,
    w_up,
    w_down,
    cotangent,
):
    full_query, full_key, full_value, full_out, full_gate, full_up, full_down = (
        lax.all_gather(w_query, "row", axis=0, tiled=True),
        lax.all_gather(w_key, "row", axis=0, tiled=True),
        lax.all_gather(w_value, "row", axis=0, tiled=True),
        lax.all_gather(w_out, "row", axis=1, tiled=True),
        lax.all_gather(w_gate, "row", axis=0, tiled=True),
        lax.all_gather(w_up, "row", axis=0, tiled=True),
        lax.all_gather(w_down, "row", axis=1, tiled=True),
    )
    row_pos = lax.axis_index("row")
    col_pos = lax.axis_index("col")
    row_count = lax.axis_size("row")
    col_count = lax.axis_size("col")
    seq_len = DEVICE_TOKENS * row_count * col_count
    query_group_width = QUERY_HEADS // KEY_VALUE_HEADS
    lengths = seq_lengths[0]
    place_local = (row_pos * col_count + col_pos) * DEVICE_TOKENS + jnp.arange(
        DEVICE_TOKENS, dtype=jnp.int32
    )
    doc_local, local_position = documents(lengths, place_local)
    doc_all = documents(lengths, jnp.arange(seq_len, dtype=jnp.int32))[0]
    hidden_in = inputs.astype(jnp.float32)
    normed_one, inverse_one = norm_forward(hidden_in, gain_one)
    normed_full = gather_width(normed_one)
    query_lin = (matmul(normed_full, full_query) + b_query.astype(jnp.float32)).astype(jnp.bfloat16)
    projected_keys = (matmul(normed_full, full_key) + b_key.astype(jnp.float32)).astype(
        jnp.bfloat16
    )
    projected_values = (matmul(normed_full, full_value) + b_value.astype(jnp.float32)).astype(
        jnp.bfloat16
    )
    query_rows, rows_of_keys, value_rows = (
        lax.all_to_all(query_lin, "col", split_axis=0, concat_axis=1, tiled=True),
        lax.all_to_all(projected_keys, "col", split_axis=0, concat_axis=1, tiled=True),
        lax.all_to_all(projected_values, "col", split_axis=0, concat_axis=1, tiled=True),
    )
    rotated_queries = rotary_embedding(
        query_rows.astype(jnp.float32).reshape(DEVICE_TOKENS, QUERY_HEADS, HEAD_WIDTH),
        local_position,
        1.0,
    ).astype(jnp.bfloat16)
    rotated_keys = rotary_embedding(
        rows_of_keys.astype(jnp.float32).reshape(DEVICE_TOKENS, KEY_VALUE_HEADS, HEAD_WIDTH),
        local_position,
        1.0,
    ).astype(jnp.bfloat16)
    gathered_keys, gathered_values = (
        lax.all_gather(rotated_keys.reshape(DEVICE_TOKENS, KW), ("row", "col"), axis=0, tiled=True),
        lax.all_gather(value_rows, ("row", "col"), axis=0, tiled=True),
    )
    blocks = key_layout(gathered_keys, gathered_values, doc_all)
    heads_of_queries = rotated_queries.reshape(
        DEVICE_TOKENS, KEY_VALUE_HEADS, query_group_width, HEAD_WIDTH
    )
    attended, log_total = attention_forward(heads_of_queries, blocks, doc_local, place_local)
    attended_low = attended.reshape(DEVICE_TOKENS, QW).astype(jnp.bfloat16)
    attended_cols = lax.all_to_all(attended_low, "col", split_axis=1, concat_axis=0, tiled=True)
    hidden_mid = hidden_in + sum_width(matmul(attended_cols, full_out))
    normed_two, inverse_two = norm_forward(hidden_mid, gain_two)
    normed_wide = gather_width(normed_two)
    gate = matmul(normed_wide, full_gate)
    up_proj = matmul(normed_wide, full_up)
    sigmoid_gate = jax.nn.sigmoid(gate)
    silu_gate = gate * sigmoid_gate
    mixed = (silu_gate * up_proj).astype(jnp.bfloat16)
    result = (hidden_mid + sum_width(matmul(mixed, full_down))).astype(jnp.bfloat16)
    grad_full = gather_width(cotangent)
    grad_w_down = matmul_tn(mixed, grad_full)
    grad_mixed = matmul_nt(grad_full, full_down)
    grad_gate = (grad_mixed * up_proj * sigmoid_gate * (1.0 + gate * (1.0 - sigmoid_gate))).astype(
        jnp.bfloat16
    )
    grad_up = (grad_mixed * silu_gate).astype(jnp.bfloat16)
    grad_w_gate = matmul_tn(normed_wide, grad_gate)
    grad_w_up = matmul_tn(normed_wide, grad_up)
    grad_normed_two = sum_width(matmul_nt(grad_gate, full_gate) + matmul_nt(grad_up, full_up))
    grad_back_two, grad_gain_two = norm_backward(hidden_mid, gain_two, inverse_two, grad_normed_two)
    grad_mid = cotangent.astype(jnp.float32) + grad_back_two
    grad_attn_full = gather_width(grad_mid.astype(jnp.bfloat16))
    grad_w_out = matmul_tn(attended_cols, grad_attn_full)
    grad_attended_cols = matmul_nt(grad_attn_full, full_out).astype(jnp.bfloat16)
    attended_gradient = lax.all_to_all(
        grad_attended_cols, "col", split_axis=0, concat_axis=1, tiled=True
    )
    heads_gradient = attended_gradient.reshape(
        DEVICE_TOKENS, KEY_VALUE_HEADS, query_group_width, HEAD_WIDTH
    )
    grad_query_rot, key_grads, value_grads = attention_backward(
        heads_of_queries, blocks, doc_local, place_local, log_total, attended, heads_gradient
    )
    rotated_key_gradient, grad_value = (
        lax.psum_scatter(
            key_grads.astype(jnp.bfloat16), ("row", "col"), scatter_dimension=0, tiled=True
        ).astype(jnp.float32),
        lax.psum_scatter(
            value_grads.astype(jnp.bfloat16), ("row", "col"), scatter_dimension=0, tiled=True
        ).astype(jnp.float32),
    )
    grad_query_lin = (
        rotary_embedding(
            grad_query_rot.reshape(DEVICE_TOKENS, QUERY_HEADS, HEAD_WIDTH), local_position, -1.0
        )
        .reshape(DEVICE_TOKENS, QW)
        .astype(jnp.bfloat16)
    )
    grad_key_lin = (
        rotary_embedding(
            rotated_key_gradient.reshape(DEVICE_TOKENS, KEY_VALUE_HEADS, HEAD_WIDTH),
            local_position,
            -1.0,
        )
        .reshape(DEVICE_TOKENS, KW)
        .astype(jnp.bfloat16)
    )
    grad_value_lin = grad_value.astype(jnp.bfloat16)
    query_grad_cols, key_grad_cols, value_grad_cols = (
        lax.all_to_all(grad_query_lin, "col", split_axis=1, concat_axis=0, tiled=True),
        lax.all_to_all(grad_key_lin, "col", split_axis=1, concat_axis=0, tiled=True),
        lax.all_to_all(grad_value_lin, "col", split_axis=1, concat_axis=0, tiled=True),
    )
    grad_b_query = jnp.sum(query_grad_cols.astype(jnp.float32), axis=0)
    grad_b_key = jnp.sum(key_grad_cols.astype(jnp.float32), axis=0)
    grad_b_value = jnp.sum(value_grad_cols.astype(jnp.float32), axis=0)
    grad_w_query = matmul_tn(normed_full, query_grad_cols)
    grad_w_key = matmul_tn(normed_full, key_grad_cols)
    grad_w_value = matmul_tn(normed_full, value_grad_cols)
    grad_normed_one = sum_width(
        matmul_nt(query_grad_cols, full_query)
        + matmul_nt(key_grad_cols, full_key)
        + matmul_nt(value_grad_cols, full_value)
    )
    grad_back_one, grad_gain_one = norm_backward(hidden_in, gain_one, inverse_one, grad_normed_one)
    grad_inputs = (grad_mid + grad_back_one).astype(jnp.bfloat16)
    summed = (
        lax.psum(grad_w_query.astype(jnp.bfloat16), ("dp", "row")).astype(jnp.float32),
        lax.psum(grad_w_key.astype(jnp.bfloat16), ("dp", "row")).astype(jnp.float32),
        lax.psum(grad_w_value.astype(jnp.bfloat16), ("dp", "row")).astype(jnp.float32),
        lax.psum(grad_w_out.astype(jnp.bfloat16), ("dp", "row")).astype(jnp.float32),
        lax.psum(grad_w_gate.astype(jnp.bfloat16), ("dp", "row")).astype(jnp.float32),
        lax.psum(grad_w_up.astype(jnp.bfloat16), ("dp", "row")).astype(jnp.float32),
        lax.psum(grad_w_down.astype(jnp.bfloat16), ("dp", "row")).astype(jnp.float32),
        lax.psum(grad_gain_one.astype(jnp.bfloat16), ("dp", "row")).astype(jnp.float32),
        lax.psum(grad_b_query.astype(jnp.bfloat16), ("dp", "row")).astype(jnp.float32),
        lax.psum(grad_b_key.astype(jnp.bfloat16), ("dp", "row")).astype(jnp.float32),
        lax.psum(grad_b_value.astype(jnp.bfloat16), ("dp", "row")).astype(jnp.float32),
        lax.psum(grad_gain_two.astype(jnp.bfloat16), ("dp", "row")).astype(jnp.float32),
    )
    rows_each = D // row_count
    split_dims = (0, 0, 0, 1, 0, 0, 1)
    weight_sums = tuple(
        (
            lax.dynamic_slice_in_dim(
                summed[member], row_pos * rows_each, rows_each, split_dims[member]
            )
            for member in range(7)
        )
    )
    small_sums = summed[7:]
    return (
        result,
        grad_inputs,
        small_sums[0],
        weight_sums[0],
        small_sums[1],
        weight_sums[1],
        small_sums[2],
        weight_sums[2],
        small_sums[3],
        weight_sums[3],
        small_sums[4],
        weight_sums[4],
        weight_sums[5],
        weight_sums[6],
    )


MESH = pl.DeviceIdType.MESH
NEG = -1e30
SCALE = HEAD_WIDTH ** (-0.5)


def vmem_spec():
    return pl.BlockSpec(memory_space=pltpu.VMEM)


def any_spec():
    return pl.BlockSpec(memory_space=pl.ANY)


def remote(src, dst, send_sem, recv_sem, device):
    return pltpu.make_async_remote_copy(
        src_ref=src,
        dst_ref=dst,
        send_sem=send_sem,
        recv_sem=recv_sem,
        device_id=device,
        device_id_type=MESH,
    )


def greet(peers):
    barrier = pltpu.get_barrier_semaphore()
    for peer in peers:
        pl.semaphore_signal(barrier, inc=1, device_id=peer, device_id_type=MESH)
    pl.semaphore_wait(barrier, len(peers))


def rows_at(first, count):
    return pl.ds(pl.multiple_of(first, 16), count)


def lanes_at(first, count):
    return pl.ds(pl.multiple_of(first, 128), count)


class Chain:
    def __init__(self, place, own, full, sends, recvs, count, chunks):
        self.dp, self.row, self.col = place
        self.own, self.full, self.sends, self.recvs = own, full, sends, recvs
        self.count, self.chunks = count, chunks
        self.width = full.shape[1] // count
        self.rows = full.shape[0] // chunks

    def block(self, shard, chunk):
        return self.full.at[
            rows_at(chunk * self.rows, self.rows), lanes_at(shard * self.width, self.width)
        ]

    def copy(self, way, step, shard, chunk):
        src = self.block(shard, chunk)
        if step == 0:
            src = self.own.at[rows_at(chunk * self.rows, self.rows)]
        device = (self.dp, self.row, self.col + (1 if way == 0 else -1))
        return remote(
            src,
            self.block(shard, chunk),
            self.sends.at[way, step, chunk],
            self.recvs.at[shard, chunk],
            device,
        )

    def start_own(self, chunk):
        @pl.when(self.col < self.count - 1)
        def _():
            self.copy(0, 0, self.col, chunk).start()

        @pl.when(self.col > 0)
        def _():
            self.copy(1, 0, self.col, chunk).start()

    def step(self, step, chunk):
        left, right = self.col - step, self.col + step

        @pl.when(left >= 0)
        def _():
            self.copy(0, step, left, chunk).wait_recv()

        if step < self.count - 1:

            @pl.when((left >= 0) & (self.col < self.count - 1))
            def _():
                self.copy(0, step, left, chunk).start()

        @pl.when(right < self.count)
        def _():
            self.copy(1, step, right, chunk).wait_recv()

        if step < self.count - 1:

            @pl.when((right < self.count) & (self.col > 0))
            def _():
                self.copy(1, step, right, chunk).start()

    def finish(self):
        for step in range(self.count - 1):
            left, right = self.col - step, self.col + step

            @pl.when((left >= 0) & (self.col < self.count - 1))
            def _():
                @pl.loop(0, self.chunks)
                def _(chunk):
                    self.copy(0, step, left, chunk).wait_send()

            @pl.when((right < self.count) & (self.col > 0))
            def _():
                @pl.loop(0, self.chunks)
                def _(chunk):
                    self.copy(1, step, right, chunk).wait_send()


def doc_start(lengths, place):
    first = jnp.zeros_like(place)
    end = 0
    for doc in range(lengths.shape[1]):
        end = end + lengths[0, doc]
        first = jnp.where(place >= end, end, first)
    return first


def rotate(values, cosine, sine):
    return values * cosine + pltpu.roll(values, HEAD_WIDTH // 2, 1) * sine


def allowed_keys(lengths, first_query, queries, first_key, keys):
    query = first_query + lax.broadcasted_iota(jnp.int32, (queries, 1), 0)
    key = first_key + lax.broadcasted_iota(jnp.int32, (1, keys), 1)
    return (key >= doc_start(lengths, query)) & (key <= query)


def front_kernel(
    heads,
    dims,
    aux,
    x,
    cot,
    wq,
    wkv,
    wout,
    w_gate,
    w_up,
    w_down,
    lengths,
    freq,
    x_out,
    n1_out,
    cot_out,
    q_out,
    kv_out,
    att_out,
    lse_out,
    attl_out,
    hid_out,
    n2_out,
    trig_out,
    aux_out,
    wall_out,
    wof_out,
    peer_gate,
    peer_up,
    peer_down,
    x_full,
    n1,
    cot_full,
    att_low,
    x_send,
    x_recv,
    c_send,
    c_recv,
    local_sem,
    aux_send,
    aux_recv,
    wall_send,
    wall_recv,
    z_send,
    z_recv,
    d_send,
    d_recv,
    r_send,
    r_recv,
    kv_send,
    kv_recv,
    a2a_send,
    a2a_recv,
    m_send,
    m_recv,
):
    count, planes = dims
    f32, bf16 = jnp.float32, jnp.bfloat16
    dp, row, col = lax.axis_index("dp"), lax.axis_index("row"), lax.axis_index("col")
    place = (dp, row, col)
    rows, width = x.shape
    part = rows // count
    half = wq.shape[0]
    member = lax.rem(col, 2)
    mate = col + 1 - 2 * member
    col_peers = [(dp, row, lax.rem(col + k, count)) for k in range(1, count)]
    dp_peers = [(lax.rem(dp + k, planes), row, col) for k in range(1, planes)]
    partner = (dp, 1 - row, col)
    across = (dp, 1 - row, mate)
    greet(col_peers + dp_peers + [partner, across])

    chain_x = Chain(place, x, x_full, x_send, x_recv, count, count)
    chain_c = Chain(place, cot, cot_full, c_send, c_recv, count, count)
    own_lanes = lanes_at(col * width, width)
    copy_x = pltpu.make_async_copy(x, x_full.at[:, own_lanes], local_sem.at[0])
    copy_x.start()
    aux_copies = [
        remote(aux, aux_out.at[col], aux_send.at[k], aux_recv.at[k], peer)
        for k, peer in enumerate(col_peers)
    ]
    for copy in aux_copies:
        copy.start()

    @pl.loop(0, count)
    def _(chunk):
        chain_x.start_own(chunk)

    own_half = rows_at(row * half, half)
    kv_lanes = lanes_at(width + member * HEAD_WIDTH, HEAD_WIDTH)
    copy_q = pltpu.make_async_copy(wq, wall_out.at[own_half, pl.ds(0, width)], local_sem.at[1])
    copy_kv = pltpu.make_async_copy(wkv, wall_out.at[own_half, kv_lanes], local_sem.at[2])
    copy_q.start()
    copy_kv.start()
    wall_copies = [
        remote(
            wq, wall_out.at[own_half, pl.ds(0, width)], wall_send.at[0], wall_recv.at[0], partner
        )
    ] + [
        remote(wkv, wall_out.at[own_half, kv_lanes], wall_send.at[k], wall_recv.at[k], peer)
        for k, peer in ((1, partner), (2, (dp, row, mate)), (3, across))
    ]
    for copy in wall_copies:
        copy.start()
    mlp_copies = [
        remote(src, dst, m_send.at[k], m_recv.at[k], partner)
        for k, (src, dst) in enumerate(
            ((w_gate, peer_gate), (w_up, peer_up), (w_down, peer_down))
        )
    ]
    for copy in mlp_copies:
        copy.start()
    copy_c = pltpu.make_async_copy(cot, cot_full.at[:, own_lanes], local_sem.at[3])
    copy_c.start()
    quarter = wout.shape[0] // planes
    out_lanes = lanes_at(row * half, half)

    def wof_block(shard, plane, side):
        return wof_out.at[
            shard, rows_at(plane * quarter, quarter), lanes_at(side * half, half)
        ]

    def wof_blocks(plane, side):
        return wof_out.at[:, rows_at(plane * quarter, quarter), lanes_at(side * half, half)]

    own_quarter = wout.at[rows_at(dp * quarter, quarter)]
    copy_o = pltpu.make_async_copy(own_quarter, wof_block(col, dp, row), local_sem.at[4])
    copy_o.start()

    token = row * rows + lax.broadcasted_iota(jnp.int32, (rows, 1), 0)
    position = (token - doc_start(lengths, token)).astype(f32)
    angle = position * freq[...]
    trig_out[0] = jnp.cos(angle)
    lane = lax.broadcasted_iota(jnp.int32, (1, HEAD_WIDTH), 1)
    trig_out[1] = jnp.sin(angle) * jnp.where(lane < HEAD_WIDTH // 2, -1.0, 1.0)
    aux_out[col] = aux[...]

    for step in range(1, count - 1):

        @pl.loop(0, count)
        def _(chunk):
            chain_x.step(step, chunk)

    z_copies = [
        remote(own_quarter, wof_block(col, dp, row), z_send.at[k], z_recv.at[k], peer)
        for k, peer in enumerate(col_peers)
    ]
    for copy in z_copies:
        copy.start()

    @pl.loop(0, count)
    def _(chunk):
        chain_c.start_own(chunk)

    copy_x.wait()
    copy_q.wait()
    copy_kv.wait()
    for copy in aux_copies:
        copy.wait_recv()
    for k, (side, who) in enumerate(
        ((1 - row, None), (1 - row, member), (row, 1 - member), (1 - row, 1 - member))
    ):
        side_rows = rows_at(side * half, half)
        if who is None:
            dst, src = wall_out.at[side_rows, pl.ds(0, width)], wq
        else:
            dst = wall_out.at[side_rows, lanes_at(width + who * HEAD_WIDTH, HEAD_WIDTH)]
            src = wkv
        remote(src, dst, wall_send.at[k], wall_recv.at[k], partner).wait_recv()

    mate_aux = aux_out[mate]
    even = jnp.where(member == 0, aux[3:4, :HEAD_WIDTH], mate_aux[3:4, :HEAD_WIDTH])
    odd = jnp.where(member == 0, mate_aux[3:4, :HEAD_WIDTH], aux[3:4, :HEAD_WIDTH])
    low_lanes = lane < HEAD_WIDTH // 2
    key_bias = jnp.where(low_lanes, even, pltpu.roll(odd, HEAD_WIDTH // 2, 1))
    value_bias = jnp.where(low_lanes, pltpu.roll(even, HEAD_WIDTH // 2, 1), odd)

    def kv_chunk(side, chunk):
        return kv_out.at[rows_at(side * rows + chunk * part, part)]

    def kv_copy(chunk):
        return remote(
            kv_chunk(row, chunk),
            kv_chunk(row, chunk),
            kv_send.at[chunk],
            kv_recv.at[chunk],
            partner,
        )

    @pl.loop(0, count)
    def _(chunk):
        chain_x.step(count - 1, chunk)
        here = rows_at(chunk * part, part)
        squares = jnp.zeros((part, 1), f32)
        for shard in range(count):
            piece = x_full[here, shard * width : (shard + 1) * width].astype(f32)
            squares = squares + jnp.sum(piece * piece, axis=1, keepdims=True)
        inverse = lax.rsqrt(squares / D + eps)
        for shard in range(count):
            lanes = slice(shard * width, (shard + 1) * width)
            piece = x_full[here, lanes].astype(f32)
            n1[here, lanes] = (piece * inverse * aux_out[shard, 0:1, :]).astype(bf16)
        lin = matmul(n1[here, :], wall_out[...])
        cosine, sine = trig_out[0, here, :], trig_out[1, here, :]
        for head in range(heads):
            lanes = slice(head * HEAD_WIDTH, (head + 1) * HEAD_WIDTH)
            query = (lin[:, lanes] + aux[2:3, lanes]).astype(bf16).astype(f32)
            q_out[head, here, :] = rotate(query, cosine, sine).astype(bf16)
        first = lin[:, width : width + HEAD_WIDTH]
        second = lin[:, width + HEAD_WIDTH : width + 2 * HEAD_WIDTH]
        turn = HEAD_WIDTH // 2
        key = jnp.where(low_lanes, first, pltpu.roll(second, turn, 1)) + key_bias
        value = jnp.where(low_lanes, pltpu.roll(first, turn, 1), second) + value_bias
        there = rows_at(row * rows + chunk * part, part)
        kv_out[there, :HEAD_WIDTH] = rotate(
            key.astype(bf16).astype(f32), cosine, sine
        ).astype(bf16)
        kv_out[there, HEAD_WIDTH:] = value.astype(bf16)
        kv_copy(chunk).start()

    n1_copy = pltpu.make_async_copy(n1, n1_out, local_sem.at[5])
    n1_copy.start()
    x_copy = pltpu.make_async_copy(x_full, x_out, local_sem.at[6])
    x_copy.start()

    copy_o.wait()
    for k in range(1, count):
        shard = lax.rem(col + count - k, count)
        remote(
            own_quarter, wof_block(shard, dp, row), z_send.at[k - 1], z_recv.at[k - 1], partner
        ).wait_recv()
    d_copies = [
        remote(wof_blocks(dp, row), wof_blocks(dp, row), d_send.at[k], d_recv.at[k], peer)
        for k, peer in enumerate(dp_peers)
    ]
    r_copies = [
        remote(
            wof_blocks(lax.rem(dp + planes - k, planes), row),
            wof_blocks(lax.rem(dp + planes - k, planes), row),
            r_send.at[k],
            r_recv.at[k],
            partner,
        )
        for k in range(planes)
    ]
    for copy in d_copies:
        copy.start()
    r_copies[0].start()

    @pl.loop(0, count)
    def _(chunk):
        remote(
            kv_chunk(row, chunk),
            kv_chunk(1 - row, chunk),
            kv_send.at[chunk],
            kv_recv.at[chunk],
            partner,
        ).wait_recv()

    span = min(512, rows)

    def a2a_copy(block):
        return remote(
            att_low.at[block],
            attl_out.at[:, own_lanes],
            a2a_send.at[block],
            a2a_recv.at[col],
            (dp, row, block),
        )

    @pl.loop(0, count)
    def _(block):
        here = rows_at(block * part, part)
        first_query = row * rows + block * part
        query = q_out[:, here, :].reshape(heads * part, HEAD_WIDTH)

        def body(index, state):
            largest, total, acc = state
            keys = rows_at(index * span, span)
            scores = matmul_nt(query, kv_out[keys, :HEAD_WIDTH]) * SCALE
            allowed = allowed_keys(lengths, first_query, part, index * span, span)
            scores = jnp.where(allowed[None], scores.reshape(heads, part, span), NEG)
            scores = scores.reshape(heads * part, span)
            new = jnp.maximum(largest, jnp.max(scores, axis=1, keepdims=True))
            raised = jnp.exp(scores - new)
            alpha = jnp.exp(largest - new)
            total = total * alpha + jnp.sum(raised, axis=1, keepdims=True)
            acc = acc * alpha + matmul(raised.astype(bf16), kv_out[keys, HEAD_WIDTH:])
            return new, total, acc

        state = (
            jnp.full((heads * part, 1), NEG, f32),
            jnp.zeros((heads * part, 1), f32),
            jnp.zeros((heads * part, HEAD_WIDTH), f32),
        )
        blocks = (first_query + part + span - 1) // span
        largest, total, acc = lax.fori_loop(0, blocks, body, state)
        attended = (acc / total).reshape(heads, part, HEAD_WIDTH)
        att_out[:, here, :] = attended
        log_total = (largest + jnp.log(total)).reshape(heads, part, 1)
        lse_out[:, here, :] = jnp.broadcast_to(log_total, (heads, part, HEAD_WIDTH))
        for head in range(heads):
            lanes = slice(head * HEAD_WIDTH, (head + 1) * HEAD_WIDTH)
            att_low[block, :, lanes] = attended[head].astype(bf16)

        @pl.when(block != col)
        def _():
            a2a_copy(block).start()

        chain_c.step(1, block)

    attl_out[:, own_lanes] = att_low[col]
    for step in range(2, count - 1):

        @pl.loop(0, count)
        def _(chunk):
            chain_c.step(step, chunk)

    for k in range(1, planes):
        remote(
            wof_blocks(dp, row),
            wof_blocks(lax.rem(dp + planes - k, planes), row),
            d_send.at[k - 1],
            d_recv.at[k - 1],
            partner,
        ).wait_recv()
        r_copies[k].start()
    for k in range(planes):
        other = wof_blocks(lax.rem(dp + planes - k, planes), 1 - row)
        remote(other, other, r_send.at[k], r_recv.at[k], partner).wait_recv()

    @pl.loop(0, count)
    def _(block):
        @pl.when(block != col)
        def _():
            remote(
                att_low.at[block],
                attl_out.at[:, lanes_at(block * width, width)],
                a2a_send.at[block],
                a2a_recv.at[block],
                (dp, row, block),
            ).wait_recv()

    mine = rows_at(col * part, part)
    step_lanes = D // 4
    squares = jnp.zeros((part, 1), f32)
    for piece in range(4):
        lanes = slice(piece * step_lanes, (piece + 1) * step_lanes)
        total = x_full[mine, lanes].astype(f32)
        weights = wof_out[:, :, lanes].reshape(D, step_lanes)
        total = total + matmul(attl_out[...], weights)
        hid_out[:, lanes] = total
        squares = squares + jnp.sum(total * total, axis=1, keepdims=True)
    inverse = lax.rsqrt(squares / D + eps)
    for shard in range(count):
        lanes = slice(shard * width, (shard + 1) * width)
        n2_out[:, lanes] = (hid_out[:, lanes] * inverse * aux_out[shard, 1:2, :]).astype(bf16)

    @pl.loop(0, count)
    def _(chunk):
        chain_c.step(count - 1, chunk)

    copy_c.wait()
    c_copy = pltpu.make_async_copy(cot_full, cot_out, local_sem.at[7])
    c_copy.start()

    chain_x.finish()
    chain_c.finish()
    for copy in aux_copies + wall_copies + z_copies + d_copies + r_copies:
        copy.wait_send()
    for copy in mlp_copies:
        copy.wait()

    @pl.loop(0, count)
    def _(chunk):
        kv_copy(chunk).wait_send()

        @pl.when(chunk != col)
        def _():
            a2a_copy(chunk).wait_send()

    for copy in (n1_copy, x_copy, c_copy):
        copy.wait()


def front(dims, aux, x, cot, wq, wkv, wout, w_gate, w_up, w_down, lengths, freq):
    count, planes = dims
    rows, width = x.shape
    part = rows // count
    heads = width // HEAD_WIDTH
    f32, bf16 = jnp.float32, jnp.bfloat16
    shape = jax.ShapeDtypeStruct
    wall = width + 2 * HEAD_WIDTH
    outs = [
        (shape((rows, D), bf16), any_spec()),
        (shape((rows, D), bf16), any_spec()),
        (shape((rows, D), bf16), any_spec()),
        (shape((heads, rows, HEAD_WIDTH), bf16), vmem_spec()),
        (shape((2 * rows, 2 * HEAD_WIDTH), bf16), vmem_spec()),
        (shape((heads, rows, HEAD_WIDTH), f32), vmem_spec()),
        (shape((heads, rows, HEAD_WIDTH), f32), vmem_spec()),
        (shape((part, D), bf16), vmem_spec()),
        (shape((part, D), f32), vmem_spec()),
        (shape((part, D), bf16), vmem_spec()),
        (shape((2, rows, HEAD_WIDTH), f32), vmem_spec()),
        (shape((count,) + aux.shape, f32), vmem_spec()),
        (shape((D, wall), bf16), vmem_spec()),
        (shape((count, wout.shape[0], D), bf16), vmem_spec()),
        (shape(w_gate.shape, bf16), any_spec()),
        (shape(w_up.shape, bf16), any_spec()),
        (shape(w_down.shape, bf16), any_spec()),
    ]
    dma = pltpu.SemaphoreType.DMA
    return pl.pallas_call(
        functools.partial(front_kernel, heads, dims),
        out_shape=[o[0] for o in outs],
        in_specs=[vmem_spec()]
        + [any_spec()] * 8
        + [pl.BlockSpec(memory_space=pltpu.SMEM), vmem_spec()],
        out_specs=[o[1] for o in outs],
        scratch_shapes=[
            pltpu.VMEM((rows, D), bf16),
            pltpu.VMEM((rows, D), bf16),
            pltpu.VMEM((rows, D), bf16),
            pltpu.VMEM((count, part, width), bf16),
            dma((2, count - 1, count)),
            dma((count, count)),
            dma((2, count - 1, count)),
            dma((count, count)),
            dma((8,)),
            dma((count - 1,)),
            dma((count - 1,)),
            dma((4,)),
            dma((4,)),
            dma((count - 1,)),
            dma((count - 1,)),
            dma((planes - 1,)),
            dma((planes - 1,)),
            dma((planes,)),
            dma((planes,)),
            dma((count,)),
            dma((count,)),
            dma((count,)),
            dma((count,)),
            dma((3,)),
            dma((3,)),
        ],
        compiler_params=pltpu.CompilerParams(
            collective_id=1, has_side_effects=True, vmem_limit_bytes=52 * 2**20
        ),
        cost_estimate=pl.CostEstimate(
            flops=10 * 10**9, bytes_accessed=60 * 10**6, transcendentals=10**7
        ),
        name="front",
    )(aux, x, cot, wq, wkv, wout, w_gate, w_up, w_down, lengths, freq)

def norm_rows(hidden, gain):
    inverse = lax.rsqrt(jnp.mean(hidden * hidden, axis=1, keepdims=True) + eps)
    return ((hidden * inverse * gain[None, :]).astype(jnp.bfloat16), inverse)


def per_device(
    inputs,
    seq_lengths,
    gain_one,
    w_query,
    b_query,
    w_key,
    b_key,
    w_value,
    b_value,
    w_out,
    gain_two,
    w_gate,
    w_up,
    w_down,
    cotangent,
):
    row_pos = lax.axis_index("row")
    col_pos = lax.axis_index("col")
    row_count = lax.axis_size("row")
    col_count = lax.axis_size("col")
    rows = inputs.shape[0]
    part = rows // col_count
    seq_len = rows * row_count
    heads = QUERY_HEADS // col_count
    share = col_count // KEY_VALUE_HEADS
    groups = [[g * share + s for s in range(share)] for g in range(KEY_VALUE_HEADS)]
    f32, bf16 = jnp.float32, jnp.bfloat16

    half = HEAD_WIDTH // 2
    freq = theta_base ** (-(jnp.arange(half, dtype=f32) * 2.0) / HEAD_WIDTH)
    freq = jnp.concatenate([freq, freq]).reshape(1, HEAD_WIDTH)
    kv_cols = w_key.shape[1]
    biases = jnp.concatenate([b_key, b_value]).astype(f32)
    aux = jnp.stack(
        [gain_one, gain_two, b_query.astype(f32), jnp.pad(biases, (0, gain_one.shape[0] - 2 * kv_cols))]
    )
    aux = jnp.pad(aux, ((0, 4), (0, 0)))
    own_kv = jnp.concatenate([w_key, w_value], axis=1)
    (
        inputs_full, normed_one, cot_full, query_rot, seq_kv, attended_f32, lse, att_own, hidden_mid, normed_part, trig, aux_all, wall, wof, peer_gate, peer_up, peer_down,
    ) = front(
        (col_count, lax.axis_size("dp")), aux, inputs, cotangent, w_query, own_kv, w_out, w_gate, w_up, w_down, seq_lengths, freq
    )
    gain_one_full = aux_all[:, 0].reshape(D)
    gain_two_full = aux_all[:, 1].reshape(D)
    full_query = wall[:, : heads * HEAD_WIDTH]
    own_kv = lax.dynamic_slice_in_dim(wall, heads * HEAD_WIDTH + lax.rem(col_pos, 2) * HEAD_WIDTH, HEAD_WIDTH, 1)

    def both(own, peer, axis):
        return lax.cond(row_pos == 0, lambda: jnp.concatenate([own, peer], axis), lambda: jnp.concatenate([peer, own], axis))

    full_gate = both(w_gate, peer_gate, 0)
    full_up = both(w_up, peer_up, 0)
    full_down = both(w_down, peer_down, 1)
    full_out = wof[col_pos]
    lengths = seq_lengths[0]
    place_local = row_pos * rows + jnp.arange(rows, dtype=jnp.int32)
    doc_local, local_position = documents(lengths, place_local)
    doc_all = documents(lengths, jnp.arange(seq_len, dtype=jnp.int32))[0]

    hidden_in = inputs_full.astype(f32)
    inverse_one = norm_rows(hidden_in, gain_one_full)[1]
    blocks = key_layout(seq_kv[:, :HEAD_WIDTH], seq_kv[:, HEAD_WIDTH:], doc_all)
    heads_of_queries = query_rot.transpose(1, 0, 2)[:, None]
    attended = attended_f32.transpose(1, 0, 2)[:, None]
    log_total = lse[:, :, 0].transpose(1, 0)[:, None]
    attended_cols = attended.reshape(rows, heads * HEAD_WIDTH).astype(bf16)
    start = col_pos * part
    inverse_two = norm_rows(hidden_mid, gain_two_full)[1]
    normed_two = lax.all_gather(normed_part, "col", axis=0, tiled=True)

    gate = matmul(normed_two, full_gate)
    up_proj = matmul(normed_two, full_up)
    sigmoid_gate = jax.nn.sigmoid(gate)
    silu_gate = gate * sigmoid_gate
    mixed = (silu_gate * up_proj).astype(bf16)
    grad_mixed = matmul_nt(cot_full, full_down)
    grad_gate = (grad_mixed * up_proj * sigmoid_gate * (1.0 + gate * (1.0 - sigmoid_gate))).astype(
        bf16
    )
    grad_up = (grad_mixed * silu_gate).astype(bf16)
    grad_normed_two = lax.psum_scatter(
        (matmul_nt(grad_gate, full_gate) + matmul_nt(grad_up, full_up)).astype(bf16),
        "col",
        scatter_dimension=0,
        tiled=True,
    ).astype(f32)

    def row_sum(grad, dim):
        return lax.psum_scatter(grad.astype(bf16), "row", scatter_dimension=dim, tiled=True)

    out_partial = matmul(mixed, full_down)
    out_partial = lax.dynamic_update_slice_in_dim(
        out_partial, lax.dynamic_slice_in_dim(out_partial, start, part, 0) + hidden_mid, start, 0
    )
    result = lax.psum_scatter(out_partial.astype(bf16), "col", scatter_dimension=1, tiled=True)

    wide_sums = lax.psum(
        (
            row_sum(matmul_tn(mixed, cot_full), 1),
            row_sum(matmul_tn(normed_two, grad_gate), 0),
            row_sum(matmul_tn(normed_two, grad_up), 0),
        ),
        "dp",
    )

    scaled = grad_normed_two * gain_two_full[None, :]
    inner = jnp.sum(scaled * hidden_mid, axis=1, keepdims=True)
    grad_gain_two = jnp.sum(grad_normed_two * hidden_mid * inverse_two, axis=0)
    grad_mid = (
        lax.dynamic_slice_in_dim(cot_full, start, part, 0).astype(f32)
        + inverse_two * scaled
        - hidden_mid * (inverse_two * inverse_two * inverse_two * inner / D)
    )
    grad_mid_full = lax.all_gather(grad_mid.astype(bf16), "col", axis=0, tiled=True)
    grad_attended = matmul_nt(grad_mid_full, full_out).astype(bf16)
    grad_query_rot, key_grads, value_grads = attention_backward(
        heads_of_queries,
        blocks,
        doc_local,
        place_local,
        log_total,
        attended,
        grad_attended.reshape(rows, 1, heads, HEAD_WIDTH),
    )
    grad_w_out = row_sum(matmul_tn(attended_cols, grad_mid_full), 1)
    kv_grads = lax.psum_scatter(
        jnp.concatenate([key_grads, value_grads], axis=1).astype(bf16),
        "row",
        scatter_dimension=0,
        tiled=True,
    ).astype(f32)
    grad_key_part = rotary_embedding(kv_grads[:, None, :HEAD_WIDTH], local_position, -1.0)
    kv_part = jnp.stack(
        [grad_key_part.reshape(rows, share, kv_cols), kv_grads[:, HEAD_WIDTH:].reshape(rows, share, kv_cols)],
        axis=2,
    ).reshape(rows, 2 * HEAD_WIDTH)
    kv_grad_cols = lax.psum_scatter(
        kv_part.astype(bf16), "col", scatter_dimension=1, tiled=True, axis_index_groups=groups
    )
    query_grad_cols = (
        rotary_embedding(
            grad_query_rot.reshape(rows, heads, HEAD_WIDTH), local_position, -1.0
        )
        .reshape(rows, heads * HEAD_WIDTH)
        .astype(bf16)
    )
    grad_w_query = row_sum(matmul_tn(normed_one, query_grad_cols), 0)
    grad_w_kv = row_sum(matmul_tn(normed_one, kv_grad_cols), 0)
    (grad_w_out, grad_w_query, grad_w_kv), wide_sums = lax.optimization_barrier(
        ((grad_w_out, grad_w_query, grad_w_kv), wide_sums)
    )
    grad_w_out, grad_w_query, grad_w_kv = (
        g.astype(f32) for g in lax.psum((grad_w_out, grad_w_query, grad_w_kv), "dp")
    )
    grad_w_down, grad_w_gate, grad_w_up = (g.astype(f32) for g in wide_sums)
    grad_b_query = jnp.sum(query_grad_cols.astype(f32), axis=0)
    grad_b_kv = jnp.sum(kv_grad_cols.astype(f32), axis=0)
    grad_normed_one = matmul_nt(query_grad_cols, full_query) + matmul_nt(kv_grad_cols, own_kv)
    scaled_one = grad_normed_one * gain_one_full[None, :]
    inner_one = jnp.sum(scaled_one * hidden_in, axis=1, keepdims=True)
    grad_gain_one = jnp.sum(grad_normed_one * hidden_in * inverse_one, axis=0)
    back_one = inverse_one * scaled_one - hidden_in * (
        inverse_one * inverse_one * inverse_one * inner_one / D
    )
    back_one = lax.dynamic_update_slice_in_dim(
        back_one, lax.dynamic_slice_in_dim(back_one, start, part, 0) + grad_mid, start, 0
    )
    grad_inputs = lax.psum_scatter(back_one.astype(bf16), "col", scatter_dimension=1, tiled=True)
    gains = lax.psum_scatter(
        jnp.stack([grad_gain_one, grad_gain_two]), "col", scatter_dimension=1, tiled=True
    )
    width = gains.shape[1]
    small = jnp.concatenate([gains.reshape(-1), grad_b_query, grad_b_kv])
    small = lax.psum(small, ("dp", "row"))
    biases = small[2 * width :]
    return (
        result,
        grad_inputs,
        small[:width],
        grad_w_query,
        biases[:width],
        grad_w_kv[:, :kv_cols],
        biases[width : width + kv_cols],
        grad_w_kv[:, kv_cols:],
        biases[width + kv_cols :],
        grad_w_out,
        small[width : 2 * width],
        grad_w_gate,
        grad_w_up,
        grad_w_down,
    )


def solution(mesh):
    whole_heads = dict(mesh.shape) == {"dp": 4, "row": 2, "col": 4}
    return jax.shard_map(
        per_device if whole_heads else per_device_any,
        mesh=mesh,
        in_specs=(
            P(("dp", "row"), "col"),
            P("dp", None),
            P("col"),
            P("row", "col"),
            P("col"),
            P("row", "col"),
            P("col"),
            P("row", "col"),
            P("col"),
            P("col", "row"),
            P("col"),
            P("row", "col"),
            P("row", "col"),
            P("col", "row"),
            P(("dp", "row"), "col"),
        ),
        out_specs=(
            P(("dp", "row"), "col"),
            P(("dp", "row"), "col"),
            P("col"),
            P("row", "col"),
            P("col"),
            P("row", "col"),
            P("col"),
            P("row", "col"),
            P("col"),
            P("col", "row"),
            P("col"),
            P("row", "col"),
            P("row", "col"),
            P("col", "row"),
        ),
        check_vma=False,
    )
```

```python
import functools

import jax
import jax.numpy as jnp
from jax import lax
from jax.experimental import pallas as pl
from jax.experimental.pallas import tpu as pltpu
from jax.sharding import PartitionSpec as P

D = 1536
HEAD_WIDTH = 128
QUERY_HEADS = 12
KEY_VALUE_HEADS = 2
DEVICE_TOKENS = 256
QW = 1536
KW = 256


theta_base = 1000000.0
eps = 1e-06


def matmul(left, right):
    return jnp.dot(left, right, preferred_element_type=jnp.float32)


def matmul_tn(left, right):
    return lax.dot_general(
        left, right, (((0,), (0,)), ((), ())), preferred_element_type=jnp.float32
    )


def matmul_nt(left, right):
    return lax.dot_general(
        left, right, (((1,), (1,)), ((), ())), preferred_element_type=jnp.float32
    )


def row_squares(values):
    return lax.psum(values, "col")


def gather_width(values):
    return lax.all_gather(values, "col", axis=1, tiled=True)


def sum_width(values):
    return lax.psum_scatter(
        values.astype(jnp.bfloat16), "col", scatter_dimension=1, tiled=True
    ).astype(jnp.float32)


def documents(lengths, places):
    doc_ends = jnp.cumsum(lengths)
    doc_starts = doc_ends - lengths
    doc_index = jnp.sum((places[:, None] >= doc_ends[None, :]).astype(jnp.int32), axis=1)
    chosen = doc_index[:, None] == jnp.arange(lengths.shape[0], dtype=jnp.int32)[None, :]
    offset = jnp.sum(jnp.where(chosen, doc_starts[None, :], 0), axis=1)
    return (doc_index, places - offset)


def rotary_embedding(values, token_position, direction):
    half_size = HEAD_WIDTH // 2
    frequency = theta_base ** (-(jnp.arange(half_size, dtype=jnp.float32) * 2.0) / HEAD_WIDTH)
    angles = token_position.astype(jnp.float32)[:, None] * frequency[None, :]
    cosine = jnp.cos(angles)[:, None, :]
    sine_part = direction * jnp.sin(angles)[:, None, :]
    leading = values[..., :half_size]
    second = values[..., half_size:]
    return jnp.concatenate(
        [leading * cosine - second * sine_part, second * cosine + leading * sine_part], axis=-1
    )


def norm_forward(hidden, gain):
    square_total = row_squares(jnp.sum(hidden * hidden, axis=1))
    inverse = lax.rsqrt(square_total / D + eps)
    normed = (hidden * inverse[:, None] * gain[None, :]).astype(jnp.bfloat16)
    return (normed, inverse)


def norm_backward(hidden, gain, inverse, grad_normed):
    scaled = grad_normed * gain[None, :]
    inner = row_squares(jnp.sum(scaled * hidden, axis=1))
    grad_hidden = (
        inverse[:, None] * scaled - hidden * (inverse * inverse * inverse * inner / D)[:, None]
    )
    grad_gain = jnp.sum(grad_normed * hidden * inverse[:, None], axis=0)
    return (grad_hidden, grad_gain)


def key_layout(gathered_keys, gathered_values, doc_all):
    seq_len = gathered_keys.shape[0]
    key_block_index = min(512, seq_len)
    count_blocks = seq_len // key_block_index
    blocks_of_keys = gathered_keys.reshape(
        count_blocks, key_block_index, gathered_keys.shape[1] // HEAD_WIDTH, HEAD_WIDTH
    )
    blocks_of_values = gathered_values.reshape(
        count_blocks, key_block_index, gathered_values.shape[1] // HEAD_WIDTH, HEAD_WIDTH
    )
    doc_blocks = doc_all.reshape(count_blocks, key_block_index)
    place_blocks = jnp.arange(seq_len, dtype=jnp.int32).reshape(count_blocks, key_block_index)
    return (blocks_of_keys, doc_blocks, place_blocks, blocks_of_values)


def block_scores(heads_of_queries, key_blk, doc_blk, place_blk, doc_local, place_local):
    scores = jnp.einsum(
        "tkgh,skh->tkgs", heads_of_queries, key_blk, preferred_element_type=jnp.float32
    ) * HEAD_WIDTH ** (-0.5)
    allowed = (doc_blk[None, :] == doc_local[:, None]) & (
        place_blk[None, :] <= place_local[:, None]
    )
    return (scores, allowed[:, None, None, :])


def attention_forward(heads_of_queries, blocks, doc_local, place_local):
    head_shape = heads_of_queries.shape[:3]

    def first_pass(state_in, packed):
        running_max, running_sum = state_in
        scores, allowed = block_scores(
            heads_of_queries, packed[0], packed[1], packed[2], doc_local, place_local
        )
        masked = jnp.where(allowed, scores, -1e30)
        new_max = jnp.maximum(running_max, jnp.max(masked, axis=-1))
        raised = jnp.where(allowed, jnp.exp(scores - new_max[..., None]), 0.0)
        running_sum = running_sum * jnp.exp(running_max - new_max) + jnp.sum(raised, axis=-1)
        return ((new_max, running_sum), None)

    initial = (jnp.full(head_shape, -1e30, jnp.float32), jnp.zeros(head_shape, jnp.float32))
    (running_max, running_sum), unused = lax.scan(first_pass, initial, blocks)
    log_total = running_max + jnp.log(running_sum)

    def second_pass(acc_out, packed):
        scores, allowed = block_scores(
            heads_of_queries, packed[0], packed[1], packed[2], doc_local, place_local
        )
        probs_low = jnp.where(allowed, jnp.exp(scores - log_total[..., None]), 0.0).astype(
            jnp.bfloat16
        )
        return (
            acc_out
            + jnp.einsum(
                "tkgs,skh->tkgh", probs_low, packed[3], preferred_element_type=jnp.float32
            ),
            None,
        )

    attended, unused = lax.scan(second_pass, jnp.zeros(heads_of_queries.shape, jnp.float32), blocks)
    return (attended, log_total)


def attention_backward(
    heads_of_queries, blocks, doc_local, place_local, log_total, attended, heads_gradient
):
    inner = jnp.sum(heads_gradient.astype(jnp.float32) * attended, axis=-1)
    scale_factor = HEAD_WIDTH ** (-0.5)

    def back_pass(grad_query, packed):
        scores, allowed = block_scores(
            heads_of_queries, packed[0], packed[1], packed[2], doc_local, place_local
        )
        probs = jnp.where(allowed, jnp.exp(scores - log_total[..., None]), 0.0)
        grad_probs = jnp.einsum(
            "tkgh,skh->tkgs", heads_gradient, packed[3], preferred_element_type=jnp.float32
        )
        grad_scores = (probs * (grad_probs - inner[..., None])).astype(jnp.bfloat16)
        grad_query = (
            grad_query
            + jnp.einsum(
                "tkgs,skh->tkgh", grad_scores, packed[0], preferred_element_type=jnp.float32
            )
            * scale_factor
        )
        grad_key = (
            jnp.einsum(
                "tkgs,tkgh->skh", grad_scores, heads_of_queries, preferred_element_type=jnp.float32
            )
            * scale_factor
        )
        grad_value = jnp.einsum(
            "tkgs,tkgh->skh",
            probs.astype(jnp.bfloat16),
            heads_gradient,
            preferred_element_type=jnp.float32,
        )
        return (grad_query, (grad_key, grad_value))

    grad_query, (key_grads, value_grads) = lax.scan(
        back_pass, jnp.zeros(heads_of_queries.shape, jnp.float32), blocks
    )
    seq_len = key_grads.shape[0] * key_grads.shape[1]
    return (grad_query, key_grads.reshape(seq_len, -1), value_grads.reshape(seq_len, -1))


def per_device_any(
    inputs,
    seq_lengths,
    gain_one,
    w_query,
    b_query,
    w_key,
    b_key,
    w_value,
    b_value,
    w_out,
    gain_two,
    w_gate,
    w_up,
    w_down,
    cotangent,
):
    full_query, full_key, full_value, full_out, full_gate, full_up, full_down = (
        lax.all_gather(w_query, "row", axis=0, tiled=True),
        lax.all_gather(w_key, "row", axis=0, tiled=True),
        lax.all_gather(w_value, "row", axis=0, tiled=True),
        lax.all_gather(w_out, "row", axis=1, tiled=True),
        lax.all_gather(w_gate, "row", axis=0, tiled=True),
        lax.all_gather(w_up, "row", axis=0, tiled=True),
        lax.all_gather(w_down, "row", axis=1, tiled=True),
    )
    row_pos = lax.axis_index("row")
    col_pos = lax.axis_index("col")
    row_count = lax.axis_size("row")
    col_count = lax.axis_size("col")
    seq_len = DEVICE_TOKENS * row_count * col_count
    query_group_width = QUERY_HEADS // KEY_VALUE_HEADS
    lengths = seq_lengths[0]
    place_local = (row_pos * col_count + col_pos) * DEVICE_TOKENS + jnp.arange(
        DEVICE_TOKENS, dtype=jnp.int32
    )
    doc_local, local_position = documents(lengths, place_local)
    doc_all = documents(lengths, jnp.arange(seq_len, dtype=jnp.int32))[0]
    hidden_in = inputs.astype(jnp.float32)
    normed_one, inverse_one = norm_forward(hidden_in, gain_one)
    normed_full = gather_width(normed_one)
    query_lin = (matmul(normed_full, full_query) + b_query.astype(jnp.float32)).astype(jnp.bfloat16)
    projected_keys = (matmul(normed_full, full_key) + b_key.astype(jnp.float32)).astype(
        jnp.bfloat16
    )
    projected_values = (matmul(normed_full, full_value) + b_value.astype(jnp.float32)).astype(
        jnp.bfloat16
    )
    query_rows, rows_of_keys, value_rows = (
        lax.all_to_all(query_lin, "col", split_axis=0, concat_axis=1, tiled=True),
        lax.all_to_all(projected_keys, "col", split_axis=0, concat_axis=1, tiled=True),
        lax.all_to_all(projected_values, "col", split_axis=0, concat_axis=1, tiled=True),
    )
    rotated_queries = rotary_embedding(
        query_rows.astype(jnp.float32).reshape(DEVICE_TOKENS, QUERY_HEADS, HEAD_WIDTH),
        local_position,
        1.0,
    ).astype(jnp.bfloat16)
    rotated_keys = rotary_embedding(
        rows_of_keys.astype(jnp.float32).reshape(DEVICE_TOKENS, KEY_VALUE_HEADS, HEAD_WIDTH),
        local_position,
        1.0,
    ).astype(jnp.bfloat16)
    gathered_keys, gathered_values = (
        lax.all_gather(rotated_keys.reshape(DEVICE_TOKENS, KW), ("row", "col"), axis=0, tiled=True),
        lax.all_gather(value_rows, ("row", "col"), axis=0, tiled=True),
    )
    blocks = key_layout(gathered_keys, gathered_values, doc_all)
    heads_of_queries = rotated_queries.reshape(
        DEVICE_TOKENS, KEY_VALUE_HEADS, query_group_width, HEAD_WIDTH
    )
    attended, log_total = attention_forward(heads_of_queries, blocks, doc_local, place_local)
    attended_low = attended.reshape(DEVICE_TOKENS, QW).astype(jnp.bfloat16)
    attended_cols = lax.all_to_all(attended_low, "col", split_axis=1, concat_axis=0, tiled=True)
    hidden_mid = hidden_in + sum_width(matmul(attended_cols, full_out))
    normed_two, inverse_two = norm_forward(hidden_mid, gain_two)
    normed_wide = gather_width(normed_two)
    gate = matmul(normed_wide, full_gate)
    up_proj = matmul(normed_wide, full_up)
    sigmoid_gate = jax.nn.sigmoid(gate)
    silu_gate = gate * sigmoid_gate
    mixed = (silu_gate * up_proj).astype(jnp.bfloat16)
    result = (hidden_mid + sum_width(matmul(mixed, full_down))).astype(jnp.bfloat16)
    grad_full = gather_width(cotangent)
    grad_w_down = matmul_tn(mixed, grad_full)
    grad_mixed = matmul_nt(grad_full, full_down)
    grad_gate = (grad_mixed * up_proj * sigmoid_gate * (1.0 + gate * (1.0 - sigmoid_gate))).astype(
        jnp.bfloat16
    )
    grad_up = (grad_mixed * silu_gate).astype(jnp.bfloat16)
    grad_w_gate = matmul_tn(normed_wide, grad_gate)
    grad_w_up = matmul_tn(normed_wide, grad_up)
    grad_normed_two = sum_width(matmul_nt(grad_gate, full_gate) + matmul_nt(grad_up, full_up))
    grad_back_two, grad_gain_two = norm_backward(hidden_mid, gain_two, inverse_two, grad_normed_two)
    grad_mid = cotangent.astype(jnp.float32) + grad_back_two
    grad_attn_full = gather_width(grad_mid.astype(jnp.bfloat16))
    grad_w_out = matmul_tn(attended_cols, grad_attn_full)
    grad_attended_cols = matmul_nt(grad_attn_full, full_out).astype(jnp.bfloat16)
    attended_gradient = lax.all_to_all(
        grad_attended_cols, "col", split_axis=0, concat_axis=1, tiled=True
    )
    heads_gradient = attended_gradient.reshape(
        DEVICE_TOKENS, KEY_VALUE_HEADS, query_group_width, HEAD_WIDTH
    )
    grad_query_rot, key_grads, value_grads = attention_backward(
        heads_of_queries, blocks, doc_local, place_local, log_total, attended, heads_gradient
    )
    rotated_key_gradient, grad_value = (
        lax.psum_scatter(
            key_grads.astype(jnp.bfloat16), ("row", "col"), scatter_dimension=0, tiled=True
        ).astype(jnp.float32),
        lax.psum_scatter(
            value_grads.astype(jnp.bfloat16), ("row", "col"), scatter_dimension=0, tiled=True
        ).astype(jnp.float32),
    )
    grad_query_lin = (
        rotary_embedding(
            grad_query_rot.reshape(DEVICE_TOKENS, QUERY_HEADS, HEAD_WIDTH), local_position, -1.0
        )
        .reshape(DEVICE_TOKENS, QW)
        .astype(jnp.bfloat16)
    )
    grad_key_lin = (
        rotary_embedding(
            rotated_key_gradient.reshape(DEVICE_TOKENS, KEY_VALUE_HEADS, HEAD_WIDTH),
            local_position,
            -1.0,
        )
        .reshape(DEVICE_TOKENS, KW)
        .astype(jnp.bfloat16)
    )
    grad_value_lin = grad_value.astype(jnp.bfloat16)
    query_grad_cols, key_grad_cols, value_grad_cols = (
        lax.all_to_all(grad_query_lin, "col", split_axis=1, concat_axis=0, tiled=True),
        lax.all_to_all(grad_key_lin, "col", split_axis=1, concat_axis=0, tiled=True),
        lax.all_to_all(grad_value_lin, "col", split_axis=1, concat_axis=0, tiled=True),
    )
    grad_b_query = jnp.sum(query_grad_cols.astype(jnp.float32), axis=0)
    grad_b_key = jnp.sum(key_grad_cols.astype(jnp.float32), axis=0)
    grad_b_value = jnp.sum(value_grad_cols.astype(jnp.float32), axis=0)
    grad_w_query = matmul_tn(normed_full, query_grad_cols)
    grad_w_key = matmul_tn(normed_full, key_grad_cols)
    grad_w_value = matmul_tn(normed_full, value_grad_cols)
    grad_normed_one = sum_width(
        matmul_nt(query_grad_cols, full_query)
        + matmul_nt(key_grad_cols, full_key)
        + matmul_nt(value_grad_cols, full_value)
    )
    grad_back_one, grad_gain_one = norm_backward(hidden_in, gain_one, inverse_one, grad_normed_one)
    grad_inputs = (grad_mid + grad_back_one).astype(jnp.bfloat16)
    summed = (
        lax.psum(grad_w_query.astype(jnp.bfloat16), ("dp", "row")).astype(jnp.float32),
        lax.psum(grad_w_key.astype(jnp.bfloat16), ("dp", "row")).astype(jnp.float32),
        lax.psum(grad_w_value.astype(jnp.bfloat16), ("dp", "row")).astype(jnp.float32),
        lax.psum(grad_w_out.astype(jnp.bfloat16), ("dp", "row")).astype(jnp.float32),
        lax.psum(grad_w_gate.astype(jnp.bfloat16), ("dp", "row")).astype(jnp.float32),
        lax.psum(grad_w_up.astype(jnp.bfloat16), ("dp", "row")).astype(jnp.float32),
        lax.psum(grad_w_down.astype(jnp.bfloat16), ("dp", "row")).astype(jnp.float32),
        lax.psum(grad_gain_one.astype(jnp.bfloat16), ("dp", "row")).astype(jnp.float32),
        lax.psum(grad_b_query.astype(jnp.bfloat16), ("dp", "row")).astype(jnp.float32),
        lax.psum(grad_b_key.astype(jnp.bfloat16), ("dp", "row")).astype(jnp.float32),
        lax.psum(grad_b_value.astype(jnp.bfloat16), ("dp", "row")).astype(jnp.float32),
        lax.psum(grad_gain_two.astype(jnp.bfloat16), ("dp", "row")).astype(jnp.float32),
    )
    rows_each = D // row_count
    split_dims = (0, 0, 0, 1, 0, 0, 1)
    weight_sums = tuple(
        (
            lax.dynamic_slice_in_dim(
                summed[member], row_pos * rows_each, rows_each, split_dims[member]
            )
            for member in range(7)
        )
    )
    small_sums = summed[7:]
    return (
        result,
        grad_inputs,
        small_sums[0],
        weight_sums[0],
        small_sums[1],
        weight_sums[1],
        small_sums[2],
        weight_sums[2],
        small_sums[3],
        weight_sums[3],
        small_sums[4],
        weight_sums[4],
        weight_sums[5],
        weight_sums[6],
    )


MESH = pl.DeviceIdType.MESH
NEG = -1e30
SCALE = HEAD_WIDTH ** (-0.5)


def vmem_spec():
    return pl.BlockSpec(memory_space=pltpu.VMEM)


def any_spec():
    return pl.BlockSpec(memory_space=pl.ANY)


def remote(src, dst, send_sem, recv_sem, device):
    return pltpu.make_async_remote_copy(
        src_ref=src,
        dst_ref=dst,
        send_sem=send_sem,
        recv_sem=recv_sem,
        device_id=device,
        device_id_type=MESH,
    )


def greet(peers):
    barrier = pltpu.get_barrier_semaphore()
    for peer in peers:
        pl.semaphore_signal(barrier, inc=1, device_id=peer, device_id_type=MESH)
    pl.semaphore_wait(barrier, len(peers))


def rows_at(first, count):
    return pl.ds(pl.multiple_of(first, 16), count)


def lanes_at(first, count):
    return pl.ds(pl.multiple_of(first, 128), count)


class Chain:
    def __init__(self, place, own, full, sends, recvs, count, chunks):
        self.dp, self.row, self.col = place
        self.own, self.full, self.sends, self.recvs = own, full, sends, recvs
        self.count, self.chunks = count, chunks
        self.width = full.shape[1] // count
        self.rows = full.shape[0] // chunks

    def block(self, shard, chunk):
        return self.full.at[
            rows_at(chunk * self.rows, self.rows), lanes_at(shard * self.width, self.width)
        ]

    def copy(self, way, step, shard, chunk):
        src = self.block(shard, chunk)
        if step == 0:
            src = self.own.at[rows_at(chunk * self.rows, self.rows)]
        device = (self.dp, self.row, self.col + (1 if way == 0 else -1))
        return remote(
            src,
            self.block(shard, chunk),
            self.sends.at[way, step, chunk],
            self.recvs.at[shard, chunk],
            device,
        )

    def start_own(self, chunk):
        @pl.when(self.col < self.count - 1)
        def _():
            self.copy(0, 0, self.col, chunk).start()

        @pl.when(self.col > 0)
        def _():
            self.copy(1, 0, self.col, chunk).start()

    def step(self, step, chunk):
        left, right = self.col - step, self.col + step

        @pl.when(left >= 0)
        def _():
            self.copy(0, step, left, chunk).wait_recv()

        if step < self.count - 1:

            @pl.when((left >= 0) & (self.col < self.count - 1))
            def _():
                self.copy(0, step, left, chunk).start()

        @pl.when(right < self.count)
        def _():
            self.copy(1, step, right, chunk).wait_recv()

        if step < self.count - 1:

            @pl.when((right < self.count) & (self.col > 0))
            def _():
                self.copy(1, step, right, chunk).start()

    def finish(self):
        for step in range(self.count - 1):
            left, right = self.col - step, self.col + step

            @pl.when((left >= 0) & (self.col < self.count - 1))
            def _():
                @pl.loop(0, self.chunks)
                def _(chunk):
                    self.copy(0, step, left, chunk).wait_send()

            @pl.when((right < self.count) & (self.col > 0))
            def _():
                @pl.loop(0, self.chunks)
                def _(chunk):
                    self.copy(1, step, right, chunk).wait_send()


def doc_start(lengths, place):
    first = jnp.zeros_like(place)
    end = 0
    for doc in range(lengths.shape[1]):
        end = end + lengths[0, doc]
        first = jnp.where(place >= end, end, first)
    return first


def rotate(values, cosine, sine):
    return values * cosine + pltpu.roll(values, HEAD_WIDTH // 2, 1) * sine


def allowed_keys(lengths, first_query, queries, first_key, keys):
    query = first_query + lax.broadcasted_iota(jnp.int32, (queries, 1), 0)
    key = first_key + lax.broadcasted_iota(jnp.int32, (1, keys), 1)
    return (key >= doc_start(lengths, query)) & (key <= query)


def front_kernel(
    heads,
    dims,
    aux,
    x,
    cot,
    wq,
    wkv,
    wout,
    w_gate,
    w_up,
    w_down,
    lengths,
    freq,
    x_out,
    n1_out,
    cot_out,
    q_out,
    kv_out,
    att_out,
    lse_out,
    attl_out,
    hid_out,
    n2_out,
    trig_out,
    aux_out,
    wall_out,
    wof_out,
    peer_gate,
    peer_up,
    peer_down,
    x_full,
    n1,
    cot_full,
    att_low,
    x_send,
    x_recv,
    c_send,
    c_recv,
    local_sem,
    aux_send,
    aux_recv,
    wall_send,
    wall_recv,
    z_send,
    z_recv,
    d_send,
    d_recv,
    r_send,
    r_recv,
    kv_send,
    kv_recv,
    a2a_send,
    a2a_recv,
    m_send,
    m_recv,
):
    count, planes = dims
    f32, bf16 = jnp.float32, jnp.bfloat16
    dp, row, col = lax.axis_index("dp"), lax.axis_index("row"), lax.axis_index("col")
    place = (dp, row, col)
    rows, width = x.shape
    part = rows // count
    half = wq.shape[0]
    member = lax.rem(col, 2)
    mate = col + 1 - 2 * member
    col_peers = [(dp, row, lax.rem(col + k, count)) for k in range(1, count)]
    dp_peers = [(lax.rem(dp + k, planes), row, col) for k in range(1, planes)]
    partner = (dp, 1 - row, col)
    across = (dp, 1 - row, mate)
    greet(col_peers + dp_peers + [partner, across])

    chain_x = Chain(place, x, x_full, x_send, x_recv, count, count)
    chain_c = Chain(place, cot, cot_full, c_send, c_recv, count, count)
    own_lanes = lanes_at(col * width, width)
    copy_x = pltpu.make_async_copy(x, x_full.at[:, own_lanes], local_sem.at[0])
    copy_x.start()
    aux_copies = [
        remote(aux, aux_out.at[col], aux_send.at[k], aux_recv.at[k], peer)
        for k, peer in enumerate(col_peers)
    ]
    for copy in aux_copies:
        copy.start()

    @pl.loop(0, count)
    def _(chunk):
        chain_x.start_own(chunk)

    own_half = rows_at(row * half, half)
    kv_lanes = lanes_at(width + member * HEAD_WIDTH, HEAD_WIDTH)
    copy_q = pltpu.make_async_copy(wq, wall_out.at[own_half, pl.ds(0, width)], local_sem.at[1])
    copy_kv = pltpu.make_async_copy(wkv, wall_out.at[own_half, kv_lanes], local_sem.at[2])
    copy_q.start()
    copy_kv.start()
    wall_copies = [
        remote(
            wq, wall_out.at[own_half, pl.ds(0, width)], wall_send.at[0], wall_recv.at[0], partner
        )
    ] + [
        remote(wkv, wall_out.at[own_half, kv_lanes], wall_send.at[k], wall_recv.at[k], peer)
        for k, peer in ((1, partner), (2, (dp, row, mate)), (3, across))
    ]
    for copy in wall_copies:
        copy.start()
    mlp_copies = [
        remote(src, dst, m_send.at[k], m_recv.at[k], partner)
        for k, (src, dst) in enumerate(
            ((w_gate, peer_gate), (w_up, peer_up), (w_down, peer_down))
        )
    ]
    for copy in mlp_copies:
        copy.start()
    copy_c = pltpu.make_async_copy(cot, cot_full.at[:, own_lanes], local_sem.at[3])
    copy_c.start()
    quarter = wout.shape[0] // planes
    out_lanes = lanes_at(row * half, half)

    def wof_block(shard, plane, side):
        return wof_out.at[
            shard, rows_at(plane * quarter, quarter), lanes_at(side * half, half)
        ]

    def wof_blocks(plane, side):
        return wof_out.at[:, rows_at(plane * quarter, quarter), lanes_at(side * half, half)]

    own_quarter = wout.at[rows_at(dp * quarter, quarter)]
    copy_o = pltpu.make_async_copy(own_quarter, wof_block(col, dp, row), local_sem.at[4])
    copy_o.start()

    token = row * rows + lax.broadcasted_iota(jnp.int32, (rows, 1), 0)
    position = (token - doc_start(lengths, token)).astype(f32)
    angle = position * freq[...]
    trig_out[0] = jnp.cos(angle)
    lane = lax.broadcasted_iota(jnp.int32, (1, HEAD_WIDTH), 1)
    trig_out[1] = jnp.sin(angle) * jnp.where(lane < HEAD_WIDTH // 2, -1.0, 1.0)
    aux_out[col] = aux[...]

    for step in range(1, count - 1):

        @pl.loop(0, count)
        def _(chunk):
            chain_x.step(step, chunk)

    z_copies = [
        remote(own_quarter, wof_block(col, dp, row), z_send.at[k], z_recv.at[k], peer)
        for k, peer in enumerate(col_peers)
    ]
    for copy in z_copies:
        copy.start()

    @pl.loop(0, count)
    def _(chunk):
        chain_c.start_own(chunk)

    copy_x.wait()
    copy_q.wait()
    copy_kv.wait()
    for copy in aux_copies:
        copy.wait_recv()
    for k, (side, who) in enumerate(
        ((1 - row, None), (1 - row, member), (row, 1 - member), (1 - row, 1 - member))
    ):
        side_rows = rows_at(side * half, half)
        if who is None:
            dst, src = wall_out.at[side_rows, pl.ds(0, width)], wq
        else:
            dst = wall_out.at[side_rows, lanes_at(width + who * HEAD_WIDTH, HEAD_WIDTH)]
            src = wkv
        remote(src, dst, wall_send.at[k], wall_recv.at[k], partner).wait_recv()

    mate_aux = aux_out[mate]
    even = jnp.where(member == 0, aux[3:4, :HEAD_WIDTH], mate_aux[3:4, :HEAD_WIDTH])
    odd = jnp.where(member == 0, mate_aux[3:4, :HEAD_WIDTH], aux[3:4, :HEAD_WIDTH])
    low_lanes = lane < HEAD_WIDTH // 2
    key_bias = jnp.where(low_lanes, even, pltpu.roll(odd, HEAD_WIDTH // 2, 1))
    value_bias = jnp.where(low_lanes, pltpu.roll(even, HEAD_WIDTH // 2, 1), odd)

    def kv_chunk(side, chunk):
        return kv_out.at[rows_at(side * rows + chunk * part, part)]

    def kv_copy(chunk):
        return remote(
            kv_chunk(row, chunk),
            kv_chunk(row, chunk),
            kv_send.at[chunk],
            kv_recv.at[chunk],
            partner,
        )

    @pl.loop(0, count)
    def _(chunk):
        chain_x.step(count - 1, chunk)
        here = rows_at(chunk * part, part)
        squares = jnp.zeros((part, 1), f32)
        for shard in range(count):
            piece = x_full[here, shard * width : (shard + 1) * width].astype(f32)
            squares = squares + jnp.sum(piece * piece, axis=1, keepdims=True)
        inverse = lax.rsqrt(squares / D + eps)
        for shard in range(count):
            lanes = slice(shard * width, (shard + 1) * width)
            piece = x_full[here, lanes].astype(f32)
            n1[here, lanes] = (piece * inverse * aux_out[shard, 0:1, :]).astype(bf16)
        lin = matmul(n1[here, :], wall_out[...])
        cosine, sine = trig_out[0, here, :], trig_out[1, here, :]
        for head in range(heads):
            lanes = slice(head * HEAD_WIDTH, (head + 1) * HEAD_WIDTH)
            query = (lin[:, lanes] + aux[2:3, lanes]).astype(bf16).astype(f32)
            q_out[head, here, :] = rotate(query, cosine, sine).astype(bf16)
        first = lin[:, width : width + HEAD_WIDTH]
        second = lin[:, width + HEAD_WIDTH : width + 2 * HEAD_WIDTH]
        turn = HEAD_WIDTH // 2
        key = jnp.where(low_lanes, first, pltpu.roll(second, turn, 1)) + key_bias
        value = jnp.where(low_lanes, pltpu.roll(first, turn, 1), second) + value_bias
        there = rows_at(row * rows + chunk * part, part)
        kv_out[there, :HEAD_WIDTH] = rotate(
            key.astype(bf16).astype(f32), cosine, sine
        ).astype(bf16)
        kv_out[there, HEAD_WIDTH:] = value.astype(bf16)
        kv_copy(chunk).start()

    n1_copy = pltpu.make_async_copy(n1, n1_out, local_sem.at[5])
    n1_copy.start()
    x_copy = pltpu.make_async_copy(x_full, x_out, local_sem.at[6])
    x_copy.start()

    copy_o.wait()
    for k in range(1, count):
        shard = lax.rem(col + count - k, count)
        remote(
            own_quarter, wof_block(shard, dp, row), z_send.at[k - 1], z_recv.at[k - 1], partner
        ).wait_recv()
    d_copies = [
        remote(wof_blocks(dp, row), wof_blocks(dp, row), d_send.at[k], d_recv.at[k], peer)
        for k, peer in enumerate(dp_peers)
    ]
    r_copies = [
        remote(
            wof_blocks(lax.rem(dp + planes - k, planes), row),
            wof_blocks(lax.rem(dp + planes - k, planes), row),
            r_send.at[k],
            r_recv.at[k],
            partner,
        )
        for k in range(planes)
    ]
    for copy in d_copies:
        copy.start()
    r_copies[0].start()

    @pl.loop(0, count)
    def _(chunk):
        remote(
            kv_chunk(row, chunk),
            kv_chunk(1 - row, chunk),
            kv_send.at[chunk],
            kv_recv.at[chunk],
            partner,
        ).wait_recv()

    span = min(512, rows)

    def a2a_copy(block):
        return remote(
            att_low.at[block],
            attl_out.at[:, own_lanes],
            a2a_send.at[block],
            a2a_recv.at[col],
            (dp, row, block),
        )

    @pl.loop(0, count)
    def _(block):
        here = rows_at(block * part, part)
        first_query = row * rows + block * part
        query = q_out[:, here, :].reshape(heads * part, HEAD_WIDTH)

        def body(index, state):
            largest, total, acc = state
            keys = rows_at(index * span, span)
            scores = matmul_nt(query, kv_out[keys, :HEAD_WIDTH]) * SCALE
            allowed = allowed_keys(lengths, first_query, part, index * span, span)
            scores = jnp.where(allowed[None], scores.reshape(heads, part, span), NEG)
            scores = scores.reshape(heads * part, span)
            new = jnp.maximum(largest, jnp.max(scores, axis=1, keepdims=True))
            raised = jnp.exp(scores - new)
            alpha = jnp.exp(largest - new)
            total = total * alpha + jnp.sum(raised, axis=1, keepdims=True)
            acc = acc * alpha + matmul(raised.astype(bf16), kv_out[keys, HEAD_WIDTH:])
            return new, total, acc

        state = (
            jnp.full((heads * part, 1), NEG, f32),
            jnp.zeros((heads * part, 1), f32),
            jnp.zeros((heads * part, HEAD_WIDTH), f32),
        )
        blocks = (first_query + part + span - 1) // span
        largest, total, acc = lax.fori_loop(0, blocks, body, state)
        attended = (acc / total).reshape(heads, part, HEAD_WIDTH)
        att_out[:, here, :] = attended
        log_total = (largest + jnp.log(total)).reshape(heads, part, 1)
        lse_out[:, here, :] = jnp.broadcast_to(log_total, (heads, part, HEAD_WIDTH))
        for head in range(heads):
            lanes = slice(head * HEAD_WIDTH, (head + 1) * HEAD_WIDTH)
            att_low[block, :, lanes] = attended[head].astype(bf16)

        @pl.when(block != col)
        def _():
            a2a_copy(block).start()

        chain_c.step(1, block)

    attl_out[:, own_lanes] = att_low[col]
    for step in range(2, count - 1):

        @pl.loop(0, count)
        def _(chunk):
            chain_c.step(step, chunk)

    for k in range(1, planes):
        remote(
            wof_blocks(dp, row),
            wof_blocks(lax.rem(dp + planes - k, planes), row),
            d_send.at[k - 1],
            d_recv.at[k - 1],
            partner,
        ).wait_recv()
        r_copies[k].start()
    for k in range(planes):
        other = wof_blocks(lax.rem(dp + planes - k, planes), 1 - row)
        remote(other, other, r_send.at[k], r_recv.at[k], partner).wait_recv()

    @pl.loop(0, count)
    def _(block):
        @pl.when(block != col)
        def _():
            remote(
                att_low.at[block],
                attl_out.at[:, lanes_at(block * width, width)],
                a2a_send.at[block],
                a2a_recv.at[block],
                (dp, row, block),
            ).wait_recv()

    mine = rows_at(col * part, part)
    step_lanes = D // 4
    squares = jnp.zeros((part, 1), f32)
    for piece in range(4):
        lanes = slice(piece * step_lanes, (piece + 1) * step_lanes)
        total = x_full[mine, lanes].astype(f32)
        weights = wof_out[:, :, lanes].reshape(D, step_lanes)
        total = total + matmul(attl_out[...], weights)
        hid_out[:, lanes] = total
        squares = squares + jnp.sum(total * total, axis=1, keepdims=True)
    inverse = lax.rsqrt(squares / D + eps)
    for shard in range(count):
        lanes = slice(shard * width, (shard + 1) * width)
        n2_out[:, lanes] = (hid_out[:, lanes] * inverse * aux_out[shard, 1:2, :]).astype(bf16)

    @pl.loop(0, count)
    def _(chunk):
        chain_c.step(count - 1, chunk)

    copy_c.wait()
    c_copy = pltpu.make_async_copy(cot_full, cot_out, local_sem.at[7])
    c_copy.start()

    chain_x.finish()
    chain_c.finish()
    for copy in aux_copies + wall_copies + z_copies + d_copies + r_copies:
        copy.wait_send()
    for copy in mlp_copies:
        copy.wait()

    @pl.loop(0, count)
    def _(chunk):
        kv_copy(chunk).wait_send()

        @pl.when(chunk != col)
        def _():
            a2a_copy(chunk).wait_send()

    for copy in (n1_copy, x_copy, c_copy):
        copy.wait()


def front(dims, aux, x, cot, wq, wkv, wout, w_gate, w_up, w_down, lengths, freq):
    count, planes = dims
    rows, width = x.shape
    part = rows // count
    heads = width // HEAD_WIDTH
    f32, bf16 = jnp.float32, jnp.bfloat16
    shape = jax.ShapeDtypeStruct
    wall = width + 2 * HEAD_WIDTH
    outs = [
        (shape((rows, D), bf16), any_spec()),
        (shape((rows, D), bf16), any_spec()),
        (shape((rows, D), bf16), any_spec()),
        (shape((heads, rows, HEAD_WIDTH), bf16), vmem_spec()),
        (shape((2 * rows, 2 * HEAD_WIDTH), bf16), vmem_spec()),
        (shape((heads, rows, HEAD_WIDTH), f32), vmem_spec()),
        (shape((heads, rows, HEAD_WIDTH), f32), vmem_spec()),
        (shape((part, D), bf16), vmem_spec()),
        (shape((part, D), f32), vmem_spec()),
        (shape((part, D), bf16), vmem_spec()),
        (shape((2, rows, HEAD_WIDTH), f32), vmem_spec()),
        (shape((count,) + aux.shape, f32), vmem_spec()),
        (shape((D, wall), bf16), vmem_spec()),
        (shape((count, wout.shape[0], D), bf16), vmem_spec()),
        (shape(w_gate.shape, bf16), any_spec()),
        (shape(w_up.shape, bf16), any_spec()),
        (shape(w_down.shape, bf16), any_spec()),
    ]
    dma = pltpu.SemaphoreType.DMA
    return pl.pallas_call(
        functools.partial(front_kernel, heads, dims),
        out_shape=[o[0] for o in outs],
        in_specs=[vmem_spec()]
        + [any_spec()] * 8
        + [pl.BlockSpec(memory_space=pltpu.SMEM), vmem_spec()],
        out_specs=[o[1] for o in outs],
        scratch_shapes=[
            pltpu.VMEM((rows, D), bf16),
            pltpu.VMEM((rows, D), bf16),
            pltpu.VMEM((rows, D), bf16),
            pltpu.VMEM((count, part, width), bf16),
            dma((2, count - 1, count)),
            dma((count, count)),
            dma((2, count - 1, count)),
            dma((count, count)),
            dma((8,)),
            dma((count - 1,)),
            dma((count - 1,)),
            dma((4,)),
            dma((4,)),
            dma((count - 1,)),
            dma((count - 1,)),
            dma((planes - 1,)),
            dma((planes - 1,)),
            dma((planes,)),
            dma((planes,)),
            dma((count,)),
            dma((count,)),
            dma((count,)),
            dma((count,)),
            dma((3,)),
            dma((3,)),
        ],
        compiler_params=pltpu.CompilerParams(
            collective_id=1, has_side_effects=True, vmem_limit_bytes=52 * 2**20
        ),
        cost_estimate=pl.CostEstimate(
            flops=10 * 10**9, bytes_accessed=60 * 10**6, transcendentals=10**7
        ),
        name="front",
    )(aux, x, cot, wq, wkv, wout, w_gate, w_up, w_down, lengths, freq)
TICKS = ((0, 1, 2, 4, 6, 7, 5, 3), (2, 3, 0, 4, 1, 6, 7, 5), (4, 5, 6, 2, 7, 0, 1, 3), (6, 7, 4, 2, 0, 1, 3, 5))
SLOTS = tuple(tuple(order.index(q) for q in range(8)) for order in TICKS)
ONWARD = (
    ((), (0, 1, 3), (2, 0, 1, 3, 5), ()),
    ((), (4, 6, 7, 5, 3), (6, 7, 5), ()),
)
SUMS = (
    ((2, 0), (4, 0), (6, 0), (7, 0), (5, 0), (3, 0)),
    ((4, 0), (6, 0), (7, 0), (0, 1), (5, 0), (1, 1)),
    ((2, 1), (0, 1), (1, 1), (6, 0), (3, 1), (7, 0)),
    ((4, 1), (2, 1), (0, 1), (1, 1), (3, 1), (5, 1)),
)
LINE = 4


def pick(index, values):
    out = values[0]
    for k, value in enumerate(values[1:], 1):
        out = jnp.where(index == k, value, out)
    return out


def hidden_tiles(total):
    tile = 512
    return [(first, min(tile, total - first)) for first in range(0, total, tile)]


def mlp_kernel(
    n2,
    cot_full,
    hid,
    aux_all,
    own_gate,
    own_up,
    own_down,
    peer_gate,
    peer_up,
    peer_down,
    out_part,
    sum_down,
    sum_gate,
    sum_up,
    grad_mid,
    grad_gain,
    gate_w,
    up_w,
    down_w,
    mixed,
    g_gate,
    g_up,
    n2s,
    cots,
    parts,
    coming,
    stage,
    w_sem,
    cot_sem,
    own_sem,
    ag_send,
    ag_recv,
    rs_send,
    rs_recv,
    out_sem,
    sum_sem,
    free_sem,
    swap_send,
    swap_recv,
):
    f32, bf16 = jnp.float32, jnp.bfloat16
    dp, row, col = lax.axis_index("dp"), lax.axis_index("row"), lax.axis_index("col")
    part = n2.shape[0]
    piece = part // 2
    hidden, half = own_gate.shape
    tiles = hidden_tiles(hidden)
    partner = (dp, 1 - row, col)
    greet([(dp, row, lax.rem(col + k, LINE)) for k in range(1, LINE)] + [partner])

    def slot_rows(slot):
        return rows_at(slot * piece, piece)

    def hand_on(c, way, q, source=None):
        to = c + 1 - 2 * way
        src = n2s.at[slot_rows(SLOTS[c][q])] if source is None else source
        return remote(
            src, n2s.at[slot_rows(SLOTS[to][q])], ag_send.at[way, q], ag_recv.at[q], (dp, row, to)
        )

    def got(c, q):
        rows_here = n2s.at[slot_rows(SLOTS[c][q])]
        remote(rows_here, rows_here, ag_send.at[0, q], ag_recv.at[q], partner).wait_recv()

    def ways(c):
        return [way for way in (0, 1) if 0 <= c + 1 - 2 * way < LINE]

    for c in range(LINE):

        @pl.when(col == c)
        def _():
            for way in ways(c):
                hand_on(c, way, 2 * c, n2.at[pl.ds(0, piece)]).start()
            if c in (0, LINE - 1):
                hand_on(c, ways(c)[0], 2 * c + 1, n2.at[pl.ds(piece, piece)]).start()

    own_copy = pltpu.make_async_copy(n2, n2s.at[pl.ds(0, part)], own_sem)
    own_copy.start()

    def load_copies(index, first, count):
        rows_here = pl.ds(first, count)
        copies = []
        for k, (own, peer, whole) in enumerate(
            (
                (own_gate, peer_gate, gate_w),
                (own_up, peer_up, up_w),
                (own_down, peer_down, down_w),
            )
        ):
            for side, src in ((row, own), (1 - row, peer)):
                copies.append((src.at[rows_here], whole.at[rows_here, lanes_at(side * half, half)]))
        return [
            pltpu.make_async_copy(src, dst, w_sem.at[index, k])
            for k, (src, dst) in enumerate(copies)
        ]

    def cot_copy(slot):
        q = pick(col, [order[slot] for order in TICKS])
        return pltpu.make_async_copy(
            cot_full.at[slot_rows(q)], cots.at[slot_rows(slot)], cot_sem.at[slot]
        )

    for slot in range(2):
        cot_copy(slot).start()
    for index, (first, count) in enumerate(tiles):
        for copy in load_copies(index, first, count):
            copy.start()
    for slot in range(2, 2 * LINE):
        cot_copy(slot).start()
    for h in range(2):

        @pl.when(col == 0)
        def _():
            coming[h] = jnp.zeros(coming.shape[1:], bf16)

        @pl.when(col == LINE - 1)
        def _():
            coming[2 * LINE + h] = jnp.zeros(coming.shape[1:], bf16)

    own_copy.wait()

    def onward(f):
        for c in (1, 2):
            for way in (0, 1):
                if f < len(ONWARD[way][c]):
                    q = ONWARD[way][c][f]

                    @pl.when(col == c)
                    def _():
                        if q // 2 != c:
                            got(c, q)
                        hand_on(c, way, q).start()

    def sum_copy(c, q, way):
        to = c + 1 - 2 * way
        place = 2 * LINE + q % 2 if way == 1 and q // 2 == to else q
        return remote(
            parts.at[slot_rows(SLOTS[c][q])],
            coming.at[place],
            rs_send.at[q],
            rs_recv.at[place],
            (dp, row, to),
        )

    def sum_start(e, c):
        q, way = SUMS[c][e]
        sum_copy(c, q, way).start()

    def sum_ends(e):
        for c in (0, LINE - 1):

            @pl.when(col == c)
            def _():
                sum_start(e, c)

    def sum_mids(e):
        @pl.when((col == 1) | (col == 2))
        def _():
            q = jnp.where(col == 1, SUMS[1][e][0], SUMS[2][e][0])
            slot = jnp.where(col == 1, SLOTS[1][SUMS[1][e][0]], SLOTS[2][SUMS[2][e][0]])
            here = slot_rows(slot)
            remote(parts.at[here], coming.at[q], rs_send.at[q], rs_recv.at[q], partner).wait_recv()
            parts[here, :] = (parts[here, :].astype(f32) + coming[q].astype(f32)).astype(bf16)
            for c in (1, 2):

                @pl.when(col == c)
                def _():
                    sum_start(e, c)

    def out_copies(tick):
        copies = []
        for h in range(2):
            q = pick(
                tick, [pick(col, [order[2 * t + h] for order in TICKS]) for t in range(LINE)]
            )
            copies.append(
                pltpu.make_async_copy(
                    stage.at[lax.rem(tick, 2), pl.ds(h * piece, piece)],
                    out_part.at[slot_rows(q)],
                    out_sem.at[lax.rem(tick, 2), h],
                )
            )
        return copies

    lane_tiles = [(k * 512, 512) for k in range(D // 512)]

    @pl.loop(0, LINE)
    def _(tick):
        here = rows_at(tick * part, part)
        for c in (0, LINE - 1):
            for t in range(1, LINE):

                @pl.when((col == c) & (tick == t))
                def _():
                    for h in range(2):
                        got(c, TICKS[c][2 * t + h])

        for h in range(2):
            pltpu.make_async_copy(
                cot_full.at[pl.ds(0, piece)],
                cots.at[slot_rows(2 * tick + h)],
                cot_sem.at[2 * tick + h],
            ).wait()

        for index, (first, count) in enumerate(tiles):

            @pl.when(tick == 0)
            def _():
                for copy in load_copies(index, first, count):
                    copy.wait()

            rows_here, lanes = slice(first, first + count), slice(first, first + count)
            gate = matmul_nt(n2s[here, :], gate_w[rows_here, :])
            up = matmul_nt(n2s[here, :], up_w[rows_here, :])
            grad = matmul_nt(cots[here, :], down_w[rows_here, :])
            sigmoid = jax.nn.sigmoid(gate)
            silu = gate * sigmoid
            mixed[here, lanes] = (silu * up).astype(bf16)
            g_gate[here, lanes] = (grad * up * sigmoid * (1.0 + gate * (1.0 - sigmoid))).astype(
                bf16
            )
            g_up[here, lanes] = (grad * silu).astype(bf16)
            if index == 2:

                @pl.when(tick == 0)
                def _():
                    onward(0)

                @pl.when(tick == 1)
                def _():
                    onward(2)

                @pl.when(tick == 3)
                def _():
                    sum_mids(1)

        for first, count in lane_tiles:
            lanes = slice(first, first + count)
            total = matmul(g_gate[here, :], gate_w[:, lanes])
            total = total + matmul(g_up[here, :], up_w[:, lanes])
            parts[here, lanes] = total.astype(bf16)

        @pl.when(tick == 0)
        def _():
            onward(1)

        @pl.when(tick == 1)
        def _():
            onward(3)
            onward(4)
            sum_ends(0)
            sum_ends(1)

        @pl.when(tick == 2)
        def _():
            sum_ends(2)
            sum_ends(3)
            sum_mids(0)

        @pl.when(tick == 3)
        def _():
            sum_ends(4)
            sum_ends(5)
            sum_mids(2)
            sum_mids(3)

        @pl.when(tick >= 2)
        def _():
            for copy in out_copies(tick - 2):
                copy.wait()

        own = jnp.where(tick == 0, 1.0, 0.0)
        for first, count in lane_tiles:
            lanes = slice(first, first + count)
            total = matmul(mixed[here, :], down_w[:, lanes]) + hid[:, lanes] * own
            stage[lax.rem(tick, 2), :, lanes] = total.astype(bf16)
        for copy in out_copies(tick):
            copy.start()

    pl.semaphore_signal(free_sem, inc=1, device_id=partner, device_id_type=MESH)
    pl.semaphore_wait(free_sem, 1)
    theirs, ours = lanes_at((1 - row) * half, half), lanes_at(row * half, half)
    jobs = ((mixed, cots, down_w, sum_down), (g_gate, n2s, gate_w, sum_gate), (g_up, n2s, up_w, sum_up))
    whole_tiles, tail = tiles[:-1], tiles[-1]
    tile = tiles[0][1]

    def swap_copy(k, index, rows_here):
        buffer = jobs[k][2]
        return remote(
            buffer.at[rows_here, pl.ds(0, half)],
            buffer.at[rows_here, pl.ds(half, half)],
            swap_send.at[k, index],
            swap_recv.at[k, index],
            partner,
        )

    for k, (left, right, buffer, result) in enumerate(jobs):

        def give(index, rows_here, lanes):
            buffer[rows_here, :half] = matmul_tn(left[:, lanes], right[:, theirs]).astype(bf16)
            swap_copy(k, index, rows_here).start()

        def keep(index, rows_here, lanes):
            total = matmul_tn(left[:, lanes], right[:, ours])
            swap_copy(k, index, rows_here).wait_recv()
            total = total + buffer[rows_here, half:].astype(f32)
            buffer[rows_here, half:] = total.astype(bf16)

        for act in (give, keep):

            @pl.loop(0, len(whole_tiles))
            def _(index):
                first = index * tile
                act(index, rows_at(first, tile), lanes_at(first, tile))

            act(len(whole_tiles), pl.ds(*tail), pl.ds(*tail))
        pltpu.make_async_copy(buffer.at[:, pl.ds(half, half)], result, sum_sem.at[k]).start()
        if k == 0:
            sum_mids(4)
            sum_mids(5)
        if k == 1:
            for h in range(2):
                for c in range(LINE):

                    @pl.when(col == c)
                    def _():
                        for way in ways(c):
                            place = 2 * c + h if way == 1 else 2 * LINE + h
                            remote(
                                coming.at[place],
                                coming.at[place],
                                rs_send.at[0],
                                rs_recv.at[place],
                                partner,
                            ).wait_recv()

            width = aux_all.shape[2]
            squares = jnp.zeros((part, 1), f32)
            inner = jnp.zeros((part, 1), f32)
            for shard in range(LINE):
                lanes = slice(shard * width, (shard + 1) * width)
                middle = hid[:, lanes]
                from_left = jnp.concatenate([coming[2 * col + h, :, lanes] for h in range(2)])
                from_right = jnp.concatenate([coming[2 * LINE + h, :, lanes] for h in range(2)])
                total = parts[:part, lanes].astype(f32) + from_left.astype(f32)
                total = total + from_right.astype(f32)
                grad_mid[:, lanes] = total
                squares = squares + jnp.sum(middle * middle, axis=1, keepdims=True)
                scaled = total * aux_all[shard, 1:2, :]
                inner = inner + jnp.sum(scaled * middle, axis=1, keepdims=True)
            inverse = lax.rsqrt(squares / D + eps)
            factor = inverse * inverse * inverse * inner / D
            for shard in range(LINE):
                lanes = slice(shard * width, (shard + 1) * width)
                middle, total = hid[:, lanes], grad_mid[:, lanes]
                gain = jnp.sum(total * middle * inverse, axis=0, keepdims=True)
                grad_gain[:, lanes] = jnp.broadcast_to(gain, (8, width))
                grad_mid[:, lanes] = (
                    cots[:part, lanes].astype(f32)
                    + inverse * total * aux_all[shard, 1:2, :]
                    - middle * factor
                )

    for k, (left, right, buffer, result) in enumerate(jobs):
        for index, place in enumerate(tiles):
            swap_copy(k, index, pl.ds(*place)).wait_send()
        pltpu.make_async_copy(buffer.at[:, pl.ds(half, half)], result, sum_sem.at[k]).wait()
    for tick in (LINE - 2, LINE - 1):
        for copy in out_copies(tick):
            copy.wait()
    for c in range(LINE):

        @pl.when(col == c)
        def _():
            for way in ways(c):
                hand_on(c, way, 2 * c, n2.at[pl.ds(0, piece)]).wait_send()
                if c in (0, LINE - 1):
                    hand_on(c, way, 2 * c + 1, n2.at[pl.ds(piece, piece)]).wait_send()
                for q in ONWARD[way][c]:
                    hand_on(c, way, q).wait_send()
            for q, way in SUMS[c]:
                sum_copy(c, q, way).wait_send()


def mlp(n2, cot_full, hid, aux_all, own, peer):
    f32, bf16 = jnp.float32, jnp.bfloat16
    rows = cot_full.shape[0]
    part = n2.shape[0]
    hidden, half = own[0].shape
    shape = jax.ShapeDtypeStruct
    dma = pltpu.SemaphoreType.DMA
    outs = [(shape((rows, D), bf16), any_spec())]
    outs += [(shape((hidden, half), bf16), any_spec())] * 3
    outs += [(shape((part, D), f32), vmem_spec()), (shape((8, D), f32), vmem_spec())]
    wide = pltpu.VMEM((hidden, D), bf16)
    tall = pltpu.VMEM((rows, hidden), bf16)
    full = pltpu.VMEM((rows, D), bf16)
    return pl.pallas_call(
        mlp_kernel,
        out_shape=[o[0] for o in outs],
        in_specs=[any_spec(), any_spec(), vmem_spec(), vmem_spec()] + [any_spec()] * 6,
        out_specs=[o[1] for o in outs],
        scratch_shapes=[
            wide,
            wide,
            wide,
            tall,
            tall,
            tall,
            full,
            full,
            full,
            pltpu.VMEM((2 * LINE + 2, part // 2, D), bf16),
            pltpu.VMEM((2, part, D), bf16),
            dma((len(hidden_tiles(hidden)), 6)),
            dma((2 * LINE,)),
            dma,
            dma((2, 2 * LINE)),
            dma((2 * LINE,)),
            dma((2 * LINE,)),
            dma((2 * LINE + 2,)),
            dma((2, 2)),
            dma((3,)),
            pltpu.SemaphoreType.REGULAR,
            dma((3, len(hidden_tiles(hidden)))),
            dma((3, len(hidden_tiles(hidden)))),
        ],
        compiler_params=pltpu.CompilerParams(
            collective_id=2, has_side_effects=True, vmem_limit_bytes=62 * 2**20
        ),
        cost_estimate=pl.CostEstimate(
            flops=64 * 10**9, bytes_accessed=60 * 10**6, transcendentals=10**7
        ),
        name="mlp",
    )(n2, cot_full, hid, aux_all, *own, *peer)


def norm_rows(hidden, gain):
    inverse = lax.rsqrt(jnp.mean(hidden * hidden, axis=1, keepdims=True) + eps)
    return ((hidden * inverse * gain[None, :]).astype(jnp.bfloat16), inverse)


def per_device(
    inputs,
    seq_lengths,
    gain_one,
    w_query,
    b_query,
    w_key,
    b_key,
    w_value,
    b_value,
    w_out,
    gain_two,
    w_gate,
    w_up,
    w_down,
    cotangent,
):
    row_pos = lax.axis_index("row")
    col_pos = lax.axis_index("col")
    row_count = lax.axis_size("row")
    col_count = lax.axis_size("col")
    rows = inputs.shape[0]
    part = rows // col_count
    seq_len = rows * row_count
    heads = QUERY_HEADS // col_count
    share = col_count // KEY_VALUE_HEADS
    groups = [[g * share + s for s in range(share)] for g in range(KEY_VALUE_HEADS)]
    f32, bf16 = jnp.float32, jnp.bfloat16

    half = HEAD_WIDTH // 2
    freq = theta_base ** (-(jnp.arange(half, dtype=f32) * 2.0) / HEAD_WIDTH)
    freq = jnp.concatenate([freq, freq]).reshape(1, HEAD_WIDTH)
    kv_cols = w_key.shape[1]
    biases = jnp.concatenate([b_key, b_value]).astype(f32)
    aux = jnp.stack(
        [gain_one, gain_two, b_query.astype(f32), jnp.pad(biases, (0, gain_one.shape[0] - 2 * kv_cols))]
    )
    aux = jnp.pad(aux, ((0, 4), (0, 0)))
    own_kv = jnp.concatenate([w_key, w_value], axis=1)
    (
        inputs_full, normed_one, cot_full, query_rot, seq_kv, attended_f32, lse, att_own, hidden_mid, normed_part, trig, aux_all, wall, wof, peer_gate, peer_up, peer_down,
    ) = front(
        (col_count, lax.axis_size("dp")), aux, inputs, cotangent, w_query, own_kv, w_out, w_gate.T, w_up.T, w_down, seq_lengths, freq
    )
    gain_one_full = aux_all[:, 0].reshape(D)
    gain_two_full = aux_all[:, 1].reshape(D)
    full_query = wall[:, : heads * HEAD_WIDTH]
    own_kv = lax.dynamic_slice_in_dim(wall, heads * HEAD_WIDTH + lax.rem(col_pos, 2) * HEAD_WIDTH, HEAD_WIDTH, 1)

    full_out = wof[col_pos]
    lengths = seq_lengths[0]
    place_local = row_pos * rows + jnp.arange(rows, dtype=jnp.int32)
    doc_local, local_position = documents(lengths, place_local)
    doc_all = documents(lengths, jnp.arange(seq_len, dtype=jnp.int32))[0]

    hidden_in = inputs_full.astype(f32)
    inverse_one = norm_rows(hidden_in, gain_one_full)[1]
    blocks = key_layout(seq_kv[:, :HEAD_WIDTH], seq_kv[:, HEAD_WIDTH:], doc_all)
    heads_of_queries = query_rot.transpose(1, 0, 2)[:, None]
    attended = attended_f32.transpose(1, 0, 2)[:, None]
    log_total = lse[:, :, 0].transpose(1, 0)[:, None]
    attended_cols = attended.reshape(rows, heads * HEAD_WIDTH).astype(bf16)
    start = col_pos * part
    out_part, sum_down, sum_gate, sum_up, grad_mid, grad_gain_two = mlp(
        normed_part,
        cot_full,
        hidden_mid,
        aux_all,
        (w_gate.T, w_up.T, w_down),
        (peer_gate, peer_up, peer_down),
    )
    grad_gain_two = grad_gain_two[0]
    result = lax.psum_scatter(out_part, "col", scatter_dimension=1, tiled=True)
    wide_sums = lax.psum((sum_down, sum_gate, sum_up), "dp")

    def row_sum(grad, dim):
        return lax.psum_scatter(grad.astype(bf16), "row", scatter_dimension=dim, tiled=True)

    grad_mid_full = lax.all_gather(grad_mid.astype(bf16), "col", axis=0, tiled=True)
    grad_attended = matmul_nt(grad_mid_full, full_out).astype(bf16)
    grad_query_rot, key_grads, value_grads = attention_backward(
        heads_of_queries,
        blocks,
        doc_local,
        place_local,
        log_total,
        attended,
        grad_attended.reshape(rows, 1, heads, HEAD_WIDTH),
    )
    grad_w_out = row_sum(matmul_tn(attended_cols, grad_mid_full), 1)
    kv_grads = lax.psum_scatter(
        jnp.concatenate([key_grads, value_grads], axis=1).astype(bf16),
        "row",
        scatter_dimension=0,
        tiled=True,
    ).astype(f32)
    grad_key_part = rotary_embedding(kv_grads[:, None, :HEAD_WIDTH], local_position, -1.0)
    kv_part = jnp.stack(
        [grad_key_part.reshape(rows, share, kv_cols), kv_grads[:, HEAD_WIDTH:].reshape(rows, share, kv_cols)],
        axis=2,
    ).reshape(rows, 2 * HEAD_WIDTH)
    kv_grad_cols = lax.psum_scatter(
        kv_part.astype(bf16), "col", scatter_dimension=1, tiled=True, axis_index_groups=groups
    )
    query_grad_cols = (
        rotary_embedding(
            grad_query_rot.reshape(rows, heads, HEAD_WIDTH), local_position, -1.0
        )
        .reshape(rows, heads * HEAD_WIDTH)
        .astype(bf16)
    )
    grad_w_query = row_sum(matmul_tn(normed_one, query_grad_cols), 0)
    grad_w_kv = row_sum(matmul_tn(normed_one, kv_grad_cols), 0)
    (grad_w_out, grad_w_query, grad_w_kv), wide_sums = lax.optimization_barrier(
        ((grad_w_out, grad_w_query, grad_w_kv), wide_sums)
    )
    grad_w_out, grad_w_query, grad_w_kv = (
        g.astype(f32) for g in lax.psum((grad_w_out, grad_w_query, grad_w_kv), "dp")
    )
    grad_w_down, grad_w_gate, grad_w_up = (g.astype(f32) for g in wide_sums)
    grad_w_gate, grad_w_up = grad_w_gate.T, grad_w_up.T
    grad_b_query = jnp.sum(query_grad_cols.astype(f32), axis=0)
    grad_b_kv = jnp.sum(kv_grad_cols.astype(f32), axis=0)
    grad_normed_one = matmul_nt(query_grad_cols, full_query) + matmul_nt(kv_grad_cols, own_kv)
    scaled_one = grad_normed_one * gain_one_full[None, :]
    inner_one = jnp.sum(scaled_one * hidden_in, axis=1, keepdims=True)
    grad_gain_one = jnp.sum(grad_normed_one * hidden_in * inverse_one, axis=0)
    back_one = inverse_one * scaled_one - hidden_in * (
        inverse_one * inverse_one * inverse_one * inner_one / D
    )
    back_one = lax.dynamic_update_slice_in_dim(
        back_one, lax.dynamic_slice_in_dim(back_one, start, part, 0) + grad_mid, start, 0
    )
    grad_inputs = lax.psum_scatter(back_one.astype(bf16), "col", scatter_dimension=1, tiled=True)
    gains = lax.psum_scatter(
        jnp.stack([grad_gain_one, grad_gain_two]), "col", scatter_dimension=1, tiled=True
    )
    width = gains.shape[1]
    small = jnp.concatenate([gains.reshape(-1), grad_b_query, grad_b_kv])
    small = lax.psum(small, ("dp", "row"))
    biases = small[2 * width :]
    return (
        result,
        grad_inputs,
        small[:width],
        grad_w_query,
        biases[:width],
        grad_w_kv[:, :kv_cols],
        biases[width : width + kv_cols],
        grad_w_kv[:, kv_cols:],
        biases[width + kv_cols :],
        grad_w_out,
        small[width : 2 * width],
        grad_w_gate,
        grad_w_up,
        grad_w_down,
    )


def solution(mesh):
    whole_heads = dict(mesh.shape) == {"dp": 4, "row": 2, "col": 4}
    return jax.shard_map(
        per_device if whole_heads else per_device_any,
        mesh=mesh,
        in_specs=(
            P(("dp", "row"), "col"),
            P("dp", None),
            P("col"),
            P("row", "col"),
            P("col"),
            P("row", "col"),
            P("col"),
            P("row", "col"),
            P("col"),
            P("col", "row"),
            P("col"),
            P("row", "col"),
            P("row", "col"),
            P("col", "row"),
            P(("dp", "row"), "col"),
        ),
        out_specs=(
            P(("dp", "row"), "col"),
            P(("dp", "row"), "col"),
            P("col"),
            P("row", "col"),
            P("col"),
            P("row", "col"),
            P("col"),
            P("row", "col"),
            P("col"),
            P("col", "row"),
            P("col"),
            P("row", "col"),
            P("row", "col"),
            P("col", "row"),
        ),
        check_vma=False,
    )
```

```python
import functools

import jax
import jax.numpy as jnp
from jax import lax
from jax.experimental import pallas as pl
from jax.experimental.pallas import tpu as pltpu
from jax.sharding import PartitionSpec as P

D = 1536
HEAD_WIDTH = 128
QUERY_HEADS = 12
KEY_VALUE_HEADS = 2
DEVICE_TOKENS = 256
QW = 1536
KW = 256


theta_base = 1000000.0
eps = 1e-06


def matmul(left, right):
    return jnp.dot(left, right, preferred_element_type=jnp.float32)


def matmul_tn(left, right):
    return lax.dot_general(
        left, right, (((0,), (0,)), ((), ())), preferred_element_type=jnp.float32
    )


def matmul_nt(left, right):
    return lax.dot_general(
        left, right, (((1,), (1,)), ((), ())), preferred_element_type=jnp.float32
    )


def row_squares(values):
    return lax.psum(values, "col")


def gather_width(values):
    return lax.all_gather(values, "col", axis=1, tiled=True)


def sum_width(values):
    return lax.psum_scatter(
        values.astype(jnp.bfloat16), "col", scatter_dimension=1, tiled=True
    ).astype(jnp.float32)


def documents(lengths, places):
    doc_ends = jnp.cumsum(lengths)
    doc_starts = doc_ends - lengths
    doc_index = jnp.sum((places[:, None] >= doc_ends[None, :]).astype(jnp.int32), axis=1)
    chosen = doc_index[:, None] == jnp.arange(lengths.shape[0], dtype=jnp.int32)[None, :]
    offset = jnp.sum(jnp.where(chosen, doc_starts[None, :], 0), axis=1)
    return (doc_index, places - offset)


def rotary_embedding(values, token_position, direction):
    half_size = HEAD_WIDTH // 2
    frequency = theta_base ** (-(jnp.arange(half_size, dtype=jnp.float32) * 2.0) / HEAD_WIDTH)
    angles = token_position.astype(jnp.float32)[:, None] * frequency[None, :]
    cosine = jnp.cos(angles)[:, None, :]
    sine_part = direction * jnp.sin(angles)[:, None, :]
    leading = values[..., :half_size]
    second = values[..., half_size:]
    return jnp.concatenate(
        [leading * cosine - second * sine_part, second * cosine + leading * sine_part], axis=-1
    )


def norm_forward(hidden, gain):
    square_total = row_squares(jnp.sum(hidden * hidden, axis=1))
    inverse = lax.rsqrt(square_total / D + eps)
    normed = (hidden * inverse[:, None] * gain[None, :]).astype(jnp.bfloat16)
    return (normed, inverse)


def norm_backward(hidden, gain, inverse, grad_normed):
    scaled = grad_normed * gain[None, :]
    inner = row_squares(jnp.sum(scaled * hidden, axis=1))
    grad_hidden = (
        inverse[:, None] * scaled - hidden * (inverse * inverse * inverse * inner / D)[:, None]
    )
    grad_gain = jnp.sum(grad_normed * hidden * inverse[:, None], axis=0)
    return (grad_hidden, grad_gain)


def key_layout(gathered_keys, gathered_values, doc_all):
    seq_len = gathered_keys.shape[0]
    key_block_index = min(512, seq_len)
    count_blocks = seq_len // key_block_index
    blocks_of_keys = gathered_keys.reshape(
        count_blocks, key_block_index, gathered_keys.shape[1] // HEAD_WIDTH, HEAD_WIDTH
    )
    blocks_of_values = gathered_values.reshape(
        count_blocks, key_block_index, gathered_values.shape[1] // HEAD_WIDTH, HEAD_WIDTH
    )
    doc_blocks = doc_all.reshape(count_blocks, key_block_index)
    place_blocks = jnp.arange(seq_len, dtype=jnp.int32).reshape(count_blocks, key_block_index)
    return (blocks_of_keys, doc_blocks, place_blocks, blocks_of_values)


def block_scores(heads_of_queries, key_blk, doc_blk, place_blk, doc_local, place_local):
    scores = jnp.einsum(
        "tkgh,skh->tkgs", heads_of_queries, key_blk, preferred_element_type=jnp.float32
    ) * HEAD_WIDTH ** (-0.5)
    allowed = (doc_blk[None, :] == doc_local[:, None]) & (
        place_blk[None, :] <= place_local[:, None]
    )
    return (scores, allowed[:, None, None, :])


def attention_forward(heads_of_queries, blocks, doc_local, place_local):
    head_shape = heads_of_queries.shape[:3]

    def first_pass(state_in, packed):
        running_max, running_sum = state_in
        scores, allowed = block_scores(
            heads_of_queries, packed[0], packed[1], packed[2], doc_local, place_local
        )
        masked = jnp.where(allowed, scores, -1e30)
        new_max = jnp.maximum(running_max, jnp.max(masked, axis=-1))
        raised = jnp.where(allowed, jnp.exp(scores - new_max[..., None]), 0.0)
        running_sum = running_sum * jnp.exp(running_max - new_max) + jnp.sum(raised, axis=-1)
        return ((new_max, running_sum), None)

    initial = (jnp.full(head_shape, -1e30, jnp.float32), jnp.zeros(head_shape, jnp.float32))
    (running_max, running_sum), unused = lax.scan(first_pass, initial, blocks)
    log_total = running_max + jnp.log(running_sum)

    def second_pass(acc_out, packed):
        scores, allowed = block_scores(
            heads_of_queries, packed[0], packed[1], packed[2], doc_local, place_local
        )
        probs_low = jnp.where(allowed, jnp.exp(scores - log_total[..., None]), 0.0).astype(
            jnp.bfloat16
        )
        return (
            acc_out
            + jnp.einsum(
                "tkgs,skh->tkgh", probs_low, packed[3], preferred_element_type=jnp.float32
            ),
            None,
        )

    attended, unused = lax.scan(second_pass, jnp.zeros(heads_of_queries.shape, jnp.float32), blocks)
    return (attended, log_total)


def attention_backward(
    heads_of_queries, blocks, doc_local, place_local, log_total, attended, heads_gradient
):
    inner = jnp.sum(heads_gradient.astype(jnp.float32) * attended, axis=-1)
    scale_factor = HEAD_WIDTH ** (-0.5)

    def back_pass(grad_query, packed):
        scores, allowed = block_scores(
            heads_of_queries, packed[0], packed[1], packed[2], doc_local, place_local
        )
        probs = jnp.where(allowed, jnp.exp(scores - log_total[..., None]), 0.0)
        grad_probs = jnp.einsum(
            "tkgh,skh->tkgs", heads_gradient, packed[3], preferred_element_type=jnp.float32
        )
        grad_scores = (probs * (grad_probs - inner[..., None])).astype(jnp.bfloat16)
        grad_query = (
            grad_query
            + jnp.einsum(
                "tkgs,skh->tkgh", grad_scores, packed[0], preferred_element_type=jnp.float32
            )
            * scale_factor
        )
        grad_key = (
            jnp.einsum(
                "tkgs,tkgh->skh", grad_scores, heads_of_queries, preferred_element_type=jnp.float32
            )
            * scale_factor
        )
        grad_value = jnp.einsum(
            "tkgs,tkgh->skh",
            probs.astype(jnp.bfloat16),
            heads_gradient,
            preferred_element_type=jnp.float32,
        )
        return (grad_query, (grad_key, grad_value))

    grad_query, (key_grads, value_grads) = lax.scan(
        back_pass, jnp.zeros(heads_of_queries.shape, jnp.float32), blocks
    )
    seq_len = key_grads.shape[0] * key_grads.shape[1]
    return (grad_query, key_grads.reshape(seq_len, -1), value_grads.reshape(seq_len, -1))


def per_device_any(
    inputs,
    seq_lengths,
    gain_one,
    w_query,
    b_query,
    w_key,
    b_key,
    w_value,
    b_value,
    w_out,
    gain_two,
    w_gate,
    w_up,
    w_down,
    cotangent,
):
    full_query, full_key, full_value, full_out, full_gate, full_up, full_down = (
        lax.all_gather(w_query, "row", axis=0, tiled=True),
        lax.all_gather(w_key, "row", axis=0, tiled=True),
        lax.all_gather(w_value, "row", axis=0, tiled=True),
        lax.all_gather(w_out, "row", axis=1, tiled=True),
        lax.all_gather(w_gate, "row", axis=0, tiled=True),
        lax.all_gather(w_up, "row", axis=0, tiled=True),
        lax.all_gather(w_down, "row", axis=1, tiled=True),
    )
    row_pos = lax.axis_index("row")
    col_pos = lax.axis_index("col")
    row_count = lax.axis_size("row")
    col_count = lax.axis_size("col")
    seq_len = DEVICE_TOKENS * row_count * col_count
    query_group_width = QUERY_HEADS // KEY_VALUE_HEADS
    lengths = seq_lengths[0]
    place_local = (row_pos * col_count + col_pos) * DEVICE_TOKENS + jnp.arange(
        DEVICE_TOKENS, dtype=jnp.int32
    )
    doc_local, local_position = documents(lengths, place_local)
    doc_all = documents(lengths, jnp.arange(seq_len, dtype=jnp.int32))[0]
    hidden_in = inputs.astype(jnp.float32)
    normed_one, inverse_one = norm_forward(hidden_in, gain_one)
    normed_full = gather_width(normed_one)
    query_lin = (matmul(normed_full, full_query) + b_query.astype(jnp.float32)).astype(jnp.bfloat16)
    projected_keys = (matmul(normed_full, full_key) + b_key.astype(jnp.float32)).astype(
        jnp.bfloat16
    )
    projected_values = (matmul(normed_full, full_value) + b_value.astype(jnp.float32)).astype(
        jnp.bfloat16
    )
    query_rows, rows_of_keys, value_rows = (
        lax.all_to_all(query_lin, "col", split_axis=0, concat_axis=1, tiled=True),
        lax.all_to_all(projected_keys, "col", split_axis=0, concat_axis=1, tiled=True),
        lax.all_to_all(projected_values, "col", split_axis=0, concat_axis=1, tiled=True),
    )
    rotated_queries = rotary_embedding(
        query_rows.astype(jnp.float32).reshape(DEVICE_TOKENS, QUERY_HEADS, HEAD_WIDTH),
        local_position,
        1.0,
    ).astype(jnp.bfloat16)
    rotated_keys = rotary_embedding(
        rows_of_keys.astype(jnp.float32).reshape(DEVICE_TOKENS, KEY_VALUE_HEADS, HEAD_WIDTH),
        local_position,
        1.0,
    ).astype(jnp.bfloat16)
    gathered_keys, gathered_values = (
        lax.all_gather(rotated_keys.reshape(DEVICE_TOKENS, KW), ("row", "col"), axis=0, tiled=True),
        lax.all_gather(value_rows, ("row", "col"), axis=0, tiled=True),
    )
    blocks = key_layout(gathered_keys, gathered_values, doc_all)
    heads_of_queries = rotated_queries.reshape(
        DEVICE_TOKENS, KEY_VALUE_HEADS, query_group_width, HEAD_WIDTH
    )
    attended, log_total = attention_forward(heads_of_queries, blocks, doc_local, place_local)
    attended_low = attended.reshape(DEVICE_TOKENS, QW).astype(jnp.bfloat16)
    attended_cols = lax.all_to_all(attended_low, "col", split_axis=1, concat_axis=0, tiled=True)
    hidden_mid = hidden_in + sum_width(matmul(attended_cols, full_out))
    normed_two, inverse_two = norm_forward(hidden_mid, gain_two)
    normed_wide = gather_width(normed_two)
    gate = matmul(normed_wide, full_gate)
    up_proj = matmul(normed_wide, full_up)
    sigmoid_gate = jax.nn.sigmoid(gate)
    silu_gate = gate * sigmoid_gate
    mixed = (silu_gate * up_proj).astype(jnp.bfloat16)
    result = (hidden_mid + sum_width(matmul(mixed, full_down))).astype(jnp.bfloat16)
    grad_full = gather_width(cotangent)
    grad_w_down = matmul_tn(mixed, grad_full)
    grad_mixed = matmul_nt(grad_full, full_down)
    grad_gate = (grad_mixed * up_proj * sigmoid_gate * (1.0 + gate * (1.0 - sigmoid_gate))).astype(
        jnp.bfloat16
    )
    grad_up = (grad_mixed * silu_gate).astype(jnp.bfloat16)
    grad_w_gate = matmul_tn(normed_wide, grad_gate)
    grad_w_up = matmul_tn(normed_wide, grad_up)
    grad_normed_two = sum_width(matmul_nt(grad_gate, full_gate) + matmul_nt(grad_up, full_up))
    grad_back_two, grad_gain_two = norm_backward(hidden_mid, gain_two, inverse_two, grad_normed_two)
    grad_mid = cotangent.astype(jnp.float32) + grad_back_two
    grad_attn_full = gather_width(grad_mid.astype(jnp.bfloat16))
    grad_w_out = matmul_tn(attended_cols, grad_attn_full)
    grad_attended_cols = matmul_nt(grad_attn_full, full_out).astype(jnp.bfloat16)
    attended_gradient = lax.all_to_all(
        grad_attended_cols, "col", split_axis=0, concat_axis=1, tiled=True
    )
    heads_gradient = attended_gradient.reshape(
        DEVICE_TOKENS, KEY_VALUE_HEADS, query_group_width, HEAD_WIDTH
    )
    grad_query_rot, key_grads, value_grads = attention_backward(
        heads_of_queries, blocks, doc_local, place_local, log_total, attended, heads_gradient
    )
    rotated_key_gradient, grad_value = (
        lax.psum_scatter(
            key_grads.astype(jnp.bfloat16), ("row", "col"), scatter_dimension=0, tiled=True
        ).astype(jnp.float32),
        lax.psum_scatter(
            value_grads.astype(jnp.bfloat16), ("row", "col"), scatter_dimension=0, tiled=True
        ).astype(jnp.float32),
    )
    grad_query_lin = (
        rotary_embedding(
            grad_query_rot.reshape(DEVICE_TOKENS, QUERY_HEADS, HEAD_WIDTH), local_position, -1.0
        )
        .reshape(DEVICE_TOKENS, QW)
        .astype(jnp.bfloat16)
    )
    grad_key_lin = (
        rotary_embedding(
            rotated_key_gradient.reshape(DEVICE_TOKENS, KEY_VALUE_HEADS, HEAD_WIDTH),
            local_position,
            -1.0,
        )
        .reshape(DEVICE_TOKENS, KW)
        .astype(jnp.bfloat16)
    )
    grad_value_lin = grad_value.astype(jnp.bfloat16)
    query_grad_cols, key_grad_cols, value_grad_cols = (
        lax.all_to_all(grad_query_lin, "col", split_axis=1, concat_axis=0, tiled=True),
        lax.all_to_all(grad_key_lin, "col", split_axis=1, concat_axis=0, tiled=True),
        lax.all_to_all(grad_value_lin, "col", split_axis=1, concat_axis=0, tiled=True),
    )
    grad_b_query = jnp.sum(query_grad_cols.astype(jnp.float32), axis=0)
    grad_b_key = jnp.sum(key_grad_cols.astype(jnp.float32), axis=0)
    grad_b_value = jnp.sum(value_grad_cols.astype(jnp.float32), axis=0)
    grad_w_query = matmul_tn(normed_full, query_grad_cols)
    grad_w_key = matmul_tn(normed_full, key_grad_cols)
    grad_w_value = matmul_tn(normed_full, value_grad_cols)
    grad_normed_one = sum_width(
        matmul_nt(query_grad_cols, full_query)
        + matmul_nt(key_grad_cols, full_key)
        + matmul_nt(value_grad_cols, full_value)
    )
    grad_back_one, grad_gain_one = norm_backward(hidden_in, gain_one, inverse_one, grad_normed_one)
    grad_inputs = (grad_mid + grad_back_one).astype(jnp.bfloat16)
    summed = (
        lax.psum(grad_w_query.astype(jnp.bfloat16), ("dp", "row")).astype(jnp.float32),
        lax.psum(grad_w_key.astype(jnp.bfloat16), ("dp", "row")).astype(jnp.float32),
        lax.psum(grad_w_value.astype(jnp.bfloat16), ("dp", "row")).astype(jnp.float32),
        lax.psum(grad_w_out.astype(jnp.bfloat16), ("dp", "row")).astype(jnp.float32),
        lax.psum(grad_w_gate.astype(jnp.bfloat16), ("dp", "row")).astype(jnp.float32),
        lax.psum(grad_w_up.astype(jnp.bfloat16), ("dp", "row")).astype(jnp.float32),
        lax.psum(grad_w_down.astype(jnp.bfloat16), ("dp", "row")).astype(jnp.float32),
        lax.psum(grad_gain_one.astype(jnp.bfloat16), ("dp", "row")).astype(jnp.float32),
        lax.psum(grad_b_query.astype(jnp.bfloat16), ("dp", "row")).astype(jnp.float32),
        lax.psum(grad_b_key.astype(jnp.bfloat16), ("dp", "row")).astype(jnp.float32),
        lax.psum(grad_b_value.astype(jnp.bfloat16), ("dp", "row")).astype(jnp.float32),
        lax.psum(grad_gain_two.astype(jnp.bfloat16), ("dp", "row")).astype(jnp.float32),
    )
    rows_each = D // row_count
    split_dims = (0, 0, 0, 1, 0, 0, 1)
    weight_sums = tuple(
        (
            lax.dynamic_slice_in_dim(
                summed[member], row_pos * rows_each, rows_each, split_dims[member]
            )
            for member in range(7)
        )
    )
    small_sums = summed[7:]
    return (
        result,
        grad_inputs,
        small_sums[0],
        weight_sums[0],
        small_sums[1],
        weight_sums[1],
        small_sums[2],
        weight_sums[2],
        small_sums[3],
        weight_sums[3],
        small_sums[4],
        weight_sums[4],
        weight_sums[5],
        weight_sums[6],
    )


MESH = pl.DeviceIdType.MESH
NEG = -1e30
SCALE = HEAD_WIDTH ** (-0.5)


def vmem_spec():
    return pl.BlockSpec(memory_space=pltpu.VMEM)


def any_spec():
    return pl.BlockSpec(memory_space=pl.ANY)


def remote(src, dst, send_sem, recv_sem, device):
    return pltpu.make_async_remote_copy(
        src_ref=src,
        dst_ref=dst,
        send_sem=send_sem,
        recv_sem=recv_sem,
        device_id=device,
        device_id_type=MESH,
    )


def greet(peers):
    barrier = pltpu.get_barrier_semaphore()
    for peer in peers:
        pl.semaphore_signal(barrier, inc=1, device_id=peer, device_id_type=MESH)
    pl.semaphore_wait(barrier, len(peers))


def rows_at(first, count):
    return pl.ds(pl.multiple_of(first, 16), count)


def lanes_at(first, count):
    return pl.ds(pl.multiple_of(first, 128), count)


class Chain:
    def __init__(self, place, own, full, sends, recvs, count, chunks):
        self.dp, self.row, self.col = place
        self.own, self.full, self.sends, self.recvs = own, full, sends, recvs
        self.count, self.chunks = count, chunks
        self.width = full.shape[1] // count
        self.rows = full.shape[0] // chunks

    def block(self, shard, chunk):
        return self.full.at[
            rows_at(chunk * self.rows, self.rows), lanes_at(shard * self.width, self.width)
        ]

    def copy(self, way, step, shard, chunk):
        src = self.block(shard, chunk)
        if step == 0:
            src = self.own.at[rows_at(chunk * self.rows, self.rows)]
        device = (self.dp, self.row, self.col + (1 if way == 0 else -1))
        return remote(
            src,
            self.block(shard, chunk),
            self.sends.at[way, step, chunk],
            self.recvs.at[shard, chunk],
            device,
        )

    def start_own(self, chunk):
        @pl.when(self.col < self.count - 1)
        def _():
            self.copy(0, 0, self.col, chunk).start()

        @pl.when(self.col > 0)
        def _():
            self.copy(1, 0, self.col, chunk).start()

    def step(self, step, chunk):
        left, right = self.col - step, self.col + step

        @pl.when(left >= 0)
        def _():
            self.copy(0, step, left, chunk).wait_recv()

        if step < self.count - 1:

            @pl.when((left >= 0) & (self.col < self.count - 1))
            def _():
                self.copy(0, step, left, chunk).start()

        @pl.when(right < self.count)
        def _():
            self.copy(1, step, right, chunk).wait_recv()

        if step < self.count - 1:

            @pl.when((right < self.count) & (self.col > 0))
            def _():
                self.copy(1, step, right, chunk).start()

    def finish(self):
        for step in range(self.count - 1):
            left, right = self.col - step, self.col + step

            @pl.when((left >= 0) & (self.col < self.count - 1))
            def _():
                @pl.loop(0, self.chunks)
                def _(chunk):
                    self.copy(0, step, left, chunk).wait_send()

            @pl.when((right < self.count) & (self.col > 0))
            def _():
                @pl.loop(0, self.chunks)
                def _(chunk):
                    self.copy(1, step, right, chunk).wait_send()


def doc_start(lengths, place):
    first = jnp.zeros_like(place)
    end = 0
    for doc in range(lengths.shape[1]):
        end = end + lengths[0, doc]
        first = jnp.where(place >= end, end, first)
    return first


def rotate(values, cosine, sine):
    return values * cosine + pltpu.roll(values, HEAD_WIDTH // 2, 1) * sine


def allowed_keys(lengths, first_query, queries, first_key, keys):
    query = first_query + lax.broadcasted_iota(jnp.int32, (queries, 1), 0)
    key = first_key + lax.broadcasted_iota(jnp.int32, (1, keys), 1)
    return (key >= doc_start(lengths, query)) & (key <= query)


def front_kernel(
    heads,
    dims,
    aux,
    x,
    cot,
    wq,
    wkv,
    wout,
    w_gate,
    w_up,
    w_down,
    lengths,
    freq,
    x_out,
    n1_out,
    cot_out,
    q_out,
    kv_out,
    att_out,
    lse_out,
    attl_out,
    hid_out,
    n2_out,
    trig_out,
    att_low,
    aux_out,
    wall_out,
    wof_out,
    peer_gate,
    peer_up,
    peer_down,
    x_full,
    n1,
    cot_full,
    x_send,
    x_recv,
    c_send,
    c_recv,
    local_sem,
    aux_send,
    aux_recv,
    wall_send,
    wall_recv,
    z_send,
    z_recv,
    d_send,
    d_recv,
    r_send,
    r_recv,
    kv_send,
    kv_recv,
    a2a_send,
    a2a_recv,
    m_send,
    m_recv,
):
    count, planes = dims
    f32, bf16 = jnp.float32, jnp.bfloat16
    dp, row, col = lax.axis_index("dp"), lax.axis_index("row"), lax.axis_index("col")
    place = (dp, row, col)
    rows, width = x.shape
    part = rows // count
    half = wq.shape[0]
    member = lax.rem(col, 2)
    mate = col + 1 - 2 * member
    col_peers = [(dp, row, lax.rem(col + k, count)) for k in range(1, count)]
    dp_peers = [(lax.rem(dp + k, planes), row, col) for k in range(1, planes)]
    partner = (dp, 1 - row, col)
    across = (dp, 1 - row, mate)
    greet(col_peers + dp_peers + [partner, across])

    chain_x = Chain(place, x, x_full, x_send, x_recv, count, count)
    chain_c = Chain(place, cot, cot_full, c_send, c_recv, count, count)
    own_lanes = lanes_at(col * width, width)
    copy_x = pltpu.make_async_copy(x, x_full.at[:, own_lanes], local_sem.at[0])
    copy_x.start()
    aux_copies = [
        remote(aux, aux_out.at[col], aux_send.at[k], aux_recv.at[k], peer)
        for k, peer in enumerate(col_peers)
    ]
    for copy in aux_copies:
        copy.start()

    @pl.loop(0, count)
    def _(chunk):
        chain_x.start_own(chunk)

    own_half = rows_at(row * half, half)
    kv_lanes = lanes_at(width + member * HEAD_WIDTH, HEAD_WIDTH)
    copy_q = pltpu.make_async_copy(wq, wall_out.at[own_half, pl.ds(0, width)], local_sem.at[1])
    copy_kv = pltpu.make_async_copy(wkv, wall_out.at[own_half, kv_lanes], local_sem.at[2])
    copy_q.start()
    copy_kv.start()
    wall_copies = [
        remote(
            wq, wall_out.at[own_half, pl.ds(0, width)], wall_send.at[0], wall_recv.at[0], partner
        )
    ] + [
        remote(wkv, wall_out.at[own_half, kv_lanes], wall_send.at[k], wall_recv.at[k], peer)
        for k, peer in ((1, partner), (2, (dp, row, mate)), (3, across))
    ]
    for copy in wall_copies:
        copy.start()
    mlp_copies = [
        remote(src, dst, m_send.at[k], m_recv.at[k], partner)
        for k, (src, dst) in enumerate(
            ((w_gate, peer_gate), (w_up, peer_up), (w_down, peer_down))
        )
    ]
    for copy in mlp_copies:
        copy.start()
    copy_c = pltpu.make_async_copy(cot, cot_full.at[:, own_lanes], local_sem.at[3])
    copy_c.start()
    quarter = wout.shape[0] // planes
    out_lanes = lanes_at(row * half, half)

    def wof_block(shard, plane, side):
        return wof_out.at[
            shard, rows_at(plane * quarter, quarter), lanes_at(side * half, half)
        ]

    def wof_blocks(plane, side):
        return wof_out.at[:, rows_at(plane * quarter, quarter), lanes_at(side * half, half)]

    own_quarter = wout.at[rows_at(dp * quarter, quarter)]
    copy_o = pltpu.make_async_copy(own_quarter, wof_block(col, dp, row), local_sem.at[4])
    copy_o.start()

    token = row * rows + lax.broadcasted_iota(jnp.int32, (rows, 1), 0)
    position = (token - doc_start(lengths, token)).astype(f32)
    angle = position * freq[...]
    trig_out[0] = jnp.cos(angle)
    lane = lax.broadcasted_iota(jnp.int32, (1, HEAD_WIDTH), 1)
    trig_out[1] = jnp.sin(angle) * jnp.where(lane < HEAD_WIDTH // 2, -1.0, 1.0)
    aux_out[col] = aux[...]

    for step in range(1, count - 1):

        @pl.loop(0, count)
        def _(chunk):
            chain_x.step(step, chunk)

    z_copies = [
        remote(own_quarter, wof_block(col, dp, row), z_send.at[k], z_recv.at[k], peer)
        for k, peer in enumerate(col_peers)
    ]
    for copy in z_copies:
        copy.start()

    @pl.loop(0, count)
    def _(chunk):
        chain_c.start_own(chunk)

    copy_x.wait()
    copy_q.wait()
    copy_kv.wait()
    for copy in aux_copies:
        copy.wait_recv()
    for k, (side, who) in enumerate(
        ((1 - row, None), (1 - row, member), (row, 1 - member), (1 - row, 1 - member))
    ):
        side_rows = rows_at(side * half, half)
        if who is None:
            dst, src = wall_out.at[side_rows, pl.ds(0, width)], wq
        else:
            dst = wall_out.at[side_rows, lanes_at(width + who * HEAD_WIDTH, HEAD_WIDTH)]
            src = wkv
        remote(src, dst, wall_send.at[k], wall_recv.at[k], partner).wait_recv()

    mate_aux = aux_out[mate]
    even = jnp.where(member == 0, aux[3:4, :HEAD_WIDTH], mate_aux[3:4, :HEAD_WIDTH])
    odd = jnp.where(member == 0, mate_aux[3:4, :HEAD_WIDTH], aux[3:4, :HEAD_WIDTH])
    low_lanes = lane < HEAD_WIDTH // 2
    key_bias = jnp.where(low_lanes, even, pltpu.roll(odd, HEAD_WIDTH // 2, 1))
    value_bias = jnp.where(low_lanes, pltpu.roll(even, HEAD_WIDTH // 2, 1), odd)

    def kv_chunk(side, chunk):
        return kv_out.at[rows_at(side * rows + chunk * part, part)]

    def kv_copy(chunk):
        return remote(
            kv_chunk(row, chunk),
            kv_chunk(row, chunk),
            kv_send.at[chunk],
            kv_recv.at[chunk],
            partner,
        )

    @pl.loop(0, count)
    def _(chunk):
        chain_x.step(count - 1, chunk)
        here = rows_at(chunk * part, part)
        squares = jnp.zeros((part, 1), f32)
        for shard in range(count):
            piece = x_full[here, shard * width : (shard + 1) * width].astype(f32)
            squares = squares + jnp.sum(piece * piece, axis=1, keepdims=True)
        inverse = lax.rsqrt(squares / D + eps)
        for shard in range(count):
            lanes = slice(shard * width, (shard + 1) * width)
            piece = x_full[here, lanes].astype(f32)
            n1[here, lanes] = (piece * inverse * aux_out[shard, 0:1, :]).astype(bf16)
        lin = matmul(n1[here, :], wall_out[...])
        cosine, sine = trig_out[0, here, :], trig_out[1, here, :]
        for head in range(heads):
            lanes = slice(head * HEAD_WIDTH, (head + 1) * HEAD_WIDTH)
            query = (lin[:, lanes] + aux[2:3, lanes]).astype(bf16).astype(f32)
            q_out[head, here, :] = rotate(query, cosine, sine).astype(bf16)
        first = lin[:, width : width + HEAD_WIDTH]
        second = lin[:, width + HEAD_WIDTH : width + 2 * HEAD_WIDTH]
        turn = HEAD_WIDTH // 2
        key = jnp.where(low_lanes, first, pltpu.roll(second, turn, 1)) + key_bias
        value = jnp.where(low_lanes, pltpu.roll(first, turn, 1), second) + value_bias
        there = rows_at(row * rows + chunk * part, part)
        kv_out[there, :HEAD_WIDTH] = rotate(
            key.astype(bf16).astype(f32), cosine, sine
        ).astype(bf16)
        kv_out[there, HEAD_WIDTH:] = value.astype(bf16)
        kv_copy(chunk).start()

    n1_copy = pltpu.make_async_copy(n1, n1_out, local_sem.at[5])
    n1_copy.start()
    x_copy = pltpu.make_async_copy(x_full, x_out, local_sem.at[6])
    x_copy.start()

    copy_o.wait()
    for k in range(1, count):
        shard = lax.rem(col + count - k, count)
        remote(
            own_quarter, wof_block(shard, dp, row), z_send.at[k - 1], z_recv.at[k - 1], partner
        ).wait_recv()
    d_copies = [
        remote(wof_blocks(dp, row), wof_blocks(dp, row), d_send.at[k], d_recv.at[k], peer)
        for k, peer in enumerate(dp_peers)
    ]
    r_copies = [
        remote(
            wof_blocks(lax.rem(dp + planes - k, planes), row),
            wof_blocks(lax.rem(dp + planes - k, planes), row),
            r_send.at[k],
            r_recv.at[k],
            partner,
        )
        for k in range(planes)
    ]
    for copy in d_copies:
        copy.start()
    r_copies[0].start()

    @pl.loop(0, count)
    def _(chunk):
        remote(
            kv_chunk(row, chunk),
            kv_chunk(1 - row, chunk),
            kv_send.at[chunk],
            kv_recv.at[chunk],
            partner,
        ).wait_recv()

    span = min(512, rows)

    def a2a_copy(block):
        return remote(
            att_low.at[block],
            attl_out.at[:, own_lanes],
            a2a_send.at[block],
            a2a_recv.at[col],
            (dp, row, block),
        )

    @pl.loop(0, count)
    def _(block):
        here = rows_at(block * part, part)
        first_query = row * rows + block * part
        query = q_out[:, here, :].reshape(heads * part, HEAD_WIDTH)

        def body(index, state):
            largest, total, acc = state
            keys = rows_at(index * span, span)
            scores = matmul_nt(query, kv_out[keys, :HEAD_WIDTH]) * SCALE
            allowed = allowed_keys(lengths, first_query, part, index * span, span)
            scores = jnp.where(allowed[None], scores.reshape(heads, part, span), NEG)
            scores = scores.reshape(heads * part, span)
            new = jnp.maximum(largest, jnp.max(scores, axis=1, keepdims=True))
            raised = jnp.exp(scores - new)
            alpha = jnp.exp(largest - new)
            total = total * alpha + jnp.sum(raised, axis=1, keepdims=True)
            acc = acc * alpha + matmul(raised.astype(bf16), kv_out[keys, HEAD_WIDTH:])
            return new, total, acc

        state = (
            jnp.full((heads * part, 1), NEG, f32),
            jnp.zeros((heads * part, 1), f32),
            jnp.zeros((heads * part, HEAD_WIDTH), f32),
        )
        blocks = (first_query + part + span - 1) // span
        largest, total, acc = lax.fori_loop(0, blocks, body, state)
        attended = (acc / total).reshape(heads, part, HEAD_WIDTH)
        att_out[:, here, :] = attended
        log_total = (largest + jnp.log(total)).reshape(heads, part, 1)
        spread = jnp.zeros((part, HEAD_WIDTH), f32)
        for head in range(heads):
            spread = jnp.where(lane == head, log_total[head], spread)
        lse_out[here, :] = spread
        for head in range(heads):
            lanes = slice(head * HEAD_WIDTH, (head + 1) * HEAD_WIDTH)
            att_low[block, :, lanes] = attended[head].astype(bf16)

        @pl.when(block != col)
        def _():
            a2a_copy(block).start()

        chain_c.step(1, block)

    attl_out[:, own_lanes] = att_low[col]
    for step in range(2, count - 1):

        @pl.loop(0, count)
        def _(chunk):
            chain_c.step(step, chunk)

    for k in range(1, planes):
        remote(
            wof_blocks(dp, row),
            wof_blocks(lax.rem(dp + planes - k, planes), row),
            d_send.at[k - 1],
            d_recv.at[k - 1],
            partner,
        ).wait_recv()
        r_copies[k].start()
    for k in range(planes):
        other = wof_blocks(lax.rem(dp + planes - k, planes), 1 - row)
        remote(other, other, r_send.at[k], r_recv.at[k], partner).wait_recv()

    @pl.loop(0, count)
    def _(block):
        @pl.when(block != col)
        def _():
            remote(
                att_low.at[block],
                attl_out.at[:, lanes_at(block * width, width)],
                a2a_send.at[block],
                a2a_recv.at[block],
                (dp, row, block),
            ).wait_recv()

    mine = rows_at(col * part, part)
    step_lanes = D // 4
    squares = jnp.zeros((part, 1), f32)
    for piece in range(4):
        lanes = slice(piece * step_lanes, (piece + 1) * step_lanes)
        total = x_full[mine, lanes].astype(f32)
        weights = wof_out[:, :, lanes].reshape(D, step_lanes)
        total = total + matmul(attl_out[...], weights)
        hid_out[:, lanes] = total
        squares = squares + jnp.sum(total * total, axis=1, keepdims=True)
    inverse = lax.rsqrt(squares / D + eps)
    for shard in range(count):
        lanes = slice(shard * width, (shard + 1) * width)
        n2_out[:, lanes] = (hid_out[:, lanes] * inverse * aux_out[shard, 1:2, :]).astype(bf16)

    @pl.loop(0, count)
    def _(chunk):
        chain_c.step(count - 1, chunk)

    copy_c.wait()
    c_copy = pltpu.make_async_copy(cot_full, cot_out, local_sem.at[7])
    c_copy.start()

    chain_x.finish()
    chain_c.finish()
    for copy in aux_copies + wall_copies + z_copies + d_copies + r_copies:
        copy.wait_send()
    for copy in mlp_copies:
        copy.wait()

    @pl.loop(0, count)
    def _(chunk):
        kv_copy(chunk).wait_send()

        @pl.when(chunk != col)
        def _():
            a2a_copy(chunk).wait_send()

    for copy in (n1_copy, x_copy, c_copy):
        copy.wait()


def front(dims, aux, x, cot, wq, wkv, wout, w_gate, w_up, w_down, lengths, freq):
    count, planes = dims
    rows, width = x.shape
    part = rows // count
    heads = width // HEAD_WIDTH
    f32, bf16 = jnp.float32, jnp.bfloat16
    shape = jax.ShapeDtypeStruct
    wall = width + 2 * HEAD_WIDTH
    outs = [
        (shape((rows, D), bf16), any_spec()),
        (shape((rows, D), bf16), any_spec()),
        (shape((rows, D), bf16), any_spec()),
        (shape((heads, rows, HEAD_WIDTH), bf16), vmem_spec()),
        (shape((2 * rows, 2 * HEAD_WIDTH), bf16), vmem_spec()),
        (shape((heads, rows, HEAD_WIDTH), f32), vmem_spec()),
        (shape((rows, HEAD_WIDTH), f32), vmem_spec()),
        (shape((part, D), bf16), vmem_spec()),
        (shape((part, D), f32), vmem_spec()),
        (shape((part, D), bf16), vmem_spec()),
        (shape((2, rows, HEAD_WIDTH), f32), vmem_spec()),
        (shape((count, part, width), bf16), vmem_spec()),
        (shape((count,) + aux.shape, f32), vmem_spec()),
        (shape((D, wall), bf16), vmem_spec()),
        (shape((count, wout.shape[0], D), bf16), vmem_spec()),
        (shape(w_gate.shape, bf16), any_spec()),
        (shape(w_up.shape, bf16), any_spec()),
        (shape(w_down.shape, bf16), any_spec()),
    ]
    dma = pltpu.SemaphoreType.DMA
    return pl.pallas_call(
        functools.partial(front_kernel, heads, dims),
        out_shape=[o[0] for o in outs],
        in_specs=[vmem_spec()]
        + [any_spec()] * 8
        + [pl.BlockSpec(memory_space=pltpu.SMEM), vmem_spec()],
        out_specs=[o[1] for o in outs],
        scratch_shapes=[
            pltpu.VMEM((rows, D), bf16),
            pltpu.VMEM((rows, D), bf16),
            pltpu.VMEM((rows, D), bf16),
            dma((2, count - 1, count)),
            dma((count, count)),
            dma((2, count - 1, count)),
            dma((count, count)),
            dma((8,)),
            dma((count - 1,)),
            dma((count - 1,)),
            dma((4,)),
            dma((4,)),
            dma((count - 1,)),
            dma((count - 1,)),
            dma((planes - 1,)),
            dma((planes - 1,)),
            dma((planes,)),
            dma((planes,)),
            dma((count,)),
            dma((count,)),
            dma((count,)),
            dma((count,)),
            dma((3,)),
            dma((3,)),
        ],
        compiler_params=pltpu.CompilerParams(
            collective_id=1, has_side_effects=True, vmem_limit_bytes=52 * 2**20
        ),
        cost_estimate=pl.CostEstimate(
            flops=10 * 10**9, bytes_accessed=60 * 10**6, transcendentals=10**7
        ),
        name="front",
    )(aux, x, cot, wq, wkv, wout, w_gate, w_up, w_down, lengths, freq)


TICKS = ((0, 1, 2, 4, 6, 7, 5, 3), (2, 3, 0, 4, 1, 6, 7, 5), (4, 5, 6, 2, 7, 0, 1, 3), (6, 7, 4, 2, 0, 1, 3, 5))
SLOTS = tuple(tuple(order.index(q) for q in range(8)) for order in TICKS)
ONWARD = (
    ((), (0, 1, 3), (2, 0, 1, 3, 5), ()),
    ((), (4, 6, 7, 5, 3), (6, 7, 5), ()),
)
SUMS = (
    ((2, 0), (4, 0), (6, 0), (7, 0), (5, 0), (3, 0)),
    ((4, 0), (6, 0), (7, 0), (0, 1), (5, 0), (1, 1)),
    ((2, 1), (0, 1), (1, 1), (6, 0), (3, 1), (7, 0)),
    ((4, 1), (2, 1), (0, 1), (1, 1), (3, 1), (5, 1)),
)
LINE = 4
TILE = 768


def pick(index, values):
    out = values[0]
    for k, value in enumerate(values[1:], 1):
        out = jnp.where(index == k, value, out)
    return out


def hidden_tiles(total):
    tile = 512
    return [(first, min(tile, total - first)) for first in range(0, total, tile)]


def mlp_kernel(
    n2,
    cot_full,
    hid,
    aux_all,
    own_gate,
    own_up,
    own_down,
    peer_gate,
    peer_up,
    peer_down,
    out_part,
    left_out,
    right_out,
    grad_mid,
    grad_gain,
    gate_w,
    up_w,
    down_w,
    mixed,
    g_gate,
    g_up,
    n2s,
    cots,
    parts,
    coming,
    stage,
    w_sem,
    cot_sem,
    own_sem,
    ag_send,
    ag_recv,
    rs_send,
    rs_recv,
    out_sem,
    left_sem,
    right_sem,
):
    f32, bf16 = jnp.float32, jnp.bfloat16
    dp, row, col = lax.axis_index("dp"), lax.axis_index("row"), lax.axis_index("col")
    part = n2.shape[0]
    piece = part // 2
    hidden, half = own_gate.shape
    tiles = hidden_tiles(hidden)
    partner = (dp, 1 - row, col)
    greet([(dp, row, lax.rem(col + k, LINE)) for k in range(1, LINE)] + [partner])

    def slot_rows(slot):
        return rows_at(slot * piece, piece)

    def hand_on(c, way, q, source=None):
        to = c + 1 - 2 * way
        src = n2s.at[slot_rows(SLOTS[c][q])] if source is None else source
        return remote(
            src, n2s.at[slot_rows(SLOTS[to][q])], ag_send.at[way, q], ag_recv.at[q], (dp, row, to)
        )

    def got(c, q):
        rows_here = n2s.at[slot_rows(SLOTS[c][q])]
        remote(rows_here, rows_here, ag_send.at[0, q], ag_recv.at[q], partner).wait_recv()

    def ways(c):
        return [way for way in (0, 1) if 0 <= c + 1 - 2 * way < LINE]

    for c in range(LINE):

        @pl.when(col == c)
        def _():
            for way in ways(c):
                hand_on(c, way, 2 * c, n2.at[pl.ds(0, piece)]).start()
            if c in (0, LINE - 1):
                hand_on(c, ways(c)[0], 2 * c + 1, n2.at[pl.ds(piece, piece)]).start()

    own_copy = pltpu.make_async_copy(n2, n2s.at[pl.ds(0, part)], own_sem)
    own_copy.start()

    def load_copies(index, first, count):
        rows_here = pl.ds(first, count)
        copies = []
        for k, (own, peer, whole) in enumerate(
            (
                (own_gate, peer_gate, gate_w),
                (own_up, peer_up, up_w),
                (own_down, peer_down, down_w),
            )
        ):
            for side, src in ((row, own), (1 - row, peer)):
                copies.append((src.at[rows_here], whole.at[rows_here, lanes_at(side * half, half)]))
        return [
            pltpu.make_async_copy(src, dst, w_sem.at[index, k])
            for k, (src, dst) in enumerate(copies)
        ]

    def cot_copy(slot):
        q = pick(col, [order[slot] for order in TICKS])
        return pltpu.make_async_copy(
            cot_full.at[slot_rows(q)], cots.at[slot_rows(slot)], cot_sem.at[slot]
        )

    for slot in range(2):
        cot_copy(slot).start()
    for index, (first, count) in enumerate(tiles):
        for copy in load_copies(index, first, count):
            copy.start()
    for slot in range(2, 2 * LINE):
        cot_copy(slot).start()
    for h in range(2):

        @pl.when(col == 0)
        def _():
            coming[h] = jnp.zeros(coming.shape[1:], bf16)

        @pl.when(col == LINE - 1)
        def _():
            coming[2 * LINE + h] = jnp.zeros(coming.shape[1:], bf16)

    own_copy.wait()
    for ref in (mixed, g_gate, g_up):
        ref[:, hidden:] = jnp.zeros((ref.shape[0], ref.shape[1] - hidden), bf16)

    def onward(f):
        for c in (1, 2):
            for way in (0, 1):
                if f < len(ONWARD[way][c]):
                    q = ONWARD[way][c][f]

                    @pl.when(col == c)
                    def _():
                        if q // 2 != c:
                            got(c, q)
                        hand_on(c, way, q).start()

    def sum_copy(c, q, way):
        to = c + 1 - 2 * way
        place = 2 * LINE + q % 2 if way == 1 and q // 2 == to else q
        return remote(
            parts.at[slot_rows(SLOTS[c][q])],
            coming.at[place],
            rs_send.at[q],
            rs_recv.at[place],
            (dp, row, to),
        )

    def sum_start(e, c):
        q, way = SUMS[c][e]
        sum_copy(c, q, way).start()

    def sum_ends(e):
        for c in (0, LINE - 1):

            @pl.when(col == c)
            def _():
                sum_start(e, c)

    def sum_mids(e):
        @pl.when((col == 1) | (col == 2))
        def _():
            q = jnp.where(col == 1, SUMS[1][e][0], SUMS[2][e][0])
            slot = jnp.where(col == 1, SLOTS[1][SUMS[1][e][0]], SLOTS[2][SUMS[2][e][0]])
            here = slot_rows(slot)
            remote(parts.at[here], coming.at[q], rs_send.at[q], rs_recv.at[q], partner).wait_recv()
            parts[here, :] = (parts[here, :].astype(f32) + coming[q].astype(f32)).astype(bf16)
            for c in (1, 2):

                @pl.when(col == c)
                def _():
                    sum_start(e, c)

    def out_copies(tick):
        copies = []
        for h in range(2):
            q = pick(
                tick, [pick(col, [order[2 * t + h] for order in TICKS]) for t in range(LINE)]
            )
            copies.append(
                pltpu.make_async_copy(
                    stage.at[lax.rem(tick, 2), pl.ds(h * piece, piece)],
                    out_part.at[slot_rows(q)],
                    out_sem.at[lax.rem(tick, 2), h],
                )
            )
        return copies

    def left_copies(tick):
        here = rows_at(tick * part, part)
        return [
            pltpu.make_async_copy(ref.at[here], left_out.at[k, here], left_sem.at[tick, k])
            for k, ref in enumerate((mixed, g_gate, g_up))
        ]

    def right_copy(slot):
        return pltpu.make_async_copy((cots, n2s)[slot], right_out.at[slot], right_sem.at[slot])

    lane_tiles = [(k * 512, 512) for k in range(D // 512)]

    @pl.loop(0, LINE)
    def _(tick):
        here = rows_at(tick * part, part)
        for c in (0, LINE - 1):
            for t in range(1, LINE):

                @pl.when((col == c) & (tick == t))
                def _():
                    for h in range(2):
                        got(c, TICKS[c][2 * t + h])

        for h in range(2):
            pltpu.make_async_copy(
                cot_full.at[pl.ds(0, piece)],
                cots.at[slot_rows(2 * tick + h)],
                cot_sem.at[2 * tick + h],
            ).wait()

        for index, (first, count) in enumerate(tiles):

            @pl.when(tick == 0)
            def _():
                for copy in load_copies(index, first, count):
                    copy.wait()

            rows_here, lanes = slice(first, first + count), slice(first, first + count)
            gate = matmul_nt(n2s[here, :], gate_w[rows_here, :])
            up = matmul_nt(n2s[here, :], up_w[rows_here, :])
            grad = matmul_nt(cots[here, :], down_w[rows_here, :])
            sigmoid = jax.nn.sigmoid(gate)
            silu = gate * sigmoid
            mixed[here, lanes] = (silu * up).astype(bf16)
            g_gate[here, lanes] = (grad * up * sigmoid * (1.0 + gate * (1.0 - sigmoid))).astype(
                bf16
            )
            g_up[here, lanes] = (grad * silu).astype(bf16)
            if index == 2:

                @pl.when(tick == 0)
                def _():
                    onward(0)

                @pl.when(tick == 1)
                def _():
                    onward(2)

                @pl.when(tick == 3)
                def _():
                    sum_mids(1)

        for copy in left_copies(tick):
            copy.start()
        for first, count in lane_tiles:
            lanes = slice(first, first + count)
            total = matmul(g_gate[here, :hidden], gate_w[:, lanes])
            total = total + matmul(g_up[here, :hidden], up_w[:, lanes])
            parts[here, lanes] = total.astype(bf16)

        @pl.when(tick == 0)
        def _():
            onward(1)

        @pl.when(tick == 1)
        def _():
            onward(3)
            onward(4)
            sum_ends(0)
            sum_ends(1)

        @pl.when(tick == 2)
        def _():
            sum_ends(2)
            sum_ends(3)
            sum_mids(0)

        @pl.when(tick == 3)
        def _():
            sum_ends(4)
            sum_ends(5)
            sum_mids(2)
            sum_mids(3)

        @pl.when(tick >= 2)
        def _():
            for copy in out_copies(tick - 2):
                copy.wait()

        own = jnp.where(tick == 0, 1.0, 0.0)
        for first, count in lane_tiles:
            lanes = slice(first, first + count)
            total = matmul(mixed[here, :hidden], down_w[:, lanes]) + hid[:, lanes] * own
            stage[lax.rem(tick, 2), :, lanes] = total.astype(bf16)
        for copy in out_copies(tick):
            copy.start()

    for slot in range(2):
        right_copy(slot).start()
    sum_mids(4)
    sum_mids(5)

    for h in range(2):
        for c in range(LINE):

            @pl.when(col == c)
            def _():
                for way in ways(c):
                    place = 2 * c + h if way == 1 else 2 * LINE + h
                    remote(
                        coming.at[place],
                        coming.at[place],
                        rs_send.at[0],
                        rs_recv.at[place],
                        partner,
                    ).wait_recv()

    width = aux_all.shape[2]
    squares = jnp.zeros((part, 1), f32)
    inner = jnp.zeros((part, 1), f32)
    for shard in range(LINE):
        lanes = slice(shard * width, (shard + 1) * width)
        middle = hid[:, lanes]
        from_left = jnp.concatenate([coming[2 * col + h, :, lanes] for h in range(2)])
        from_right = jnp.concatenate([coming[2 * LINE + h, :, lanes] for h in range(2)])
        total = parts[:part, lanes].astype(f32) + from_left.astype(f32)
        total = total + from_right.astype(f32)
        grad_mid[:, lanes] = total
        squares = squares + jnp.sum(middle * middle, axis=1, keepdims=True)
        scaled = total * aux_all[shard, 1:2, :]
        inner = inner + jnp.sum(scaled * middle, axis=1, keepdims=True)
    inverse = lax.rsqrt(squares / D + eps)
    factor = inverse * inverse * inverse * inner / D
    for shard in range(LINE):
        lanes = slice(shard * width, (shard + 1) * width)
        middle, total = hid[:, lanes], grad_mid[:, lanes]
        gain = jnp.sum(total * middle * inverse, axis=0, keepdims=True)
        grad_gain[:, lanes] = jnp.broadcast_to(gain, (8, width))
        grad_mid[:, lanes] = (
            cots[:part, lanes].astype(f32)
            + inverse * total * aux_all[shard, 1:2, :]
            - middle * factor
        )

    for slot in range(2):
        right_copy(slot).wait()

    @pl.loop(0, LINE)
    def _(tick):
        for copy in left_copies(tick):
            copy.wait()

    for tick in (LINE - 2, LINE - 1):
        for copy in out_copies(tick):
            copy.wait()
    for c in range(LINE):

        @pl.when(col == c)
        def _():
            for way in ways(c):
                hand_on(c, way, 2 * c, n2.at[pl.ds(0, piece)]).wait_send()
                if c in (0, LINE - 1):
                    hand_on(c, way, 2 * c + 1, n2.at[pl.ds(piece, piece)]).wait_send()
                for q in ONWARD[way][c]:
                    hand_on(c, way, q).wait_send()
            for q, way in SUMS[c]:
                sum_copy(c, q, way).wait_send()


def mlp(n2, cot_full, hid, aux_all, own, peer):
    f32, bf16 = jnp.float32, jnp.bfloat16
    rows = cot_full.shape[0]
    part = n2.shape[0]
    hidden, half = own[0].shape
    shape = jax.ShapeDtypeStruct
    dma = pltpu.SemaphoreType.DMA
    outs = [(shape((rows, D), bf16), any_spec())]
    padded = -(-hidden // TILE) * TILE
    outs += [(shape((3, rows, padded), bf16), any_spec())]
    outs += [(shape((2, rows, D), bf16), any_spec())]
    outs += [(shape((part, D), f32), vmem_spec()), (shape((8, D), f32), vmem_spec())]
    wide = pltpu.VMEM((hidden, D), bf16)
    tall = pltpu.VMEM((rows, padded), bf16)
    full = pltpu.VMEM((rows, D), bf16)
    return pl.pallas_call(
        mlp_kernel,
        out_shape=[o[0] for o in outs],
        in_specs=[any_spec(), any_spec(), vmem_spec(), vmem_spec()] + [any_spec()] * 6,
        out_specs=[o[1] for o in outs],
        scratch_shapes=[
            wide,
            wide,
            wide,
            tall,
            tall,
            tall,
            full,
            full,
            full,
            pltpu.VMEM((2 * LINE + 2, part // 2, D), bf16),
            pltpu.VMEM((2, part, D), bf16),
            dma((len(hidden_tiles(hidden)), 6)),
            dma((2 * LINE,)),
            dma,
            dma((2, 2 * LINE)),
            dma((2 * LINE,)),
            dma((2 * LINE,)),
            dma((2 * LINE + 2,)),
            dma((2, 2)),
            dma((LINE, 3)),
            dma((2,)),
        ],
        compiler_params=pltpu.CompilerParams(
            collective_id=2, has_side_effects=True, vmem_limit_bytes=62 * 2**20
        ),
        cost_estimate=pl.CostEstimate(
            flops=64 * 10**9, bytes_accessed=60 * 10**6, transcendentals=10**7
        ),
        name="mlp",
    )(n2, cot_full, hid, aux_all, *own, *peer)


CHUNK = 320
TAIL = 960
LAG = 2
RING = 12


class AllReduce:
    def __init__(self, place, total, inbox, sends, recvs, result, own_sems, chunks):
        self.dp, self.row, self.col = place
        self.total, self.inbox, self.sends, self.recvs = total, inbox, sends, recvs
        self.result, self.own_sems, self.chunks = result, own_sems, chunks
        x, y = lax.rem(self.dp, 2), self.dp // 2
        over_x = (self.dp + 1 - 2 * x, self.row, self.col)
        over_y = (self.dp + 2 - 4 * y, self.row, self.col)
        lanes = total.shape[1] // 2
        self.kinds = (
            (pl.ds(0, lanes), x, over_x, y, over_y),
            (pl.ds(lanes, lanes), y, over_y, x, over_x),
        )

    def part(self, ref, first, count, kind):
        return ref.at[rows_at(first, count), self.kinds[kind][0]]

    def places(self, chunk, kind):
        half, quarter = CHUNK // 2, CHUNK // 4
        _, bit1, peer1, bit2, peer2 = self.kinds[kind]
        own_half, far_half = chunk * CHUNK + half * bit1, chunk * CHUNK + half * (1 - bit1)
        box = lax.rem(chunk, RING) * (half + quarter)
        return (
            (own_half, far_half, box, box + half)
            + (own_half + quarter * bit2, own_half + quarter * (1 - bit2))
            + (far_half + quarter * bit2, far_half + quarter * (1 - bit2))
            + (peer1, peer2)
        )

    def copy(self, chunk, kind, stage, leaving):
        half, quarter = CHUNK // 2, CHUNK // 4
        _, far_half, box1, box2, own, mate, far, far_mate, peer1, peer2 = self.places(chunk, kind)
        count = quarter if stage else half
        if stage < 2:
            src = self.part(self.total, (far_half, mate)[stage], count, kind)
            dst = self.part(self.inbox, (box1, box2)[stage], count, kind)
        else:
            held = self.total if stage < 4 else self.result
            src = self.part(held, mate if stage == 4 else own, count, kind)
            if leaving:
                dst = self.part(self.result, mate if stage == 4 else own, count, kind)
            else:
                dst = self.part(self.result, (mate, far, far_mate)[stage - 2], count, kind)
        slot = lax.rem(chunk, RING)
        return remote(
            src,
            dst,
            self.sends.at[slot, kind, stage],
            self.recvs.at[slot, kind, stage],
            peer2 if stage in (1, 2) else peer1,
        )

    def own_copy(self, chunk, kind):
        own = self.places(chunk, kind)[4]
        return pltpu.make_async_copy(
            self.part(self.total, own, CHUNK // 4, kind),
            self.part(self.result, own, CHUNK // 4, kind),
            self.own_sems.at[lax.rem(chunk, RING), kind],
        )

    def add(self, chunk, kind, stage):
        self.copy(chunk, kind, stage, False).wait_recv()
        own_half, _, box1, box2, own, *_ = self.places(chunk, kind)
        count = CHUNK // 4 if stage else CHUNK // 2
        lanes = self.kinds[kind][0]
        mine = rows_at(own if stage else own_half, count)
        coming = self.inbox[rows_at(box2 if stage else box1, count), lanes].astype(jnp.float32)
        self.total[mine, lanes] = (
            self.total[mine, lanes].astype(jnp.float32) + coming
        ).astype(jnp.bfloat16)

    def step(self, number):
        for stage in range(5):

            @pl.when((number - stage * LAG >= 0) & (number - stage * LAG < self.chunks))
            def _():
                chunk = number - stage * LAG
                for kind in range(2):
                    if stage == 0:
                        self.copy(chunk, kind, 0, True).start()
                    elif stage == 1:
                        self.add(chunk, kind, 0)
                        self.copy(chunk, kind, 1, True).start()
                    elif stage == 2:
                        self.add(chunk, kind, 1)
                        self.copy(chunk, kind, 2, True).start()
                        self.copy(chunk, kind, 3, True).start()
                        self.own_copy(chunk, kind).start()
                    elif stage == 3:
                        self.copy(chunk, kind, 2, False).wait_recv()
                        self.copy(chunk, kind, 4, True).start()
                    else:
                        self.copy(chunk, kind, 3, False).wait_recv()
                        self.copy(chunk, kind, 4, False).wait_recv()
                        self.own_copy(chunk, kind).wait()
                        for sent in range(5):
                            self.copy(chunk, kind, sent, True).wait_send()


class RowChain(Chain):
    def block(self, shard, chunk):
        shard_rows = self.full.shape[0] // self.count
        count = shard_rows // self.chunks
        return self.full.at[rows_at(shard * shard_rows + chunk * count, count)]

    def copy(self, way, step, shard, chunk):
        self.rows = self.full.shape[0] // self.count // self.chunks
        return super().copy(way, step, shard, chunk)


def back_kernel(
    heads,
    lefts,
    rights,
    grad_mid,
    aux_all,
    gain_in,
    wof_in,
    wall_in,
    n1_in,
    x_in,
    kv_in,
    q_in,
    att_in,
    lse_in,
    trig_in,
    attl_in,
    lengths,
    grad_x,
    sums_out,
    gq_out,
    gkv_out,
    small_out,
    total,
    inbox,
    give_buf,
    got_buf,
    tiles,
    y,
    big,
    wall,
    x,
    kv,
    q,
    att,
    lse,
    trig,
    att_low,
    low,
    ga_send,
    ga,
    dkv,
    kv_give,
    kv_got,
    mate_give,
    mate_got,
    gqk,
    gn1,
    gain_sum,
    gains,
    gains_got,
    load_sem,
    y_sem,
    tile_sem,
    credit,
    swap_send,
    swap_recv,
    ar_send,
    ar_recv,
    result_sem,
    ga_ssem,
    ga_rsem,
    gm_send,
    gm_recv,
    kv_sem,
    mate_sem,
    fin_send,
    fin_recv,
    gain_ssem,
    gain_rsem,
    end_sem,
):
    f32, bf16 = jnp.float32, jnp.bfloat16
    dp, row, col = lax.axis_index("dp"), lax.axis_index("row"), lax.axis_index("col")
    place = (dp, row, col)
    part = grad_mid.shape[0]
    rows = LINE * part
    width = heads * HEAD_WIDTH
    half = TILE
    hidden = (total.shape[0] - TAIL) // 3
    member = lax.rem(col, 2)
    mate = (dp, row, col + 1 - 2 * member)
    partner = (dp, 1 - row, col)
    col_peers = [(dp, row, lax.rem(col + k, LINE)) for k in range(1, LINE)]
    bit_x, bit_y = lax.rem(dp, 2), dp // 2
    greet(
        col_peers
        + [partner, (dp + 1 - 2 * bit_x, row, col), (dp + 2 - 4 * bit_y, row, col)]
    )
    chunks = total.shape[0] // CHUNK
    reduce = AllReduce(place, total, inbox, ar_send, ar_recv, sums_out, result_sem, chunks)

    y_copies = [pltpu.make_async_copy(rights.at[k], y.at[k], y_sem.at[k]) for k in range(2)]

    def tile_copy(index):
        return pltpu.make_async_copy(
            lefts.at[index // 3, :, lanes_at(lax.rem(index, 3) * TILE, TILE)],
            tiles.at[lax.rem(index, 3)],
            tile_sem.at[lax.rem(index, 3)],
        )

    y_copies[0].start()
    for index in range(3):
        tile_copy(index).start()
    y_copies[1].start()
    loads = [
        pltpu.make_async_copy(src, dst, load_sem.at[k])
        for k, (src, dst) in enumerate(
            (
                (wof_in, big),
                (wall_in, wall),
                (x_in, x),
                (kv_in, kv),
                (q_in, q),
                (att_in, att),
                (lse_in, lse),
                (trig_in, trig),
                (attl_in, att_low),
            )
        )
    ]
    for copy in loads:
        copy.start()

    theirs, ours = lanes_at((1 - row) * half, half), lanes_at(row * half, half)

    def swap_copy(index):
        ring = rows_at(lax.rem(index, 2) * TILE, TILE)
        return remote(
            give_buf.at[ring],
            got_buf.at[ring],
            swap_send.at[lax.rem(index, 2)],
            swap_recv.at[lax.rem(index, 2)],
            partner,
        )

    jobs = 9
    y_copies[0].wait()

    @pl.loop(0, jobs + 1)
    def _(index):
        @pl.when(index == 3)
        def _():
            y_copies[1].wait()

        @pl.when(index < jobs)
        def _():
            tile_copy(index).wait()

            @pl.when(index >= 2)
            def _():
                pl.semaphore_wait(credit, 1)
                swap_copy(index - 2).wait_send()

            side = jnp.minimum(index // 3, 1)
            product = matmul_tn(tiles[lax.rem(index, 3)], y[side, :, theirs])
            give_buf[rows_at(lax.rem(index, 2) * TILE, TILE), :] = product.astype(bf16)
            swap_copy(index).start()

        @pl.when(index >= 1)
        def _():
            last = index - 1
            side = jnp.minimum(last // 3, 1)
            product = matmul_tn(tiles[lax.rem(last, 3)], y[side, :, ours])
            swap_copy(last).wait_recv()
            product = product + got_buf[rows_at(lax.rem(last, 2) * TILE, TILE), :].astype(f32)
            first = (last // 3) * hidden + lax.rem(last, 3) * TILE
            total[rows_at(first, TILE), :] = product.astype(bf16)
            pl.semaphore_signal(credit, inc=1, device_id=partner, device_id_type=MESH)

            @pl.when(last + 3 < jobs)
            def _():
                tile_copy(last + 3).start()

        @pl.when(lax.rem(index, 2) == 1)
        def _():
            reduce.step(index // 2)

    for copy in loads:
        copy.wait()
    for piece in range(LINE):
        lanes = slice(piece * width, (piece + 1) * width)
        low[:, lanes] = grad_mid[:, lanes].astype(bf16)

    def ga_copy(k):
        to = lax.rem(col + k, LINE)
        return remote(
            ga_send.at[k - 1],
            ga.at[rows_at(col * part, part)],
            ga_ssem.at[k - 1],
            ga_rsem.at[k - 1],
            (dp, row, to),
        )

    for k in (1, 2, 3, 0):
        shard = lax.rem(col + k, LINE)
        block = matmul_nt(low[...], big[shard]).astype(bf16)
        if k:
            ga_send[k - 1] = block
            ga_copy(k).start()
        else:
            ga[rows_at(col * part, part), :] = block
    n1_copy = pltpu.make_async_copy(n1_in, y.at[1], y_sem.at[1])
    reduce.step(5)

    span = min(512, rows)
    dkv[...] = jnp.zeros_like(dkv)
    chain = RowChain(place, low, y.at[0], gm_send, gm_recv, LINE, 2)

    @pl.loop(0, LINE)
    def _(turn):
        block = lax.rem(col + LINE - turn, LINE)
        here = rows_at(block * part, part)
        for k in range(1, LINE):

            @pl.when(turn == k)
            def _():
                ga_copy(k).wait_recv()

        first_query = row * rows + block * part
        query = q[:, here, :].reshape(heads * part, HEAD_WIDTH)
        back = jnp.concatenate(
            [ga[here, h * HEAD_WIDTH : (h + 1) * HEAD_WIDTH] for h in range(heads)], axis=0
        )
        attended = att[:, here, :].reshape(heads * part, HEAD_WIDTH)
        log_total = jnp.concatenate([lse[here, h : h + 1] for h in range(heads)], axis=0)
        delta = jnp.sum(back.astype(f32) * attended, axis=1, keepdims=True)

        def body(index, acc):
            keys = rows_at(index * span, span)
            key, value = kv[keys, :HEAD_WIDTH], kv[keys, HEAD_WIDTH:]
            scores = matmul_nt(query, key) * SCALE
            allowed = allowed_keys(lengths, first_query, part, index * span, span)
            probs = jnp.exp(scores - log_total).reshape(heads, part, span)
            probs = jnp.where(allowed[None], probs, 0.0).reshape(heads * part, span)
            grads = matmul_nt(back, value)
            grad_scores = (probs * (grads - delta)).astype(bf16)
            dkv[keys, :HEAD_WIDTH] += matmul_tn(grad_scores, query)
            dkv[keys, HEAD_WIDTH:] += matmul_tn(probs.astype(bf16), back)
            return acc + matmul(grad_scores, key)

        blocks = (first_query + part + span - 1) // span
        acc = lax.fori_loop(0, blocks, body, jnp.zeros((heads * part, HEAD_WIDTH), f32))
        cosine, sine = trig[0, here, :], -trig[1, here, :]
        for h in range(heads):
            grad = acc[h * part : (h + 1) * part] * SCALE
            lanes = slice(h * HEAD_WIDTH, (h + 1) * HEAD_WIDTH)
            gqk[here, lanes] = rotate(grad, cosine, sine).astype(bf16)
        reduce.step(6 + turn)

    y[0, rows_at(col * part, part), :] = low[...]
    for chunk in range(2):
        chain.start_own(chunk)
    n1_copy.start()

    other = rows_at((1 - row) * rows, rows)
    kv_give[...] = dkv[other, :].astype(bf16)
    kv_copy = remote(kv_give, kv_got, kv_sem.at[0], kv_sem.at[1], partner)
    kv_copy.start()
    reduce.step(10)
    kv_copy.wait_recv()
    lane = lax.broadcasted_iota(jnp.int32, (1, HEAD_WIDTH), 1)
    low_lanes = lane < HEAD_WIDTH // 2
    turn_by = HEAD_WIDTH // 2
    mate_copy = remote(mate_give, mate_got, mate_sem.at[0], mate_sem.at[1], mate)

    @pl.loop(0, LINE)
    def _(chunk):
        here = rows_at(chunk * part, part)
        there = rows_at(row * rows + chunk * part, part)
        both = dkv[there, :] + kv_got[here, :].astype(f32)
        key = rotate(both[:, :HEAD_WIDTH] * SCALE, trig[0, here, :], -trig[1, here, :])
        value = both[:, HEAD_WIDTH:]
        first = jnp.where(low_lanes, key, pltpu.roll(value, turn_by, 1))
        second = jnp.where(low_lanes, pltpu.roll(key, turn_by, 1), value)
        is_first = jnp.where(member == 0, 1.0, 0.0)
        kept = first * is_first + second * (1.0 - is_first)
        given = second * is_first + first * (1.0 - is_first)
        dkv[there, :HEAD_WIDTH] = kept
        mate_give[here, :] = given.astype(bf16)

    mate_copy.start()
    for chunk in range(2):
        chain.step(1, chunk)
    reduce.step(11)
    mate_copy.wait_recv()

    @pl.loop(0, LINE)
    def _(chunk):
        here = rows_at(chunk * part, part)
        there = rows_at(row * rows + chunk * part, part)
        kept = dkv[there, :HEAD_WIDTH] + mate_got[here, :].astype(f32)
        gqk[here, width:] = kept.astype(bf16)

    def share_at(chunk, shard):
        return big.at[chunk, pl.ds(0, part), lanes_at(shard * width, width)]

    def box_rows(slot, chunk):
        return tiles.at[
            slot // 2, rows_at(chunk * part, part), lanes_at(lax.rem(slot, 2) * width, width)
        ]

    def fin_copy(chunk, shard, way):
        to = col + 1 - 2 * way
        slot = jnp.where((way == 1) & (shard == to), LINE, shard)
        return remote(
            share_at(chunk, shard),
            box_rows(slot, chunk),
            fin_send.at[shard, chunk],
            fin_recv.at[slot, chunk],
            (dp, row, to),
        )

    def fin_got(chunk, slot):
        remote(
            box_rows(slot, chunk),
            box_rows(slot, chunk),
            fin_send.at[0, chunk],
            fin_recv.at[slot, chunk],
            partner,
        ).wait_recv()

    def fin_add(chunk, shard):
        fin_got(chunk, shard)
        share = share_at(chunk, shard)
        share[...] = (share[...].astype(f32) + box_rows(shard, chunk)[...].astype(f32)).astype(bf16)

    def fin_ends(chunk):
        @pl.when(col == 0)
        def _():
            for shard in (3, 2, 1):
                fin_copy(chunk, shard, 0).start()

        @pl.when(col == LINE - 1)
        def _():
            for shard in (0, 1, 2):
                fin_copy(chunk, shard, 1).start()

    def fin_near(chunk):
        for k in range(2):

            @pl.when(col == 1)
            def _():
                fin_add(chunk, 3 - k)
                fin_copy(chunk, 3 - k, 0).start()

            @pl.when(col == 2)
            def _():
                fin_add(chunk, k)
                fin_copy(chunk, k, 1).start()

    def fin_far(chunk):
        @pl.when(col == 1)
        def _():
            fin_add(chunk, 0)
            fin_copy(chunk, 0, 1).start()

        @pl.when(col == 2)
        def _():
            fin_add(chunk, 3)
            fin_copy(chunk, 3, 0).start()

    gain_sum[...] = jnp.zeros_like(gain_sum)
    kv_lanes = lanes_at(width + member * HEAD_WIDTH, HEAD_WIDTH)

    @pl.loop(0, LINE + 2)
    def _(chunk):
        @pl.when(chunk < LINE)
        def _():
            here = rows_at(chunk * part, part)
            squares = jnp.zeros((part, 1), f32)
            inner = jnp.zeros((part, 1), f32)
            for shard in range(LINE):
                lanes = slice(shard * width, (shard + 1) * width)
                grad = matmul_nt(gqk[here, :width], wall[lanes, :width])
                grad = grad + matmul_nt(gqk[here, width:], wall[lanes, kv_lanes])
                gn1[:, lanes] = grad
                value = x[here, lanes].astype(f32)
                squares = squares + jnp.sum(value * value, axis=1, keepdims=True)
                scaled = grad * aux_all[shard, 0:1, :]
                inner = inner + jnp.sum(scaled * value, axis=1, keepdims=True)
            inverse = lax.rsqrt(squares / D + eps)
            factor = inverse * inverse * inverse * inner / D
            own = jnp.where(chunk == col, 1.0, 0.0)
            for shard in range(LINE):
                lanes = slice(shard * width, (shard + 1) * width)
                grad, value = gn1[:, lanes], x[here, lanes].astype(f32)
                gain_sum[:, lanes] += jnp.sum(grad * value * inverse, axis=0, keepdims=True)
                result = inverse * grad * aux_all[shard, 0:1, :] - value * factor
                result = result + grad_mid[:, lanes] * own
                big[chunk, :part, lanes] = result.astype(bf16)
            fin_ends(chunk)

        @pl.when((chunk >= 1) & (chunk <= LINE))
        def _():
            fin_near(chunk - 1)

        @pl.when(chunk >= 2)
        def _():
            fin_far(chunk - 2)

        reduce.step(12 + chunk)

    gains[...] = gain_in[...]
    gains[0:1, :] = gain_sum[...]

    def gain_copy(k):
        to = lax.rem(col + k, LINE)
        return remote(
            gains.at[:, lanes_at(to * width, width)],
            gains_got.at[k - 1],
            gain_ssem.at[k - 1],
            gain_rsem.at[k - 1],
            (dp, row, to),
        )

    for k in range(1, LINE):
        gain_copy(k).start()

    for step in (2, 3):
        for chunk in range(2):
            chain.step(step, chunk)
    n1_copy.wait()
    reduce.step(18)
    for k in range(1, LINE):
        gain_copy(k).wait_recv()
    gain_total = gains[:, lanes_at(col * width, width)]
    for k in range(1, LINE):
        gain_total = gain_total + gains_got[k - 1]
    bias = jnp.zeros((1, width + HEAD_WIDTH), f32)
    for chunk in range(LINE):
        piece = gqk[chunk * part : (chunk + 1) * part, :].astype(f32)
        bias = bias + jnp.sum(piece, axis=0, keepdims=True)
    small = jnp.concatenate(
        [
            jnp.concatenate([gain_total, jnp.zeros((8, half - width), f32)], axis=1),
            jnp.concatenate(
                [
                    jnp.broadcast_to(bias, (8, width + HEAD_WIDTH)),
                    jnp.zeros((8, half - width - HEAD_WIDTH), f32),
                ],
                axis=1,
            ),
        ],
        axis=0,
    )
    base = 3 * hidden
    first_q, first_kv, first_small = width, width + half // 2, width + half // 2 + HEAD_WIDTH

    def projections(side_lanes, store):
        store(0, width, slice(0, half), matmul_tn(att_low[...], y[0, :, side_lanes]))
        product = matmul_tn(y[1, :, side_lanes], gqk[...])
        for k in range(2):
            store(
                first_q,
                half // 2,
                slice(k * width, (k + 1) * width),
                product[k * half // 2 : (k + 1) * half // 2, :width],
            )
        for k in range(half // HEAD_WIDTH):
            store(
                first_kv,
                HEAD_WIDTH,
                slice(k * HEAD_WIDTH, (k + 1) * HEAD_WIDTH),
                product[k * HEAD_WIDTH : (k + 1) * HEAD_WIDTH, width:],
            )
        store(first_small, 16, slice(0, half), small)
        store(first_small + 16, TAIL - first_small - 16, slice(0, half), None)

    for k in range(2):
        swap_copy(jobs - 2 + k).wait_send()
    pl.semaphore_wait(credit, 2)

    def store_give(first, count, lanes, value):
        if value is None:
            value = jnp.zeros((count, half), f32)
        give_buf[first : first + count, lanes] = value.astype(bf16)

    def store_keep(first, count, lanes, value):
        got = got_buf[first : first + count, lanes].astype(f32)
        if value is not None:
            got = got + value
        total[base + first : base + first + count, lanes] = got.astype(bf16)

    projections(theirs, store_give)
    tail = pl.ds(0, TAIL)
    tail_copy = remote(give_buf.at[tail], got_buf.at[tail], end_sem.at[0], end_sem.at[1], partner)
    tail_copy.start()
    reduce.step(19)
    tail_copy.wait_recv()
    projections(ours, store_keep)
    reduce.step(20)

    for c in range(LINE):

        @pl.when(col == c)
        def _():
            @pl.loop(0, LINE)
            def _(chunk):
                here = rows_at(chunk * part, part)
                result = big[chunk, :part, c * width : (c + 1) * width].astype(f32)
                if c > 0:
                    fin_got(chunk, c)
                    result = result + box_rows(c, chunk)[...].astype(f32)
                if c < LINE - 1:
                    fin_got(chunk, LINE)
                    result = result + box_rows(LINE, chunk)[...].astype(f32)
                grad_x[here, :] = result.astype(bf16)

    @pl.loop(21, chunks + 4 * LAG)
    def _(number):
        reduce.step(number)

    outs = [
        pltpu.make_async_copy(
            sums_out.at[pl.ds(base + first_q, half // 2), pl.ds(k * width, width)],
            gq_out.at[pl.ds(k * half // 2, half // 2)],
            load_sem.at[k],
        )
        for k in range(2)
    ]
    outs += [
        pltpu.make_async_copy(
            sums_out.at[pl.ds(base + first_kv, HEAD_WIDTH), pl.ds(k * HEAD_WIDTH, HEAD_WIDTH)],
            gkv_out.at[pl.ds(k * HEAD_WIDTH, HEAD_WIDTH)],
            load_sem.at[2 + k],
        )
        for k in range(half // HEAD_WIDTH)
    ]
    outs.append(
        pltpu.make_async_copy(
            sums_out.at[pl.ds(base + first_small, 16)], small_out, load_sem.at[8]
        )
    )
    for copy in outs:
        copy.start()

    chain.finish()
    for k in range(1, LINE):
        ga_copy(k).wait_send()
        gain_copy(k).wait_send()
    kv_copy.wait_send()
    mate_copy.wait_send()
    tail_copy.wait_send()
    for c in range(LINE):

        @pl.when(col == c)
        def _():
            for shard in range(LINE):
                if shard != c:

                    @pl.loop(0, LINE)
                    def _(chunk):
                        fin_copy(chunk, shard, 0 if shard > c else 1).wait_send()

    for copy in outs:
        copy.wait()


def back(lefts, rights, grad_mid, aux_all, gain_in, wof, wall, n1, x, kv, q, att, lse, trig, att_low, lengths, hidden):
    f32, bf16 = jnp.float32, jnp.bfloat16
    shape = jax.ShapeDtypeStruct
    dma = pltpu.SemaphoreType.DMA
    heads, rows, _ = q.shape
    width = heads * HEAD_WIDTH
    part = grad_mid.shape[0]
    total_rows = 3 * hidden + TAIL
    outs = [
        (shape((rows, width), bf16), vmem_spec()),
        (shape((total_rows, TILE), bf16), any_spec()),
        (shape((TILE, width), bf16), any_spec()),
        (shape((TILE, HEAD_WIDTH), bf16), any_spec()),
        (shape((16, TILE), bf16), vmem_spec()),
    ]
    vmem = pltpu.VMEM
    return pl.pallas_call(
        functools.partial(back_kernel, heads),
        out_shape=[o[0] for o in outs],
        in_specs=[any_spec()] * 2
        + [vmem_spec()] * 3
        + [any_spec()] * 10
        + [pl.BlockSpec(memory_space=pltpu.SMEM)],
        out_specs=[o[1] for o in outs],
        scratch_shapes=[
            vmem((total_rows, TILE), bf16),
            vmem((RING * CHUNK * 3 // 4, TILE), bf16),
            vmem((2 * TILE, TILE), bf16),
            vmem((2 * TILE, TILE), bf16),
            vmem((3, rows, TILE), bf16),
            vmem((2, rows, D), bf16),
            vmem(wof.shape, bf16),
            vmem(wall.shape, bf16),
            vmem(x.shape, bf16),
            vmem(kv.shape, bf16),
            vmem(q.shape, bf16),
            vmem(att.shape, f32),
            vmem(lse.shape, f32),
            vmem(trig.shape, f32),
            vmem(att_low.shape, bf16),
            vmem((part, D), bf16),
            vmem((LINE - 1, part, width), bf16),
            vmem((rows, width), bf16),
            vmem(kv.shape, f32),
            vmem((rows, 2 * HEAD_WIDTH), bf16),
            vmem((rows, 2 * HEAD_WIDTH), bf16),
            vmem((rows, HEAD_WIDTH), bf16),
            vmem((rows, HEAD_WIDTH), bf16),
            vmem((rows, width + HEAD_WIDTH), bf16),
            vmem((part, D), f32),
            vmem((1, D), f32),
            vmem((8, D), f32),
            vmem((LINE - 1, 8, width), f32),
            dma((9,)),
            dma((2,)),
            dma((3,)),
            pltpu.SemaphoreType.REGULAR,
            dma((2,)),
            dma((2,)),
            dma((RING, 2, 5)),
            dma((RING, 2, 5)),
            dma((RING, 2)),
            dma((LINE - 1,)),
            dma((LINE - 1,)),
            dma((2, LINE - 1, 2)),
            dma((LINE, 2)),
            dma((2,)),
            dma((2,)),
            dma((LINE, LINE)),
            dma((LINE + 1, LINE)),
            dma((LINE - 1,)),
            dma((LINE - 1,)),
            dma((2,)),
        ],
        compiler_params=pltpu.CompilerParams(
            collective_id=3, has_side_effects=True, vmem_limit_bytes=63 * 2**20
        ),
        cost_estimate=pl.CostEstimate(
            flops=64 * 10**9, bytes_accessed=60 * 10**6, transcendentals=10**7
        ),
        name="back",
    )(lefts, rights, grad_mid, aux_all, gain_in, wof, wall, n1, x, kv, q, att, lse, trig, att_low, lengths)


def per_device(
    inputs,
    seq_lengths,
    gain_one,
    w_query,
    b_query,
    w_key,
    b_key,
    w_value,
    b_value,
    w_out,
    gain_two,
    w_gate,
    w_up,
    w_down,
    cotangent,
):
    f32 = jnp.float32
    planes = lax.axis_size("dp")
    rows, width = inputs.shape
    kv_cols = w_key.shape[1]
    hidden = w_down.shape[0]
    half = HEAD_WIDTH // 2
    freq = theta_base ** (-(jnp.arange(half, dtype=f32) * 2.0) / HEAD_WIDTH)
    freq = jnp.concatenate([freq, freq]).reshape(1, HEAD_WIDTH)
    biases = jnp.concatenate([b_key, b_value]).astype(f32)
    biases = jnp.pad(biases, (0, width - 2 * kv_cols))
    aux = jnp.stack([gain_one, gain_two, b_query.astype(f32), biases])
    aux = jnp.pad(aux, ((0, 4), (0, 0)))
    own_kv = jnp.concatenate([w_key, w_value], axis=1)
    own = (w_gate.T, w_up.T, w_down)
    (
        x_full,
        normed_one,
        cot_full,
        queries,
        keys_values,
        attended,
        log_total,
        att_own,
        hidden_mid,
        normed_two,
        trig,
        att_low,
        aux_all,
        wall,
        wof,
        *peer,
    ) = front(
        (LINE, planes),
        aux,
        inputs,
        cotangent,
        w_query,
        own_kv,
        w_out,
        *own,
        seq_lengths,
        freq,
    )
    out_part, lefts, rights, grad_mid, grad_gain_two = mlp(
        normed_two, cot_full, hidden_mid, aux_all, own, peer
    )
    grad_inputs, sums, grad_w_query, grad_kv, small = back(
        lefts,
        rights,
        grad_mid,
        aux_all,
        grad_gain_two,
        wof,
        wall,
        normed_one,
        x_full,
        keys_values,
        queries,
        attended,
        log_total,
        trig,
        att_low.reshape(rows, width),
        seq_lengths,
        hidden,
    )
    result = lax.psum_scatter(out_part, "col", scatter_dimension=1, tiled=True)
    grad_w_down, grad_w_gate, grad_w_up = (
        sums[k * hidden : (k + 1) * hidden].astype(f32) for k in range(3)
    )
    grad_w_out = sums[3 * hidden : 3 * hidden + width].astype(f32)
    grad_kv = grad_kv.astype(f32)
    small = small.astype(f32)
    bias = small[8]
    return (
        result,
        grad_inputs,
        small[0, :width],
        grad_w_query.astype(f32),
        bias[:width],
        grad_kv[:, :kv_cols],
        bias[width : width + kv_cols],
        grad_kv[:, kv_cols:],
        bias[width + kv_cols : width + 2 * kv_cols],
        grad_w_out,
        small[1, :width],
        grad_w_gate.T,
        grad_w_up.T,
        grad_w_down,
    )


def solution(mesh):
    whole_heads = dict(mesh.shape) == {"dp": 4, "row": 2, "col": LINE}
    return jax.shard_map(
        per_device if whole_heads else per_device_any,
        mesh=mesh,
        in_specs=(
            P(("dp", "row"), "col"),
            P("dp", None),
            P("col"),
            P("row", "col"),
            P("col"),
            P("row", "col"),
            P("col"),
            P("row", "col"),
            P("col"),
            P("col", "row"),
            P("col"),
            P("row", "col"),
            P("row", "col"),
            P("col", "row"),
            P(("dp", "row"), "col"),
        ),
        out_specs=(
            P(("dp", "row"), "col"),
            P(("dp", "row"), "col"),
            P("col"),
            P("row", "col"),
            P("col"),
            P("row", "col"),
            P("col"),
            P("row", "col"),
            P("col"),
            P("col", "row"),
            P("col"),
            P("row", "col"),
            P("row", "col"),
            P("col", "row"),
        ),
        check_vma=False,
    )
```

```python
import functools

import jax
import jax.numpy as jnp
from jax import lax
from jax.experimental import pallas as pl
from jax.experimental.pallas import tpu as pltpu
from jax.sharding import PartitionSpec as P

D = 1536
HEAD_WIDTH = 128
QUERY_HEADS = 12
KEY_VALUE_HEADS = 2
DEVICE_TOKENS = 256
QW = 1536
KW = 256


theta_base = 1000000.0
eps = 1e-06


def matmul(left, right):
    return jnp.dot(left, right, preferred_element_type=jnp.float32)


def matmul_tn(left, right):
    return lax.dot_general(
        left, right, (((0,), (0,)), ((), ())), preferred_element_type=jnp.float32
    )


def matmul_nt(left, right):
    return lax.dot_general(
        left, right, (((1,), (1,)), ((), ())), preferred_element_type=jnp.float32
    )


def row_squares(values):
    return lax.psum(values, "col")


def gather_width(values):
    return lax.all_gather(values, "col", axis=1, tiled=True)


def sum_width(values):
    return lax.psum_scatter(
        values.astype(jnp.bfloat16), "col", scatter_dimension=1, tiled=True
    ).astype(jnp.float32)


def documents(lengths, places):
    doc_ends = jnp.cumsum(lengths)
    doc_starts = doc_ends - lengths
    doc_index = jnp.sum((places[:, None] >= doc_ends[None, :]).astype(jnp.int32), axis=1)
    chosen = doc_index[:, None] == jnp.arange(lengths.shape[0], dtype=jnp.int32)[None, :]
    offset = jnp.sum(jnp.where(chosen, doc_starts[None, :], 0), axis=1)
    return (doc_index, places - offset)


def rotary_embedding(values, token_position, direction):
    half_size = HEAD_WIDTH // 2
    frequency = theta_base ** (-(jnp.arange(half_size, dtype=jnp.float32) * 2.0) / HEAD_WIDTH)
    angles = token_position.astype(jnp.float32)[:, None] * frequency[None, :]
    cosine = jnp.cos(angles)[:, None, :]
    sine_part = direction * jnp.sin(angles)[:, None, :]
    leading = values[..., :half_size]
    second = values[..., half_size:]
    return jnp.concatenate(
        [leading * cosine - second * sine_part, second * cosine + leading * sine_part], axis=-1
    )


def norm_forward(hidden, gain):
    square_total = row_squares(jnp.sum(hidden * hidden, axis=1))
    inverse = lax.rsqrt(square_total / D + eps)
    normed = (hidden * inverse[:, None] * gain[None, :]).astype(jnp.bfloat16)
    return (normed, inverse)


def norm_backward(hidden, gain, inverse, grad_normed):
    scaled = grad_normed * gain[None, :]
    inner = row_squares(jnp.sum(scaled * hidden, axis=1))
    grad_hidden = (
        inverse[:, None] * scaled - hidden * (inverse * inverse * inverse * inner / D)[:, None]
    )
    grad_gain = jnp.sum(grad_normed * hidden * inverse[:, None], axis=0)
    return (grad_hidden, grad_gain)


def key_layout(gathered_keys, gathered_values, doc_all):
    seq_len = gathered_keys.shape[0]
    key_block_index = min(512, seq_len)
    count_blocks = seq_len // key_block_index
    blocks_of_keys = gathered_keys.reshape(
        count_blocks, key_block_index, gathered_keys.shape[1] // HEAD_WIDTH, HEAD_WIDTH
    )
    blocks_of_values = gathered_values.reshape(
        count_blocks, key_block_index, gathered_values.shape[1] // HEAD_WIDTH, HEAD_WIDTH
    )
    doc_blocks = doc_all.reshape(count_blocks, key_block_index)
    place_blocks = jnp.arange(seq_len, dtype=jnp.int32).reshape(count_blocks, key_block_index)
    return (blocks_of_keys, doc_blocks, place_blocks, blocks_of_values)


def block_scores(heads_of_queries, key_blk, doc_blk, place_blk, doc_local, place_local):
    scores = jnp.einsum(
        "tkgh,skh->tkgs", heads_of_queries, key_blk, preferred_element_type=jnp.float32
    ) * HEAD_WIDTH ** (-0.5)
    allowed = (doc_blk[None, :] == doc_local[:, None]) & (
        place_blk[None, :] <= place_local[:, None]
    )
    return (scores, allowed[:, None, None, :])


def attention_forward(heads_of_queries, blocks, doc_local, place_local):
    head_shape = heads_of_queries.shape[:3]

    def first_pass(state_in, packed):
        running_max, running_sum = state_in
        scores, allowed = block_scores(
            heads_of_queries, packed[0], packed[1], packed[2], doc_local, place_local
        )
        masked = jnp.where(allowed, scores, -1e30)
        new_max = jnp.maximum(running_max, jnp.max(masked, axis=-1))
        raised = jnp.where(allowed, jnp.exp(scores - new_max[..., None]), 0.0)
        running_sum = running_sum * jnp.exp(running_max - new_max) + jnp.sum(raised, axis=-1)
        return ((new_max, running_sum), None)

    initial = (jnp.full(head_shape, -1e30, jnp.float32), jnp.zeros(head_shape, jnp.float32))
    (running_max, running_sum), unused = lax.scan(first_pass, initial, blocks)
    log_total = running_max + jnp.log(running_sum)

    def second_pass(acc_out, packed):
        scores, allowed = block_scores(
            heads_of_queries, packed[0], packed[1], packed[2], doc_local, place_local
        )
        probs_low = jnp.where(allowed, jnp.exp(scores - log_total[..., None]), 0.0).astype(
            jnp.bfloat16
        )
        return (
            acc_out
            + jnp.einsum(
                "tkgs,skh->tkgh", probs_low, packed[3], preferred_element_type=jnp.float32
            ),
            None,
        )

    attended, unused = lax.scan(second_pass, jnp.zeros(heads_of_queries.shape, jnp.float32), blocks)
    return (attended, log_total)


def attention_backward(
    heads_of_queries, blocks, doc_local, place_local, log_total, attended, heads_gradient
):
    inner = jnp.sum(heads_gradient.astype(jnp.float32) * attended, axis=-1)
    scale_factor = HEAD_WIDTH ** (-0.5)

    def back_pass(grad_query, packed):
        scores, allowed = block_scores(
            heads_of_queries, packed[0], packed[1], packed[2], doc_local, place_local
        )
        probs = jnp.where(allowed, jnp.exp(scores - log_total[..., None]), 0.0)
        grad_probs = jnp.einsum(
            "tkgh,skh->tkgs", heads_gradient, packed[3], preferred_element_type=jnp.float32
        )
        grad_scores = (probs * (grad_probs - inner[..., None])).astype(jnp.bfloat16)
        grad_query = (
            grad_query
            + jnp.einsum(
                "tkgs,skh->tkgh", grad_scores, packed[0], preferred_element_type=jnp.float32
            )
            * scale_factor
        )
        grad_key = (
            jnp.einsum(
                "tkgs,tkgh->skh", grad_scores, heads_of_queries, preferred_element_type=jnp.float32
            )
            * scale_factor
        )
        grad_value = jnp.einsum(
            "tkgs,tkgh->skh",
            probs.astype(jnp.bfloat16),
            heads_gradient,
            preferred_element_type=jnp.float32,
        )
        return (grad_query, (grad_key, grad_value))

    grad_query, (key_grads, value_grads) = lax.scan(
        back_pass, jnp.zeros(heads_of_queries.shape, jnp.float32), blocks
    )
    seq_len = key_grads.shape[0] * key_grads.shape[1]
    return (grad_query, key_grads.reshape(seq_len, -1), value_grads.reshape(seq_len, -1))


def per_device_any(
    inputs,
    seq_lengths,
    gain_one,
    w_query,
    b_query,
    w_key,
    b_key,
    w_value,
    b_value,
    w_out,
    gain_two,
    w_gate,
    w_up,
    w_down,
    cotangent,
):
    full_query, full_key, full_value, full_out, full_gate, full_up, full_down = (
        lax.all_gather(w_query, "row", axis=0, tiled=True),
        lax.all_gather(w_key, "row", axis=0, tiled=True),
        lax.all_gather(w_value, "row", axis=0, tiled=True),
        lax.all_gather(w_out, "row", axis=1, tiled=True),
        lax.all_gather(w_gate, "row", axis=0, tiled=True),
        lax.all_gather(w_up, "row", axis=0, tiled=True),
        lax.all_gather(w_down, "row", axis=1, tiled=True),
    )
    row_pos = lax.axis_index("row")
    col_pos = lax.axis_index("col")
    row_count = lax.axis_size("row")
    col_count = lax.axis_size("col")
    seq_len = DEVICE_TOKENS * row_count * col_count
    query_group_width = QUERY_HEADS // KEY_VALUE_HEADS
    lengths = seq_lengths[0]
    place_local = (row_pos * col_count + col_pos) * DEVICE_TOKENS + jnp.arange(
        DEVICE_TOKENS, dtype=jnp.int32
    )
    doc_local, local_position = documents(lengths, place_local)
    doc_all = documents(lengths, jnp.arange(seq_len, dtype=jnp.int32))[0]
    hidden_in = inputs.astype(jnp.float32)
    normed_one, inverse_one = norm_forward(hidden_in, gain_one)
    normed_full = gather_width(normed_one)
    query_lin = (matmul(normed_full, full_query) + b_query.astype(jnp.float32)).astype(jnp.bfloat16)
    projected_keys = (matmul(normed_full, full_key) + b_key.astype(jnp.float32)).astype(
        jnp.bfloat16
    )
    projected_values = (matmul(normed_full, full_value) + b_value.astype(jnp.float32)).astype(
        jnp.bfloat16
    )
    query_rows, rows_of_keys, value_rows = (
        lax.all_to_all(query_lin, "col", split_axis=0, concat_axis=1, tiled=True),
        lax.all_to_all(projected_keys, "col", split_axis=0, concat_axis=1, tiled=True),
        lax.all_to_all(projected_values, "col", split_axis=0, concat_axis=1, tiled=True),
    )
    rotated_queries = rotary_embedding(
        query_rows.astype(jnp.float32).reshape(DEVICE_TOKENS, QUERY_HEADS, HEAD_WIDTH),
        local_position,
        1.0,
    ).astype(jnp.bfloat16)
    rotated_keys = rotary_embedding(
        rows_of_keys.astype(jnp.float32).reshape(DEVICE_TOKENS, KEY_VALUE_HEADS, HEAD_WIDTH),
        local_position,
        1.0,
    ).astype(jnp.bfloat16)
    gathered_keys, gathered_values = (
        lax.all_gather(rotated_keys.reshape(DEVICE_TOKENS, KW), ("row", "col"), axis=0, tiled=True),
        lax.all_gather(value_rows, ("row", "col"), axis=0, tiled=True),
    )
    blocks = key_layout(gathered_keys, gathered_values, doc_all)
    heads_of_queries = rotated_queries.reshape(
        DEVICE_TOKENS, KEY_VALUE_HEADS, query_group_width, HEAD_WIDTH
    )
    attended, log_total = attention_forward(heads_of_queries, blocks, doc_local, place_local)
    attended_low = attended.reshape(DEVICE_TOKENS, QW).astype(jnp.bfloat16)
    attended_cols = lax.all_to_all(attended_low, "col", split_axis=1, concat_axis=0, tiled=True)
    hidden_mid = hidden_in + sum_width(matmul(attended_cols, full_out))
    normed_two, inverse_two = norm_forward(hidden_mid, gain_two)
    normed_wide = gather_width(normed_two)
    gate = matmul(normed_wide, full_gate)
    up_proj = matmul(normed_wide, full_up)
    sigmoid_gate = jax.nn.sigmoid(gate)
    silu_gate = gate * sigmoid_gate
    mixed = (silu_gate * up_proj).astype(jnp.bfloat16)
    result = (hidden_mid + sum_width(matmul(mixed, full_down))).astype(jnp.bfloat16)
    grad_full = gather_width(cotangent)
    grad_w_down = matmul_tn(mixed, grad_full)
    grad_mixed = matmul_nt(grad_full, full_down)
    grad_gate = (grad_mixed * up_proj * sigmoid_gate * (1.0 + gate * (1.0 - sigmoid_gate))).astype(
        jnp.bfloat16
    )
    grad_up = (grad_mixed * silu_gate).astype(jnp.bfloat16)
    grad_w_gate = matmul_tn(normed_wide, grad_gate)
    grad_w_up = matmul_tn(normed_wide, grad_up)
    grad_normed_two = sum_width(matmul_nt(grad_gate, full_gate) + matmul_nt(grad_up, full_up))
    grad_back_two, grad_gain_two = norm_backward(hidden_mid, gain_two, inverse_two, grad_normed_two)
    grad_mid = cotangent.astype(jnp.float32) + grad_back_two
    grad_attn_full = gather_width(grad_mid.astype(jnp.bfloat16))
    grad_w_out = matmul_tn(attended_cols, grad_attn_full)
    grad_attended_cols = matmul_nt(grad_attn_full, full_out).astype(jnp.bfloat16)
    attended_gradient = lax.all_to_all(
        grad_attended_cols, "col", split_axis=0, concat_axis=1, tiled=True
    )
    heads_gradient = attended_gradient.reshape(
        DEVICE_TOKENS, KEY_VALUE_HEADS, query_group_width, HEAD_WIDTH
    )
    grad_query_rot, key_grads, value_grads = attention_backward(
        heads_of_queries, blocks, doc_local, place_local, log_total, attended, heads_gradient
    )
    rotated_key_gradient, grad_value = (
        lax.psum_scatter(
            key_grads.astype(jnp.bfloat16), ("row", "col"), scatter_dimension=0, tiled=True
        ).astype(jnp.float32),
        lax.psum_scatter(
            value_grads.astype(jnp.bfloat16), ("row", "col"), scatter_dimension=0, tiled=True
        ).astype(jnp.float32),
    )
    grad_query_lin = (
        rotary_embedding(
            grad_query_rot.reshape(DEVICE_TOKENS, QUERY_HEADS, HEAD_WIDTH), local_position, -1.0
        )
        .reshape(DEVICE_TOKENS, QW)
        .astype(jnp.bfloat16)
    )
    grad_key_lin = (
        rotary_embedding(
            rotated_key_gradient.reshape(DEVICE_TOKENS, KEY_VALUE_HEADS, HEAD_WIDTH),
            local_position,
            -1.0,
        )
        .reshape(DEVICE_TOKENS, KW)
        .astype(jnp.bfloat16)
    )
    grad_value_lin = grad_value.astype(jnp.bfloat16)
    query_grad_cols, key_grad_cols, value_grad_cols = (
        lax.all_to_all(grad_query_lin, "col", split_axis=1, concat_axis=0, tiled=True),
        lax.all_to_all(grad_key_lin, "col", split_axis=1, concat_axis=0, tiled=True),
        lax.all_to_all(grad_value_lin, "col", split_axis=1, concat_axis=0, tiled=True),
    )
    grad_b_query = jnp.sum(query_grad_cols.astype(jnp.float32), axis=0)
    grad_b_key = jnp.sum(key_grad_cols.astype(jnp.float32), axis=0)
    grad_b_value = jnp.sum(value_grad_cols.astype(jnp.float32), axis=0)
    grad_w_query = matmul_tn(normed_full, query_grad_cols)
    grad_w_key = matmul_tn(normed_full, key_grad_cols)
    grad_w_value = matmul_tn(normed_full, value_grad_cols)
    grad_normed_one = sum_width(
        matmul_nt(query_grad_cols, full_query)
        + matmul_nt(key_grad_cols, full_key)
        + matmul_nt(value_grad_cols, full_value)
    )
    grad_back_one, grad_gain_one = norm_backward(hidden_in, gain_one, inverse_one, grad_normed_one)
    grad_inputs = (grad_mid + grad_back_one).astype(jnp.bfloat16)
    summed = (
        lax.psum(grad_w_query.astype(jnp.bfloat16), ("dp", "row")).astype(jnp.float32),
        lax.psum(grad_w_key.astype(jnp.bfloat16), ("dp", "row")).astype(jnp.float32),
        lax.psum(grad_w_value.astype(jnp.bfloat16), ("dp", "row")).astype(jnp.float32),
        lax.psum(grad_w_out.astype(jnp.bfloat16), ("dp", "row")).astype(jnp.float32),
        lax.psum(grad_w_gate.astype(jnp.bfloat16), ("dp", "row")).astype(jnp.float32),
        lax.psum(grad_w_up.astype(jnp.bfloat16), ("dp", "row")).astype(jnp.float32),
        lax.psum(grad_w_down.astype(jnp.bfloat16), ("dp", "row")).astype(jnp.float32),
        lax.psum(grad_gain_one.astype(jnp.bfloat16), ("dp", "row")).astype(jnp.float32),
        lax.psum(grad_b_query.astype(jnp.bfloat16), ("dp", "row")).astype(jnp.float32),
        lax.psum(grad_b_key.astype(jnp.bfloat16), ("dp", "row")).astype(jnp.float32),
        lax.psum(grad_b_value.astype(jnp.bfloat16), ("dp", "row")).astype(jnp.float32),
        lax.psum(grad_gain_two.astype(jnp.bfloat16), ("dp", "row")).astype(jnp.float32),
    )
    rows_each = D // row_count
    split_dims = (0, 0, 0, 1, 0, 0, 1)
    weight_sums = tuple(
        (
            lax.dynamic_slice_in_dim(
                summed[member], row_pos * rows_each, rows_each, split_dims[member]
            )
            for member in range(7)
        )
    )
    small_sums = summed[7:]
    return (
        result,
        grad_inputs,
        small_sums[0],
        weight_sums[0],
        small_sums[1],
        weight_sums[1],
        small_sums[2],
        weight_sums[2],
        small_sums[3],
        weight_sums[3],
        small_sums[4],
        weight_sums[4],
        weight_sums[5],
        weight_sums[6],
    )


MESH = pl.DeviceIdType.MESH
NEG = -1e30
SCALE = HEAD_WIDTH ** (-0.5)


def vmem_spec():
    return pl.BlockSpec(memory_space=pltpu.VMEM)


def any_spec():
    return pl.BlockSpec(memory_space=pl.ANY)


def remote(src, dst, send_sem, recv_sem, device):
    return pltpu.make_async_remote_copy(
        src_ref=src,
        dst_ref=dst,
        send_sem=send_sem,
        recv_sem=recv_sem,
        device_id=device,
        device_id_type=MESH,
    )


def greet(peers):
    barrier = pltpu.get_barrier_semaphore()
    for peer in peers:
        pl.semaphore_signal(barrier, inc=1, device_id=peer, device_id_type=MESH)
    pl.semaphore_wait(barrier, len(peers))


def rows_at(first, count):
    return pl.ds(pl.multiple_of(first, 16), count)


def lanes_at(first, count):
    return pl.ds(pl.multiple_of(first, 128), count)


class Chain:
    def __init__(self, place, own, full, sends, recvs, count, chunks):
        self.dp, self.row, self.col = place
        self.own, self.full, self.sends, self.recvs = own, full, sends, recvs
        self.count, self.chunks = count, chunks
        self.width = full.shape[1] // count
        self.rows = full.shape[0] // chunks

    def block(self, shard, chunk):
        return self.full.at[
            rows_at(chunk * self.rows, self.rows), lanes_at(shard * self.width, self.width)
        ]

    def copy(self, way, step, shard, chunk):
        src = self.block(shard, chunk)
        if step == 0:
            src = self.own.at[rows_at(chunk * self.rows, self.rows)]
        device = (self.dp, self.row, self.col + (1 if way == 0 else -1))
        return remote(
            src,
            self.block(shard, chunk),
            self.sends.at[way, step, chunk],
            self.recvs.at[shard, chunk],
            device,
        )

    def start_own(self, chunk):
        @pl.when(self.col < self.count - 1)
        def _():
            self.copy(0, 0, self.col, chunk).start()

        @pl.when(self.col > 0)
        def _():
            self.copy(1, 0, self.col, chunk).start()

    def step(self, step, chunk):
        left, right = self.col - step, self.col + step

        @pl.when(left >= 0)
        def _():
            self.copy(0, step, left, chunk).wait_recv()

        if step < self.count - 1:

            @pl.when((left >= 0) & (self.col < self.count - 1))
            def _():
                self.copy(0, step, left, chunk).start()

        @pl.when(right < self.count)
        def _():
            self.copy(1, step, right, chunk).wait_recv()

        if step < self.count - 1:

            @pl.when((right < self.count) & (self.col > 0))
            def _():
                self.copy(1, step, right, chunk).start()

    def finish(self):
        for step in range(self.count - 1):
            left, right = self.col - step, self.col + step

            @pl.when((left >= 0) & (self.col < self.count - 1))
            def _():
                @pl.loop(0, self.chunks)
                def _(chunk):
                    self.copy(0, step, left, chunk).wait_send()

            @pl.when((right < self.count) & (self.col > 0))
            def _():
                @pl.loop(0, self.chunks)
                def _(chunk):
                    self.copy(1, step, right, chunk).wait_send()


def doc_start(lengths, place):
    first = jnp.zeros_like(place)
    end = 0
    for doc in range(lengths.shape[1]):
        end = end + lengths[0, doc]
        first = jnp.where(place >= end, end, first)
    return first


def rotate(values, cosine, sine):
    return values * cosine + pltpu.roll(values, HEAD_WIDTH // 2, 1) * sine


def allowed_keys(lengths, first_query, queries, first_key, keys):
    query = first_query + lax.broadcasted_iota(jnp.int32, (queries, 1), 0)
    key = first_key + lax.broadcasted_iota(jnp.int32, (1, keys), 1)
    return (key >= doc_start(lengths, query)) & (key <= query)


def front_kernel(
    heads,
    dims,
    aux,
    x,
    cot,
    wq,
    wkv,
    wout,
    w_gate,
    w_up,
    w_down,
    lengths,
    freq,
    x_out,
    n1_out,
    cot_out,
    q_out,
    kv_out,
    att_out,
    lse_out,
    attl_out,
    hid_out,
    n2_out,
    trig_out,
    att_low,
    aux_out,
    wall_out,
    wof_out,
    peer_gate,
    peer_up,
    peer_down,
    x_full,
    n1,
    cot_full,
    x_send,
    x_recv,
    c_send,
    c_recv,
    local_sem,
    aux_send,
    aux_recv,
    wall_send,
    wall_recv,
    z_send,
    z_recv,
    d_send,
    d_recv,
    r_send,
    r_recv,
    kv_send,
    kv_recv,
    a2a_send,
    a2a_recv,
    m_send,
    m_recv,
):
    count, planes = dims
    f32, bf16 = jnp.float32, jnp.bfloat16
    dp, row, col = lax.axis_index("dp"), lax.axis_index("row"), lax.axis_index("col")
    place = (dp, row, col)
    rows, width = x.shape
    part = rows // count
    half = wq.shape[0]
    member = lax.rem(col, 2)
    mate = col + 1 - 2 * member
    col_peers = [(dp, row, lax.rem(col + k, count)) for k in range(1, count)]
    dp_peers = [(lax.rem(dp + k, planes), row, col) for k in range(1, planes)]
    partner = (dp, 1 - row, col)
    across = (dp, 1 - row, mate)
    greet(col_peers + dp_peers + [partner, across])

    chain_x = Chain(place, x, x_full, x_send, x_recv, count, count)
    chain_c = Chain(place, cot, cot_full, c_send, c_recv, count, count)
    own_lanes = lanes_at(col * width, width)
    copy_x = pltpu.make_async_copy(x, x_full.at[:, own_lanes], local_sem.at[0])
    copy_x.start()
    aux_copies = [
        remote(aux, aux_out.at[col], aux_send.at[k], aux_recv.at[k], peer)
        for k, peer in enumerate(col_peers)
    ]
    for copy in aux_copies:
        copy.start()

    @pl.loop(0, count)
    def _(chunk):
        chain_x.start_own(chunk)

    own_half = rows_at(row * half, half)
    kv_lanes = lanes_at(width + member * HEAD_WIDTH, HEAD_WIDTH)
    copy_q = pltpu.make_async_copy(wq, wall_out.at[own_half, pl.ds(0, width)], local_sem.at[1])
    copy_kv = pltpu.make_async_copy(wkv, wall_out.at[own_half, kv_lanes], local_sem.at[2])
    copy_q.start()
    copy_kv.start()
    wall_copies = [
        remote(
            wq, wall_out.at[own_half, pl.ds(0, width)], wall_send.at[0], wall_recv.at[0], partner
        )
    ] + [
        remote(wkv, wall_out.at[own_half, kv_lanes], wall_send.at[k], wall_recv.at[k], peer)
        for k, peer in ((1, partner), (2, (dp, row, mate)), (3, across))
    ]
    for copy in wall_copies:
        copy.start()
    mlp_copies = [
        remote(src, dst, m_send.at[k], m_recv.at[k], partner)
        for k, (src, dst) in enumerate(
            ((w_gate, peer_gate), (w_up, peer_up), (w_down, peer_down))
        )
    ]
    for copy in mlp_copies:
        copy.start()
    copy_c = pltpu.make_async_copy(cot, cot_full.at[:, own_lanes], local_sem.at[3])
    copy_c.start()
    quarter = wout.shape[0] // planes
    out_lanes = lanes_at(row * half, half)

    def wof_block(shard, plane, side):
        return wof_out.at[
            shard, rows_at(plane * quarter, quarter), lanes_at(side * half, half)
        ]

    def wof_blocks(plane, side):
        return wof_out.at[:, rows_at(plane * quarter, quarter), lanes_at(side * half, half)]

    own_quarter = wout.at[rows_at(dp * quarter, quarter)]
    copy_o = pltpu.make_async_copy(own_quarter, wof_block(col, dp, row), local_sem.at[4])
    copy_o.start()

    token = row * rows + lax.broadcasted_iota(jnp.int32, (rows, 1), 0)
    position = (token - doc_start(lengths, token)).astype(f32)
    angle = position * freq[...]
    trig_out[0] = jnp.cos(angle)
    lane = lax.broadcasted_iota(jnp.int32, (1, HEAD_WIDTH), 1)
    trig_out[1] = jnp.sin(angle) * jnp.where(lane < HEAD_WIDTH // 2, -1.0, 1.0)
    aux_out[col] = aux[...]

    for step in range(1, count - 1):

        @pl.loop(0, count)
        def _(chunk):
            chain_x.step(step, chunk)

    z_copies = [
        remote(own_quarter, wof_block(col, dp, row), z_send.at[k], z_recv.at[k], peer)
        for k, peer in enumerate(col_peers)
    ]
    for copy in z_copies:
        copy.start()

    @pl.loop(0, count)
    def _(chunk):
        chain_c.start_own(chunk)

    copy_x.wait()
    copy_q.wait()
    copy_kv.wait()
    for copy in aux_copies:
        copy.wait_recv()
    for k, (side, who) in enumerate(
        ((1 - row, None), (1 - row, member), (row, 1 - member), (1 - row, 1 - member))
    ):
        side_rows = rows_at(side * half, half)
        if who is None:
            dst, src = wall_out.at[side_rows, pl.ds(0, width)], wq
        else:
            dst = wall_out.at[side_rows, lanes_at(width + who * HEAD_WIDTH, HEAD_WIDTH)]
            src = wkv
        remote(src, dst, wall_send.at[k], wall_recv.at[k], partner).wait_recv()

    mate_aux = aux_out[mate]
    even = jnp.where(member == 0, aux[3:4, :HEAD_WIDTH], mate_aux[3:4, :HEAD_WIDTH])
    odd = jnp.where(member == 0, mate_aux[3:4, :HEAD_WIDTH], aux[3:4, :HEAD_WIDTH])
    low_lanes = lane < HEAD_WIDTH // 2
    key_bias = jnp.where(low_lanes, even, pltpu.roll(odd, HEAD_WIDTH // 2, 1))
    value_bias = jnp.where(low_lanes, pltpu.roll(even, HEAD_WIDTH // 2, 1), odd)

    def kv_chunk(side, chunk):
        return kv_out.at[rows_at(side * rows + chunk * part, part)]

    def kv_copy(chunk):
        return remote(
            kv_chunk(row, chunk),
            kv_chunk(row, chunk),
            kv_send.at[chunk],
            kv_recv.at[chunk],
            partner,
        )

    @pl.loop(0, count)
    def _(chunk):
        chain_x.step(count - 1, chunk)
        here = rows_at(chunk * part, part)
        squares = jnp.zeros((part, 1), f32)
        for shard in range(count):
            piece = x_full[here, shard * width : (shard + 1) * width].astype(f32)
            squares = squares + jnp.sum(piece * piece, axis=1, keepdims=True)
        inverse = lax.rsqrt(squares / D + eps)
        for shard in range(count):
            lanes = slice(shard * width, (shard + 1) * width)
            piece = x_full[here, lanes].astype(f32)
            n1[here, lanes] = (piece * inverse * aux_out[shard, 0:1, :]).astype(bf16)
        lin = matmul(n1[here, :], wall_out[...])
        cosine, sine = trig_out[0, here, :], trig_out[1, here, :]
        for head in range(heads):
            lanes = slice(head * HEAD_WIDTH, (head + 1) * HEAD_WIDTH)
            query = (lin[:, lanes] + aux[2:3, lanes]).astype(bf16).astype(f32)
            q_out[head, here, :] = rotate(query, cosine, sine).astype(bf16)
        first = lin[:, width : width + HEAD_WIDTH]
        second = lin[:, width + HEAD_WIDTH : width + 2 * HEAD_WIDTH]
        turn = HEAD_WIDTH // 2
        key = jnp.where(low_lanes, first, pltpu.roll(second, turn, 1)) + key_bias
        value = jnp.where(low_lanes, pltpu.roll(first, turn, 1), second) + value_bias
        there = rows_at(row * rows + chunk * part, part)
        kv_out[there, :HEAD_WIDTH] = rotate(
            key.astype(bf16).astype(f32), cosine, sine
        ).astype(bf16)
        kv_out[there, HEAD_WIDTH:] = value.astype(bf16)
        kv_copy(chunk).start()

    n1_copy = pltpu.make_async_copy(n1, n1_out, local_sem.at[5])
    n1_copy.start()
    x_copy = pltpu.make_async_copy(x_full, x_out, local_sem.at[6])
    x_copy.start()

    copy_o.wait()
    for k in range(1, count):
        shard = lax.rem(col + count - k, count)
        remote(
            own_quarter, wof_block(shard, dp, row), z_send.at[k - 1], z_recv.at[k - 1], partner
        ).wait_recv()
    d_copies = [
        remote(wof_blocks(dp, row), wof_blocks(dp, row), d_send.at[k], d_recv.at[k], peer)
        for k, peer in enumerate(dp_peers)
    ]
    r_copies = [
        remote(
            wof_blocks(lax.rem(dp + planes - k, planes), row),
            wof_blocks(lax.rem(dp + planes - k, planes), row),
            r_send.at[k],
            r_recv.at[k],
            partner,
        )
        for k in range(planes)
    ]
    for copy in d_copies:
        copy.start()
    r_copies[0].start()

    @pl.loop(0, count)
    def _(chunk):
        remote(
            kv_chunk(row, chunk),
            kv_chunk(1 - row, chunk),
            kv_send.at[chunk],
            kv_recv.at[chunk],
            partner,
        ).wait_recv()

    span = min(512, rows)

    def a2a_copy(block):
        return remote(
            att_low.at[block],
            attl_out.at[:, own_lanes],
            a2a_send.at[block],
            a2a_recv.at[col],
            (dp, row, block),
        )

    @pl.loop(0, count)
    def _(block):
        here = rows_at(block * part, part)
        first_query = row * rows + block * part
        query = q_out[:, here, :].reshape(heads * part, HEAD_WIDTH)

        def body(index, state):
            largest, total, acc = state
            keys = rows_at(index * span, span)
            scores = matmul_nt(query, kv_out[keys, :HEAD_WIDTH]) * SCALE
            allowed = allowed_keys(lengths, first_query, part, index * span, span)
            scores = jnp.where(allowed[None], scores.reshape(heads, part, span), NEG)
            scores = scores.reshape(heads * part, span)
            new = jnp.maximum(largest, jnp.max(scores, axis=1, keepdims=True))
            raised = jnp.exp(scores - new)
            alpha = jnp.exp(largest - new)
            total = total * alpha + jnp.sum(raised, axis=1, keepdims=True)
            acc = acc * alpha + matmul(raised.astype(bf16), kv_out[keys, HEAD_WIDTH:])
            return new, total, acc

        state = (
            jnp.full((heads * part, 1), NEG, f32),
            jnp.zeros((heads * part, 1), f32),
            jnp.zeros((heads * part, HEAD_WIDTH), f32),
        )
        blocks = (first_query + part + span - 1) // span
        largest, total, acc = lax.fori_loop(0, blocks, body, state)
        attended = (acc / total).reshape(heads, part, HEAD_WIDTH)
        att_out[:, here, :] = attended
        log_total = (largest + jnp.log(total)).reshape(heads, part, 1)
        spread = jnp.zeros((part, HEAD_WIDTH), f32)
        for head in range(heads):
            spread = jnp.where(lane == head, log_total[head], spread)
        lse_out[here, :] = spread
        for head in range(heads):
            lanes = slice(head * HEAD_WIDTH, (head + 1) * HEAD_WIDTH)
            att_low[block, :, lanes] = attended[head].astype(bf16)

        @pl.when(block != col)
        def _():
            a2a_copy(block).start()

        chain_c.step(1, block)

    attl_out[:, own_lanes] = att_low[col]
    for step in range(2, count - 1):

        @pl.loop(0, count)
        def _(chunk):
            chain_c.step(step, chunk)

    for k in range(1, planes):
        remote(
            wof_blocks(dp, row),
            wof_blocks(lax.rem(dp + planes - k, planes), row),
            d_send.at[k - 1],
            d_recv.at[k - 1],
            partner,
        ).wait_recv()
        r_copies[k].start()
    for k in range(planes):
        other = wof_blocks(lax.rem(dp + planes - k, planes), 1 - row)
        remote(other, other, r_send.at[k], r_recv.at[k], partner).wait_recv()

    @pl.loop(0, count)
    def _(block):
        @pl.when(block != col)
        def _():
            remote(
                att_low.at[block],
                attl_out.at[:, lanes_at(block * width, width)],
                a2a_send.at[block],
                a2a_recv.at[block],
                (dp, row, block),
            ).wait_recv()

    mine = rows_at(col * part, part)
    step_lanes = D // 4
    squares = jnp.zeros((part, 1), f32)
    for piece in range(4):
        lanes = slice(piece * step_lanes, (piece + 1) * step_lanes)
        total = x_full[mine, lanes].astype(f32)
        weights = wof_out[:, :, lanes].reshape(D, step_lanes)
        total = total + matmul(attl_out[...], weights)
        hid_out[:, lanes] = total
        squares = squares + jnp.sum(total * total, axis=1, keepdims=True)
    inverse = lax.rsqrt(squares / D + eps)
    for shard in range(count):
        lanes = slice(shard * width, (shard + 1) * width)
        n2_out[:, lanes] = (hid_out[:, lanes] * inverse * aux_out[shard, 1:2, :]).astype(bf16)

    @pl.loop(0, count)
    def _(chunk):
        chain_c.step(count - 1, chunk)

    copy_c.wait()
    c_copy = pltpu.make_async_copy(cot_full, cot_out, local_sem.at[7])
    c_copy.start()

    chain_x.finish()
    chain_c.finish()
    for copy in aux_copies + wall_copies + z_copies + d_copies + r_copies:
        copy.wait_send()
    for copy in mlp_copies:
        copy.wait()

    @pl.loop(0, count)
    def _(chunk):
        kv_copy(chunk).wait_send()

        @pl.when(chunk != col)
        def _():
            a2a_copy(chunk).wait_send()

    for copy in (n1_copy, x_copy, c_copy):
        copy.wait()


def front(dims, aux, x, cot, wq, wkv, wout, w_gate, w_up, w_down, lengths, freq):
    count, planes = dims
    rows, width = x.shape
    part = rows // count
    heads = width // HEAD_WIDTH
    f32, bf16 = jnp.float32, jnp.bfloat16
    shape = jax.ShapeDtypeStruct
    wall = width + 2 * HEAD_WIDTH
    outs = [
        (shape((rows, D), bf16), any_spec()),
        (shape((rows, D), bf16), any_spec()),
        (shape((rows, D), bf16), any_spec()),
        (shape((heads, rows, HEAD_WIDTH), bf16), vmem_spec()),
        (shape((2 * rows, 2 * HEAD_WIDTH), bf16), vmem_spec()),
        (shape((heads, rows, HEAD_WIDTH), f32), vmem_spec()),
        (shape((rows, HEAD_WIDTH), f32), vmem_spec()),
        (shape((part, D), bf16), vmem_spec()),
        (shape((part, D), f32), vmem_spec()),
        (shape((part, D), bf16), vmem_spec()),
        (shape((2, rows, HEAD_WIDTH), f32), vmem_spec()),
        (shape((count, part, width), bf16), vmem_spec()),
        (shape((count,) + aux.shape, f32), vmem_spec()),
        (shape((D, wall), bf16), vmem_spec()),
        (shape((count, wout.shape[0], D), bf16), vmem_spec()),
        (shape(w_gate.shape, bf16), any_spec()),
        (shape(w_up.shape, bf16), any_spec()),
        (shape(w_down.shape, bf16), any_spec()),
    ]
    dma = pltpu.SemaphoreType.DMA
    return pl.pallas_call(
        functools.partial(front_kernel, heads, dims),
        out_shape=[o[0] for o in outs],
        in_specs=[vmem_spec()]
        + [any_spec()] * 8
        + [pl.BlockSpec(memory_space=pltpu.SMEM), vmem_spec()],
        out_specs=[o[1] for o in outs],
        scratch_shapes=[
            pltpu.VMEM((rows, D), bf16),
            pltpu.VMEM((rows, D), bf16),
            pltpu.VMEM((rows, D), bf16),
            dma((2, count - 1, count)),
            dma((count, count)),
            dma((2, count - 1, count)),
            dma((count, count)),
            dma((8,)),
            dma((count - 1,)),
            dma((count - 1,)),
            dma((4,)),
            dma((4,)),
            dma((count - 1,)),
            dma((count - 1,)),
            dma((planes - 1,)),
            dma((planes - 1,)),
            dma((planes,)),
            dma((planes,)),
            dma((count,)),
            dma((count,)),
            dma((count,)),
            dma((count,)),
            dma((3,)),
            dma((3,)),
        ],
        compiler_params=pltpu.CompilerParams(
            collective_id=1, has_side_effects=True, vmem_limit_bytes=52 * 2**20
        ),
        cost_estimate=pl.CostEstimate(
            flops=10 * 10**9, bytes_accessed=60 * 10**6, transcendentals=10**7
        ),
        name="front",
    )(aux, x, cot, wq, wkv, wout, w_gate, w_up, w_down, lengths, freq)


LINE = 4
TILE = 768
ORDER = ((0, 1, 2, 3), (1, 0, 2, 3), (2, 1, 3, 0), (3, 2, 1, 0))


def pick(index, values):
    out = values[0]
    for k, value in enumerate(values[1:], 1):
        out = jnp.where(index == k, value, out)
    return out


def hidden_tiles(total):
    tile = 512
    return [(first, min(tile, total - first)) for first in range(0, total, tile)]


class RowChain(Chain):
    def block(self, shard, chunk):
        shard_rows = self.full.shape[0] // self.count
        count = shard_rows // self.chunks
        return self.full.at[rows_at(shard * shard_rows + chunk * count, count)]

    def copy(self, way, step, shard, chunk):
        self.rows = self.full.shape[0] // self.count // self.chunks
        return super().copy(way, step, shard, chunk)


class LineSum:
    def __init__(self, place, share, box, sends, recvs, chunks):
        self.dp, self.row, self.col = place
        self.share, self.box, self.sends, self.recvs = share, box, sends, recvs
        self.chunks = chunks

    def copy(self, c, chunk, shard):
        to = c + 1 if shard > c else c - 1
        slot = LINE if to < c and shard == to else shard
        return remote(
            self.share(chunk, shard),
            self.box(slot, chunk),
            self.sends.at[shard, chunk],
            self.recvs.at[slot, chunk],
            (self.dp, self.row, to),
        )

    def got(self, chunk, slot):
        box = self.box(slot, chunk)
        partner = (self.dp, 1 - self.row, self.col)
        remote(box, box, self.sends.at[0, chunk], self.recvs.at[slot, chunk], partner).wait_recv()

    def onward(self, c, chunk, shard):
        self.got(chunk, shard)
        share, box = self.share(chunk, shard), self.box(shard, chunk)
        share[...] = (share[...].astype(jnp.float32) + box[...].astype(jnp.float32)).astype(
            jnp.bfloat16
        )
        self.copy(c, chunk, shard).start()

    def left_end(self, chunk):
        @pl.when(self.col == 0)
        def _():
            for shard in (3, 2, 1):
                self.copy(0, chunk, shard).start()

    def right_end(self, chunk):
        @pl.when(self.col == LINE - 1)
        def _():
            for shard in (0, 1, 2):
                self.copy(LINE - 1, chunk, shard).start()

    def ends(self, chunk):
        self.left_end(chunk)
        self.right_end(chunk)

    def near_left(self, chunk):
        @pl.when(self.col == 1)
        def _():
            for shard in (3, 2):
                self.onward(1, chunk, shard)

    def near_right(self, chunk):
        @pl.when(self.col == 2)
        def _():
            for shard in (0, 1):
                self.onward(2, chunk, shard)

    def near(self, chunk):
        self.near_left(chunk)
        self.near_right(chunk)

    def far(self, chunk):
        @pl.when(self.col == 1)
        def _():
            self.onward(1, chunk, 0)

        @pl.when(self.col == 2)
        def _():
            self.onward(2, chunk, 3)

    def clear_ends(self):
        for c, slot in ((0, 0), (LINE - 1, LINE)):

            @pl.when(self.col == c)
            def _():
                for chunk in range(self.chunks):
                    box = self.box(slot, chunk)
                    box[...] = jnp.zeros(box.shape, jnp.bfloat16)

    def wait_own(self, chunk):
        @pl.when(self.col > 0)
        def _():
            self.got(chunk, self.col)

        @pl.when(self.col < LINE - 1)
        def _():
            self.got(chunk, LINE)

    def own(self, chunk):
        self.wait_own(chunk)
        refs = (self.share(chunk, self.col), self.box(self.col, chunk), self.box(LINE, chunk))
        return sum(ref[...].astype(jnp.float32) for ref in refs)

    def finish(self):
        for c in range(LINE):

            @pl.when(self.col == c)
            def _():
                @pl.loop(0, self.chunks)
                def _(chunk):
                    for shard in range(LINE):
                        if shard != c:
                            self.copy(c, chunk, shard).wait_send()


def mlp_kernel(
    n2,
    cot_full,
    hid,
    own_gate,
    own_up,
    own_down,
    peer_gate,
    peer_up,
    peer_down,
    left_out,
    n2_out,
    result,
    out_rest,
    gate_w,
    up_w,
    down_w,
    hidden_parts,
    n2s,
    cots,
    w_sem,
    cot_sem,
    own_sem,
    ag_send,
    ag_recv,
    left_sem,
    n2_sem,
    shares,
    boxes,
    stage,
    out_send,
    out_recv,
    out_sem,
):
    f32, bf16 = jnp.float32, jnp.bfloat16
    dp, row, col = lax.axis_index("dp"), lax.axis_index("row"), lax.axis_index("col")
    part = n2.shape[0]
    hidden, half = own_gate.shape
    tiles = hidden_tiles(hidden)
    greet([(dp, row, lax.rem(col + k, LINE)) for k in range(1, LINE)])
    chain = RowChain((dp, row, col), n2, n2s, ag_send, ag_recv, LINE, 2)
    for chunk in range(2):
        chain.start_own(chunk)
    own_copy = pltpu.make_async_copy(n2, n2s.at[rows_at(col * part, part)], own_sem)
    own_copy.start()

    def cot_copy(tick):
        here = rows_at(pick(col, [order[tick] for order in ORDER]) * part, part)
        return pltpu.make_async_copy(cot_full.at[here], cots.at[here], cot_sem.at[tick])

    def load_copies(index, first, count):
        rows_here = pl.ds(first, count)
        copies = []
        for own, peer, whole in (
            (own_gate, peer_gate, gate_w),
            (own_up, peer_up, up_w),
            (own_down, peer_down, down_w),
        ):
            for side, src in ((row, own), (1 - row, peer)):
                copies.append((src.at[rows_here], whole.at[rows_here, lanes_at(side * half, half)]))
        return [
            pltpu.make_async_copy(src, dst, w_sem.at[index, k])
            for k, (src, dst) in enumerate(copies)
        ]

    cot_copy(0).start()
    for index, (first, count) in enumerate(tiles):
        for copy in load_copies(index, first, count):
            copy.start()
    for tick in range(1, LINE):
        cot_copy(tick).start()
    hidden_parts[:, :, :, hidden:] = jnp.zeros(
        hidden_parts.shape[:3] + (hidden_parts.shape[3] - hidden,), bf16
    )
    own_copy.wait()
    width = D // LINE
    line = LineSum(
        (dp, row, col),
        lambda chunk, shard: shares.at[chunk + 1, :, lanes_at(shard * width, width)],
        lambda slot, chunk: boxes.at[slot, chunk],
        out_send,
        out_recv,
        2,
    )
    line.clear_ends()
    is_end = (col == 0) | (col == LINE - 1)

    def left_copies(tick):
        shard = pick(tick, [pick(col, [order[t] for order in ORDER]) for t in range(LINE)])
        here = rows_at(shard * part, part)
        slot = lax.rem(tick, 2)
        return [
            pltpu.make_async_copy(
                hidden_parts.at[slot, k], left_out.at[k, here], left_sem.at[slot, k]
            )
            for k in range(3)
        ]

    @pl.loop(0, LINE)
    def _(tick):
        @pl.when(tick == 1)
        def _():
            for chunk in range(2):
                chain.step(1, chunk)

        @pl.when(((tick == 2) & is_end) | ((tick == 3) & jnp.logical_not(is_end)))
        def _():
            for chunk in range(2):
                chain.step(2, chunk)

        @pl.when((tick == 3) & is_end)
        def _():
            for chunk in range(2):
                chain.step(3, chunk)

        shard = pick(tick, [pick(col, [order[t] for order in ORDER]) for t in range(LINE)])
        here = rows_at(shard * part, part)
        slot = lax.rem(tick, 2)
        pltpu.make_async_copy(cot_full.at[here], cots.at[here], cot_sem.at[tick]).wait()

        @pl.when(tick >= 2)
        def _():
            for copy in left_copies(tick - 2):
                copy.wait()

        for index, (first, count) in enumerate(tiles):

            @pl.when(tick == 0)
            def _():
                for copy in load_copies(index, first, count):
                    copy.wait()

            rows_here, lanes = slice(first, first + count), slice(first, first + count)
            gate = matmul_nt(n2s[here, :], gate_w[rows_here, :])
            up = matmul_nt(n2s[here, :], up_w[rows_here, :])
            grad = matmul_nt(cots[here, :], down_w[rows_here, :])
            sigmoid = jax.nn.sigmoid(gate)
            silu = gate * sigmoid
            hidden_parts[slot, 0, :, lanes] = (silu * up).astype(bf16)
            hidden_parts[slot, 1, :, lanes] = (
                grad * up * sigmoid * (1.0 + gate * (1.0 - sigmoid))
            ).astype(bf16)
            hidden_parts[slot, 2, :, lanes] = (grad * silu).astype(bf16)
        for copy in left_copies(tick):
            copy.start()
        own = jnp.where(tick == 0, 1.0, 0.0)
        for first in range(0, D, 512):
            lanes = slice(first, first + 512)
            total = matmul(hidden_parts[slot, 0, :, :hidden], down_w[:, lanes])
            shares[shard, :, lanes] = (total + hid[:, lanes] * own).astype(bf16)

        @pl.when(tick == 1)
        def _():
            line.left_end(0)
            line.right_end(1)

        @pl.when(tick == 2)
        def _():
            line.left_end(1)
            line.right_end(0)
            line.near_left(0)
            line.near_right(1)

    rest_copies = [
        pltpu.make_async_copy(shares.at[shard], out_rest.at[k], out_sem.at[2 + k])
        for k, shard in enumerate((0, LINE - 1))
    ]
    for copy in rest_copies:
        copy.start()
    n2_copy = pltpu.make_async_copy(n2s, n2_out, n2_sem)
    n2_copy.start()
    line.near_left(1)
    line.near_right(0)
    for chunk in range(2):
        line.far(chunk)
    result_copies = []
    for chunk in range(2):
        stage[chunk] = line.own(chunk).astype(bf16)
        result_copies.append(
            pltpu.make_async_copy(
                stage.at[chunk], result.at[pl.ds((chunk + 1) * part, part)], out_sem.at[chunk]
            )
        )
        result_copies[chunk].start()
    for tick in (LINE - 2, LINE - 1):
        for copy in left_copies(tick):
            copy.wait()
    n2_copy.wait()
    chain.finish()
    line.finish()
    for copy in rest_copies + result_copies:
        copy.wait()


def mlp(n2, cot_full, hid, own, peer):
    bf16 = jnp.bfloat16
    rows = cot_full.shape[0]
    part = n2.shape[0]
    hidden = own[0].shape[0]
    shape = jax.ShapeDtypeStruct
    dma = pltpu.SemaphoreType.DMA
    padded = -(-hidden // TILE) * TILE
    wide = pltpu.VMEM((hidden, D), bf16)
    full = pltpu.VMEM((rows, D), bf16)
    return pl.pallas_call(
        mlp_kernel,
        out_shape=[
            shape((3, rows, padded), bf16),
            shape((rows, D), bf16),
            shape((rows, D // LINE), bf16),
            shape((2, part, D), bf16),
        ],
        in_specs=[any_spec()] * 2 + [vmem_spec()] + [any_spec()] * 6,
        out_specs=[any_spec()] * 4,
        scratch_shapes=[
            wide,
            wide,
            wide,
            pltpu.VMEM((2, 3, part, padded), bf16),
            full,
            full,
            dma((len(hidden_tiles(hidden)), 6)),
            dma((LINE,)),
            dma,
            dma((2, LINE - 1, 2)),
            dma((LINE, 2)),
            dma((2, 3)),
            dma,
            pltpu.VMEM((LINE, part, D), bf16),
            pltpu.VMEM((LINE + 1, 2, part, D // LINE), bf16),
            pltpu.VMEM((2, part, D // LINE), bf16),
            dma((LINE, 2)),
            dma((LINE + 1, 2)),
            dma((4,)),
        ],
        compiler_params=pltpu.CompilerParams(
            collective_id=2, has_side_effects=True, vmem_limit_bytes=56 * 2**20
        ),
        cost_estimate=pl.CostEstimate(
            flops=21 * 10**9, bytes_accessed=60 * 10**6, transcendentals=10**7
        ),
        name="mlp",
    )(n2, cot_full, hid, *own, *peer)


CHUNK = 320
TAIL = 960
LAG = 1
RING = 7
HALF_TILE = 384


class AllReduce:
    def __init__(self, place, total, inbox, sends, recvs, result, own_sems, chunks):
        self.dp, self.row, self.col = place
        self.total, self.inbox, self.sends, self.recvs = total, inbox, sends, recvs
        self.result, self.own_sems, self.chunks = result, own_sems, chunks
        x, y = lax.rem(self.dp, 2), self.dp // 2
        over_x = (self.dp + 1 - 2 * x, self.row, self.col)
        over_y = (self.dp + 2 - 4 * y, self.row, self.col)
        lanes = total.shape[1] // 2
        self.kinds = (
            (pl.ds(0, lanes), x, over_x, y, over_y),
            (pl.ds(lanes, lanes), y, over_y, x, over_x),
        )

    def part(self, ref, first, count, kind):
        return ref.at[rows_at(first, count), self.kinds[kind][0]]

    def places(self, chunk, kind):
        half, quarter = CHUNK // 2, CHUNK // 4
        _, bit1, peer1, bit2, peer2 = self.kinds[kind]
        own_half, far_half = chunk * CHUNK + half * bit1, chunk * CHUNK + half * (1 - bit1)
        box = lax.rem(chunk, RING) * (half + quarter)
        return (
            (own_half, far_half, box, box + half)
            + (own_half + quarter * bit2, own_half + quarter * (1 - bit2))
            + (far_half + quarter * bit2, far_half + quarter * (1 - bit2))
            + (peer1, peer2)
        )

    def copy(self, chunk, kind, stage, leaving):
        half, quarter = CHUNK // 2, CHUNK // 4
        _, far_half, box1, box2, own, mate, far, far_mate, peer1, peer2 = self.places(chunk, kind)
        count = quarter if stage else half
        if stage < 2:
            src = self.part(self.total, (far_half, mate)[stage], count, kind)
            dst = self.part(self.inbox, (box1, box2)[stage], count, kind)
        else:
            held = self.total if stage < 4 else self.result
            src = self.part(held, mate if stage == 4 else own, count, kind)
            if leaving:
                dst = self.part(self.result, mate if stage == 4 else own, count, kind)
            else:
                dst = self.part(self.result, (mate, far, far_mate)[stage - 2], count, kind)
        slot = lax.rem(chunk, RING)
        return remote(
            src,
            dst,
            self.sends.at[slot, kind, stage],
            self.recvs.at[slot, kind, stage],
            peer2 if stage in (1, 2) else peer1,
        )

    def own_copy(self, chunk, kind):
        own = self.places(chunk, kind)[4]
        return pltpu.make_async_copy(
            self.part(self.total, own, CHUNK // 4, kind),
            self.part(self.result, own, CHUNK // 4, kind),
            self.own_sems.at[lax.rem(chunk, RING), kind],
        )

    def add(self, chunk, kind, stage):
        self.copy(chunk, kind, stage, False).wait_recv()
        own_half, _, box1, box2, own, *_ = self.places(chunk, kind)
        count = CHUNK // 4 if stage else CHUNK // 2
        lanes = self.kinds[kind][0]
        mine = rows_at(own if stage else own_half, count)
        coming = self.inbox[rows_at(box2 if stage else box1, count), lanes].astype(jnp.float32)
        self.total[mine, lanes] = (
            self.total[mine, lanes].astype(jnp.float32) + coming
        ).astype(jnp.bfloat16)

    def step(self, number):
        for stage in range(5):

            @pl.when((number - stage * LAG >= 0) & (number - stage * LAG < self.chunks))
            def _():
                chunk = number - stage * LAG
                for kind in range(2):
                    if stage == 0:
                        self.copy(chunk, kind, 0, True).start()
                    elif stage == 1:
                        self.add(chunk, kind, 0)
                        self.copy(chunk, kind, 1, True).start()
                    elif stage == 2:
                        self.add(chunk, kind, 1)
                        self.copy(chunk, kind, 2, True).start()
                        self.copy(chunk, kind, 3, True).start()
                        self.own_copy(chunk, kind).start()
                    elif stage == 3:
                        self.copy(chunk, kind, 2, False).wait_recv()
                        self.copy(chunk, kind, 4, True).start()
                    else:
                        self.copy(chunk, kind, 3, False).wait_recv()
                        self.copy(chunk, kind, 4, False).wait_recv()
                        self.own_copy(chunk, kind).wait()
                        for sent in range(5):
                            self.copy(chunk, kind, sent, True).wait_send()


def back_kernel(
    heads,
    lefts,
    n2_in,
    cot_in,
    hid_in,
    rest_in,
    own_gate,
    own_up,
    peer_gate,
    peer_up,
    aux_all,
    wof_in,
    wall_in,
    n1_in,
    x_in,
    kv_in,
    q_in,
    att_in,
    lse_in,
    trig_in,
    attl_in,
    lengths,
    result_in,
    grad_x,
    result,
    sums_out,
    gq_out,
    gkv_out,
    small_out,
    total,
    inbox,
    give_buf,
    got_buf,
    tiles,
    y,
    wt,
    acc,
    parts,
    boxes,
    kv,
    q,
    att_low,
    mid,
    low,
    ga_send,
    ga,
    kv_give,
    kv_got,
    mate_got,
    gkv,
    gain_sum,
    gains,
    gains_got,
    load_sem,
    y_sem,
    tile_sem,
    wt_sem,
    att_sem,
    credit,
    free_sem,
    swap_send,
    swap_recv,
    ar_send,
    ar_recv,
    own_sem,
    gn_send,
    gn_recv,
    out_send,
    out_recv,
    ga_ssem,
    ga_rsem,
    gm_send,
    gm_recv,
    kv_sem,
    mate_sem,
    fin_send,
    fin_recv,
    gain_ssem,
    gain_rsem,
    end_sem,
    rest_sem,
    wall_sem,
):
    f32, bf16 = jnp.float32, jnp.bfloat16
    dp, row, col = lax.axis_index("dp"), lax.axis_index("row"), lax.axis_index("col")
    place = (dp, row, col)
    part = hid_in.shape[0]
    rows = LINE * part
    width = heads * HEAD_WIDTH
    half = TILE
    hidden = own_gate.shape[0]
    member = lax.rem(col, 2)
    mate = (dp, row, col + 1 - 2 * member)
    partner = (dp, 1 - row, col)
    col_peers = [(dp, row, lax.rem(col + k, LINE)) for k in range(1, LINE)]
    bit_x, bit_y = lax.rem(dp, 2), dp // 2
    greet(
        col_peers
        + [partner, (dp + 1 - 2 * bit_x, row, col), (dp + 2 - 4 * bit_y, row, col)]
    )
    chunks = total.shape[0] // CHUNK
    reduce = AllReduce(place, total, inbox, ar_send, ar_recv, sums_out, own_sem, chunks)

    n2_copy = pltpu.make_async_copy(n2_in, y.at[0], y_sem.at[0])
    cot_copy = pltpu.make_async_copy(cot_in, y.at[1], y_sem.at[1])
    rest_copies = [
        pltpu.make_async_copy(rest_in.at[k], y.at[1, pl.ds(k * part, part)], rest_sem.at[k])
        for k in range(2)
    ]

    products, early, jobs = 6, 3, 9
    steps = products + jobs - early

    def tile_copy(step):
        job = jnp.where(step < products, step, step - products + early)
        return pltpu.make_async_copy(
            lefts.at[lax.rem(job // 3 + 1, 3), :, lanes_at(lax.rem(job, 3) * TILE, TILE)],
            tiles.at[lax.rem(step, 3)],
            tile_sem.at[lax.rem(step, 3)],
        )

    def weight_copies(index, act):
        slot = lax.rem(index, 2)
        last = hidden - 2 * TILE
        for k, pair in enumerate(((own_gate, peer_gate), (own_up, peer_up))):
            for tail, count in ((0, TILE), (1, last)):

                @pl.when((index // 3 == k) & (lax.rem(index, 3) // 2 == tail))
                def _():
                    here = rows_at(lax.rem(index, 3) * TILE, count)
                    for n, (side, src) in enumerate(((row, pair[0]), (1 - row, pair[1]))):
                        dst = wt.at[slot, pl.ds(0, count), lanes_at(side * half, half)]
                        act(pltpu.make_async_copy(src.at[here], dst, wt_sem.at[slot, n]))

    for copy in rest_copies:
        copy.start()
    tile_copy(0).start()
    weight_copies(jnp.int32(0), lambda copy: copy.start())
    n2_copy.start()
    weight_copies(jnp.int32(1), lambda copy: copy.start())
    for step in range(1, 3):
        tile_copy(step).start()
    loads = [
        pltpu.make_async_copy(src, dst, load_sem.at[k])
        for k, (src, dst) in enumerate(
            (
                (hid_in, mid),
                (kv_in, kv),
                (q_in, q),
                (attl_in, att_low),
            )
        )
    ]
    for copy in loads:
        copy.start()
    acc[...] = jnp.zeros_like(acc)

    grain = part // LINE

    gn = LineSum(
        place,
        lambda chunk, shard: parts.at[rows_at(shard * part + chunk * grain, grain)],
        lambda slot, chunk: boxes.at[slot, rows_at(chunk * grain, grain)],
        gn_send,
        gn_recv,
        LINE,
    )
    def out_box(slot, chunk):
        if isinstance(slot, int) and slot == LINE:
            return ga_send.at[chunk]
        place_of = slot * 2 + chunk
        return y.at[
            1,
            rows_at(2 * part + place_of // LINE * part, part),
            lanes_at(lax.rem(place_of, LINE) * width, width),
        ]

    out = LineSum(
        place,
        lambda chunk, shard: y.at[1, rows_at(chunk * part, part), lanes_at(shard * width, width)],
        out_box,
        out_send,
        out_recv,
        2,
    )
    fin = LineSum(
        place,
        lambda chunk, shard: wt.at[
            chunk // 2, rows_at(lax.rem(chunk, 2) * part, part), lanes_at(shard * width, width)
        ],
        lambda slot, chunk: tiles.at[
            slot // 2, rows_at(chunk * part, part), lanes_at(lax.rem(slot, 2) * width, width)
        ],
        fin_send,
        fin_recv,
        LINE,
    )

    gn.clear_ends()
    out.clear_ends()
    for copy in rest_copies:
        copy.wait()
    for chunk in range(2):
        out.ends(chunk)

    theirs, ours = lanes_at((1 - row) * half, half), lanes_at(row * half, half)

    def swap_copy(index):
        ring = rows_at(lax.rem(index, 2) * TILE, TILE)
        return remote(
            give_buf.at[ring],
            got_buf.at[ring],
            swap_send.at[lax.rem(index, 2)],
            swap_recv.at[lax.rem(index, 2)],
            partner,
        )

    n2_copy.wait()

    @pl.loop(0, steps + 1)
    def _(step):
        @pl.when(step < steps)
        def _():
            tile_copy(step).wait()

        @pl.when(step < products)
        def _():
            weight_copies(step, lambda copy: copy.wait())

            @pl.loop(0, 2)
            def _(side):
                here = rows_at(side * 2 * part, 2 * part)
                for lane in range(0, D, 512):
                    lanes = slice(lane, lane + 512)
                    acc[here, lanes] += matmul(
                        tiles[lax.rem(step, 3), here, :], wt[lax.rem(step, 2), :, lanes]
                    )

            @pl.when(step + 2 < products)
            def _():
                weight_copies(step + 2, lambda copy: copy.start())

        @pl.when(step == products)
        def _():
            @pl.loop(0, LINE)
            def _(shard):
                here = rows_at(shard * part, part)
                parts[here, :] = acc[here, :].astype(bf16)

            @pl.loop(0, LINE)
            def _(chunk):
                gn.ends(chunk)

        @pl.when((step < early) | ((step >= products) & (step < steps)))
        def _():
            job = jnp.where(step < early, step, step - products + early)

            @pl.when(job >= 2)
            def _():
                pl.semaphore_wait(credit, 1)
                swap_copy(job - 2).wait_send()

            for first in range(0, TILE, HALF_TILE):
                lanes = slice(first, first + HALF_TILE)
                product = matmul_tn(tiles[lax.rem(step, 3), :, lanes], y[job // 6, :, theirs])
                here = rows_at(lax.rem(job, 2) * TILE + first, HALF_TILE)
                give_buf[here, :] = product.astype(bf16)
            swap_copy(job).start()

        @pl.when(((step >= 1) & (step <= early)) | (step >= products + 1))
        def _():
            job = jnp.where(step <= early, step - 1, step - products + early - 1)
            swap_copy(job).wait_recv()
            base_row = (job // 3) * hidden + lax.rem(job, 3) * TILE
            for first in range(0, TILE, HALF_TILE):
                lanes = slice(first, first + HALF_TILE)
                product = matmul_tn(tiles[lax.rem(step + 2, 3), :, lanes], y[job // 6, :, ours])
                here = rows_at(lax.rem(job, 2) * TILE + first, HALF_TILE)
                product = product + got_buf[here, :].astype(f32)
                total[rows_at(base_row + first, HALF_TILE), :] = product.astype(bf16)
            pl.semaphore_signal(credit, inc=1, device_id=partner, device_id_type=MESH)

        @pl.when((step >= 1) & (step + 2 < steps))
        def _():
            tile_copy(step + 2).start()

        for number, when in enumerate((1, 2, 3, 5, 7, 9, 11)):

            @pl.when(step == when)
            def _():
                reduce.step(number)

        @pl.when(step == 3)
        def _():
            out.near(0)

        @pl.when(step == 5)
        def _():
            out.near(1)
            out.far(0)

        @pl.when(step == 7)
        def _():
            gn.near(0)
            out.far(1)
            out.finish()
            for chunk in range(2):
                low[:, chunk * width : (chunk + 1) * width] = out.own(chunk).astype(bf16)
            cot_copy.start()

        @pl.when(step == 8)
        def _():
            cot_copy.wait()

        @pl.when(step == 10)
        def _():
            gn.near(1)
            gn.far(0)

        @pl.when(step == 12)
        def _():
            gn.near(2)
            gn.far(1)

    wof_copies = [
        pltpu.make_async_copy(
            wof_in.at[shard],
            wt.at[shard // 2, pl.ds(shard % 2 * width, width)],
            att_sem.at[shard],
        )
        for shard in range(LINE)
    ]
    for copy in wof_copies:
        copy.start()
    own_rows = rows_at(col * part, part)
    rest_copies = [
        pltpu.make_async_copy(
            low.at[:, pl.ds(chunk * width, width)],
            result.at[pl.ds(chunk * (LINE - 1) * part, part)],
            rest_sem.at[chunk],
        )
        for chunk in range(2)
    ]
    for copy in rest_copies:
        copy.start()
    for copy in rest_copies:
        copy.wait()
    low[...] = y[1, own_rows, :]
    n1_copy = pltpu.make_async_copy(n1_in, y.at[1], y_sem.at[1])
    n1_copy.start()
    for copy in loads:
        copy.wait()
    gn.near(3)
    gn.far(2)
    reduce.step(7)
    gn.far(3)
    reduce.step(8)

    gain_sum[...] = jnp.zeros_like(gain_sum)

    @pl.loop(0, LINE)
    def _(chunk):
        gn.wait_own(chunk)
        here = rows_at(chunk * grain, grain)
        squares = jnp.zeros((grain, 1), f32)
        inner = jnp.zeros((grain, 1), f32)
        grads = []
        for shard in range(LINE):
            lanes = slice(shard * width, (shard + 1) * width)
            middle = mid[here, lanes]
            grad = parts[rows_at(col * part + chunk * grain, grain), lanes].astype(f32)
            grad = grad + boxes[col, here, lanes].astype(f32)
            grad = grad + boxes[LINE, here, lanes].astype(f32)
            grads.append(grad)
            squares = squares + jnp.sum(middle * middle, axis=1, keepdims=True)
            inner = inner + jnp.sum(
                grad * aux_all[shard, 1:2, :] * middle, axis=1, keepdims=True
            )
        inverse = lax.rsqrt(squares / D + eps)
        factor = inverse * inverse * inverse * inner / D
        for shard in range(LINE):
            lanes = slice(shard * width, (shard + 1) * width)
            middle, grad = mid[here, lanes], grads[shard]
            gain_sum[1:2, lanes] += jnp.sum(grad * middle * inverse, axis=0, keepdims=True)
            new = inverse * grad * aux_all[shard, 1:2, :] - middle * factor
            new = new + low[here, lanes].astype(f32)
            mid[here, lanes] = new
            low[here, lanes] = new.astype(bf16)

    @pl.when(col > 0)
    def _():
        pl.semaphore_signal(
            free_sem.at[1], inc=1, device_id=(dp, row, col - 1), device_id_type=MESH
        )

    @pl.when(col < LINE - 1)
    def _():
        pl.semaphore_signal(
            free_sem.at[0], inc=1, device_id=(dp, row, col + 1), device_id_type=MESH
        )

    def ga_copy(k):
        to = lax.rem(col + k, LINE)
        return remote(
            ga_send.at[k - 1],
            ga.at[own_rows],
            ga_ssem.at[k - 1],
            ga_rsem.at[k - 1],
            (dp, row, to),
        )

    for copy in wof_copies:
        copy.wait()
    for k in (1, 2, 3, 0):
        shard = lax.rem(col + k, LINE)
        weights = wt[shard // 2, rows_at(lax.rem(shard, 2) * width, width), :]
        block = matmul_nt(low[...], weights).astype(bf16)
        if k:
            ga_send[k - 1] = block
            ga_copy(k).start()
        else:
            ga[own_rows, :] = block
    reduce.step(9)

    held = [att_in.at[h] for h in range(heads)] + [trig_in.at[0], trig_in.at[1], lse_in]
    att_copies = [
        pltpu.make_async_copy(src, acc.at[:, pl.ds(512 + k * HEAD_WIDTH, HEAD_WIDTH)], att_sem.at[k])
        for k, src in enumerate(held)
    ]
    trig_lanes = [
        slice(512 + (heads + k) * HEAD_WIDTH, 512 + (heads + k + 1) * HEAD_WIDTH) for k in range(2)
    ]
    lse_lanes = 512 + (heads + 2) * HEAD_WIDTH
    for copy in att_copies:
        copy.start()
    acc[:, :512] = jnp.zeros((rows, 512), f32)
    gn.finish()
    wall_width = width + 2 * HEAD_WIDTH
    wall_copies = [
        pltpu.make_async_copy(
            wall_in.at[pl.ds(shard * width, width)],
            parts.at[
                pl.ds(shard % 2 * width, width), pl.ds(shard // 2 * wall_width, wall_width)
            ],
            wall_sem.at[shard],
        )
        for shard in range(LINE)
    ]
    for copy in wall_copies:
        copy.start()
    y[0, own_rows, :] = low[...]

    chain = RowChain(place, low, y.at[0], gm_send, gm_recv, LINE, 2)

    @pl.when(col > 0)
    def _():
        pl.semaphore_wait(free_sem.at[0], 1)

    @pl.when(col < LINE - 1)
    def _():
        pl.semaphore_wait(free_sem.at[1], 1)

    for chunk in range(2):
        chain.start_own(chunk)

    span = min(512, rows)
    per_side = rows // span
    for copy in att_copies:
        copy.wait()

    def key_rows(index):
        return rows_at(lax.rem(index, per_side) * span, span)

    def key_lanes(index, which):
        return lanes_at(index // per_side * 2 * HEAD_WIDTH + which * HEAD_WIDTH, HEAD_WIDTH)

    @pl.loop(0, LINE)
    def _(turn):
        block = lax.rem(col + LINE - turn, LINE)
        here = rows_at(block * part, part)
        for k in range(1, LINE):

            @pl.when(turn == k)
            def _():
                ga_copy(k).wait_recv()

        first_query = row * rows + block * part
        query = q[:, here, :].reshape(heads * part, HEAD_WIDTH)
        back = jnp.concatenate(
            [ga[here, h * HEAD_WIDTH : (h + 1) * HEAD_WIDTH] for h in range(heads)], axis=0
        )
        attended = jnp.concatenate(
            [
                acc[here, 512 + h * HEAD_WIDTH : 512 + (h + 1) * HEAD_WIDTH]
                for h in range(heads)
            ],
            axis=0,
        )
        log_total = jnp.concatenate(
            [acc[here, lse_lanes + h : lse_lanes + h + 1] for h in range(heads)], axis=0
        )
        delta = jnp.sum(back.astype(f32) * attended, axis=1, keepdims=True)

        def body(index, grad):
            keys = rows_at(index * span, span)
            key, value = kv[keys, :HEAD_WIDTH], kv[keys, HEAD_WIDTH:]
            scores = matmul_nt(query, key) * SCALE
            allowed = allowed_keys(lengths, first_query, part, index * span, span)
            probs = jnp.exp(scores - log_total).reshape(heads, part, span)
            probs = jnp.where(allowed[None], probs, 0.0).reshape(heads * part, span)
            grads = matmul_nt(back, value)
            grad_scores = (probs * (grads - delta)).astype(bf16)
            acc[key_rows(index), key_lanes(index, 0)] += matmul_tn(grad_scores, query)
            acc[key_rows(index), key_lanes(index, 1)] += matmul_tn(probs.astype(bf16), back)
            return grad + matmul(grad_scores, key)

        blocks = (first_query + part + span - 1) // span
        grad = lax.fori_loop(0, blocks, body, jnp.zeros((heads * part, HEAD_WIDTH), f32))
        cosine, sine = acc[here, trig_lanes[0]], -acc[here, trig_lanes[1]]
        for h in range(heads):
            lanes = slice(h * HEAD_WIDTH, (h + 1) * HEAD_WIDTH)
            turned = rotate(grad[h * part : (h + 1) * part] * SCALE, cosine, sine)
            ga[here, lanes] = turned.astype(bf16)
        reduce.step(10 + turn)

        @pl.when(turn == LINE - 1)
        def _():
            for chunk in range(2):
                chain.step(1, chunk)

    kv_give[...] = acc[:, lanes_at((1 - row) * 2 * HEAD_WIDTH, 2 * HEAD_WIDTH)].astype(bf16)
    kv_copy = remote(kv_give, kv_got, kv_sem.at[0], kv_sem.at[1], partner)
    kv_copy.start()
    reduce.step(14)
    kv_copy.wait()
    lane = lax.broadcasted_iota(jnp.int32, (1, HEAD_WIDTH), 1)
    low_lanes = lane < HEAD_WIDTH // 2
    turn_by = HEAD_WIDTH // 2
    mate_give = kv_give.at[:, pl.ds(0, HEAD_WIDTH)]
    mate_copy = remote(mate_give, mate_got, mate_sem.at[0], mate_sem.at[1], mate)
    own_lanes = lanes_at(row * 2 * HEAD_WIDTH, 2 * HEAD_WIDTH)

    @pl.loop(0, LINE)
    def _(chunk):
        here = rows_at(chunk * part, part)
        both = acc[here, own_lanes] + kv_got[here, :].astype(f32)
        key = rotate(
            both[:, :HEAD_WIDTH] * SCALE, acc[here, trig_lanes[0]], -acc[here, trig_lanes[1]]
        )
        value = both[:, HEAD_WIDTH:]
        first = jnp.where(low_lanes, key, pltpu.roll(value, turn_by, 1))
        second = jnp.where(low_lanes, pltpu.roll(key, turn_by, 1), value)
        is_first = jnp.where(member == 0, 1.0, 0.0)
        kept = first * is_first + second * (1.0 - is_first)
        given = second * is_first + first * (1.0 - is_first)
        acc[here, 512 : 512 + HEAD_WIDTH] = kept
        kv_give[here, :HEAD_WIDTH] = given.astype(bf16)

    mate_copy.start()
    reduce.step(15)
    mate_copy.wait_recv()

    @pl.loop(0, LINE)
    def _(chunk):
        here = rows_at(chunk * part, part)
        kept = acc[here, 512 : 512 + HEAD_WIDTH] + mate_got[here, :].astype(f32)
        gkv[here, :] = kept.astype(bf16)

    n1_copy.wait()
    base = 3 * hidden
    first_kv, first_out = half // 2, half // 2 + HEAD_WIDTH
    first_small = first_out + width

    def projections(side_lanes, store):
        product = matmul_tn(y[1, :, side_lanes], ga[...])
        for k in range(2):
            store(
                0,
                half // 2,
                slice(k * width, (k + 1) * width),
                product[k * half // 2 : (k + 1) * half // 2],
            )
        product = matmul_tn(y[1, :, side_lanes], gkv[...])
        for k in range(half // HEAD_WIDTH):
            store(
                first_kv,
                HEAD_WIDTH,
                slice(k * HEAD_WIDTH, (k + 1) * HEAD_WIDTH),
                product[k * HEAD_WIDTH : (k + 1) * HEAD_WIDTH],
            )

    for k in range(2):
        swap_copy(jobs - 2 + k).wait_send()
    pl.semaphore_wait(credit, 2)

    def store_give(first, count, lanes, value):
        give_buf[first : first + count, lanes] = value.astype(bf16)

    def store_keep(first, count, lanes, value):
        got = got_buf[first : first + count, lanes].astype(f32)
        total[base + first : base + first + count, lanes] = (got + value).astype(bf16)

    projections(theirs, store_give)
    tail = pl.ds(0, first_out)
    tail_copy = remote(give_buf.at[tail], got_buf.at[tail], end_sem.at[0], end_sem.at[1], partner)
    tail_copy.start()
    for chunk in range(2):
        chain.step(2, chunk)
    reduce.step(16)
    tail_copy.wait_recv()
    projections(ours, store_keep)
    x_copy = pltpu.make_async_copy(x_in, y.at[1], y_sem.at[1])
    x_copy.start()

    fin.clear_ends()

    for copy in wall_copies:
        copy.wait()
    x_copy.wait()

    @pl.loop(0, LINE + 2)
    def _(chunk):
        @pl.when(chunk < LINE)
        def _():
            here = rows_at(chunk * part, part)
            squares = jnp.zeros((part, 1), f32)
            inner = jnp.zeros((part, 1), f32)
            for shard in range(LINE):
                lanes = slice(shard * width, (shard + 1) * width)
                there = slice(shard % 2 * width, (shard % 2 + 1) * width)
                first = shard // 2 * wall_width
                kv_lanes = lanes_at(first + width + member * HEAD_WIDTH, HEAD_WIDTH)
                grad = matmul_nt(ga[here, :], parts[there, first : first + width])
                grad = grad + matmul_nt(gkv[here, :], parts[there, kv_lanes])
                acc[:part, lanes] = grad
                value = y[1, here, lanes].astype(f32)
                squares = squares + jnp.sum(value * value, axis=1, keepdims=True)
                scaled = grad * aux_all[shard, 0:1, :]
                inner = inner + jnp.sum(scaled * value, axis=1, keepdims=True)
            inverse = lax.rsqrt(squares / D + eps)
            factor = inverse * inverse * inverse * inner / D
            own = jnp.where(chunk == col, 1.0, 0.0)
            there = rows_at(lax.rem(chunk, 2) * part, part)
            for shard in range(LINE):
                lanes = slice(shard * width, (shard + 1) * width)
                grad, value = acc[:part, lanes], y[1, here, lanes].astype(f32)
                gain_sum[0:1, lanes] += jnp.sum(grad * value * inverse, axis=0, keepdims=True)
                share = inverse * grad * aux_all[shard, 0:1, :] - value * factor
                share = share + mid[:, lanes] * own
                wt[chunk // 2, there, lanes] = share.astype(bf16)
            fin.ends(chunk)
            reduce.step(17 + chunk)

        @pl.when((chunk >= 1) & (chunk <= LINE))
        def _():
            fin.near(chunk - 1)

        @pl.when(chunk >= 2)
        def _():
            fin.far(chunk - 2)

    gains[...] = gain_sum[...]

    def gain_copy(k):
        to = lax.rem(col + k, LINE)
        return remote(
            gains.at[:, lanes_at(to * width, width)],
            gains_got.at[k - 1],
            gain_ssem.at[k - 1],
            gain_rsem.at[k - 1],
            (dp, row, to),
        )

    for k in range(1, LINE):
        gain_copy(k).start()
    reduce.step(21)
    bias = jnp.concatenate(
        [jnp.sum(ref[...].astype(f32), axis=0, keepdims=True) for ref in (ga, gkv)], axis=1
    )
    for k in range(1, LINE):
        gain_copy(k).wait_recv()
    gain_total = gains[:, lanes_at(col * width, width)]
    for k in range(1, LINE):
        gain_total = gain_total + gains_got[k - 1]
    small = jnp.concatenate(
        [
            jnp.concatenate([gain_total, jnp.zeros((8, half - width), f32)], axis=1),
            jnp.concatenate(
                [
                    jnp.broadcast_to(bias, (8, width + HEAD_WIDTH)),
                    jnp.zeros((8, half - width - HEAD_WIDTH), f32),
                ],
                axis=1,
            ),
        ],
        axis=0,
    )
    small_rows = pl.ds(first_out, width + 16)
    for chunk in range(2):
        chain.step(3, chunk)
    product = matmul_tn(att_low[...], y[0, :, theirs])
    give_buf[first_out:first_small, :] = product.astype(bf16)
    give_buf[first_small : first_small + 16, :] = small.astype(bf16)
    small_copy = remote(
        give_buf.at[small_rows], got_buf.at[small_rows], end_sem.at[2], end_sem.at[3], partner
    )
    small_copy.start()
    product = matmul_tn(att_low[...], y[0, :, ours])
    small_copy.wait_recv()
    product = product + got_buf[first_out:first_small, :].astype(f32)
    total[base + first_out : base + first_small, :] = product.astype(bf16)
    small = small + got_buf[first_small : first_small + 16, :].astype(f32)
    total[base + first_small : base + first_small + 16, :] = small.astype(bf16)
    rest = TAIL - first_small - 16
    total[base + first_small + 16 : base + TAIL, :] = jnp.zeros((rest, half), bf16)
    for number in (22, 23):
        reduce.step(number)

    @pl.loop(0, LINE)
    def _(chunk):
        ga[rows_at(chunk * part, part), :] = fin.own(chunk).astype(bf16)

    grad_copy = pltpu.make_async_copy(ga, grad_x, att_sem.at[1])
    grad_copy.start()

    @pl.loop(24, chunks + 4 * LAG)
    def _(number):
        reduce.step(number)

    outs = [
        pltpu.make_async_copy(
            sums_out.at[pl.ds(base, half // 2), pl.ds(k * width, width)],
            gq_out.at[pl.ds(k * half // 2, half // 2)],
            load_sem.at[k],
        )
        for k in range(2)
    ]
    outs += [
        pltpu.make_async_copy(
            sums_out.at[pl.ds(base + first_kv, HEAD_WIDTH), pl.ds(k * HEAD_WIDTH, HEAD_WIDTH)],
            gkv_out.at[pl.ds(k * HEAD_WIDTH, HEAD_WIDTH)],
            load_sem.at[2 + k],
        )
        for k in range(half // HEAD_WIDTH)
    ]
    outs.append(
        pltpu.make_async_copy(
            sums_out.at[pl.ds(base + first_small, 16)], small_out, load_sem.at[8]
        )
    )
    for copy in outs:
        copy.start()

    chain.finish()
    fin.finish()
    for k in range(1, LINE):
        ga_copy(k).wait_send()
        gain_copy(k).wait_send()
    for copy in (mate_copy, tail_copy, small_copy):
        copy.wait_send()
    for copy in outs + [grad_copy]:
        copy.wait()


def back(lefts, n2, cot, hid, rest, result, own, peer, aux_all, wof, wall, n1, x, kv, q, att, lse, trig, att_low, lengths):
    f32, bf16 = jnp.float32, jnp.bfloat16
    shape = jax.ShapeDtypeStruct
    dma = pltpu.SemaphoreType.DMA
    heads, rows, _ = q.shape
    width = heads * HEAD_WIDTH
    part = hid.shape[0]
    hidden = own[0].shape[0]
    total_rows = 3 * hidden + TAIL
    outs = [
        (shape((rows, width), bf16), any_spec()),
        (shape((rows, width), bf16), any_spec()),
        (shape((total_rows, TILE), bf16), any_spec()),
        (shape((TILE, width), bf16), any_spec()),
        (shape((TILE, HEAD_WIDTH), bf16), any_spec()),
        (shape((16, TILE), bf16), vmem_spec()),
    ]
    vmem = pltpu.VMEM
    return pl.pallas_call(
        functools.partial(back_kernel, heads),
        out_shape=[o[0] for o in outs],
        in_specs=[any_spec()] * 9
        + [vmem_spec()]
        + [any_spec()] * 10
        + [pl.BlockSpec(memory_space=pltpu.SMEM), any_spec()],
        out_specs=[o[1] for o in outs],
        scratch_shapes=[
            vmem((total_rows, TILE), bf16),
            vmem((RING * CHUNK * 3 // 4, TILE), bf16),
            vmem((2 * TILE, TILE), bf16),
            vmem((2 * TILE, TILE), bf16),
            vmem((3, rows, TILE), bf16),
            vmem((2, rows, D), bf16),
            vmem((2, TILE, D), bf16),
            vmem((rows, D), f32),
            vmem((rows, D), bf16),
            vmem((LINE + 1, part, D), bf16),
            vmem(kv.shape, bf16),
            vmem(q.shape, bf16),
            vmem(att_low.shape, bf16),
            vmem((part, D), f32),
            vmem((part, D), bf16),
            vmem((LINE - 1, part, width), bf16),
            vmem((rows, width), bf16),
            vmem((rows, 2 * HEAD_WIDTH), bf16),
            vmem((rows, 2 * HEAD_WIDTH), bf16),
            vmem((rows, HEAD_WIDTH), bf16),
            vmem((rows, HEAD_WIDTH), bf16),
            vmem((8, D), f32),
            vmem((8, D), f32),
            vmem((LINE - 1, 8, width), f32),
            dma((9,)),
            dma((2,)),
            dma((3,)),
            dma((2, 2)),
            dma((6,)),
            pltpu.SemaphoreType.REGULAR,
            pltpu.SemaphoreType.REGULAR((2,)),
            dma((2,)),
            dma((2,)),
            dma((RING, 2, 5)),
            dma((RING, 2, 5)),
            dma((RING, 2)),
            dma((LINE, LINE)),
            dma((LINE + 1, LINE)),
            dma((LINE, 2)),
            dma((LINE + 1, 2)),
            dma((LINE - 1,)),
            dma((LINE - 1,)),
            dma((2, LINE - 1, 2)),
            dma((LINE, 2)),
            dma((2,)),
            dma((2,)),
            dma((LINE, LINE)),
            dma((LINE + 1, LINE)),
            dma((LINE - 1,)),
            dma((LINE - 1,)),
            dma((4,)),
            dma((2,)),
            dma((LINE,)),
        ],
        compiler_params=pltpu.CompilerParams(
            collective_id=3, has_side_effects=True, vmem_limit_bytes=63 * 2**20
        ),
        cost_estimate=pl.CostEstimate(
            flops=64 * 10**9, bytes_accessed=60 * 10**6, transcendentals=10**7
        ),
        input_output_aliases={21: 1},
        name="back",
    )(
        lefts, n2, cot, hid, rest, *own[:2], *peer[:2], aux_all, wof, wall, n1, x, kv, q, att, lse, trig, att_low, lengths, result
    )


def per_device(
    inputs,
    seq_lengths,
    gain_one,
    w_query,
    b_query,
    w_key,
    b_key,
    w_value,
    b_value,
    w_out,
    gain_two,
    w_gate,
    w_up,
    w_down,
    cotangent,
):
    f32 = jnp.float32
    planes = lax.axis_size("dp")
    rows, width = inputs.shape
    kv_cols = w_key.shape[1]
    hidden = w_down.shape[0]
    half = HEAD_WIDTH // 2
    freq = theta_base ** (-(jnp.arange(half, dtype=f32) * 2.0) / HEAD_WIDTH)
    freq = jnp.concatenate([freq, freq]).reshape(1, HEAD_WIDTH)
    biases = jnp.concatenate([b_key, b_value]).astype(f32)
    biases = jnp.pad(biases, (0, width - 2 * kv_cols))
    aux = jnp.stack([gain_one, gain_two, b_query.astype(f32), biases])
    aux = jnp.pad(aux, ((0, 4), (0, 0)))
    own_kv = jnp.concatenate([w_key, w_value], axis=1)
    own = (w_gate.T, w_up.T, w_down)
    (
        x_full,
        normed_one,
        cot_full,
        queries,
        keys_values,
        attended,
        log_total,
        att_own,
        hidden_mid,
        normed_two,
        trig,
        att_low,
        aux_all,
        wall,
        wof,
        *peer,
    ) = front(
        (LINE, planes),
        aux,
        inputs,
        cotangent,
        w_query,
        own_kv,
        w_out,
        *own,
        seq_lengths,
        freq,
    )
    lefts, normed_full, result, rest = mlp(normed_two, cot_full, hidden_mid, own, peer)
    grad_inputs, result, sums, grad_w_query, grad_kv, small = back(
        lefts,
        normed_full,
        cot_full,
        hidden_mid,
        rest,
        result,
        own,
        peer,
        aux_all,
        wof,
        wall,
        normed_one,
        x_full,
        keys_values,
        queries,
        attended,
        log_total,
        trig,
        att_low.reshape(rows, width),
        seq_lengths,
    )
    grad_w_gate, grad_w_up, grad_w_down = (
        sums[k * hidden : (k + 1) * hidden].astype(f32) for k in range(3)
    )
    first = 3 * hidden + TILE // 2 + HEAD_WIDTH
    grad_w_out = sums[first : first + width].astype(f32)
    grad_kv = grad_kv.astype(f32)
    small = small.astype(f32)
    bias = small[8]
    return (
        result,
        grad_inputs,
        small[0, :width],
        grad_w_query.astype(f32),
        bias[:width],
        grad_kv[:, :kv_cols],
        bias[width : width + kv_cols],
        grad_kv[:, kv_cols:],
        bias[width + kv_cols : width + 2 * kv_cols],
        grad_w_out,
        small[1, :width],
        grad_w_gate.T,
        grad_w_up.T,
        grad_w_down,
    )


def solution(mesh):
    whole_heads = dict(mesh.shape) == {"dp": 4, "row": 2, "col": LINE}
    return jax.shard_map(
        per_device if whole_heads else per_device_any,
        mesh=mesh,
        in_specs=(
            P(("dp", "row"), "col"),
            P("dp", None),
            P("col"),
            P("row", "col"),
            P("col"),
            P("row", "col"),
            P("col"),
            P("row", "col"),
            P("col"),
            P("col", "row"),
            P("col"),
            P("row", "col"),
            P("row", "col"),
            P("col", "row"),
            P(("dp", "row"), "col"),
        ),
        out_specs=(
            P(("dp", "row"), "col"),
            P(("dp", "row"), "col"),
            P("col"),
            P("row", "col"),
            P("col"),
            P("row", "col"),
            P("col"),
            P("row", "col"),
            P("col"),
            P("col", "row"),
            P("col"),
            P("row", "col"),
            P("row", "col"),
            P("col", "row"),
        ),
        check_vma=False,
    )
```

```python
import functools

import jax
import jax.numpy as jnp
from jax import lax
from jax.experimental import pallas as pl
from jax.experimental.pallas import tpu as pltpu
from jax.sharding import PartitionSpec as P

D = 1536
HEAD_WIDTH = 128
QUERY_HEADS = 12
KEY_VALUE_HEADS = 2
DEVICE_TOKENS = 256
QW = 1536
KW = 256


theta_base = 1000000.0
eps = 1e-06


def matmul(left, right):
    return jnp.dot(left, right, preferred_element_type=jnp.float32)


def matmul_tn(left, right):
    return lax.dot_general(
        left, right, (((0,), (0,)), ((), ())), preferred_element_type=jnp.float32
    )


def matmul_nt(left, right):
    return lax.dot_general(
        left, right, (((1,), (1,)), ((), ())), preferred_element_type=jnp.float32
    )


def row_squares(values):
    return lax.psum(values, "col")


def gather_width(values):
    return lax.all_gather(values, "col", axis=1, tiled=True)


def sum_width(values):
    return lax.psum_scatter(
        values.astype(jnp.bfloat16), "col", scatter_dimension=1, tiled=True
    ).astype(jnp.float32)


def documents(lengths, places):
    doc_ends = jnp.cumsum(lengths)
    doc_starts = doc_ends - lengths
    doc_index = jnp.sum((places[:, None] >= doc_ends[None, :]).astype(jnp.int32), axis=1)
    chosen = doc_index[:, None] == jnp.arange(lengths.shape[0], dtype=jnp.int32)[None, :]
    offset = jnp.sum(jnp.where(chosen, doc_starts[None, :], 0), axis=1)
    return (doc_index, places - offset)


def rotary_embedding(values, token_position, direction):
    half_size = HEAD_WIDTH // 2
    frequency = theta_base ** (-(jnp.arange(half_size, dtype=jnp.float32) * 2.0) / HEAD_WIDTH)
    angles = token_position.astype(jnp.float32)[:, None] * frequency[None, :]
    cosine = jnp.cos(angles)[:, None, :]
    sine_part = direction * jnp.sin(angles)[:, None, :]
    leading = values[..., :half_size]
    second = values[..., half_size:]
    return jnp.concatenate(
        [leading * cosine - second * sine_part, second * cosine + leading * sine_part], axis=-1
    )


def norm_forward(hidden, gain):
    square_total = row_squares(jnp.sum(hidden * hidden, axis=1))
    inverse = lax.rsqrt(square_total / D + eps)
    normed = (hidden * inverse[:, None] * gain[None, :]).astype(jnp.bfloat16)
    return (normed, inverse)


def norm_backward(hidden, gain, inverse, grad_normed):
    scaled = grad_normed * gain[None, :]
    inner = row_squares(jnp.sum(scaled * hidden, axis=1))
    grad_hidden = (
        inverse[:, None] * scaled - hidden * (inverse * inverse * inverse * inner / D)[:, None]
    )
    grad_gain = jnp.sum(grad_normed * hidden * inverse[:, None], axis=0)
    return (grad_hidden, grad_gain)


def key_layout(gathered_keys, gathered_values, doc_all):
    seq_len = gathered_keys.shape[0]
    key_block_index = min(512, seq_len)
    count_blocks = seq_len // key_block_index
    blocks_of_keys = gathered_keys.reshape(
        count_blocks, key_block_index, gathered_keys.shape[1] // HEAD_WIDTH, HEAD_WIDTH
    )
    blocks_of_values = gathered_values.reshape(
        count_blocks, key_block_index, gathered_values.shape[1] // HEAD_WIDTH, HEAD_WIDTH
    )
    doc_blocks = doc_all.reshape(count_blocks, key_block_index)
    place_blocks = jnp.arange(seq_len, dtype=jnp.int32).reshape(count_blocks, key_block_index)
    return (blocks_of_keys, doc_blocks, place_blocks, blocks_of_values)


def block_scores(heads_of_queries, key_blk, doc_blk, place_blk, doc_local, place_local):
    scores = jnp.einsum(
        "tkgh,skh->tkgs", heads_of_queries, key_blk, preferred_element_type=jnp.float32
    ) * HEAD_WIDTH ** (-0.5)
    allowed = (doc_blk[None, :] == doc_local[:, None]) & (
        place_blk[None, :] <= place_local[:, None]
    )
    return (scores, allowed[:, None, None, :])


def attention_forward(heads_of_queries, blocks, doc_local, place_local):
    head_shape = heads_of_queries.shape[:3]

    def first_pass(state_in, packed):
        running_max, running_sum = state_in
        scores, allowed = block_scores(
            heads_of_queries, packed[0], packed[1], packed[2], doc_local, place_local
        )
        masked = jnp.where(allowed, scores, -1e30)
        new_max = jnp.maximum(running_max, jnp.max(masked, axis=-1))
        raised = jnp.where(allowed, jnp.exp(scores - new_max[..., None]), 0.0)
        running_sum = running_sum * jnp.exp(running_max - new_max) + jnp.sum(raised, axis=-1)
        return ((new_max, running_sum), None)

    initial = (jnp.full(head_shape, -1e30, jnp.float32), jnp.zeros(head_shape, jnp.float32))
    (running_max, running_sum), unused = lax.scan(first_pass, initial, blocks)
    log_total = running_max + jnp.log(running_sum)

    def second_pass(acc_out, packed):
        scores, allowed = block_scores(
            heads_of_queries, packed[0], packed[1], packed[2], doc_local, place_local
        )
        probs_low = jnp.where(allowed, jnp.exp(scores - log_total[..., None]), 0.0).astype(
            jnp.bfloat16
        )
        return (
            acc_out
            + jnp.einsum(
                "tkgs,skh->tkgh", probs_low, packed[3], preferred_element_type=jnp.float32
            ),
            None,
        )

    attended, unused = lax.scan(second_pass, jnp.zeros(heads_of_queries.shape, jnp.float32), blocks)
    return (attended, log_total)


def attention_backward(
    heads_of_queries, blocks, doc_local, place_local, log_total, attended, heads_gradient
):
    inner = jnp.sum(heads_gradient.astype(jnp.float32) * attended, axis=-1)
    scale_factor = HEAD_WIDTH ** (-0.5)

    def back_pass(grad_query, packed):
        scores, allowed = block_scores(
            heads_of_queries, packed[0], packed[1], packed[2], doc_local, place_local
        )
        probs = jnp.where(allowed, jnp.exp(scores - log_total[..., None]), 0.0)
        grad_probs = jnp.einsum(
            "tkgh,skh->tkgs", heads_gradient, packed[3], preferred_element_type=jnp.float32
        )
        grad_scores = (probs * (grad_probs - inner[..., None])).astype(jnp.bfloat16)
        grad_query = (
            grad_query
            + jnp.einsum(
                "tkgs,skh->tkgh", grad_scores, packed[0], preferred_element_type=jnp.float32
            )
            * scale_factor
        )
        grad_key = (
            jnp.einsum(
                "tkgs,tkgh->skh", grad_scores, heads_of_queries, preferred_element_type=jnp.float32
            )
            * scale_factor
        )
        grad_value = jnp.einsum(
            "tkgs,tkgh->skh",
            probs.astype(jnp.bfloat16),
            heads_gradient,
            preferred_element_type=jnp.float32,
        )
        return (grad_query, (grad_key, grad_value))

    grad_query, (key_grads, value_grads) = lax.scan(
        back_pass, jnp.zeros(heads_of_queries.shape, jnp.float32), blocks
    )
    seq_len = key_grads.shape[0] * key_grads.shape[1]
    return (grad_query, key_grads.reshape(seq_len, -1), value_grads.reshape(seq_len, -1))


def per_device_any(
    inputs,
    seq_lengths,
    gain_one,
    w_query,
    b_query,
    w_key,
    b_key,
    w_value,
    b_value,
    w_out,
    gain_two,
    w_gate,
    w_up,
    w_down,
    cotangent,
):
    full_query, full_key, full_value, full_out, full_gate, full_up, full_down = (
        lax.all_gather(w_query, "row", axis=0, tiled=True),
        lax.all_gather(w_key, "row", axis=0, tiled=True),
        lax.all_gather(w_value, "row", axis=0, tiled=True),
        lax.all_gather(w_out, "row", axis=1, tiled=True),
        lax.all_gather(w_gate, "row", axis=0, tiled=True),
        lax.all_gather(w_up, "row", axis=0, tiled=True),
        lax.all_gather(w_down, "row", axis=1, tiled=True),
    )
    row_pos = lax.axis_index("row")
    col_pos = lax.axis_index("col")
    row_count = lax.axis_size("row")
    col_count = lax.axis_size("col")
    seq_len = DEVICE_TOKENS * row_count * col_count
    query_group_width = QUERY_HEADS // KEY_VALUE_HEADS
    lengths = seq_lengths[0]
    place_local = (row_pos * col_count + col_pos) * DEVICE_TOKENS + jnp.arange(
        DEVICE_TOKENS, dtype=jnp.int32
    )
    doc_local, local_position = documents(lengths, place_local)
    doc_all = documents(lengths, jnp.arange(seq_len, dtype=jnp.int32))[0]
    hidden_in = inputs.astype(jnp.float32)
    normed_one, inverse_one = norm_forward(hidden_in, gain_one)
    normed_full = gather_width(normed_one)
    query_lin = (matmul(normed_full, full_query) + b_query.astype(jnp.float32)).astype(jnp.bfloat16)
    projected_keys = (matmul(normed_full, full_key) + b_key.astype(jnp.float32)).astype(
        jnp.bfloat16
    )
    projected_values = (matmul(normed_full, full_value) + b_value.astype(jnp.float32)).astype(
        jnp.bfloat16
    )
    query_rows, rows_of_keys, value_rows = (
        lax.all_to_all(query_lin, "col", split_axis=0, concat_axis=1, tiled=True),
        lax.all_to_all(projected_keys, "col", split_axis=0, concat_axis=1, tiled=True),
        lax.all_to_all(projected_values, "col", split_axis=0, concat_axis=1, tiled=True),
    )
    rotated_queries = rotary_embedding(
        query_rows.astype(jnp.float32).reshape(DEVICE_TOKENS, QUERY_HEADS, HEAD_WIDTH),
        local_position,
        1.0,
    ).astype(jnp.bfloat16)
    rotated_keys = rotary_embedding(
        rows_of_keys.astype(jnp.float32).reshape(DEVICE_TOKENS, KEY_VALUE_HEADS, HEAD_WIDTH),
        local_position,
        1.0,
    ).astype(jnp.bfloat16)
    gathered_keys, gathered_values = (
        lax.all_gather(rotated_keys.reshape(DEVICE_TOKENS, KW), ("row", "col"), axis=0, tiled=True),
        lax.all_gather(value_rows, ("row", "col"), axis=0, tiled=True),
    )
    blocks = key_layout(gathered_keys, gathered_values, doc_all)
    heads_of_queries = rotated_queries.reshape(
        DEVICE_TOKENS, KEY_VALUE_HEADS, query_group_width, HEAD_WIDTH
    )
    attended, log_total = attention_forward(heads_of_queries, blocks, doc_local, place_local)
    attended_low = attended.reshape(DEVICE_TOKENS, QW).astype(jnp.bfloat16)
    attended_cols = lax.all_to_all(attended_low, "col", split_axis=1, concat_axis=0, tiled=True)
    hidden_mid = hidden_in + sum_width(matmul(attended_cols, full_out))
    normed_two, inverse_two = norm_forward(hidden_mid, gain_two)
    normed_wide = gather_width(normed_two)
    gate = matmul(normed_wide, full_gate)
    up_proj = matmul(normed_wide, full_up)
    sigmoid_gate = jax.nn.sigmoid(gate)
    silu_gate = gate * sigmoid_gate
    mixed = (silu_gate * up_proj).astype(jnp.bfloat16)
    result = (hidden_mid + sum_width(matmul(mixed, full_down))).astype(jnp.bfloat16)
    grad_full = gather_width(cotangent)
    grad_w_down = matmul_tn(mixed, grad_full)
    grad_mixed = matmul_nt(grad_full, full_down)
    grad_gate = (grad_mixed * up_proj * sigmoid_gate * (1.0 + gate * (1.0 - sigmoid_gate))).astype(
        jnp.bfloat16
    )
    grad_up = (grad_mixed * silu_gate).astype(jnp.bfloat16)
    grad_w_gate = matmul_tn(normed_wide, grad_gate)
    grad_w_up = matmul_tn(normed_wide, grad_up)
    grad_normed_two = sum_width(matmul_nt(grad_gate, full_gate) + matmul_nt(grad_up, full_up))
    grad_back_two, grad_gain_two = norm_backward(hidden_mid, gain_two, inverse_two, grad_normed_two)
    grad_mid = cotangent.astype(jnp.float32) + grad_back_two
    grad_attn_full = gather_width(grad_mid.astype(jnp.bfloat16))
    grad_w_out = matmul_tn(attended_cols, grad_attn_full)
    grad_attended_cols = matmul_nt(grad_attn_full, full_out).astype(jnp.bfloat16)
    attended_gradient = lax.all_to_all(
        grad_attended_cols, "col", split_axis=0, concat_axis=1, tiled=True
    )
    heads_gradient = attended_gradient.reshape(
        DEVICE_TOKENS, KEY_VALUE_HEADS, query_group_width, HEAD_WIDTH
    )
    grad_query_rot, key_grads, value_grads = attention_backward(
        heads_of_queries, blocks, doc_local, place_local, log_total, attended, heads_gradient
    )
    rotated_key_gradient, grad_value = (
        lax.psum_scatter(
            key_grads.astype(jnp.bfloat16), ("row", "col"), scatter_dimension=0, tiled=True
        ).astype(jnp.float32),
        lax.psum_scatter(
            value_grads.astype(jnp.bfloat16), ("row", "col"), scatter_dimension=0, tiled=True
        ).astype(jnp.float32),
    )
    grad_query_lin = (
        rotary_embedding(
            grad_query_rot.reshape(DEVICE_TOKENS, QUERY_HEADS, HEAD_WIDTH), local_position, -1.0
        )
        .reshape(DEVICE_TOKENS, QW)
        .astype(jnp.bfloat16)
    )
    grad_key_lin = (
        rotary_embedding(
            rotated_key_gradient.reshape(DEVICE_TOKENS, KEY_VALUE_HEADS, HEAD_WIDTH),
            local_position,
            -1.0,
        )
        .reshape(DEVICE_TOKENS, KW)
        .astype(jnp.bfloat16)
    )
    grad_value_lin = grad_value.astype(jnp.bfloat16)
    query_grad_cols, key_grad_cols, value_grad_cols = (
        lax.all_to_all(grad_query_lin, "col", split_axis=1, concat_axis=0, tiled=True),
        lax.all_to_all(grad_key_lin, "col", split_axis=1, concat_axis=0, tiled=True),
        lax.all_to_all(grad_value_lin, "col", split_axis=1, concat_axis=0, tiled=True),
    )
    grad_b_query = jnp.sum(query_grad_cols.astype(jnp.float32), axis=0)
    grad_b_key = jnp.sum(key_grad_cols.astype(jnp.float32), axis=0)
    grad_b_value = jnp.sum(value_grad_cols.astype(jnp.float32), axis=0)
    grad_w_query = matmul_tn(normed_full, query_grad_cols)
    grad_w_key = matmul_tn(normed_full, key_grad_cols)
    grad_w_value = matmul_tn(normed_full, value_grad_cols)
    grad_normed_one = sum_width(
        matmul_nt(query_grad_cols, full_query)
        + matmul_nt(key_grad_cols, full_key)
        + matmul_nt(value_grad_cols, full_value)
    )
    grad_back_one, grad_gain_one = norm_backward(hidden_in, gain_one, inverse_one, grad_normed_one)
    grad_inputs = (grad_mid + grad_back_one).astype(jnp.bfloat16)
    summed = (
        lax.psum(grad_w_query.astype(jnp.bfloat16), ("dp", "row")).astype(jnp.float32),
        lax.psum(grad_w_key.astype(jnp.bfloat16), ("dp", "row")).astype(jnp.float32),
        lax.psum(grad_w_value.astype(jnp.bfloat16), ("dp", "row")).astype(jnp.float32),
        lax.psum(grad_w_out.astype(jnp.bfloat16), ("dp", "row")).astype(jnp.float32),
        lax.psum(grad_w_gate.astype(jnp.bfloat16), ("dp", "row")).astype(jnp.float32),
        lax.psum(grad_w_up.astype(jnp.bfloat16), ("dp", "row")).astype(jnp.float32),
        lax.psum(grad_w_down.astype(jnp.bfloat16), ("dp", "row")).astype(jnp.float32),
        lax.psum(grad_gain_one.astype(jnp.bfloat16), ("dp", "row")).astype(jnp.float32),
        lax.psum(grad_b_query.astype(jnp.bfloat16), ("dp", "row")).astype(jnp.float32),
        lax.psum(grad_b_key.astype(jnp.bfloat16), ("dp", "row")).astype(jnp.float32),
        lax.psum(grad_b_value.astype(jnp.bfloat16), ("dp", "row")).astype(jnp.float32),
        lax.psum(grad_gain_two.astype(jnp.bfloat16), ("dp", "row")).astype(jnp.float32),
    )
    rows_each = D // row_count
    split_dims = (0, 0, 0, 1, 0, 0, 1)
    weight_sums = tuple(
        (
            lax.dynamic_slice_in_dim(
                summed[member], row_pos * rows_each, rows_each, split_dims[member]
            )
            for member in range(7)
        )
    )
    small_sums = summed[7:]
    return (
        result,
        grad_inputs,
        small_sums[0],
        weight_sums[0],
        small_sums[1],
        weight_sums[1],
        small_sums[2],
        weight_sums[2],
        small_sums[3],
        weight_sums[3],
        small_sums[4],
        weight_sums[4],
        weight_sums[5],
        weight_sums[6],
    )


MESH = pl.DeviceIdType.MESH
NEG = -1e30
SCALE = HEAD_WIDTH ** (-0.5)


def vmem_spec():
    return pl.BlockSpec(memory_space=pltpu.VMEM)


def any_spec():
    return pl.BlockSpec(memory_space=pl.ANY)


def remote(src, dst, send_sem, recv_sem, device):
    return pltpu.make_async_remote_copy(
        src_ref=src,
        dst_ref=dst,
        send_sem=send_sem,
        recv_sem=recv_sem,
        device_id=device,
        device_id_type=MESH,
    )


def greet(peers):
    barrier = pltpu.get_barrier_semaphore()
    for peer in peers:
        pl.semaphore_signal(barrier, inc=1, device_id=peer, device_id_type=MESH)
    pl.semaphore_wait(barrier, len(peers))


def rows_at(first, count):
    return pl.ds(pl.multiple_of(first, 16), count)


def lanes_at(first, count):
    return pl.ds(pl.multiple_of(first, 128), count)


class Chain:
    def __init__(self, place, own, full, sends, recvs, count, chunks):
        self.dp, self.row, self.col = place
        self.own, self.full, self.sends, self.recvs = own, full, sends, recvs
        self.count, self.chunks = count, chunks
        self.width = full.shape[1] // count
        self.rows = full.shape[0] // chunks

    def block(self, shard, chunk):
        return self.full.at[
            rows_at(chunk * self.rows, self.rows), lanes_at(shard * self.width, self.width)
        ]

    def copy(self, way, step, shard, chunk):
        src = self.block(shard, chunk)
        if step == 0:
            src = self.own.at[rows_at(chunk * self.rows, self.rows)]
        device = (self.dp, self.row, self.col + (1 if way == 0 else -1))
        return remote(
            src,
            self.block(shard, chunk),
            self.sends.at[way, step, chunk],
            self.recvs.at[shard, chunk],
            device,
        )

    def start_own(self, chunk):
        @pl.when(self.col < self.count - 1)
        def _():
            self.copy(0, 0, self.col, chunk).start()

        @pl.when(self.col > 0)
        def _():
            self.copy(1, 0, self.col, chunk).start()

    def step(self, step, chunk):
        left, right = self.col - step, self.col + step

        @pl.when(left >= 0)
        def _():
            self.copy(0, step, left, chunk).wait_recv()

        if step < self.count - 1:

            @pl.when((left >= 0) & (self.col < self.count - 1))
            def _():
                self.copy(0, step, left, chunk).start()

        @pl.when(right < self.count)
        def _():
            self.copy(1, step, right, chunk).wait_recv()

        if step < self.count - 1:

            @pl.when((right < self.count) & (self.col > 0))
            def _():
                self.copy(1, step, right, chunk).start()

    def finish(self):
        for step in range(self.count - 1):
            left, right = self.col - step, self.col + step

            @pl.when((left >= 0) & (self.col < self.count - 1))
            def _():
                @pl.loop(0, self.chunks)
                def _(chunk):
                    self.copy(0, step, left, chunk).wait_send()

            @pl.when((right < self.count) & (self.col > 0))
            def _():
                @pl.loop(0, self.chunks)
                def _(chunk):
                    self.copy(1, step, right, chunk).wait_send()


def doc_start(lengths, place):
    first = jnp.zeros_like(place)
    end = 0
    for doc in range(lengths.shape[1]):
        end = end + lengths[0, doc]
        first = jnp.where(place >= end, end, first)
    return first


def rotate(values, cosine, sine):
    return values * cosine + pltpu.roll(values, HEAD_WIDTH // 2, 1) * sine


def allowed_keys(lengths, first_query, queries, first_key, keys):
    query = first_query + lax.broadcasted_iota(jnp.int32, (queries, 1), 0)
    key = first_key + lax.broadcasted_iota(jnp.int32, (1, keys), 1)
    return (key >= doc_start(lengths, query)) & (key <= query)


def front_kernel(
    heads,
    dims,
    aux,
    x,
    cot,
    wq,
    wkv,
    wout,
    w_gate,
    w_up,
    w_down,
    lengths,
    freq,
    x_out,
    n1_out,
    cot_out,
    q_out,
    kv_out,
    att_hbm,
    lse_out,
    attl_out,
    hid_out,
    n2_out,
    trig_out,
    att_low,
    aux_out,
    wall_hbm,
    wof_hbm,
    peer_gate,
    peer_up,
    peer_down,
    x_full,
    n1,
    cot_full,
    x_send,
    x_recv,
    c_send,
    c_recv,
    local_sem,
    aux_send,
    aux_recv,
    wall_send,
    wall_recv,
    z_send,
    z_recv,
    d_send,
    d_recv,
    r_send,
    r_recv,
    kv_send,
    kv_recv,
    a2a_send,
    a2a_recv,
    m_send,
    m_recv,
    att_out,
    wall_out,
    wof_out,
    out_sem,
):
    count, planes = dims
    f32, bf16 = jnp.float32, jnp.bfloat16
    dp, row, col = lax.axis_index("dp"), lax.axis_index("row"), lax.axis_index("col")
    place = (dp, row, col)
    rows, width = x.shape
    part = rows // count
    half = wq.shape[0]
    member = lax.rem(col, 2)
    mate = col + 1 - 2 * member
    col_peers = [(dp, row, lax.rem(col + k, count)) for k in range(1, count)]
    dp_peers = [(lax.rem(dp + k, planes), row, col) for k in range(1, planes)]
    partner = (dp, 1 - row, col)
    across = (dp, 1 - row, mate)
    greet(col_peers + dp_peers + [partner, across])

    chain_x = Chain(place, x, x_full, x_send, x_recv, count, count)
    chain_c = Chain(place, cot, cot_full, c_send, c_recv, count, count)
    own_lanes = lanes_at(col * width, width)
    copy_x = pltpu.make_async_copy(x, x_full.at[:, own_lanes], local_sem.at[0])
    copy_x.start()
    aux_copies = [
        remote(aux, aux_out.at[col], aux_send.at[k], aux_recv.at[k], peer)
        for k, peer in enumerate(col_peers)
    ]
    for copy in aux_copies:
        copy.start()

    @pl.loop(0, count)
    def _(chunk):
        chain_x.start_own(chunk)

    own_half = rows_at(row * half, half)
    kv_lanes = lanes_at(width + member * HEAD_WIDTH, HEAD_WIDTH)
    copy_q = pltpu.make_async_copy(wq, wall_out.at[own_half, pl.ds(0, width)], local_sem.at[1])
    copy_kv = pltpu.make_async_copy(wkv, wall_out.at[own_half, kv_lanes], local_sem.at[2])
    copy_q.start()
    copy_kv.start()
    wall_copies = [
        remote(
            wq, wall_out.at[own_half, pl.ds(0, width)], wall_send.at[0], wall_recv.at[0], partner
        )
    ] + [
        remote(wkv, wall_out.at[own_half, kv_lanes], wall_send.at[k], wall_recv.at[k], peer)
        for k, peer in ((1, partner), (2, (dp, row, mate)), (3, across))
    ]
    for copy in wall_copies:
        copy.start()
    mlp_copies = [
        remote(src, dst, m_send.at[k], m_recv.at[k], partner)
        for k, (src, dst) in enumerate(
            ((w_gate, peer_gate), (w_up, peer_up), (w_down, peer_down))
        )
    ]
    for copy in mlp_copies:
        copy.start()
    copy_c = pltpu.make_async_copy(cot, cot_full.at[:, own_lanes], local_sem.at[3])
    copy_c.start()
    quarter = wout.shape[0] // planes
    out_lanes = lanes_at(row * half, half)

    def wof_block(shard, plane, side):
        return wof_out.at[
            shard, rows_at(plane * quarter, quarter), lanes_at(side * half, half)
        ]

    def wof_blocks(plane, side):
        return wof_out.at[:, rows_at(plane * quarter, quarter), lanes_at(side * half, half)]

    own_quarter = wout.at[rows_at(dp * quarter, quarter)]
    copy_o = pltpu.make_async_copy(own_quarter, wof_block(col, dp, row), local_sem.at[4])
    copy_o.start()

    token = row * rows + lax.broadcasted_iota(jnp.int32, (rows, 1), 0)
    position = (token - doc_start(lengths, token)).astype(f32)
    angle = position * freq[...]
    trig_out[0] = jnp.cos(angle)
    lane = lax.broadcasted_iota(jnp.int32, (1, HEAD_WIDTH), 1)
    trig_out[1] = jnp.sin(angle) * jnp.where(lane < HEAD_WIDTH // 2, -1.0, 1.0)
    aux_out[col] = aux[...]

    for step in range(1, count - 1):

        @pl.loop(0, count)
        def _(chunk):
            chain_x.step(step, chunk)

    z_copies = [
        remote(own_quarter, wof_block(col, dp, row), z_send.at[k], z_recv.at[k], peer)
        for k, peer in enumerate(col_peers)
    ]
    for copy in z_copies:
        copy.start()

    @pl.loop(0, count)
    def _(chunk):
        chain_c.start_own(chunk)

    copy_x.wait()
    copy_q.wait()
    copy_kv.wait()
    for copy in aux_copies:
        copy.wait_recv()
    for k, (side, who) in enumerate(
        ((1 - row, None), (1 - row, member), (row, 1 - member), (1 - row, 1 - member))
    ):
        side_rows = rows_at(side * half, half)
        if who is None:
            dst, src = wall_out.at[side_rows, pl.ds(0, width)], wq
        else:
            dst = wall_out.at[side_rows, lanes_at(width + who * HEAD_WIDTH, HEAD_WIDTH)]
            src = wkv
        remote(src, dst, wall_send.at[k], wall_recv.at[k], partner).wait_recv()

    mate_aux = aux_out[mate]
    even = jnp.where(member == 0, aux[3:4, :HEAD_WIDTH], mate_aux[3:4, :HEAD_WIDTH])
    odd = jnp.where(member == 0, mate_aux[3:4, :HEAD_WIDTH], aux[3:4, :HEAD_WIDTH])
    low_lanes = lane < HEAD_WIDTH // 2
    key_bias = jnp.where(low_lanes, even, pltpu.roll(odd, HEAD_WIDTH // 2, 1))
    value_bias = jnp.where(low_lanes, pltpu.roll(even, HEAD_WIDTH // 2, 1), odd)

    def kv_chunk(side, chunk):
        return kv_out.at[rows_at(side * rows + chunk * part, part)]

    def kv_copy(chunk):
        return remote(
            kv_chunk(row, chunk),
            kv_chunk(row, chunk),
            kv_send.at[chunk],
            kv_recv.at[chunk],
            partner,
        )

    @pl.loop(0, count)
    def _(chunk):
        chain_x.step(count - 1, chunk)
        here = rows_at(chunk * part, part)
        squares = jnp.zeros((part, 1), f32)
        for shard in range(count):
            piece = x_full[here, shard * width : (shard + 1) * width].astype(f32)
            squares = squares + jnp.sum(piece * piece, axis=1, keepdims=True)
        inverse = lax.rsqrt(squares / D + eps)
        for shard in range(count):
            lanes = slice(shard * width, (shard + 1) * width)
            piece = x_full[here, lanes].astype(f32)
            n1[here, lanes] = (piece * inverse * aux_out[shard, 0:1, :]).astype(bf16)
        lin = matmul(n1[here, :], wall_out[...])
        cosine, sine = trig_out[0, here, :], trig_out[1, here, :]
        for head in range(heads):
            lanes = slice(head * HEAD_WIDTH, (head + 1) * HEAD_WIDTH)
            query = (lin[:, lanes] + aux[2:3, lanes]).astype(bf16).astype(f32)
            q_out[head, here, :] = rotate(query, cosine, sine).astype(bf16)
        first = lin[:, width : width + HEAD_WIDTH]
        second = lin[:, width + HEAD_WIDTH : width + 2 * HEAD_WIDTH]
        turn = HEAD_WIDTH // 2
        key = jnp.where(low_lanes, first, pltpu.roll(second, turn, 1)) + key_bias
        value = jnp.where(low_lanes, pltpu.roll(first, turn, 1), second) + value_bias
        there = rows_at(row * rows + chunk * part, part)
        kv_out[there, :HEAD_WIDTH] = rotate(
            key.astype(bf16).astype(f32), cosine, sine
        ).astype(bf16)
        kv_out[there, HEAD_WIDTH:] = value.astype(bf16)
        kv_copy(chunk).start()

    n1_copy = pltpu.make_async_copy(n1, n1_out, local_sem.at[5])
    n1_copy.start()
    x_copy = pltpu.make_async_copy(x_full, x_out, local_sem.at[6])
    x_copy.start()
    wall_copy = pltpu.make_async_copy(wall_out, wall_hbm, out_sem.at[0])
    wall_copy.start()

    copy_o.wait()
    for k in range(1, count):
        shard = lax.rem(col + count - k, count)
        remote(
            own_quarter, wof_block(shard, dp, row), z_send.at[k - 1], z_recv.at[k - 1], partner
        ).wait_recv()
    d_copies = [
        remote(wof_blocks(dp, row), wof_blocks(dp, row), d_send.at[k], d_recv.at[k], peer)
        for k, peer in enumerate(dp_peers)
    ]
    r_copies = [
        remote(
            wof_blocks(lax.rem(dp + planes - k, planes), row),
            wof_blocks(lax.rem(dp + planes - k, planes), row),
            r_send.at[k],
            r_recv.at[k],
            partner,
        )
        for k in range(planes)
    ]
    for copy in d_copies:
        copy.start()
    r_copies[0].start()

    @pl.loop(0, count)
    def _(chunk):
        remote(
            kv_chunk(row, chunk),
            kv_chunk(1 - row, chunk),
            kv_send.at[chunk],
            kv_recv.at[chunk],
            partner,
        ).wait_recv()

    span = min(512, rows)

    def a2a_copy(block):
        return remote(
            att_low.at[block],
            attl_out.at[:, own_lanes],
            a2a_send.at[block],
            a2a_recv.at[col],
            (dp, row, block),
        )

    @pl.loop(0, count)
    def _(block):
        here = rows_at(block * part, part)
        first_query = row * rows + block * part
        query = q_out[:, here, :].reshape(heads * part, HEAD_WIDTH)

        def body(index, state):
            largest, total, acc = state
            keys = rows_at(index * span, span)
            scores = matmul_nt(query, kv_out[keys, :HEAD_WIDTH]) * SCALE
            allowed = allowed_keys(lengths, first_query, part, index * span, span)
            scores = jnp.where(allowed[None], scores.reshape(heads, part, span), NEG)
            scores = scores.reshape(heads * part, span)
            new = jnp.maximum(largest, jnp.max(scores, axis=1, keepdims=True))
            raised = jnp.exp(scores - new)
            alpha = jnp.exp(largest - new)
            total = total * alpha + jnp.sum(raised, axis=1, keepdims=True)
            acc = acc * alpha + matmul(raised.astype(bf16), kv_out[keys, HEAD_WIDTH:])
            return new, total, acc

        state = (
            jnp.full((heads * part, 1), NEG, f32),
            jnp.zeros((heads * part, 1), f32),
            jnp.zeros((heads * part, HEAD_WIDTH), f32),
        )
        blocks = (first_query + part + span - 1) // span
        largest, total, acc = lax.fori_loop(0, blocks, body, state)
        attended = (acc / total).reshape(heads, part, HEAD_WIDTH)
        att_out[:, here, :] = attended
        log_total = (largest + jnp.log(total)).reshape(heads, part, 1)
        spread = jnp.zeros((part, HEAD_WIDTH), f32)
        for head in range(heads):
            spread = jnp.where(lane == head, log_total[head], spread)
        lse_out[here, :] = spread
        for head in range(heads):
            lanes = slice(head * HEAD_WIDTH, (head + 1) * HEAD_WIDTH)
            att_low[block, :, lanes] = attended[head].astype(bf16)

        @pl.when(block != col)
        def _():
            a2a_copy(block).start()

        chain_c.step(1, block)

    attl_out[:, own_lanes] = att_low[col]
    att_copy = pltpu.make_async_copy(att_out, att_hbm, out_sem.at[1])
    att_copy.start()
    for step in range(2, count - 1):

        @pl.loop(0, count)
        def _(chunk):
            chain_c.step(step, chunk)

    for k in range(1, planes):
        remote(
            wof_blocks(dp, row),
            wof_blocks(lax.rem(dp + planes - k, planes), row),
            d_send.at[k - 1],
            d_recv.at[k - 1],
            partner,
        ).wait_recv()
        r_copies[k].start()
    for k in range(planes):
        other = wof_blocks(lax.rem(dp + planes - k, planes), 1 - row)
        remote(other, other, r_send.at[k], r_recv.at[k], partner).wait_recv()

    wof_copy = pltpu.make_async_copy(wof_out, wof_hbm, out_sem.at[2])
    wof_copy.start()

    @pl.loop(0, count)
    def _(block):
        @pl.when(block != col)
        def _():
            remote(
                att_low.at[block],
                attl_out.at[:, lanes_at(block * width, width)],
                a2a_send.at[block],
                a2a_recv.at[block],
                (dp, row, block),
            ).wait_recv()

    mine = rows_at(col * part, part)
    step_lanes = D // 4
    squares = jnp.zeros((part, 1), f32)
    for piece in range(4):
        lanes = slice(piece * step_lanes, (piece + 1) * step_lanes)
        total = x_full[mine, lanes].astype(f32)
        weights = wof_out[:, :, lanes].reshape(D, step_lanes)
        total = total + matmul(attl_out[...], weights)
        hid_out[:, lanes] = total
        squares = squares + jnp.sum(total * total, axis=1, keepdims=True)
    inverse = lax.rsqrt(squares / D + eps)
    for shard in range(count):
        lanes = slice(shard * width, (shard + 1) * width)
        n2_out[:, lanes] = (hid_out[:, lanes] * inverse * aux_out[shard, 1:2, :]).astype(bf16)

    @pl.loop(0, count)
    def _(chunk):
        chain_c.step(count - 1, chunk)

    copy_c.wait()
    c_copy = pltpu.make_async_copy(cot_full, cot_out, local_sem.at[7])
    c_copy.start()

    chain_x.finish()
    chain_c.finish()
    for copy in aux_copies + wall_copies + z_copies + d_copies + r_copies:
        copy.wait_send()
    for copy in mlp_copies:
        copy.wait()

    @pl.loop(0, count)
    def _(chunk):
        kv_copy(chunk).wait_send()

        @pl.when(chunk != col)
        def _():
            a2a_copy(chunk).wait_send()

    for copy in (n1_copy, x_copy, c_copy, wall_copy, att_copy, wof_copy):
        copy.wait()


def front(dims, aux, x, cot, wq, wkv, wout, w_gate, w_up, w_down, lengths, freq):
    count, planes = dims
    rows, width = x.shape
    part = rows // count
    heads = width // HEAD_WIDTH
    f32, bf16 = jnp.float32, jnp.bfloat16
    shape = jax.ShapeDtypeStruct
    wall = width + 2 * HEAD_WIDTH
    outs = [
        (shape((rows, D), bf16), any_spec()),
        (shape((rows, D), bf16), any_spec()),
        (shape((rows, D), bf16), any_spec()),
        (shape((heads, rows, HEAD_WIDTH), bf16), vmem_spec()),
        (shape((2 * rows, 2 * HEAD_WIDTH), bf16), vmem_spec()),
        (shape((heads, rows, HEAD_WIDTH), f32), any_spec()),
        (shape((rows, HEAD_WIDTH), f32), vmem_spec()),
        (shape((part, D), bf16), vmem_spec()),
        (shape((part, D), f32), vmem_spec()),
        (shape((part, D), bf16), vmem_spec()),
        (shape((2, rows, HEAD_WIDTH), f32), vmem_spec()),
        (shape((count, part, width), bf16), vmem_spec()),
        (shape((count,) + aux.shape, f32), vmem_spec()),
        (shape((D, wall), bf16), any_spec()),
        (shape((count, wout.shape[0], D), bf16), any_spec()),
        (shape(w_gate.shape, bf16), any_spec()),
        (shape(w_up.shape, bf16), any_spec()),
        (shape(w_down.shape, bf16), any_spec()),
    ]
    dma = pltpu.SemaphoreType.DMA
    return pl.pallas_call(
        functools.partial(front_kernel, heads, dims),
        out_shape=[o[0] for o in outs],
        in_specs=[vmem_spec()]
        + [any_spec()] * 8
        + [pl.BlockSpec(memory_space=pltpu.SMEM), vmem_spec()],
        out_specs=[o[1] for o in outs],
        scratch_shapes=[
            pltpu.VMEM((rows, D), bf16),
            pltpu.VMEM((rows, D), bf16),
            pltpu.VMEM((rows, D), bf16),
            dma((2, count - 1, count)),
            dma((count, count)),
            dma((2, count - 1, count)),
            dma((count, count)),
            dma((8,)),
            dma((count - 1,)),
            dma((count - 1,)),
            dma((4,)),
            dma((4,)),
            dma((count - 1,)),
            dma((count - 1,)),
            dma((planes - 1,)),
            dma((planes - 1,)),
            dma((planes,)),
            dma((planes,)),
            dma((count,)),
            dma((count,)),
            dma((count,)),
            dma((count,)),
            dma((3,)),
            dma((3,)),
            pltpu.VMEM((heads, rows, HEAD_WIDTH), f32),
            pltpu.VMEM((D, wall), bf16),
            pltpu.VMEM((count, wout.shape[0], D), bf16),
            dma((3,)),
        ],
        compiler_params=pltpu.CompilerParams(
            collective_id=1, has_side_effects=True, vmem_limit_bytes=52 * 2**20
        ),
        cost_estimate=pl.CostEstimate(
            flops=10 * 10**9, bytes_accessed=60 * 10**6, transcendentals=10**7
        ),
        name="front",
    )(aux, x, cot, wq, wkv, wout, w_gate, w_up, w_down, lengths, freq)


LINE = 4
TILE = 768
ORDER = ((0, 1, 2, 3), (1, 0, 2, 3), (2, 1, 3, 0), (3, 2, 1, 0))


def pick(index, values):
    out = values[0]
    for k, value in enumerate(values[1:], 1):
        out = jnp.where(index == k, value, out)
    return out


def hidden_tiles(total):
    tile = 512
    return [(first, min(tile, total - first)) for first in range(0, total, tile)]


class RowChain(Chain):
    def block(self, shard, chunk):
        shard_rows = self.full.shape[0] // self.count
        count = shard_rows // self.chunks
        return self.full.at[rows_at(shard * shard_rows + chunk * count, count)]

    def copy(self, way, step, shard, chunk):
        self.rows = self.full.shape[0] // self.count // self.chunks
        return super().copy(way, step, shard, chunk)


class LineSum:
    def __init__(self, place, share, box, sends, recvs, chunks):
        self.dp, self.row, self.col = place
        self.share, self.box, self.sends, self.recvs = share, box, sends, recvs
        self.chunks = chunks

    def copy(self, c, chunk, shard):
        to = c + 1 if shard > c else c - 1
        slot = LINE if to < c and shard == to else shard
        return remote(
            self.share(chunk, shard),
            self.box(slot, chunk),
            self.sends.at[shard, chunk],
            self.recvs.at[slot, chunk],
            (self.dp, self.row, to),
        )

    def got(self, chunk, slot):
        box = self.box(slot, chunk)
        partner = (self.dp, 1 - self.row, self.col)
        remote(box, box, self.sends.at[0, chunk], self.recvs.at[slot, chunk], partner).wait_recv()

    def onward(self, c, chunk, shard):
        self.got(chunk, shard)
        share, box = self.share(chunk, shard), self.box(shard, chunk)
        share[...] = (share[...].astype(jnp.float32) + box[...].astype(jnp.float32)).astype(
            jnp.bfloat16
        )
        self.copy(c, chunk, shard).start()

    def left_end(self, chunk):
        @pl.when(self.col == 0)
        def _():
            for shard in (3, 2, 1):
                self.copy(0, chunk, shard).start()

    def right_end(self, chunk):
        @pl.when(self.col == LINE - 1)
        def _():
            for shard in (0, 1, 2):
                self.copy(LINE - 1, chunk, shard).start()

    def ends(self, chunk):
        self.left_end(chunk)
        self.right_end(chunk)

    def near_left(self, chunk):
        @pl.when(self.col == 1)
        def _():
            for shard in (3, 2):
                self.onward(1, chunk, shard)

    def near_right(self, chunk):
        @pl.when(self.col == 2)
        def _():
            for shard in (0, 1):
                self.onward(2, chunk, shard)

    def near(self, chunk):
        self.near_left(chunk)
        self.near_right(chunk)

    def far(self, chunk):
        @pl.when(self.col == 1)
        def _():
            self.onward(1, chunk, 0)

        @pl.when(self.col == 2)
        def _():
            self.onward(2, chunk, 3)

    def clear_ends(self):
        for c, slot in ((0, 0), (LINE - 1, LINE)):

            @pl.when(self.col == c)
            def _():
                for chunk in range(self.chunks):
                    box = self.box(slot, chunk)
                    box[...] = jnp.zeros(box.shape, jnp.bfloat16)

    def wait_own(self, chunk):
        @pl.when(self.col > 0)
        def _():
            self.got(chunk, self.col)

        @pl.when(self.col < LINE - 1)
        def _():
            self.got(chunk, LINE)

    def own(self, chunk):
        self.wait_own(chunk)
        refs = (self.share(chunk, self.col), self.box(self.col, chunk), self.box(LINE, chunk))
        return sum(ref[...].astype(jnp.float32) for ref in refs)

    def finish(self):
        for c in range(LINE):

            @pl.when(self.col == c)
            def _():
                @pl.loop(0, self.chunks)
                def _(chunk):
                    for shard in range(LINE):
                        if shard != c:
                            self.copy(c, chunk, shard).wait_send()


def mlp_kernel(
    n2,
    cot_full,
    hid,
    own_gate,
    own_up,
    own_down,
    peer_gate,
    peer_up,
    peer_down,
    left_out,
    n2_out,
    result,
    out_rest,
    gate_w,
    up_w,
    down_w,
    hidden_parts,
    n2s,
    cots,
    w_sem,
    cot_sem,
    own_sem,
    ag_send,
    ag_recv,
    left_sem,
    n2_sem,
    shares,
    boxes,
    stage,
    out_send,
    out_recv,
    out_sem,
):
    f32, bf16 = jnp.float32, jnp.bfloat16
    dp, row, col = lax.axis_index("dp"), lax.axis_index("row"), lax.axis_index("col")
    part = n2.shape[0]
    hidden, half = own_gate.shape
    tiles = hidden_tiles(hidden)
    greet([(dp, row, lax.rem(col + k, LINE)) for k in range(1, LINE)])
    chain = RowChain((dp, row, col), n2, n2s, ag_send, ag_recv, LINE, 2)
    for chunk in range(2):
        chain.start_own(chunk)
    own_copy = pltpu.make_async_copy(n2, n2s.at[rows_at(col * part, part)], own_sem)
    own_copy.start()

    def cot_copy(tick):
        here = rows_at(pick(col, [order[tick] for order in ORDER]) * part, part)
        return pltpu.make_async_copy(cot_full.at[here], cots.at[here], cot_sem.at[tick])

    def load_copies(index, first, count):
        rows_here = pl.ds(first, count)
        copies = []
        for own, peer, whole in (
            (own_gate, peer_gate, gate_w),
            (own_up, peer_up, up_w),
            (own_down, peer_down, down_w),
        ):
            for side, src in ((row, own), (1 - row, peer)):
                copies.append((src.at[rows_here], whole.at[rows_here, lanes_at(side * half, half)]))
        return [
            pltpu.make_async_copy(src, dst, w_sem.at[index, k])
            for k, (src, dst) in enumerate(copies)
        ]

    cot_copy(0).start()
    for index, (first, count) in enumerate(tiles):
        for copy in load_copies(index, first, count):
            copy.start()
    for tick in range(1, LINE):
        cot_copy(tick).start()
    hidden_parts[:, :, :, hidden:] = jnp.zeros(
        hidden_parts.shape[:3] + (hidden_parts.shape[3] - hidden,), bf16
    )
    own_copy.wait()
    width = D // LINE
    line = LineSum(
        (dp, row, col),
        lambda chunk, shard: shares.at[chunk + 1, :, lanes_at(shard * width, width)],
        lambda slot, chunk: boxes.at[slot, chunk],
        out_send,
        out_recv,
        2,
    )
    line.clear_ends()
    is_end = (col == 0) | (col == LINE - 1)

    def left_copies(tick):
        shard = pick(tick, [pick(col, [order[t] for order in ORDER]) for t in range(LINE)])
        here = rows_at(shard * part, part)
        slot = lax.rem(tick, 2)
        return [
            pltpu.make_async_copy(
                hidden_parts.at[slot, k], left_out.at[k, here], left_sem.at[slot, k]
            )
            for k in range(3)
        ]

    @pl.loop(0, LINE)
    def _(tick):
        @pl.when(tick == 1)
        def _():
            for chunk in range(2):
                chain.step(1, chunk)

        @pl.when(((tick == 2) & is_end) | ((tick == 3) & jnp.logical_not(is_end)))
        def _():
            for chunk in range(2):
                chain.step(2, chunk)

        @pl.when((tick == 3) & is_end)
        def _():
            for chunk in range(2):
                chain.step(3, chunk)

        shard = pick(tick, [pick(col, [order[t] for order in ORDER]) for t in range(LINE)])
        here = rows_at(shard * part, part)
        slot = lax.rem(tick, 2)
        pltpu.make_async_copy(cot_full.at[here], cots.at[here], cot_sem.at[tick]).wait()

        @pl.when(tick >= 2)
        def _():
            for copy in left_copies(tick - 2):
                copy.wait()

        for index, (first, count) in enumerate(tiles):

            @pl.when(tick == 0)
            def _():
                for copy in load_copies(index, first, count):
                    copy.wait()

            rows_here, lanes = slice(first, first + count), slice(first, first + count)
            gate = matmul_nt(n2s[here, :], gate_w[rows_here, :])
            up = matmul_nt(n2s[here, :], up_w[rows_here, :])
            grad = matmul_nt(cots[here, :], down_w[rows_here, :])
            sigmoid = jax.nn.sigmoid(gate)
            silu = gate * sigmoid
            hidden_parts[slot, 0, :, lanes] = (silu * up).astype(bf16)
            hidden_parts[slot, 1, :, lanes] = (
                grad * up * sigmoid * (1.0 + gate * (1.0 - sigmoid))
            ).astype(bf16)
            hidden_parts[slot, 2, :, lanes] = (grad * silu).astype(bf16)
        for copy in left_copies(tick):
            copy.start()
        own = jnp.where(tick == 0, 1.0, 0.0)
        for first in range(0, D, 512):
            lanes = slice(first, first + 512)
            total = matmul(hidden_parts[slot, 0, :, :hidden], down_w[:, lanes])
            shares[shard, :, lanes] = (total + hid[:, lanes] * own).astype(bf16)

        @pl.when(tick == 1)
        def _():
            line.left_end(0)
            line.right_end(1)

        @pl.when(tick == 2)
        def _():
            line.left_end(1)
            line.right_end(0)
            line.near_left(0)
            line.near_right(1)

    rest_copies = [
        pltpu.make_async_copy(shares.at[shard], out_rest.at[k], out_sem.at[2 + k])
        for k, shard in enumerate((0, LINE - 1))
    ]
    for copy in rest_copies:
        copy.start()
    n2_copy = pltpu.make_async_copy(n2s, n2_out, n2_sem)
    n2_copy.start()
    line.near_left(1)
    line.near_right(0)
    for chunk in range(2):
        line.far(chunk)
    result_copies = []
    for chunk in range(2):
        stage[chunk] = line.own(chunk).astype(bf16)
        result_copies.append(
            pltpu.make_async_copy(
                stage.at[chunk], result.at[pl.ds((chunk + 1) * part, part)], out_sem.at[chunk]
            )
        )
        result_copies[chunk].start()
    for tick in (LINE - 2, LINE - 1):
        for copy in left_copies(tick):
            copy.wait()
    n2_copy.wait()
    chain.finish()
    line.finish()
    for copy in rest_copies + result_copies:
        copy.wait()


def mlp(n2, cot_full, hid, own, peer):
    bf16 = jnp.bfloat16
    rows = cot_full.shape[0]
    part = n2.shape[0]
    hidden = own[0].shape[0]
    shape = jax.ShapeDtypeStruct
    dma = pltpu.SemaphoreType.DMA
    padded = -(-hidden // TILE) * TILE
    wide = pltpu.VMEM((hidden, D), bf16)
    full = pltpu.VMEM((rows, D), bf16)
    return pl.pallas_call(
        mlp_kernel,
        out_shape=[
            shape((3, rows, padded), bf16),
            shape((rows, D), bf16),
            shape((rows, D // LINE), bf16),
            shape((2, part, D), bf16),
        ],
        in_specs=[any_spec()] * 2 + [vmem_spec()] + [any_spec()] * 6,
        out_specs=[any_spec()] * 4,
        scratch_shapes=[
            wide,
            wide,
            wide,
            pltpu.VMEM((2, 3, part, padded), bf16),
            full,
            full,
            dma((len(hidden_tiles(hidden)), 6)),
            dma((LINE,)),
            dma,
            dma((2, LINE - 1, 2)),
            dma((LINE, 2)),
            dma((2, 3)),
            dma,
            pltpu.VMEM((LINE, part, D), bf16),
            pltpu.VMEM((LINE + 1, 2, part, D // LINE), bf16),
            pltpu.VMEM((2, part, D // LINE), bf16),
            dma((LINE, 2)),
            dma((LINE + 1, 2)),
            dma((4,)),
        ],
        compiler_params=pltpu.CompilerParams(
            collective_id=2, has_side_effects=True, vmem_limit_bytes=56 * 2**20
        ),
        cost_estimate=pl.CostEstimate(
            flops=21 * 10**9, bytes_accessed=60 * 10**6, transcendentals=10**7
        ),
        name="mlp",
    )(n2, cot_full, hid, *own, *peer)


CHUNK = 320
TAIL = 960
LAG = 1
RING = 7
HALF_TILE = 384


class AllReduce:
    def __init__(self, place, total, inbox, sends, recvs, result, own_sems, chunks):
        self.dp, self.row, self.col = place
        self.total, self.inbox, self.sends, self.recvs = total, inbox, sends, recvs
        self.result, self.own_sems, self.chunks = result, own_sems, chunks
        x, y = lax.rem(self.dp, 2), self.dp // 2
        over_x = (self.dp + 1 - 2 * x, self.row, self.col)
        over_y = (self.dp + 2 - 4 * y, self.row, self.col)
        lanes = total.shape[1] // 2
        self.kinds = (
            (pl.ds(0, lanes), x, over_x, y, over_y),
            (pl.ds(lanes, lanes), y, over_y, x, over_x),
        )

    def part(self, ref, first, count, kind):
        return ref.at[rows_at(first, count), self.kinds[kind][0]]

    def places(self, chunk, kind):
        half, quarter = CHUNK // 2, CHUNK // 4
        _, bit1, peer1, bit2, peer2 = self.kinds[kind]
        own_half, far_half = chunk * CHUNK + half * bit1, chunk * CHUNK + half * (1 - bit1)
        box = lax.rem(chunk, RING) * (half + quarter)
        return (
            (own_half, far_half, box, box + half)
            + (own_half + quarter * bit2, own_half + quarter * (1 - bit2))
            + (far_half + quarter * bit2, far_half + quarter * (1 - bit2))
            + (peer1, peer2)
        )

    def copy(self, chunk, kind, stage, leaving):
        half, quarter = CHUNK // 2, CHUNK // 4
        _, far_half, box1, box2, own, mate, far, far_mate, peer1, peer2 = self.places(chunk, kind)
        count = quarter if stage else half
        if stage < 2:
            src = self.part(self.total, (far_half, mate)[stage], count, kind)
            dst = self.part(self.inbox, (box1, box2)[stage], count, kind)
        else:
            held = self.total if stage < 4 else self.result
            src = self.part(held, mate if stage == 4 else own, count, kind)
            if leaving:
                dst = self.part(self.result, mate if stage == 4 else own, count, kind)
            else:
                dst = self.part(self.result, (mate, far, far_mate)[stage - 2], count, kind)
        slot = lax.rem(chunk, RING)
        return remote(
            src,
            dst,
            self.sends.at[slot, kind, stage],
            self.recvs.at[slot, kind, stage],
            peer2 if stage in (1, 2) else peer1,
        )

    def own_copy(self, chunk, kind):
        own = self.places(chunk, kind)[4]
        return pltpu.make_async_copy(
            self.part(self.total, own, CHUNK // 4, kind),
            self.part(self.result, own, CHUNK // 4, kind),
            self.own_sems.at[lax.rem(chunk, RING), kind],
        )

    def add(self, chunk, kind, stage):
        self.copy(chunk, kind, stage, False).wait_recv()
        own_half, _, box1, box2, own, *_ = self.places(chunk, kind)
        count = CHUNK // 4 if stage else CHUNK // 2
        lanes = self.kinds[kind][0]
        mine = rows_at(own if stage else own_half, count)
        coming = self.inbox[rows_at(box2 if stage else box1, count), lanes].astype(jnp.float32)
        self.total[mine, lanes] = (
            self.total[mine, lanes].astype(jnp.float32) + coming
        ).astype(jnp.bfloat16)

    def step(self, number):
        for stage in range(5):

            @pl.when((number - stage * LAG >= 0) & (number - stage * LAG < self.chunks))
            def _():
                chunk = number - stage * LAG
                for kind in range(2):
                    if stage == 0:
                        self.copy(chunk, kind, 0, True).start()
                    elif stage == 1:
                        self.add(chunk, kind, 0)
                        self.copy(chunk, kind, 1, True).start()
                    elif stage == 2:
                        self.add(chunk, kind, 1)
                        self.copy(chunk, kind, 2, True).start()
                        self.copy(chunk, kind, 3, True).start()
                        self.own_copy(chunk, kind).start()
                    elif stage == 3:
                        self.copy(chunk, kind, 2, False).wait_recv()
                        self.copy(chunk, kind, 4, True).start()
                    else:
                        self.copy(chunk, kind, 3, False).wait_recv()
                        self.copy(chunk, kind, 4, False).wait_recv()
                        self.own_copy(chunk, kind).wait()
                        for sent in range(5):
                            self.copy(chunk, kind, sent, True).wait_send()


def back_kernel(
    heads,
    lefts,
    n2_in,
    cot_in,
    hid_in,
    rest_in,
    own_gate,
    own_up,
    peer_gate,
    peer_up,
    aux_all,
    wof_in,
    wall_in,
    n1_in,
    x_in,
    kv_in,
    q_in,
    att_in,
    lse_in,
    trig_in,
    attl_in,
    lengths,
    result_in,
    grad_x,
    result,
    sums_out,
    gq_out,
    gkv_out,
    small_out,
    total,
    inbox,
    give_buf,
    got_buf,
    tiles,
    y,
    wt,
    acc,
    parts,
    boxes,
    kv,
    q,
    att_low,
    mid,
    low,
    ga_send,
    ga,
    kv_give,
    kv_got,
    mate_got,
    gkv,
    gain_sum,
    gains,
    gains_got,
    load_sem,
    y_sem,
    tile_sem,
    wt_sem,
    att_sem,
    credit,
    free_sem,
    swap_send,
    swap_recv,
    ar_send,
    ar_recv,
    own_sem,
    gn_send,
    gn_recv,
    out_send,
    out_recv,
    ga_ssem,
    ga_rsem,
    gm_send,
    gm_recv,
    kv_sem,
    mate_sem,
    fin_send,
    fin_recv,
    gain_ssem,
    gain_rsem,
    end_sem,
    rest_sem,
    wall_sem,
):
    f32, bf16 = jnp.float32, jnp.bfloat16
    dp, row, col = lax.axis_index("dp"), lax.axis_index("row"), lax.axis_index("col")
    place = (dp, row, col)
    part = hid_in.shape[0]
    rows = LINE * part
    width = heads * HEAD_WIDTH
    half = TILE
    hidden = own_gate.shape[0]
    member = lax.rem(col, 2)
    mate = (dp, row, col + 1 - 2 * member)
    partner = (dp, 1 - row, col)
    col_peers = [(dp, row, lax.rem(col + k, LINE)) for k in range(1, LINE)]
    bit_x, bit_y = lax.rem(dp, 2), dp // 2
    greet(
        col_peers
        + [partner, (dp + 1 - 2 * bit_x, row, col), (dp + 2 - 4 * bit_y, row, col)]
    )
    chunks = total.shape[0] // CHUNK
    reduce = AllReduce(place, total, inbox, ar_send, ar_recv, sums_out, own_sem, chunks)

    n2_copy = pltpu.make_async_copy(n2_in, y.at[0], y_sem.at[0])
    cot_copy = pltpu.make_async_copy(cot_in, y.at[1], y_sem.at[1])
    rest_copies = [
        pltpu.make_async_copy(rest_in.at[k], y.at[1, pl.ds(k * part, part)], rest_sem.at[k])
        for k in range(2)
    ]

    products, early, jobs = 6, 3, 9
    steps = products + jobs - early

    def tile_copy(step):
        job = jnp.where(step < products, step, step - products + early)
        return pltpu.make_async_copy(
            lefts.at[lax.rem(job // 3 + 1, 3), :, lanes_at(lax.rem(job, 3) * TILE, TILE)],
            tiles.at[lax.rem(step, 3)],
            tile_sem.at[lax.rem(step, 3)],
        )

    def weight_copies(index, act):
        slot = lax.rem(index, 2)
        last = hidden - 2 * TILE
        for k, pair in enumerate(((own_gate, peer_gate), (own_up, peer_up))):
            for tail, count in ((0, TILE), (1, last)):

                @pl.when((index // 3 == k) & (lax.rem(index, 3) // 2 == tail))
                def _():
                    here = rows_at(lax.rem(index, 3) * TILE, count)
                    for n, (side, src) in enumerate(((row, pair[0]), (1 - row, pair[1]))):
                        dst = wt.at[slot, pl.ds(0, count), lanes_at(side * half, half)]
                        act(pltpu.make_async_copy(src.at[here], dst, wt_sem.at[slot, n]))

    for copy in rest_copies:
        copy.start()
    tile_copy(0).start()
    weight_copies(jnp.int32(0), lambda copy: copy.start())
    n2_copy.start()
    weight_copies(jnp.int32(1), lambda copy: copy.start())
    for step in range(1, 3):
        tile_copy(step).start()
    loads = [
        pltpu.make_async_copy(src, dst, load_sem.at[k])
        for k, (src, dst) in enumerate(
            (
                (hid_in, mid),
                (kv_in, kv),
                (q_in, q),
                (attl_in, att_low),
            )
        )
    ]
    for copy in loads:
        copy.start()
    acc[...] = jnp.zeros_like(acc)

    grain = part // LINE

    gn = LineSum(
        place,
        lambda chunk, shard: parts.at[rows_at(shard * part + chunk * grain, grain)],
        lambda slot, chunk: boxes.at[slot, rows_at(chunk * grain, grain)],
        gn_send,
        gn_recv,
        LINE,
    )
    def out_box(slot, chunk):
        if isinstance(slot, int) and slot == LINE:
            return ga_send.at[chunk]
        place_of = slot * 2 + chunk
        return y.at[
            1,
            rows_at(2 * part + place_of // LINE * part, part),
            lanes_at(lax.rem(place_of, LINE) * width, width),
        ]

    out = LineSum(
        place,
        lambda chunk, shard: y.at[1, rows_at(chunk * part, part), lanes_at(shard * width, width)],
        out_box,
        out_send,
        out_recv,
        2,
    )
    fin = LineSum(
        place,
        lambda chunk, shard: wt.at[
            chunk // 2, rows_at(lax.rem(chunk, 2) * part, part), lanes_at(shard * width, width)
        ],
        lambda slot, chunk: tiles.at[
            slot // 2, rows_at(chunk * part, part), lanes_at(lax.rem(slot, 2) * width, width)
        ],
        fin_send,
        fin_recv,
        LINE,
    )

    gn.clear_ends()
    out.clear_ends()
    for copy in rest_copies:
        copy.wait()
    for chunk in range(2):
        out.ends(chunk)

    theirs, ours = lanes_at((1 - row) * half, half), lanes_at(row * half, half)

    def swap_copy(index):
        ring = rows_at(lax.rem(index, 2) * TILE, TILE)
        return remote(
            give_buf.at[ring],
            got_buf.at[ring],
            swap_send.at[lax.rem(index, 2)],
            swap_recv.at[lax.rem(index, 2)],
            partner,
        )

    n2_copy.wait()

    @pl.loop(0, steps + 1)
    def _(step):
        @pl.when(step < steps)
        def _():
            tile_copy(step).wait()

        @pl.when(step < products)
        def _():
            weight_copies(step, lambda copy: copy.wait())

            @pl.loop(0, 2)
            def _(side):
                here = rows_at(side * 2 * part, 2 * part)
                for lane in range(0, D, 512):
                    lanes = slice(lane, lane + 512)
                    acc[here, lanes] += matmul(
                        tiles[lax.rem(step, 3), here, :], wt[lax.rem(step, 2), :, lanes]
                    )

            @pl.when(step + 2 < products)
            def _():
                weight_copies(step + 2, lambda copy: copy.start())

        @pl.when(step == products)
        def _():
            @pl.loop(0, LINE)
            def _(shard):
                here = rows_at(shard * part, part)
                parts[here, :] = acc[here, :].astype(bf16)

            @pl.loop(0, LINE)
            def _(chunk):
                gn.ends(chunk)

        @pl.when((step < early) | ((step >= products) & (step < steps)))
        def _():
            job = jnp.where(step < early, step, step - products + early)

            @pl.when(job >= 2)
            def _():
                pl.semaphore_wait(credit, 1)
                swap_copy(job - 2).wait_send()

            for first in range(0, TILE, HALF_TILE):
                lanes = slice(first, first + HALF_TILE)
                product = matmul_tn(tiles[lax.rem(step, 3), :, lanes], y[job // 6, :, theirs])
                here = rows_at(lax.rem(job, 2) * TILE + first, HALF_TILE)
                give_buf[here, :] = product.astype(bf16)
            swap_copy(job).start()

        @pl.when(((step >= 1) & (step <= early)) | (step >= products + 1))
        def _():
            job = jnp.where(step <= early, step - 1, step - products + early - 1)
            swap_copy(job).wait_recv()
            base_row = (job // 3) * hidden + lax.rem(job, 3) * TILE
            for first in range(0, TILE, HALF_TILE):
                lanes = slice(first, first + HALF_TILE)
                product = matmul_tn(tiles[lax.rem(step + 2, 3), :, lanes], y[job // 6, :, ours])
                here = rows_at(lax.rem(job, 2) * TILE + first, HALF_TILE)
                product = product + got_buf[here, :].astype(f32)
                total[rows_at(base_row + first, HALF_TILE), :] = product.astype(bf16)
            pl.semaphore_signal(credit, inc=1, device_id=partner, device_id_type=MESH)

        @pl.when((step >= 1) & (step + 2 < steps))
        def _():
            tile_copy(step + 2).start()

        @pl.when(step == 3)
        def _():
            out.near(0)

        @pl.when(step == 5)
        def _():
            out.near(1)
            out.far(0)

        @pl.when(step == 7)
        def _():
            gn.near(0)
            out.far(1)
            out.finish()
            for chunk in range(2):
                low[:, chunk * width : (chunk + 1) * width] = out.own(chunk).astype(bf16)
            cot_copy.start()

        @pl.when(step == 8)
        def _():
            cot_copy.wait()

        @pl.when(step == 10)
        def _():
            gn.near(1)
            gn.far(0)

        @pl.when(step == 12)
        def _():
            gn.near(2)
            gn.far(1)

        for number, when in enumerate((1, 2, 3, 5, 7, 9, 11)):

            @pl.when(step == when)
            def _():
                reduce.step(number)

    wof_copies = [
        pltpu.make_async_copy(
            wof_in.at[shard],
            wt.at[shard // 2, pl.ds(shard % 2 * width, width)],
            att_sem.at[shard],
        )
        for shard in range(LINE)
    ]
    for copy in wof_copies:
        copy.start()
    own_rows = rows_at(col * part, part)
    rest_copies = [
        pltpu.make_async_copy(
            low.at[:, pl.ds(chunk * width, width)],
            result.at[pl.ds(chunk * (LINE - 1) * part, part)],
            rest_sem.at[chunk],
        )
        for chunk in range(2)
    ]
    for copy in rest_copies:
        copy.start()
    for copy in rest_copies:
        copy.wait()
    low[...] = y[1, own_rows, :]
    n1_copy = pltpu.make_async_copy(n1_in, y.at[1], y_sem.at[1])
    n1_copy.start()
    for copy in loads:
        copy.wait()
    gn.near(3)
    gn.far(2)
    gn.far(3)
    reduce.step(7)
    reduce.step(8)

    gain_sum[...] = jnp.zeros_like(gain_sum)

    @pl.loop(0, LINE)
    def _(chunk):
        gn.wait_own(chunk)
        here = rows_at(chunk * grain, grain)
        squares = jnp.zeros((grain, 1), f32)
        inner = jnp.zeros((grain, 1), f32)
        grads = []
        for shard in range(LINE):
            lanes = slice(shard * width, (shard + 1) * width)
            middle = mid[here, lanes]
            grad = parts[rows_at(col * part + chunk * grain, grain), lanes].astype(f32)
            grad = grad + boxes[col, here, lanes].astype(f32)
            grad = grad + boxes[LINE, here, lanes].astype(f32)
            grads.append(grad)
            squares = squares + jnp.sum(middle * middle, axis=1, keepdims=True)
            inner = inner + jnp.sum(
                grad * aux_all[shard, 1:2, :] * middle, axis=1, keepdims=True
            )
        inverse = lax.rsqrt(squares / D + eps)
        factor = inverse * inverse * inverse * inner / D
        for shard in range(LINE):
            lanes = slice(shard * width, (shard + 1) * width)
            middle, grad = mid[here, lanes], grads[shard]
            gain_sum[1:2, lanes] += jnp.sum(grad * middle * inverse, axis=0, keepdims=True)
            new = inverse * grad * aux_all[shard, 1:2, :] - middle * factor
            new = new + low[here, lanes].astype(f32)
            mid[here, lanes] = new
            low[here, lanes] = new.astype(bf16)

    @pl.when(col > 0)
    def _():
        pl.semaphore_signal(
            free_sem.at[1], inc=1, device_id=(dp, row, col - 1), device_id_type=MESH
        )

    @pl.when(col < LINE - 1)
    def _():
        pl.semaphore_signal(
            free_sem.at[0], inc=1, device_id=(dp, row, col + 1), device_id_type=MESH
        )

    def ga_copy(k):
        to = lax.rem(col + k, LINE)
        return remote(
            ga_send.at[k - 1],
            ga.at[own_rows],
            ga_ssem.at[k - 1],
            ga_rsem.at[k - 1],
            (dp, row, to),
        )

    for copy in wof_copies:
        copy.wait()
    for k in (1, 2, 3, 0):
        shard = lax.rem(col + k, LINE)
        weights = wt[shard // 2, rows_at(lax.rem(shard, 2) * width, width), :]
        block = matmul_nt(low[...], weights).astype(bf16)
        if k:
            ga_send[k - 1] = block
            ga_copy(k).start()
        else:
            ga[own_rows, :] = block
    reduce.step(9)

    held = [att_in.at[h] for h in range(heads)] + [trig_in.at[0], trig_in.at[1], lse_in]
    att_copies = [
        pltpu.make_async_copy(src, acc.at[:, pl.ds(512 + k * HEAD_WIDTH, HEAD_WIDTH)], att_sem.at[k])
        for k, src in enumerate(held)
    ]
    trig_lanes = [
        slice(512 + (heads + k) * HEAD_WIDTH, 512 + (heads + k + 1) * HEAD_WIDTH) for k in range(2)
    ]
    lse_lanes = 512 + (heads + 2) * HEAD_WIDTH
    for copy in att_copies:
        copy.start()
    acc[:, :512] = jnp.zeros((rows, 512), f32)
    gn.finish()
    wall_width = width + 2 * HEAD_WIDTH
    wall_copies = [
        pltpu.make_async_copy(
            wall_in.at[pl.ds(shard * width, width)],
            parts.at[
                pl.ds(shard % 2 * width, width), pl.ds(shard // 2 * wall_width, wall_width)
            ],
            wall_sem.at[shard],
        )
        for shard in range(LINE)
    ]
    for copy in wall_copies:
        copy.start()
    y[0, own_rows, :] = low[...]

    chain = RowChain(place, low, y.at[0], gm_send, gm_recv, LINE, 2)

    @pl.when(col > 0)
    def _():
        pl.semaphore_wait(free_sem.at[0], 1)

    @pl.when(col < LINE - 1)
    def _():
        pl.semaphore_wait(free_sem.at[1], 1)

    for chunk in range(2):
        chain.start_own(chunk)

    span = min(512, rows)
    per_side = rows // span
    for copy in att_copies:
        copy.wait()

    def key_rows(index):
        return rows_at(lax.rem(index, per_side) * span, span)

    def key_lanes(index, which):
        return lanes_at(index // per_side * 2 * HEAD_WIDTH + which * HEAD_WIDTH, HEAD_WIDTH)

    @pl.loop(0, LINE)
    def _(turn):
        block = lax.rem(col + LINE - turn, LINE)
        here = rows_at(block * part, part)
        for k in range(1, LINE):

            @pl.when(turn == k)
            def _():
                ga_copy(k).wait_recv()

        first_query = row * rows + block * part
        query = q[:, here, :].reshape(heads * part, HEAD_WIDTH)
        back = jnp.concatenate(
            [ga[here, h * HEAD_WIDTH : (h + 1) * HEAD_WIDTH] for h in range(heads)], axis=0
        )
        attended = jnp.concatenate(
            [
                acc[here, 512 + h * HEAD_WIDTH : 512 + (h + 1) * HEAD_WIDTH]
                for h in range(heads)
            ],
            axis=0,
        )
        log_total = jnp.concatenate(
            [acc[here, lse_lanes + h : lse_lanes + h + 1] for h in range(heads)], axis=0
        )
        delta = jnp.sum(back.astype(f32) * attended, axis=1, keepdims=True)

        def body(index, grad):
            keys = rows_at(index * span, span)
            key, value = kv[keys, :HEAD_WIDTH], kv[keys, HEAD_WIDTH:]
            scores = matmul_nt(query, key) * SCALE
            allowed = allowed_keys(lengths, first_query, part, index * span, span)
            probs = jnp.exp(scores - log_total).reshape(heads, part, span)
            probs = jnp.where(allowed[None], probs, 0.0).reshape(heads * part, span)
            grads = matmul_nt(back, value)
            grad_scores = (probs * (grads - delta)).astype(bf16)
            acc[key_rows(index), key_lanes(index, 0)] += matmul_tn(grad_scores, query)
            acc[key_rows(index), key_lanes(index, 1)] += matmul_tn(probs.astype(bf16), back)
            return grad + matmul(grad_scores, key)

        blocks = (first_query + part + span - 1) // span
        grad = lax.fori_loop(0, blocks, body, jnp.zeros((heads * part, HEAD_WIDTH), f32))
        cosine, sine = acc[here, trig_lanes[0]], -acc[here, trig_lanes[1]]
        for h in range(heads):
            lanes = slice(h * HEAD_WIDTH, (h + 1) * HEAD_WIDTH)
            turned = rotate(grad[h * part : (h + 1) * part] * SCALE, cosine, sine)
            ga[here, lanes] = turned.astype(bf16)
        @pl.when(turn == LINE - 1)
        def _():
            for chunk in range(2):
                chain.step(1, chunk)

        reduce.step(10 + turn)

    kv_give[...] = acc[:, lanes_at((1 - row) * 2 * HEAD_WIDTH, 2 * HEAD_WIDTH)].astype(bf16)
    kv_copy = remote(kv_give, kv_got, kv_sem.at[0], kv_sem.at[1], partner)
    kv_copy.start()
    reduce.step(14)
    kv_copy.wait()
    lane = lax.broadcasted_iota(jnp.int32, (1, HEAD_WIDTH), 1)
    low_lanes = lane < HEAD_WIDTH // 2
    turn_by = HEAD_WIDTH // 2
    mate_give = kv_give.at[:, pl.ds(0, HEAD_WIDTH)]
    mate_copy = remote(mate_give, mate_got, mate_sem.at[0], mate_sem.at[1], mate)
    own_lanes = lanes_at(row * 2 * HEAD_WIDTH, 2 * HEAD_WIDTH)

    @pl.loop(0, LINE)
    def _(chunk):
        here = rows_at(chunk * part, part)
        both = acc[here, own_lanes] + kv_got[here, :].astype(f32)
        key = rotate(
            both[:, :HEAD_WIDTH] * SCALE, acc[here, trig_lanes[0]], -acc[here, trig_lanes[1]]
        )
        value = both[:, HEAD_WIDTH:]
        first = jnp.where(low_lanes, key, pltpu.roll(value, turn_by, 1))
        second = jnp.where(low_lanes, pltpu.roll(key, turn_by, 1), value)
        is_first = jnp.where(member == 0, 1.0, 0.0)
        kept = first * is_first + second * (1.0 - is_first)
        given = second * is_first + first * (1.0 - is_first)
        acc[here, 512 : 512 + HEAD_WIDTH] = kept
        kv_give[here, :HEAD_WIDTH] = given.astype(bf16)

    mate_copy.start()
    reduce.step(15)
    mate_copy.wait_recv()

    @pl.loop(0, LINE)
    def _(chunk):
        here = rows_at(chunk * part, part)
        kept = acc[here, 512 : 512 + HEAD_WIDTH] + mate_got[here, :].astype(f32)
        gkv[here, :] = kept.astype(bf16)

    n1_copy.wait()
    base = 3 * hidden
    first_kv, first_out = half // 2, half // 2 + HEAD_WIDTH
    first_small = first_out + width

    def projections(side_lanes, store):
        product = matmul_tn(y[1, :, side_lanes], ga[...])
        for k in range(2):
            store(
                0,
                half // 2,
                slice(k * width, (k + 1) * width),
                product[k * half // 2 : (k + 1) * half // 2],
            )
        product = matmul_tn(y[1, :, side_lanes], gkv[...])
        for k in range(half // HEAD_WIDTH):
            store(
                first_kv,
                HEAD_WIDTH,
                slice(k * HEAD_WIDTH, (k + 1) * HEAD_WIDTH),
                product[k * HEAD_WIDTH : (k + 1) * HEAD_WIDTH],
            )

    for k in range(2):
        swap_copy(jobs - 2 + k).wait_send()
    pl.semaphore_wait(credit, 2)

    def store_give(first, count, lanes, value):
        give_buf[first : first + count, lanes] = value.astype(bf16)

    def store_keep(first, count, lanes, value):
        got = got_buf[first : first + count, lanes].astype(f32)
        total[base + first : base + first + count, lanes] = (got + value).astype(bf16)

    projections(theirs, store_give)
    tail = pl.ds(0, first_out)
    tail_copy = remote(give_buf.at[tail], got_buf.at[tail], end_sem.at[0], end_sem.at[1], partner)
    tail_copy.start()
    for chunk in range(2):
        chain.step(2, chunk)
    reduce.step(16)
    tail_copy.wait_recv()
    projections(ours, store_keep)
    x_copy = pltpu.make_async_copy(x_in, y.at[1], y_sem.at[1])
    x_copy.start()

    fin.clear_ends()

    for copy in wall_copies:
        copy.wait()
    x_copy.wait()

    @pl.loop(0, LINE + 2)
    def _(chunk):
        @pl.when(chunk < LINE)
        def _():
            here = rows_at(chunk * part, part)
            squares = jnp.zeros((part, 1), f32)
            inner = jnp.zeros((part, 1), f32)
            for shard in range(LINE):
                lanes = slice(shard * width, (shard + 1) * width)
                there = slice(shard % 2 * width, (shard % 2 + 1) * width)
                first = shard // 2 * wall_width
                kv_lanes = lanes_at(first + width + member * HEAD_WIDTH, HEAD_WIDTH)
                grad = matmul_nt(ga[here, :], parts[there, first : first + width])
                grad = grad + matmul_nt(gkv[here, :], parts[there, kv_lanes])
                acc[:part, lanes] = grad
                value = y[1, here, lanes].astype(f32)
                squares = squares + jnp.sum(value * value, axis=1, keepdims=True)
                scaled = grad * aux_all[shard, 0:1, :]
                inner = inner + jnp.sum(scaled * value, axis=1, keepdims=True)
            inverse = lax.rsqrt(squares / D + eps)
            factor = inverse * inverse * inverse * inner / D
            own = jnp.where(chunk == col, 1.0, 0.0)
            there = rows_at(lax.rem(chunk, 2) * part, part)
            for shard in range(LINE):
                lanes = slice(shard * width, (shard + 1) * width)
                grad, value = acc[:part, lanes], y[1, here, lanes].astype(f32)
                gain_sum[0:1, lanes] += jnp.sum(grad * value * inverse, axis=0, keepdims=True)
                share = inverse * grad * aux_all[shard, 0:1, :] - value * factor
                share = share + mid[:, lanes] * own
                wt[chunk // 2, there, lanes] = share.astype(bf16)
            fin.ends(chunk)

        @pl.when((chunk >= 1) & (chunk <= LINE))
        def _():
            fin.near(chunk - 1)

        @pl.when(chunk >= 2)
        def _():
            fin.far(chunk - 2)

        @pl.when(chunk < LINE)
        def _():
            reduce.step(17 + chunk)

    gains[...] = gain_sum[...]

    def gain_copy(k):
        to = lax.rem(col + k, LINE)
        return remote(
            gains.at[:, lanes_at(to * width, width)],
            gains_got.at[k - 1],
            gain_ssem.at[k - 1],
            gain_rsem.at[k - 1],
            (dp, row, to),
        )

    for k in range(1, LINE):
        gain_copy(k).start()
    reduce.step(21)
    bias = jnp.concatenate(
        [jnp.sum(ref[...].astype(f32), axis=0, keepdims=True) for ref in (ga, gkv)], axis=1
    )
    for k in range(1, LINE):
        gain_copy(k).wait_recv()
    gain_total = gains[:, lanes_at(col * width, width)]
    for k in range(1, LINE):
        gain_total = gain_total + gains_got[k - 1]
    small = jnp.concatenate(
        [
            jnp.concatenate([gain_total, jnp.zeros((8, half - width), f32)], axis=1),
            jnp.concatenate(
                [
                    jnp.broadcast_to(bias, (8, width + HEAD_WIDTH)),
                    jnp.zeros((8, half - width - HEAD_WIDTH), f32),
                ],
                axis=1,
            ),
        ],
        axis=0,
    )
    small_rows = pl.ds(first_out, width + 16)
    for chunk in range(2):
        chain.step(3, chunk)
    product = matmul_tn(att_low[...], y[0, :, theirs])
    give_buf[first_out:first_small, :] = product.astype(bf16)
    give_buf[first_small : first_small + 16, :] = small.astype(bf16)
    small_copy = remote(
        give_buf.at[small_rows], got_buf.at[small_rows], end_sem.at[2], end_sem.at[3], partner
    )
    small_copy.start()
    product = matmul_tn(att_low[...], y[0, :, ours])
    small_copy.wait_recv()
    product = product + got_buf[first_out:first_small, :].astype(f32)
    total[base + first_out : base + first_small, :] = product.astype(bf16)
    small = small + got_buf[first_small : first_small + 16, :].astype(f32)
    total[base + first_small : base + first_small + 16, :] = small.astype(bf16)
    rest = TAIL - first_small - 16
    total[base + first_small + 16 : base + TAIL, :] = jnp.zeros((rest, half), bf16)
    for number in (22, 23):
        reduce.step(number)

    @pl.loop(0, LINE)
    def _(chunk):
        ga[rows_at(chunk * part, part), :] = fin.own(chunk).astype(bf16)

    grad_copy = pltpu.make_async_copy(ga, grad_x, att_sem.at[1])
    grad_copy.start()

    @pl.loop(24, chunks + 4 * LAG)
    def _(number):
        reduce.step(number)

    outs = [
        pltpu.make_async_copy(
            sums_out.at[pl.ds(base, half // 2), pl.ds(k * width, width)],
            gq_out.at[pl.ds(k * half // 2, half // 2)],
            load_sem.at[k],
        )
        for k in range(2)
    ]
    outs += [
        pltpu.make_async_copy(
            sums_out.at[pl.ds(base + first_kv, HEAD_WIDTH), pl.ds(k * HEAD_WIDTH, HEAD_WIDTH)],
            gkv_out.at[pl.ds(k * HEAD_WIDTH, HEAD_WIDTH)],
            load_sem.at[2 + k],
        )
        for k in range(half // HEAD_WIDTH)
    ]
    outs.append(
        pltpu.make_async_copy(
            sums_out.at[pl.ds(base + first_small, 16)], small_out, load_sem.at[8]
        )
    )
    for copy in outs:
        copy.start()

    chain.finish()
    fin.finish()
    for k in range(1, LINE):
        ga_copy(k).wait_send()
        gain_copy(k).wait_send()
    for copy in (mate_copy, tail_copy, small_copy):
        copy.wait_send()
    for copy in outs + [grad_copy]:
        copy.wait()


def back(lefts, n2, cot, hid, rest, result, own, peer, aux_all, wof, wall, n1, x, kv, q, att, lse, trig, att_low, lengths):
    f32, bf16 = jnp.float32, jnp.bfloat16
    shape = jax.ShapeDtypeStruct
    dma = pltpu.SemaphoreType.DMA
    heads, rows, _ = q.shape
    width = heads * HEAD_WIDTH
    part = hid.shape[0]
    hidden = own[0].shape[0]
    total_rows = 3 * hidden + TAIL
    outs = [
        (shape((rows, width), bf16), any_spec()),
        (shape((rows, width), bf16), any_spec()),
        (shape((total_rows, TILE), bf16), any_spec()),
        (shape((TILE, width), bf16), any_spec()),
        (shape((TILE, HEAD_WIDTH), bf16), any_spec()),
        (shape((16, TILE), bf16), vmem_spec()),
    ]
    vmem = pltpu.VMEM
    return pl.pallas_call(
        functools.partial(back_kernel, heads),
        out_shape=[o[0] for o in outs],
        in_specs=[any_spec()] * 9
        + [vmem_spec()]
        + [any_spec()] * 10
        + [pl.BlockSpec(memory_space=pltpu.SMEM), any_spec()],
        out_specs=[o[1] for o in outs],
        scratch_shapes=[
            vmem((total_rows, TILE), bf16),
            vmem((RING * CHUNK * 3 // 4, TILE), bf16),
            vmem((2 * TILE, TILE), bf16),
            vmem((2 * TILE, TILE), bf16),
            vmem((3, rows, TILE), bf16),
            vmem((2, rows, D), bf16),
            vmem((2, TILE, D), bf16),
            vmem((rows, D), f32),
            vmem((rows, D), bf16),
            vmem((LINE + 1, part, D), bf16),
            vmem(kv.shape, bf16),
            vmem(q.shape, bf16),
            vmem(att_low.shape, bf16),
            vmem((part, D), f32),
            vmem((part, D), bf16),
            vmem((LINE - 1, part, width), bf16),
            vmem((rows, width), bf16),
            vmem((rows, 2 * HEAD_WIDTH), bf16),
            vmem((rows, 2 * HEAD_WIDTH), bf16),
            vmem((rows, HEAD_WIDTH), bf16),
            vmem((rows, HEAD_WIDTH), bf16),
            vmem((8, D), f32),
            vmem((8, D), f32),
            vmem((LINE - 1, 8, width), f32),
            dma((9,)),
            dma((2,)),
            dma((3,)),
            dma((2, 2)),
            dma((6,)),
            pltpu.SemaphoreType.REGULAR,
            pltpu.SemaphoreType.REGULAR((2,)),
            dma((2,)),
            dma((2,)),
            dma((RING, 2, 5)),
            dma((RING, 2, 5)),
            dma((RING, 2)),
            dma((LINE, LINE)),
            dma((LINE + 1, LINE)),
            dma((LINE, 2)),
            dma((LINE + 1, 2)),
            dma((LINE - 1,)),
            dma((LINE - 1,)),
            dma((2, LINE - 1, 2)),
            dma((LINE, 2)),
            dma((2,)),
            dma((2,)),
            dma((LINE, LINE)),
            dma((LINE + 1, LINE)),
            dma((LINE - 1,)),
            dma((LINE - 1,)),
            dma((4,)),
            dma((2,)),
            dma((LINE,)),
        ],
        compiler_params=pltpu.CompilerParams(
            collective_id=3, has_side_effects=True, vmem_limit_bytes=63 * 2**20
        ),
        cost_estimate=pl.CostEstimate(
            flops=64 * 10**9, bytes_accessed=60 * 10**6, transcendentals=10**7
        ),
        input_output_aliases={21: 1},
        name="back",
    )(
        lefts, n2, cot, hid, rest, *own[:2], *peer[:2], aux_all, wof, wall, n1, x, kv, q, att, lse, trig, att_low, lengths, result
    )


def per_device(
    inputs,
    seq_lengths,
    gain_one,
    w_query,
    b_query,
    w_key,
    b_key,
    w_value,
    b_value,
    w_out,
    gain_two,
    w_gate,
    w_up,
    w_down,
    cotangent,
):
    f32 = jnp.float32
    planes = lax.axis_size("dp")
    rows, width = inputs.shape
    kv_cols = w_key.shape[1]
    hidden = w_down.shape[0]
    half = HEAD_WIDTH // 2
    freq = theta_base ** (-(jnp.arange(half, dtype=f32) * 2.0) / HEAD_WIDTH)
    freq = jnp.concatenate([freq, freq]).reshape(1, HEAD_WIDTH)
    biases = jnp.concatenate([b_key, b_value]).astype(f32)
    biases = jnp.pad(biases, (0, width - 2 * kv_cols))
    aux = jnp.stack([gain_one, gain_two, b_query.astype(f32), biases])
    aux = jnp.pad(aux, ((0, 4), (0, 0)))
    own_kv = jnp.concatenate([w_key, w_value], axis=1)
    own = (w_gate.T, w_up.T, w_down)
    (
        x_full,
        normed_one,
        cot_full,
        queries,
        keys_values,
        attended,
        log_total,
        att_own,
        hidden_mid,
        normed_two,
        trig,
        att_low,
        aux_all,
        wall,
        wof,
        *peer,
    ) = front(
        (LINE, planes),
        aux,
        inputs,
        cotangent,
        w_query,
        own_kv,
        w_out,
        *own,
        seq_lengths,
        freq,
    )
    lefts, normed_full, result, rest = mlp(normed_two, cot_full, hidden_mid, own, peer)
    grad_inputs, result, sums, grad_w_query, grad_kv, small = back(
        lefts,
        normed_full,
        cot_full,
        hidden_mid,
        rest,
        result,
        own,
        peer,
        aux_all,
        wof,
        wall,
        normed_one,
        x_full,
        keys_values,
        queries,
        attended,
        log_total,
        trig,
        att_low.reshape(rows, width),
        seq_lengths,
    )
    grad_w_gate, grad_w_up, grad_w_down = (
        sums[k * hidden : (k + 1) * hidden].astype(f32) for k in range(3)
    )
    first = 3 * hidden + TILE // 2 + HEAD_WIDTH
    grad_w_out = sums[first : first + width].astype(f32)
    grad_kv = grad_kv.astype(f32)
    small = small.astype(f32)
    bias = small[8]
    return (
        result,
        grad_inputs,
        small[0, :width],
        grad_w_query.astype(f32),
        bias[:width],
        grad_kv[:, :kv_cols],
        bias[width : width + kv_cols],
        grad_kv[:, kv_cols:],
        bias[width + kv_cols : width + 2 * kv_cols],
        grad_w_out,
        small[1, :width],
        grad_w_gate.T,
        grad_w_up.T,
        grad_w_down,
    )


def solution(mesh):
    whole_heads = dict(mesh.shape) == {"dp": 4, "row": 2, "col": LINE}
    return jax.shard_map(
        per_device if whole_heads else per_device_any,
        mesh=mesh,
        in_specs=(
            P(("dp", "row"), "col"),
            P("dp", None),
            P("col"),
            P("row", "col"),
            P("col"),
            P("row", "col"),
            P("col"),
            P("row", "col"),
            P("col"),
            P("col", "row"),
            P("col"),
            P("row", "col"),
            P("row", "col"),
            P("col", "row"),
            P(("dp", "row"), "col"),
        ),
        out_specs=(
            P(("dp", "row"), "col"),
            P(("dp", "row"), "col"),
            P("col"),
            P("row", "col"),
            P("col"),
            P("row", "col"),
            P("col"),
            P("row", "col"),
            P("col"),
            P("col", "row"),
            P("col"),
            P("row", "col"),
            P("row", "col"),
            P("col", "row"),
        ),
        check_vma=False,
    )
```

```python
import functools

import jax
import jax.numpy as jnp
from jax import lax
from jax.experimental import pallas as pl
from jax.experimental.pallas import tpu as pltpu
from jax.sharding import PartitionSpec as P

D = 1536
HEAD_WIDTH = 128
QUERY_HEADS = 12
KEY_VALUE_HEADS = 2
DEVICE_TOKENS = 256
QW = 1536
KW = 256


theta_base = 1000000.0
eps = 1e-06


def matmul(left, right):
    return jnp.dot(left, right, preferred_element_type=jnp.float32)


def matmul_tn(left, right):
    return lax.dot_general(
        left, right, (((0,), (0,)), ((), ())), preferred_element_type=jnp.float32
    )


def matmul_nt(left, right):
    return lax.dot_general(
        left, right, (((1,), (1,)), ((), ())), preferred_element_type=jnp.float32
    )


def row_squares(values):
    return lax.psum(values, "col")


def gather_width(values):
    return lax.all_gather(values, "col", axis=1, tiled=True)


def sum_width(values):
    return lax.psum_scatter(
        values.astype(jnp.bfloat16), "col", scatter_dimension=1, tiled=True
    ).astype(jnp.float32)


def documents(lengths, places):
    doc_ends = jnp.cumsum(lengths)
    doc_starts = doc_ends - lengths
    doc_index = jnp.sum((places[:, None] >= doc_ends[None, :]).astype(jnp.int32), axis=1)
    chosen = doc_index[:, None] == jnp.arange(lengths.shape[0], dtype=jnp.int32)[None, :]
    offset = jnp.sum(jnp.where(chosen, doc_starts[None, :], 0), axis=1)
    return (doc_index, places - offset)


def rotary_embedding(values, token_position, direction):
    half_size = HEAD_WIDTH // 2
    frequency = theta_base ** (-(jnp.arange(half_size, dtype=jnp.float32) * 2.0) / HEAD_WIDTH)
    angles = token_position.astype(jnp.float32)[:, None] * frequency[None, :]
    cosine = jnp.cos(angles)[:, None, :]
    sine_part = direction * jnp.sin(angles)[:, None, :]
    leading = values[..., :half_size]
    second = values[..., half_size:]
    return jnp.concatenate(
        [leading * cosine - second * sine_part, second * cosine + leading * sine_part], axis=-1
    )


def norm_forward(hidden, gain):
    square_total = row_squares(jnp.sum(hidden * hidden, axis=1))
    inverse = lax.rsqrt(square_total / D + eps)
    normed = (hidden * inverse[:, None] * gain[None, :]).astype(jnp.bfloat16)
    return (normed, inverse)


def norm_backward(hidden, gain, inverse, grad_normed):
    scaled = grad_normed * gain[None, :]
    inner = row_squares(jnp.sum(scaled * hidden, axis=1))
    grad_hidden = (
        inverse[:, None] * scaled - hidden * (inverse * inverse * inverse * inner / D)[:, None]
    )
    grad_gain = jnp.sum(grad_normed * hidden * inverse[:, None], axis=0)
    return (grad_hidden, grad_gain)


def key_layout(gathered_keys, gathered_values, doc_all):
    seq_len = gathered_keys.shape[0]
    key_block_index = min(512, seq_len)
    count_blocks = seq_len // key_block_index
    blocks_of_keys = gathered_keys.reshape(
        count_blocks, key_block_index, gathered_keys.shape[1] // HEAD_WIDTH, HEAD_WIDTH
    )
    blocks_of_values = gathered_values.reshape(
        count_blocks, key_block_index, gathered_values.shape[1] // HEAD_WIDTH, HEAD_WIDTH
    )
    doc_blocks = doc_all.reshape(count_blocks, key_block_index)
    place_blocks = jnp.arange(seq_len, dtype=jnp.int32).reshape(count_blocks, key_block_index)
    return (blocks_of_keys, doc_blocks, place_blocks, blocks_of_values)


def block_scores(heads_of_queries, key_blk, doc_blk, place_blk, doc_local, place_local):
    scores = jnp.einsum(
        "tkgh,skh->tkgs", heads_of_queries, key_blk, preferred_element_type=jnp.float32
    ) * HEAD_WIDTH ** (-0.5)
    allowed = (doc_blk[None, :] == doc_local[:, None]) & (
        place_blk[None, :] <= place_local[:, None]
    )
    return (scores, allowed[:, None, None, :])


def attention_forward(heads_of_queries, blocks, doc_local, place_local):
    head_shape = heads_of_queries.shape[:3]

    def first_pass(state_in, packed):
        running_max, running_sum = state_in
        scores, allowed = block_scores(
            heads_of_queries, packed[0], packed[1], packed[2], doc_local, place_local
        )
        masked = jnp.where(allowed, scores, -1e30)
        new_max = jnp.maximum(running_max, jnp.max(masked, axis=-1))
        raised = jnp.where(allowed, jnp.exp(scores - new_max[..., None]), 0.0)
        running_sum = running_sum * jnp.exp(running_max - new_max) + jnp.sum(raised, axis=-1)
        return ((new_max, running_sum), None)

    initial = (jnp.full(head_shape, -1e30, jnp.float32), jnp.zeros(head_shape, jnp.float32))
    (running_max, running_sum), unused = lax.scan(first_pass, initial, blocks)
    log_total = running_max + jnp.log(running_sum)

    def second_pass(acc_out, packed):
        scores, allowed = block_scores(
            heads_of_queries, packed[0], packed[1], packed[2], doc_local, place_local
        )
        probs_low = jnp.where(allowed, jnp.exp(scores - log_total[..., None]), 0.0).astype(
            jnp.bfloat16
        )
        return (
            acc_out
            + jnp.einsum(
                "tkgs,skh->tkgh", probs_low, packed[3], preferred_element_type=jnp.float32
            ),
            None,
        )

    attended, unused = lax.scan(second_pass, jnp.zeros(heads_of_queries.shape, jnp.float32), blocks)
    return (attended, log_total)


def attention_backward(
    heads_of_queries, blocks, doc_local, place_local, log_total, attended, heads_gradient
):
    inner = jnp.sum(heads_gradient.astype(jnp.float32) * attended, axis=-1)
    scale_factor = HEAD_WIDTH ** (-0.5)

    def back_pass(grad_query, packed):
        scores, allowed = block_scores(
            heads_of_queries, packed[0], packed[1], packed[2], doc_local, place_local
        )
        probs = jnp.where(allowed, jnp.exp(scores - log_total[..., None]), 0.0)
        grad_probs = jnp.einsum(
            "tkgh,skh->tkgs", heads_gradient, packed[3], preferred_element_type=jnp.float32
        )
        grad_scores = (probs * (grad_probs - inner[..., None])).astype(jnp.bfloat16)
        grad_query = (
            grad_query
            + jnp.einsum(
                "tkgs,skh->tkgh", grad_scores, packed[0], preferred_element_type=jnp.float32
            )
            * scale_factor
        )
        grad_key = (
            jnp.einsum(
                "tkgs,tkgh->skh", grad_scores, heads_of_queries, preferred_element_type=jnp.float32
            )
            * scale_factor
        )
        grad_value = jnp.einsum(
            "tkgs,tkgh->skh",
            probs.astype(jnp.bfloat16),
            heads_gradient,
            preferred_element_type=jnp.float32,
        )
        return (grad_query, (grad_key, grad_value))

    grad_query, (key_grads, value_grads) = lax.scan(
        back_pass, jnp.zeros(heads_of_queries.shape, jnp.float32), blocks
    )
    seq_len = key_grads.shape[0] * key_grads.shape[1]
    return (grad_query, key_grads.reshape(seq_len, -1), value_grads.reshape(seq_len, -1))


def per_device_any(
    inputs,
    seq_lengths,
    gain_one,
    w_query,
    b_query,
    w_key,
    b_key,
    w_value,
    b_value,
    w_out,
    gain_two,
    w_gate,
    w_up,
    w_down,
    cotangent,
):
    full_query, full_key, full_value, full_out, full_gate, full_up, full_down = (
        lax.all_gather(w_query, "row", axis=0, tiled=True),
        lax.all_gather(w_key, "row", axis=0, tiled=True),
        lax.all_gather(w_value, "row", axis=0, tiled=True),
        lax.all_gather(w_out, "row", axis=1, tiled=True),
        lax.all_gather(w_gate, "row", axis=0, tiled=True),
        lax.all_gather(w_up, "row", axis=0, tiled=True),
        lax.all_gather(w_down, "row", axis=1, tiled=True),
    )
    row_pos = lax.axis_index("row")
    col_pos = lax.axis_index("col")
    row_count = lax.axis_size("row")
    col_count = lax.axis_size("col")
    seq_len = DEVICE_TOKENS * row_count * col_count
    query_group_width = QUERY_HEADS // KEY_VALUE_HEADS
    lengths = seq_lengths[0]
    place_local = (row_pos * col_count + col_pos) * DEVICE_TOKENS + jnp.arange(
        DEVICE_TOKENS, dtype=jnp.int32
    )
    doc_local, local_position = documents(lengths, place_local)
    doc_all = documents(lengths, jnp.arange(seq_len, dtype=jnp.int32))[0]
    hidden_in = inputs.astype(jnp.float32)
    normed_one, inverse_one = norm_forward(hidden_in, gain_one)
    normed_full = gather_width(normed_one)
    query_lin = (matmul(normed_full, full_query) + b_query.astype(jnp.float32)).astype(jnp.bfloat16)
    projected_keys = (matmul(normed_full, full_key) + b_key.astype(jnp.float32)).astype(
        jnp.bfloat16
    )
    projected_values = (matmul(normed_full, full_value) + b_value.astype(jnp.float32)).astype(
        jnp.bfloat16
    )
    query_rows, rows_of_keys, value_rows = (
        lax.all_to_all(query_lin, "col", split_axis=0, concat_axis=1, tiled=True),
        lax.all_to_all(projected_keys, "col", split_axis=0, concat_axis=1, tiled=True),
        lax.all_to_all(projected_values, "col", split_axis=0, concat_axis=1, tiled=True),
    )
    rotated_queries = rotary_embedding(
        query_rows.astype(jnp.float32).reshape(DEVICE_TOKENS, QUERY_HEADS, HEAD_WIDTH),
        local_position,
        1.0,
    ).astype(jnp.bfloat16)
    rotated_keys = rotary_embedding(
        rows_of_keys.astype(jnp.float32).reshape(DEVICE_TOKENS, KEY_VALUE_HEADS, HEAD_WIDTH),
        local_position,
        1.0,
    ).astype(jnp.bfloat16)
    gathered_keys, gathered_values = (
        lax.all_gather(rotated_keys.reshape(DEVICE_TOKENS, KW), ("row", "col"), axis=0, tiled=True),
        lax.all_gather(value_rows, ("row", "col"), axis=0, tiled=True),
    )
    blocks = key_layout(gathered_keys, gathered_values, doc_all)
    heads_of_queries = rotated_queries.reshape(
        DEVICE_TOKENS, KEY_VALUE_HEADS, query_group_width, HEAD_WIDTH
    )
    attended, log_total = attention_forward(heads_of_queries, blocks, doc_local, place_local)
    attended_low = attended.reshape(DEVICE_TOKENS, QW).astype(jnp.bfloat16)
    attended_cols = lax.all_to_all(attended_low, "col", split_axis=1, concat_axis=0, tiled=True)
    hidden_mid = hidden_in + sum_width(matmul(attended_cols, full_out))
    normed_two, inverse_two = norm_forward(hidden_mid, gain_two)
    normed_wide = gather_width(normed_two)
    gate = matmul(normed_wide, full_gate)
    up_proj = matmul(normed_wide, full_up)
    sigmoid_gate = jax.nn.sigmoid(gate)
    silu_gate = gate * sigmoid_gate
    mixed = (silu_gate * up_proj).astype(jnp.bfloat16)
    result = (hidden_mid + sum_width(matmul(mixed, full_down))).astype(jnp.bfloat16)
    grad_full = gather_width(cotangent)
    grad_w_down = matmul_tn(mixed, grad_full)
    grad_mixed = matmul_nt(grad_full, full_down)
    grad_gate = (grad_mixed * up_proj * sigmoid_gate * (1.0 + gate * (1.0 - sigmoid_gate))).astype(
        jnp.bfloat16
    )
    grad_up = (grad_mixed * silu_gate).astype(jnp.bfloat16)
    grad_w_gate = matmul_tn(normed_wide, grad_gate)
    grad_w_up = matmul_tn(normed_wide, grad_up)
    grad_normed_two = sum_width(matmul_nt(grad_gate, full_gate) + matmul_nt(grad_up, full_up))
    grad_back_two, grad_gain_two = norm_backward(hidden_mid, gain_two, inverse_two, grad_normed_two)
    grad_mid = cotangent.astype(jnp.float32) + grad_back_two
    grad_attn_full = gather_width(grad_mid.astype(jnp.bfloat16))
    grad_w_out = matmul_tn(attended_cols, grad_attn_full)
    grad_attended_cols = matmul_nt(grad_attn_full, full_out).astype(jnp.bfloat16)
    attended_gradient = lax.all_to_all(
        grad_attended_cols, "col", split_axis=0, concat_axis=1, tiled=True
    )
    heads_gradient = attended_gradient.reshape(
        DEVICE_TOKENS, KEY_VALUE_HEADS, query_group_width, HEAD_WIDTH
    )
    grad_query_rot, key_grads, value_grads = attention_backward(
        heads_of_queries, blocks, doc_local, place_local, log_total, attended, heads_gradient
    )
    rotated_key_gradient, grad_value = (
        lax.psum_scatter(
            key_grads.astype(jnp.bfloat16), ("row", "col"), scatter_dimension=0, tiled=True
        ).astype(jnp.float32),
        lax.psum_scatter(
            value_grads.astype(jnp.bfloat16), ("row", "col"), scatter_dimension=0, tiled=True
        ).astype(jnp.float32),
    )
    grad_query_lin = (
        rotary_embedding(
            grad_query_rot.reshape(DEVICE_TOKENS, QUERY_HEADS, HEAD_WIDTH), local_position, -1.0
        )
        .reshape(DEVICE_TOKENS, QW)
        .astype(jnp.bfloat16)
    )
    grad_key_lin = (
        rotary_embedding(
            rotated_key_gradient.reshape(DEVICE_TOKENS, KEY_VALUE_HEADS, HEAD_WIDTH),
            local_position,
            -1.0,
        )
        .reshape(DEVICE_TOKENS, KW)
        .astype(jnp.bfloat16)
    )
    grad_value_lin = grad_value.astype(jnp.bfloat16)
    query_grad_cols, key_grad_cols, value_grad_cols = (
        lax.all_to_all(grad_query_lin, "col", split_axis=1, concat_axis=0, tiled=True),
        lax.all_to_all(grad_key_lin, "col", split_axis=1, concat_axis=0, tiled=True),
        lax.all_to_all(grad_value_lin, "col", split_axis=1, concat_axis=0, tiled=True),
    )
    grad_b_query = jnp.sum(query_grad_cols.astype(jnp.float32), axis=0)
    grad_b_key = jnp.sum(key_grad_cols.astype(jnp.float32), axis=0)
    grad_b_value = jnp.sum(value_grad_cols.astype(jnp.float32), axis=0)
    grad_w_query = matmul_tn(normed_full, query_grad_cols)
    grad_w_key = matmul_tn(normed_full, key_grad_cols)
    grad_w_value = matmul_tn(normed_full, value_grad_cols)
    grad_normed_one = sum_width(
        matmul_nt(query_grad_cols, full_query)
        + matmul_nt(key_grad_cols, full_key)
        + matmul_nt(value_grad_cols, full_value)
    )
    grad_back_one, grad_gain_one = norm_backward(hidden_in, gain_one, inverse_one, grad_normed_one)
    grad_inputs = (grad_mid + grad_back_one).astype(jnp.bfloat16)
    summed = (
        lax.psum(grad_w_query.astype(jnp.bfloat16), ("dp", "row")).astype(jnp.float32),
        lax.psum(grad_w_key.astype(jnp.bfloat16), ("dp", "row")).astype(jnp.float32),
        lax.psum(grad_w_value.astype(jnp.bfloat16), ("dp", "row")).astype(jnp.float32),
        lax.psum(grad_w_out.astype(jnp.bfloat16), ("dp", "row")).astype(jnp.float32),
        lax.psum(grad_w_gate.astype(jnp.bfloat16), ("dp", "row")).astype(jnp.float32),
        lax.psum(grad_w_up.astype(jnp.bfloat16), ("dp", "row")).astype(jnp.float32),
        lax.psum(grad_w_down.astype(jnp.bfloat16), ("dp", "row")).astype(jnp.float32),
        lax.psum(grad_gain_one.astype(jnp.bfloat16), ("dp", "row")).astype(jnp.float32),
        lax.psum(grad_b_query.astype(jnp.bfloat16), ("dp", "row")).astype(jnp.float32),
        lax.psum(grad_b_key.astype(jnp.bfloat16), ("dp", "row")).astype(jnp.float32),
        lax.psum(grad_b_value.astype(jnp.bfloat16), ("dp", "row")).astype(jnp.float32),
        lax.psum(grad_gain_two.astype(jnp.bfloat16), ("dp", "row")).astype(jnp.float32),
    )
    rows_each = D // row_count
    split_dims = (0, 0, 0, 1, 0, 0, 1)
    weight_sums = tuple(
        (
            lax.dynamic_slice_in_dim(
                summed[member], row_pos * rows_each, rows_each, split_dims[member]
            )
            for member in range(7)
        )
    )
    small_sums = summed[7:]
    return (
        result,
        grad_inputs,
        small_sums[0],
        weight_sums[0],
        small_sums[1],
        weight_sums[1],
        small_sums[2],
        weight_sums[2],
        small_sums[3],
        weight_sums[3],
        small_sums[4],
        weight_sums[4],
        weight_sums[5],
        weight_sums[6],
    )


MESH = pl.DeviceIdType.MESH
NEG = -1e30
SCALE = HEAD_WIDTH ** (-0.5)


def vmem_spec():
    return pl.BlockSpec(memory_space=pltpu.VMEM)


def any_spec():
    return pl.BlockSpec(memory_space=pl.ANY)


def remote(src, dst, send_sem, recv_sem, device):
    return pltpu.make_async_remote_copy(
        src_ref=src,
        dst_ref=dst,
        send_sem=send_sem,
        recv_sem=recv_sem,
        device_id=device,
        device_id_type=MESH,
    )


def greet(peers):
    barrier = pltpu.get_barrier_semaphore()
    for peer in peers:
        pl.semaphore_signal(barrier, inc=1, device_id=peer, device_id_type=MESH)
    pl.semaphore_wait(barrier, len(peers))


def rows_at(first, count):
    return pl.ds(pl.multiple_of(first, 16), count)


def lanes_at(first, count):
    return pl.ds(pl.multiple_of(first, 128), count)


class Chain:
    def __init__(self, place, own, full, sends, recvs, count, chunks):
        self.dp, self.row, self.col = place
        self.own, self.full, self.sends, self.recvs = own, full, sends, recvs
        self.count, self.chunks = count, chunks
        self.width = full.shape[1] // count
        self.rows = full.shape[0] // chunks

    def block(self, shard, chunk):
        return self.full.at[
            rows_at(chunk * self.rows, self.rows), lanes_at(shard * self.width, self.width)
        ]

    def copy(self, way, step, shard, chunk):
        src = self.block(shard, chunk)
        if step == 0:
            src = self.own.at[rows_at(chunk * self.rows, self.rows)]
        device = (self.dp, self.row, self.col + (1 if way == 0 else -1))
        return remote(
            src,
            self.block(shard, chunk),
            self.sends.at[way, step, chunk],
            self.recvs.at[shard, chunk],
            device,
        )

    def start_own(self, chunk):
        @pl.when(self.col < self.count - 1)
        def _():
            self.copy(0, 0, self.col, chunk).start()

        @pl.when(self.col > 0)
        def _():
            self.copy(1, 0, self.col, chunk).start()

    def step(self, step, chunk):
        left, right = self.col - step, self.col + step

        @pl.when(left >= 0)
        def _():
            self.copy(0, step, left, chunk).wait_recv()

        if step < self.count - 1:

            @pl.when((left >= 0) & (self.col < self.count - 1))
            def _():
                self.copy(0, step, left, chunk).start()

        @pl.when(right < self.count)
        def _():
            self.copy(1, step, right, chunk).wait_recv()

        if step < self.count - 1:

            @pl.when((right < self.count) & (self.col > 0))
            def _():
                self.copy(1, step, right, chunk).start()

    def finish(self):
        for step in range(self.count - 1):
            left, right = self.col - step, self.col + step

            @pl.when((left >= 0) & (self.col < self.count - 1))
            def _():
                @pl.loop(0, self.chunks)
                def _(chunk):
                    self.copy(0, step, left, chunk).wait_send()

            @pl.when((right < self.count) & (self.col > 0))
            def _():
                @pl.loop(0, self.chunks)
                def _(chunk):
                    self.copy(1, step, right, chunk).wait_send()


def doc_start(lengths, place):
    first = jnp.zeros_like(place)
    end = 0
    for doc in range(lengths.shape[1]):
        end = end + lengths[0, doc]
        first = jnp.where(place >= end, end, first)
    return first


def rotate(values, cosine, sine):
    return values * cosine + pltpu.roll(values, HEAD_WIDTH // 2, 1) * sine


def allowed_keys(lengths, first_query, queries, first_key, keys):
    query = first_query + lax.broadcasted_iota(jnp.int32, (queries, 1), 0)
    key = first_key + lax.broadcasted_iota(jnp.int32, (1, keys), 1)
    return (key >= doc_start(lengths, query)) & (key <= query)


def front_kernel(
    heads,
    dims,
    aux,
    x,
    cot,
    wq,
    wkv,
    wout,
    w_gate,
    w_up,
    w_down,
    lengths,
    freq,
    x_out,
    n1_out,
    cot_out,
    q_out,
    kv_out,
    att_hbm,
    lse_out,
    attl_out,
    hid_out,
    n2_out,
    trig_out,
    att_low,
    aux_out,
    wall_hbm,
    wof_hbm,
    peer_gate,
    peer_up,
    peer_down,
    x_full,
    n1,
    cot_full,
    x_send,
    x_recv,
    c_send,
    c_recv,
    local_sem,
    aux_send,
    aux_recv,
    wall_send,
    wall_recv,
    z_send,
    z_recv,
    d_send,
    d_recv,
    r_send,
    r_recv,
    kv_send,
    kv_recv,
    a2a_send,
    a2a_recv,
    m_send,
    m_recv,
    att_out,
    wall_out,
    wof_out,
    out_sem,
):
    count, planes = dims
    f32, bf16 = jnp.float32, jnp.bfloat16
    dp, row, col = lax.axis_index("dp"), lax.axis_index("row"), lax.axis_index("col")
    place = (dp, row, col)
    rows, width = x.shape
    part = rows // count
    half = wq.shape[0]
    member = lax.rem(col, 2)
    mate = col + 1 - 2 * member
    col_peers = [(dp, row, lax.rem(col + k, count)) for k in range(1, count)]
    dp_peers = [(lax.rem(dp + k, planes), row, col) for k in range(1, planes)]
    partner = (dp, 1 - row, col)
    across = (dp, 1 - row, mate)
    greet(col_peers + dp_peers + [partner, across])

    chain_x = Chain(place, x, x_full, x_send, x_recv, count, count)
    chain_c = Chain(place, cot, cot_full, c_send, c_recv, count, count)
    own_lanes = lanes_at(col * width, width)
    copy_x = pltpu.make_async_copy(x, x_full.at[:, own_lanes], local_sem.at[0])
    copy_x.start()
    aux_copies = [
        remote(aux, aux_out.at[col], aux_send.at[k], aux_recv.at[k], peer)
        for k, peer in enumerate(col_peers)
    ]
    for copy in aux_copies:
        copy.start()

    @pl.loop(0, count)
    def _(chunk):
        chain_x.start_own(chunk)

    own_half = rows_at(row * half, half)
    kv_lanes = lanes_at(width + member * HEAD_WIDTH, HEAD_WIDTH)
    copy_q = pltpu.make_async_copy(wq, wall_out.at[own_half, pl.ds(0, width)], local_sem.at[1])
    copy_kv = pltpu.make_async_copy(wkv, wall_out.at[own_half, kv_lanes], local_sem.at[2])
    copy_q.start()
    copy_kv.start()
    wall_copies = [
        remote(
            wq, wall_out.at[own_half, pl.ds(0, width)], wall_send.at[0], wall_recv.at[0], partner
        )
    ] + [
        remote(wkv, wall_out.at[own_half, kv_lanes], wall_send.at[k], wall_recv.at[k], peer)
        for k, peer in ((1, partner), (2, (dp, row, mate)), (3, across))
    ]
    for copy in wall_copies:
        copy.start()
    mlp_copies = [
        remote(src, dst, m_send.at[k], m_recv.at[k], partner)
        for k, (src, dst) in enumerate(
            ((w_gate, peer_gate), (w_up, peer_up), (w_down, peer_down))
        )
    ]
    for copy in mlp_copies:
        copy.start()
    copy_c = pltpu.make_async_copy(cot, cot_full.at[:, own_lanes], local_sem.at[3])
    copy_c.start()
    quarter = wout.shape[0] // planes
    out_lanes = lanes_at(row * half, half)

    def wof_block(shard, plane, side):
        return wof_out.at[
            shard, rows_at(plane * quarter, quarter), lanes_at(side * half, half)
        ]

    def wof_blocks(plane, side):
        return wof_out.at[:, rows_at(plane * quarter, quarter), lanes_at(side * half, half)]

    own_quarter = wout.at[rows_at(dp * quarter, quarter)]
    copy_o = pltpu.make_async_copy(own_quarter, wof_block(col, dp, row), local_sem.at[4])
    copy_o.start()

    token = row * rows + lax.broadcasted_iota(jnp.int32, (rows, 1), 0)
    position = (token - doc_start(lengths, token)).astype(f32)
    angle = position * freq[...]
    trig_out[0] = jnp.cos(angle)
    lane = lax.broadcasted_iota(jnp.int32, (1, HEAD_WIDTH), 1)
    trig_out[1] = jnp.sin(angle) * jnp.where(lane < HEAD_WIDTH // 2, -1.0, 1.0)
    aux_out[col] = aux[...]

    for step in range(1, count - 1):

        @pl.loop(0, count)
        def _(chunk):
            chain_x.step(step, chunk)

    z_copies = [
        remote(own_quarter, wof_block(col, dp, row), z_send.at[k], z_recv.at[k], peer)
        for k, peer in enumerate(col_peers)
    ]
    for copy in z_copies:
        copy.start()

    @pl.loop(0, count)
    def _(chunk):
        chain_c.start_own(chunk)

    copy_x.wait()
    copy_q.wait()
    copy_kv.wait()
    for copy in aux_copies:
        copy.wait_recv()
    for k, (side, who) in enumerate(
        ((1 - row, None), (1 - row, member), (row, 1 - member), (1 - row, 1 - member))
    ):
        side_rows = rows_at(side * half, half)
        if who is None:
            dst, src = wall_out.at[side_rows, pl.ds(0, width)], wq
        else:
            dst = wall_out.at[side_rows, lanes_at(width + who * HEAD_WIDTH, HEAD_WIDTH)]
            src = wkv
        remote(src, dst, wall_send.at[k], wall_recv.at[k], partner).wait_recv()

    mate_aux = aux_out[mate]
    even = jnp.where(member == 0, aux[3:4, :HEAD_WIDTH], mate_aux[3:4, :HEAD_WIDTH])
    odd = jnp.where(member == 0, mate_aux[3:4, :HEAD_WIDTH], aux[3:4, :HEAD_WIDTH])
    low_lanes = lane < HEAD_WIDTH // 2
    key_bias = jnp.where(low_lanes, even, pltpu.roll(odd, HEAD_WIDTH // 2, 1))
    value_bias = jnp.where(low_lanes, pltpu.roll(even, HEAD_WIDTH // 2, 1), odd)

    def kv_chunk(side, chunk):
        return kv_out.at[rows_at(side * rows + chunk * part, part)]

    def kv_copy(chunk):
        return remote(
            kv_chunk(row, chunk),
            kv_chunk(row, chunk),
            kv_send.at[chunk],
            kv_recv.at[chunk],
            partner,
        )

    @pl.loop(0, count)
    def _(chunk):
        chain_x.step(count - 1, chunk)
        here = rows_at(chunk * part, part)
        squares = jnp.zeros((part, 1), f32)
        for shard in range(count):
            piece = x_full[here, shard * width : (shard + 1) * width].astype(f32)
            squares = squares + jnp.sum(piece * piece, axis=1, keepdims=True)
        inverse = lax.rsqrt(squares / D + eps)
        for shard in range(count):
            lanes = slice(shard * width, (shard + 1) * width)
            piece = x_full[here, lanes].astype(f32)
            n1[here, lanes] = (piece * inverse * aux_out[shard, 0:1, :]).astype(bf16)
        lin = matmul(n1[here, :], wall_out[...])
        cosine, sine = trig_out[0, here, :], trig_out[1, here, :]
        for head in range(heads):
            lanes = slice(head * HEAD_WIDTH, (head + 1) * HEAD_WIDTH)
            query = (lin[:, lanes] + aux[2:3, lanes]).astype(bf16).astype(f32)
            q_out[head, here, :] = rotate(query, cosine, sine).astype(bf16)
        first = lin[:, width : width + HEAD_WIDTH]
        second = lin[:, width + HEAD_WIDTH : width + 2 * HEAD_WIDTH]
        turn = HEAD_WIDTH // 2
        key = jnp.where(low_lanes, first, pltpu.roll(second, turn, 1)) + key_bias
        value = jnp.where(low_lanes, pltpu.roll(first, turn, 1), second) + value_bias
        there = rows_at(row * rows + chunk * part, part)
        kv_out[there, :HEAD_WIDTH] = rotate(
            key.astype(bf16).astype(f32), cosine, sine
        ).astype(bf16)
        kv_out[there, HEAD_WIDTH:] = value.astype(bf16)
        kv_copy(chunk).start()

    n1_copy = pltpu.make_async_copy(n1, n1_out, local_sem.at[5])
    n1_copy.start()
    x_copy = pltpu.make_async_copy(x_full, x_out, local_sem.at[6])
    x_copy.start()
    wall_copy = pltpu.make_async_copy(wall_out, wall_hbm, out_sem.at[0])
    wall_copy.start()

    copy_o.wait()
    for k in range(1, count):
        shard = lax.rem(col + count - k, count)
        remote(
            own_quarter, wof_block(shard, dp, row), z_send.at[k - 1], z_recv.at[k - 1], partner
        ).wait_recv()
    d_copies = [
        remote(wof_blocks(dp, row), wof_blocks(dp, row), d_send.at[k], d_recv.at[k], peer)
        for k, peer in enumerate(dp_peers)
    ]
    r_copies = [
        remote(
            wof_blocks(lax.rem(dp + planes - k, planes), row),
            wof_blocks(lax.rem(dp + planes - k, planes), row),
            r_send.at[k],
            r_recv.at[k],
            partner,
        )
        for k in range(planes)
    ]
    for copy in d_copies:
        copy.start()
    r_copies[0].start()

    @pl.loop(0, count)
    def _(chunk):
        remote(
            kv_chunk(row, chunk),
            kv_chunk(1 - row, chunk),
            kv_send.at[chunk],
            kv_recv.at[chunk],
            partner,
        ).wait_recv()

    span = min(512, rows)

    def a2a_copy(block):
        return remote(
            att_low.at[block],
            attl_out.at[:, own_lanes],
            a2a_send.at[block],
            a2a_recv.at[col],
            (dp, row, block),
        )

    @pl.loop(0, count)
    def _(block):
        here = rows_at(block * part, part)
        first_query = row * rows + block * part
        query = q_out[:, here, :].reshape(heads * part, HEAD_WIDTH)

        def body(index, state):
            largest, total, acc = state
            keys = rows_at(index * span, span)
            scores = matmul_nt(query, kv_out[keys, :HEAD_WIDTH]) * SCALE
            allowed = allowed_keys(lengths, first_query, part, index * span, span)
            scores = jnp.where(allowed[None], scores.reshape(heads, part, span), NEG)
            scores = scores.reshape(heads * part, span)
            new = jnp.maximum(largest, jnp.max(scores, axis=1, keepdims=True))
            raised = jnp.exp(scores - new)
            alpha = jnp.exp(largest - new)
            total = total * alpha + jnp.sum(raised, axis=1, keepdims=True)
            acc = acc * alpha + matmul(raised.astype(bf16), kv_out[keys, HEAD_WIDTH:])
            return new, total, acc

        state = (
            jnp.full((heads * part, 1), NEG, f32),
            jnp.zeros((heads * part, 1), f32),
            jnp.zeros((heads * part, HEAD_WIDTH), f32),
        )
        blocks = (first_query + part + span - 1) // span
        largest, total, acc = lax.fori_loop(0, blocks, body, state)
        attended = (acc / total).reshape(heads, part, HEAD_WIDTH)
        att_out[:, here, :] = attended
        log_total = (largest + jnp.log(total)).reshape(heads, part, 1)
        spread = jnp.zeros((part, HEAD_WIDTH), f32)
        for head in range(heads):
            spread = jnp.where(lane == head, log_total[head], spread)
        lse_out[here, :] = spread
        for head in range(heads):
            lanes = slice(head * HEAD_WIDTH, (head + 1) * HEAD_WIDTH)
            att_low[block, :, lanes] = attended[head].astype(bf16)

        @pl.when(block != col)
        def _():
            a2a_copy(block).start()

        chain_c.step(1, block)

    attl_out[:, own_lanes] = att_low[col]
    att_copy = pltpu.make_async_copy(att_out, att_hbm, out_sem.at[1])
    att_copy.start()
    for k in range(1, planes):
        remote(
            wof_blocks(dp, row),
            wof_blocks(lax.rem(dp + planes - k, planes), row),
            d_send.at[k - 1],
            d_recv.at[k - 1],
            partner,
        ).wait_recv()
        r_copies[k].start()
    for step in range(2, count - 1):

        @pl.loop(0, count)
        def _(chunk):
            chain_c.step(step, chunk)

    for k in range(planes):
        other = wof_blocks(lax.rem(dp + planes - k, planes), 1 - row)
        remote(other, other, r_send.at[k], r_recv.at[k], partner).wait_recv()

    wof_copy = pltpu.make_async_copy(wof_out, wof_hbm, out_sem.at[2])
    wof_copy.start()

    @pl.loop(0, count)
    def _(block):
        @pl.when(block != col)
        def _():
            remote(
                att_low.at[block],
                attl_out.at[:, lanes_at(block * width, width)],
                a2a_send.at[block],
                a2a_recv.at[block],
                (dp, row, block),
            ).wait_recv()

    mine = rows_at(col * part, part)
    step_lanes = D // 4
    squares = jnp.zeros((part, 1), f32)
    for piece in range(4):
        lanes = slice(piece * step_lanes, (piece + 1) * step_lanes)
        total = x_full[mine, lanes].astype(f32)
        weights = wof_out[:, :, lanes].reshape(D, step_lanes)
        total = total + matmul(attl_out[...], weights)
        hid_out[:, lanes] = total
        squares = squares + jnp.sum(total * total, axis=1, keepdims=True)
    inverse = lax.rsqrt(squares / D + eps)
    for shard in range(count):
        lanes = slice(shard * width, (shard + 1) * width)
        n2_out[:, lanes] = (hid_out[:, lanes] * inverse * aux_out[shard, 1:2, :]).astype(bf16)

    @pl.loop(0, count)
    def _(chunk):
        chain_c.step(count - 1, chunk)

    copy_c.wait()
    c_copy = pltpu.make_async_copy(cot_full, cot_out, local_sem.at[7])
    c_copy.start()

    chain_x.finish()
    chain_c.finish()
    for copy in aux_copies + wall_copies + z_copies + d_copies + r_copies:
        copy.wait_send()
    for copy in mlp_copies:
        copy.wait()

    @pl.loop(0, count)
    def _(chunk):
        kv_copy(chunk).wait_send()

        @pl.when(chunk != col)
        def _():
            a2a_copy(chunk).wait_send()

    for copy in (n1_copy, x_copy, c_copy, wall_copy, att_copy, wof_copy):
        copy.wait()


def front(dims, aux, x, cot, wq, wkv, wout, w_gate, w_up, w_down, lengths, freq):
    count, planes = dims
    rows, width = x.shape
    part = rows // count
    heads = width // HEAD_WIDTH
    f32, bf16 = jnp.float32, jnp.bfloat16
    shape = jax.ShapeDtypeStruct
    wall = width + 2 * HEAD_WIDTH
    outs = [
        (shape((rows, D), bf16), any_spec()),
        (shape((rows, D), bf16), any_spec()),
        (shape((rows, D), bf16), any_spec()),
        (shape((heads, rows, HEAD_WIDTH), bf16), vmem_spec()),
        (shape((2 * rows, 2 * HEAD_WIDTH), bf16), vmem_spec()),
        (shape((heads, rows, HEAD_WIDTH), f32), any_spec()),
        (shape((rows, HEAD_WIDTH), f32), vmem_spec()),
        (shape((part, D), bf16), vmem_spec()),
        (shape((part, D), f32), vmem_spec()),
        (shape((part, D), bf16), vmem_spec()),
        (shape((2, rows, HEAD_WIDTH), f32), vmem_spec()),
        (shape((count, part, width), bf16), vmem_spec()),
        (shape((count,) + aux.shape, f32), vmem_spec()),
        (shape((D, wall), bf16), any_spec()),
        (shape((count, wout.shape[0], D), bf16), any_spec()),
        (shape(w_gate.shape, bf16), any_spec()),
        (shape(w_up.shape, bf16), any_spec()),
        (shape(w_down.shape, bf16), any_spec()),
    ]
    dma = pltpu.SemaphoreType.DMA
    return pl.pallas_call(
        functools.partial(front_kernel, heads, dims),
        out_shape=[o[0] for o in outs],
        in_specs=[vmem_spec()]
        + [any_spec()] * 8
        + [pl.BlockSpec(memory_space=pltpu.SMEM), vmem_spec()],
        out_specs=[o[1] for o in outs],
        scratch_shapes=[
            pltpu.VMEM((rows, D), bf16),
            pltpu.VMEM((rows, D), bf16),
            pltpu.VMEM((rows, D), bf16),
            dma((2, count - 1, count)),
            dma((count, count)),
            dma((2, count - 1, count)),
            dma((count, count)),
            dma((8,)),
            dma((count - 1,)),
            dma((count - 1,)),
            dma((4,)),
            dma((4,)),
            dma((count - 1,)),
            dma((count - 1,)),
            dma((planes - 1,)),
            dma((planes - 1,)),
            dma((planes,)),
            dma((planes,)),
            dma((count,)),
            dma((count,)),
            dma((count,)),
            dma((count,)),
            dma((3,)),
            dma((3,)),
            pltpu.VMEM((heads, rows, HEAD_WIDTH), f32),
            pltpu.VMEM((D, wall), bf16),
            pltpu.VMEM((count, wout.shape[0], D), bf16),
            dma((3,)),
        ],
        compiler_params=pltpu.CompilerParams(
            collective_id=1, has_side_effects=True, vmem_limit_bytes=52 * 2**20
        ),
        cost_estimate=pl.CostEstimate(
            flops=10 * 10**9, bytes_accessed=60 * 10**6, transcendentals=10**7
        ),
        name="front",
    )(aux, x, cot, wq, wkv, wout, w_gate, w_up, w_down, lengths, freq)


LINE = 4
TILE = 768
ORDER = ((0, 1, 2, 3), (1, 0, 2, 3), (2, 1, 3, 0), (3, 2, 1, 0))


def pick(index, values):
    out = values[0]
    for k, value in enumerate(values[1:], 1):
        out = jnp.where(index == k, value, out)
    return out


def hidden_tiles(total):
    tile = 512
    return [(first, min(tile, total - first)) for first in range(0, total, tile)]


class RowChain(Chain):
    def block(self, shard, chunk):
        shard_rows = self.full.shape[0] // self.count
        count = shard_rows // self.chunks
        return self.full.at[rows_at(shard * shard_rows + chunk * count, count)]

    def copy(self, way, step, shard, chunk):
        self.rows = self.full.shape[0] // self.count // self.chunks
        return super().copy(way, step, shard, chunk)


class LineSum:
    def __init__(self, place, share, box, sends, recvs, chunks):
        self.dp, self.row, self.col = place
        self.share, self.box, self.sends, self.recvs = share, box, sends, recvs
        self.chunks = chunks

    def copy(self, c, chunk, shard):
        to = c + 1 if shard > c else c - 1
        slot = LINE if to < c and shard == to else shard
        return remote(
            self.share(chunk, shard),
            self.box(slot, chunk),
            self.sends.at[shard, chunk],
            self.recvs.at[slot, chunk],
            (self.dp, self.row, to),
        )

    def got(self, chunk, slot):
        box = self.box(slot, chunk)
        partner = (self.dp, 1 - self.row, self.col)
        remote(box, box, self.sends.at[0, chunk], self.recvs.at[slot, chunk], partner).wait_recv()

    def onward(self, c, chunk, shard):
        self.got(chunk, shard)
        share, box = self.share(chunk, shard), self.box(shard, chunk)
        share[...] = (share[...].astype(jnp.float32) + box[...].astype(jnp.float32)).astype(
            jnp.bfloat16
        )
        self.copy(c, chunk, shard).start()

    def left_end(self, chunk):
        @pl.when(self.col == 0)
        def _():
            for shard in (3, 2, 1):
                self.copy(0, chunk, shard).start()

    def right_end(self, chunk):
        @pl.when(self.col == LINE - 1)
        def _():
            for shard in (0, 1, 2):
                self.copy(LINE - 1, chunk, shard).start()

    def ends(self, chunk):
        self.left_end(chunk)
        self.right_end(chunk)

    def near_left(self, chunk):
        @pl.when(self.col == 1)
        def _():
            for shard in (3, 2):
                self.onward(1, chunk, shard)

    def near_right(self, chunk):
        @pl.when(self.col == 2)
        def _():
            for shard in (0, 1):
                self.onward(2, chunk, shard)

    def near(self, chunk):
        self.near_left(chunk)
        self.near_right(chunk)

    def far(self, chunk):
        @pl.when(self.col == 1)
        def _():
            self.onward(1, chunk, 0)

        @pl.when(self.col == 2)
        def _():
            self.onward(2, chunk, 3)

    def clear_ends(self):
        for c, slot in ((0, 0), (LINE - 1, LINE)):

            @pl.when(self.col == c)
            def _():
                for chunk in range(self.chunks):
                    box = self.box(slot, chunk)
                    box[...] = jnp.zeros(box.shape, jnp.bfloat16)

    def wait_own(self, chunk):
        @pl.when(self.col > 0)
        def _():
            self.got(chunk, self.col)

        @pl.when(self.col < LINE - 1)
        def _():
            self.got(chunk, LINE)

    def own(self, chunk):
        self.wait_own(chunk)
        refs = (self.share(chunk, self.col), self.box(self.col, chunk), self.box(LINE, chunk))
        return sum(ref[...].astype(jnp.float32) for ref in refs)

    def finish(self):
        for c in range(LINE):

            @pl.when(self.col == c)
            def _():
                @pl.loop(0, self.chunks)
                def _(chunk):
                    for shard in range(LINE):
                        if shard != c:
                            self.copy(c, chunk, shard).wait_send()


def mlp_kernel(
    n2,
    cot_full,
    hid,
    own_gate,
    own_up,
    own_down,
    peer_gate,
    peer_up,
    peer_down,
    left_out,
    n2_out,
    result,
    out_rest,
    gate_w,
    up_w,
    down_w,
    hidden_parts,
    n2s,
    cots,
    w_sem,
    cot_sem,
    own_sem,
    ag_send,
    ag_recv,
    left_sem,
    n2_sem,
    shares,
    boxes,
    stage,
    out_send,
    out_recv,
    out_sem,
):
    f32, bf16 = jnp.float32, jnp.bfloat16
    dp, row, col = lax.axis_index("dp"), lax.axis_index("row"), lax.axis_index("col")
    part = n2.shape[0]
    hidden, half = own_gate.shape
    tiles = hidden_tiles(hidden)
    greet([(dp, row, lax.rem(col + k, LINE)) for k in range(1, LINE)])
    chain = RowChain((dp, row, col), n2, n2s, ag_send, ag_recv, LINE, 2)
    for chunk in range(2):
        chain.start_own(chunk)
    own_copy = pltpu.make_async_copy(n2, n2s.at[rows_at(col * part, part)], own_sem)
    own_copy.start()

    def cot_copy(tick):
        here = rows_at(pick(col, [order[tick] for order in ORDER]) * part, part)
        return pltpu.make_async_copy(cot_full.at[here], cots.at[here], cot_sem.at[tick])

    def load_copies(index, first, count):
        rows_here = pl.ds(first, count)
        copies = []
        for own, peer, whole in (
            (own_gate, peer_gate, gate_w),
            (own_up, peer_up, up_w),
            (own_down, peer_down, down_w),
        ):
            for side, src in ((row, own), (1 - row, peer)):
                copies.append((src.at[rows_here], whole.at[rows_here, lanes_at(side * half, half)]))
        return [
            pltpu.make_async_copy(src, dst, w_sem.at[index, k])
            for k, (src, dst) in enumerate(copies)
        ]

    cot_copy(0).start()
    for index, (first, count) in enumerate(tiles):
        for copy in load_copies(index, first, count):
            copy.start()
    for tick in range(1, LINE):
        cot_copy(tick).start()
    hidden_parts[:, :, :, hidden:] = jnp.zeros(
        hidden_parts.shape[:3] + (hidden_parts.shape[3] - hidden,), bf16
    )
    own_copy.wait()
    width = D // LINE
    line = LineSum(
        (dp, row, col),
        lambda chunk, shard: shares.at[chunk + 1, :, lanes_at(shard * width, width)],
        lambda slot, chunk: boxes.at[slot, chunk],
        out_send,
        out_recv,
        2,
    )
    line.clear_ends()
    is_end = (col == 0) | (col == LINE - 1)

    def left_copies(tick):
        shard = pick(tick, [pick(col, [order[t] for order in ORDER]) for t in range(LINE)])
        here = rows_at(shard * part, part)
        slot = lax.rem(tick, 2)
        return [
            pltpu.make_async_copy(
                hidden_parts.at[slot, k], left_out.at[k, here], left_sem.at[slot, k]
            )
            for k in range(3)
        ]

    @pl.loop(0, LINE)
    def _(tick):
        @pl.when(tick == 1)
        def _():
            for chunk in range(2):
                chain.step(1, chunk)

        @pl.when(((tick == 2) & is_end) | ((tick == 3) & jnp.logical_not(is_end)))
        def _():
            for chunk in range(2):
                chain.step(2, chunk)

        @pl.when((tick == 3) & is_end)
        def _():
            for chunk in range(2):
                chain.step(3, chunk)

        shard = pick(tick, [pick(col, [order[t] for order in ORDER]) for t in range(LINE)])
        here = rows_at(shard * part, part)
        slot = lax.rem(tick, 2)
        pltpu.make_async_copy(cot_full.at[here], cots.at[here], cot_sem.at[tick]).wait()

        @pl.when(tick >= 2)
        def _():
            for copy in left_copies(tick - 2):
                copy.wait()

        for index, (first, count) in enumerate(tiles):

            @pl.when(tick == 0)
            def _():
                for copy in load_copies(index, first, count):
                    copy.wait()

            rows_here, lanes = slice(first, first + count), slice(first, first + count)
            gate = matmul_nt(n2s[here, :], gate_w[rows_here, :])
            up = matmul_nt(n2s[here, :], up_w[rows_here, :])
            grad = matmul_nt(cots[here, :], down_w[rows_here, :])
            sigmoid = jax.nn.sigmoid(gate)
            silu = gate * sigmoid
            hidden_parts[slot, 0, :, lanes] = (silu * up).astype(bf16)
            hidden_parts[slot, 1, :, lanes] = (
                grad * up * sigmoid * (1.0 + gate * (1.0 - sigmoid))
            ).astype(bf16)
            hidden_parts[slot, 2, :, lanes] = (grad * silu).astype(bf16)
        for copy in left_copies(tick):
            copy.start()
        own = jnp.where(tick == 0, 1.0, 0.0)
        for first in range(0, D, 512):
            lanes = slice(first, first + 512)
            total = matmul(hidden_parts[slot, 0, :, :hidden], down_w[:, lanes])
            shares[shard, :, lanes] = (total + hid[:, lanes] * own).astype(bf16)

        @pl.when(tick == 1)
        def _():
            line.left_end(0)
            line.right_end(1)

        @pl.when(tick == 2)
        def _():
            line.left_end(1)
            line.right_end(0)
            line.near_left(0)
            line.near_right(1)

    rest_copies = [
        pltpu.make_async_copy(shares.at[shard], out_rest.at[k], out_sem.at[2 + k])
        for k, shard in enumerate((0, LINE - 1))
    ]
    for copy in rest_copies:
        copy.start()
    n2_copy = pltpu.make_async_copy(n2s, n2_out, n2_sem)
    n2_copy.start()
    line.near_left(1)
    line.near_right(0)
    for chunk in range(2):
        line.far(chunk)
    result_copies = []
    for chunk in range(2):
        stage[chunk] = line.own(chunk).astype(bf16)
        result_copies.append(
            pltpu.make_async_copy(
                stage.at[chunk], result.at[pl.ds((chunk + 1) * part, part)], out_sem.at[chunk]
            )
        )
        result_copies[chunk].start()
    for tick in (LINE - 2, LINE - 1):
        for copy in left_copies(tick):
            copy.wait()
    n2_copy.wait()
    chain.finish()
    line.finish()
    for copy in rest_copies + result_copies:
        copy.wait()


def mlp(n2, cot_full, hid, own, peer):
    bf16 = jnp.bfloat16
    rows = cot_full.shape[0]
    part = n2.shape[0]
    hidden = own[0].shape[0]
    shape = jax.ShapeDtypeStruct
    dma = pltpu.SemaphoreType.DMA
    padded = -(-hidden // TILE) * TILE
    wide = pltpu.VMEM((hidden, D), bf16)
    full = pltpu.VMEM((rows, D), bf16)
    return pl.pallas_call(
        mlp_kernel,
        out_shape=[
            shape((3, rows, padded), bf16),
            shape((rows, D), bf16),
            shape((rows, D // LINE), bf16),
            shape((2, part, D), bf16),
        ],
        in_specs=[any_spec()] * 2 + [vmem_spec()] + [any_spec()] * 6,
        out_specs=[any_spec()] * 4,
        scratch_shapes=[
            wide,
            wide,
            wide,
            pltpu.VMEM((2, 3, part, padded), bf16),
            full,
            full,
            dma((len(hidden_tiles(hidden)), 6)),
            dma((LINE,)),
            dma,
            dma((2, LINE - 1, 2)),
            dma((LINE, 2)),
            dma((2, 3)),
            dma,
            pltpu.VMEM((LINE, part, D), bf16),
            pltpu.VMEM((LINE + 1, 2, part, D // LINE), bf16),
            pltpu.VMEM((2, part, D // LINE), bf16),
            dma((LINE, 2)),
            dma((LINE + 1, 2)),
            dma((4,)),
        ],
        compiler_params=pltpu.CompilerParams(
            collective_id=2, has_side_effects=True, vmem_limit_bytes=56 * 2**20
        ),
        cost_estimate=pl.CostEstimate(
            flops=21 * 10**9, bytes_accessed=60 * 10**6, transcendentals=10**7
        ),
        name="mlp",
    )(n2, cot_full, hid, *own, *peer)


CHUNK = 320
TAIL = 960
LAG = 1
RING = 7
HALF_TILE = 384


class AllReduce:
    def __init__(self, place, total, inbox, sends, recvs, result, own_sems, chunks):
        self.dp, self.row, self.col = place
        self.total, self.inbox, self.sends, self.recvs = total, inbox, sends, recvs
        self.result, self.own_sems, self.chunks = result, own_sems, chunks
        x, y = lax.rem(self.dp, 2), self.dp // 2
        over_x = (self.dp + 1 - 2 * x, self.row, self.col)
        over_y = (self.dp + 2 - 4 * y, self.row, self.col)
        lanes = total.shape[1] // 2
        self.kinds = (
            (pl.ds(0, lanes), x, over_x, y, over_y),
            (pl.ds(lanes, lanes), y, over_y, x, over_x),
        )

    def part(self, ref, first, count, kind):
        return ref.at[rows_at(first, count), self.kinds[kind][0]]

    def places(self, chunk, kind):
        half, quarter = CHUNK // 2, CHUNK // 4
        _, bit1, peer1, bit2, peer2 = self.kinds[kind]
        own_half, far_half = chunk * CHUNK + half * bit1, chunk * CHUNK + half * (1 - bit1)
        box = lax.rem(chunk, RING) * (half + quarter)
        return (
            (own_half, far_half, box, box + half)
            + (own_half + quarter * bit2, own_half + quarter * (1 - bit2))
            + (far_half + quarter * bit2, far_half + quarter * (1 - bit2))
            + (peer1, peer2)
        )

    def copy(self, chunk, kind, stage, leaving):
        half, quarter = CHUNK // 2, CHUNK // 4
        _, far_half, box1, box2, own, mate, far, far_mate, peer1, peer2 = self.places(chunk, kind)
        count = quarter if stage else half
        if stage < 2:
            src = self.part(self.total, (far_half, mate)[stage], count, kind)
            dst = self.part(self.inbox, (box1, box2)[stage], count, kind)
        else:
            held = self.total if stage < 4 else self.result
            src = self.part(held, mate if stage == 4 else own, count, kind)
            if leaving:
                dst = self.part(self.result, mate if stage == 4 else own, count, kind)
            else:
                dst = self.part(self.result, (mate, far, far_mate)[stage - 2], count, kind)
        slot = lax.rem(chunk, RING)
        return remote(
            src,
            dst,
            self.sends.at[slot, kind, stage],
            self.recvs.at[slot, kind, stage],
            peer2 if stage in (1, 2) else peer1,
        )

    def own_copy(self, chunk, kind):
        own = self.places(chunk, kind)[4]
        return pltpu.make_async_copy(
            self.part(self.total, own, CHUNK // 4, kind),
            self.part(self.result, own, CHUNK // 4, kind),
            self.own_sems.at[lax.rem(chunk, RING), kind],
        )

    def add(self, chunk, kind, stage):
        self.copy(chunk, kind, stage, False).wait_recv()
        own_half, _, box1, box2, own, *_ = self.places(chunk, kind)
        count = CHUNK // 4 if stage else CHUNK // 2
        lanes = self.kinds[kind][0]
        mine = rows_at(own if stage else own_half, count)
        coming = self.inbox[rows_at(box2 if stage else box1, count), lanes].astype(jnp.float32)
        self.total[mine, lanes] = (
            self.total[mine, lanes].astype(jnp.float32) + coming
        ).astype(jnp.bfloat16)

    def step(self, number):
        for stage in range(5):

            @pl.when((number - stage * LAG >= 0) & (number - stage * LAG < self.chunks))
            def _():
                chunk = number - stage * LAG
                for kind in range(2):
                    if stage == 0:
                        self.copy(chunk, kind, 0, True).start()
                    elif stage == 1:
                        self.add(chunk, kind, 0)
                        self.copy(chunk, kind, 1, True).start()
                    elif stage == 2:
                        self.add(chunk, kind, 1)
                        self.copy(chunk, kind, 2, True).start()
                        self.copy(chunk, kind, 3, True).start()
                        self.own_copy(chunk, kind).start()
                    elif stage == 3:
                        self.copy(chunk, kind, 2, False).wait_recv()
                        self.copy(chunk, kind, 4, True).start()
                    else:
                        self.copy(chunk, kind, 3, False).wait_recv()
                        self.copy(chunk, kind, 4, False).wait_recv()
                        self.own_copy(chunk, kind).wait()
                        for sent in range(5):
                            self.copy(chunk, kind, sent, True).wait_send()


def back_kernel(
    heads,
    lefts,
    n2_in,
    cot_in,
    hid_in,
    rest_in,
    own_gate,
    own_up,
    peer_gate,
    peer_up,
    aux_all,
    wof_in,
    wall_in,
    n1_in,
    x_in,
    kv_in,
    q_in,
    att_in,
    lse_in,
    trig_in,
    attl_in,
    lengths,
    result_in,
    grad_x,
    result,
    sums_out,
    gq_out,
    gkv_out,
    small_out,
    total,
    inbox,
    give_buf,
    got_buf,
    tiles,
    y,
    wt,
    acc,
    parts,
    boxes,
    kv,
    q,
    att_low,
    mid,
    low,
    ga_send,
    ga,
    kv_give,
    kv_got,
    mate_got,
    gkv,
    gain_sum,
    gains,
    gains_got,
    load_sem,
    y_sem,
    tile_sem,
    wt_sem,
    att_sem,
    credit,
    free_sem,
    swap_send,
    swap_recv,
    ar_send,
    ar_recv,
    own_sem,
    gn_send,
    gn_recv,
    out_send,
    out_recv,
    ga_ssem,
    ga_rsem,
    gm_send,
    gm_recv,
    kv_sem,
    mate_sem,
    fin_send,
    fin_recv,
    gain_ssem,
    gain_rsem,
    end_sem,
    rest_sem,
    wall_sem,
):
    f32, bf16 = jnp.float32, jnp.bfloat16
    dp, row, col = lax.axis_index("dp"), lax.axis_index("row"), lax.axis_index("col")
    place = (dp, row, col)
    part = hid_in.shape[0]
    rows = LINE * part
    width = heads * HEAD_WIDTH
    half = TILE
    hidden = own_gate.shape[0]
    member = lax.rem(col, 2)
    mate = (dp, row, col + 1 - 2 * member)
    partner = (dp, 1 - row, col)
    col_peers = [(dp, row, lax.rem(col + k, LINE)) for k in range(1, LINE)]
    bit_x, bit_y = lax.rem(dp, 2), dp // 2
    greet(
        col_peers
        + [partner, (dp + 1 - 2 * bit_x, row, col), (dp + 2 - 4 * bit_y, row, col)]
    )
    chunks = total.shape[0] // CHUNK
    reduce = AllReduce(place, total, inbox, ar_send, ar_recv, sums_out, own_sem, chunks)

    n2_copy = pltpu.make_async_copy(n2_in, y.at[0], y_sem.at[0])
    cot_copy = pltpu.make_async_copy(cot_in, y.at[1], y_sem.at[1])
    rest_copies = [
        pltpu.make_async_copy(rest_in.at[k], y.at[1, pl.ds(k * part, part)], rest_sem.at[k])
        for k in range(2)
    ]

    products, early, jobs = 6, 3, 9
    steps = products + jobs - early

    def tile_copy(step):
        job = jnp.where(step < products, step, step - products + early)
        return pltpu.make_async_copy(
            lefts.at[lax.rem(job // 3 + 1, 3), :, lanes_at(lax.rem(job, 3) * TILE, TILE)],
            tiles.at[lax.rem(step, 3)],
            tile_sem.at[lax.rem(step, 3)],
        )

    def weight_copies(index, act):
        slot = lax.rem(index, 2)
        last = hidden - 2 * TILE
        for k, pair in enumerate(((own_gate, peer_gate), (own_up, peer_up))):
            for tail, count in ((0, TILE), (1, last)):

                @pl.when((index // 3 == k) & (lax.rem(index, 3) // 2 == tail))
                def _():
                    here = rows_at(lax.rem(index, 3) * TILE, count)
                    for n, (side, src) in enumerate(((row, pair[0]), (1 - row, pair[1]))):
                        dst = wt.at[slot, pl.ds(0, count), lanes_at(side * half, half)]
                        act(pltpu.make_async_copy(src.at[here], dst, wt_sem.at[slot, n]))

    for copy in rest_copies:
        copy.start()
    tile_copy(0).start()
    weight_copies(jnp.int32(0), lambda copy: copy.start())
    n2_copy.start()
    weight_copies(jnp.int32(1), lambda copy: copy.start())
    for step in range(1, 3):
        tile_copy(step).start()
    loads = [
        pltpu.make_async_copy(src, dst, load_sem.at[k])
        for k, (src, dst) in enumerate(
            (
                (hid_in, mid),
                (kv_in, kv),
                (q_in, q),
                (attl_in, att_low),
            )
        )
    ]
    for copy in loads:
        copy.start()
    acc[...] = jnp.zeros_like(acc)

    grain = part // LINE

    gn = LineSum(
        place,
        lambda chunk, shard: parts.at[rows_at(shard * part + chunk * grain, grain)],
        lambda slot, chunk: boxes.at[slot, rows_at(chunk * grain, grain)],
        gn_send,
        gn_recv,
        LINE,
    )
    def out_box(slot, chunk):
        if isinstance(slot, int) and slot == LINE:
            return ga_send.at[chunk]
        place_of = slot * 2 + chunk
        return y.at[
            1,
            rows_at(2 * part + place_of // LINE * part, part),
            lanes_at(lax.rem(place_of, LINE) * width, width),
        ]

    out = LineSum(
        place,
        lambda chunk, shard: y.at[1, rows_at(chunk * part, part), lanes_at(shard * width, width)],
        out_box,
        out_send,
        out_recv,
        2,
    )
    fin = LineSum(
        place,
        lambda chunk, shard: wt.at[
            chunk // 2, rows_at(lax.rem(chunk, 2) * part, part), lanes_at(shard * width, width)
        ],
        lambda slot, chunk: tiles.at[
            slot // 2, rows_at(chunk * part, part), lanes_at(lax.rem(slot, 2) * width, width)
        ],
        fin_send,
        fin_recv,
        LINE,
    )

    gn.clear_ends()
    out.clear_ends()
    for copy in rest_copies:
        copy.wait()
    for chunk in range(2):
        out.ends(chunk)

    theirs, ours = lanes_at((1 - row) * half, half), lanes_at(row * half, half)

    def swap_copy(index):
        ring = rows_at(lax.rem(index, 2) * TILE, TILE)
        return remote(
            give_buf.at[ring],
            got_buf.at[ring],
            swap_send.at[lax.rem(index, 2)],
            swap_recv.at[lax.rem(index, 2)],
            partner,
        )

    n2_copy.wait()

    @pl.loop(0, steps + 1)
    def _(step):
        @pl.when(step < steps)
        def _():
            tile_copy(step).wait()

        @pl.when(step < products)
        def _():
            weight_copies(step, lambda copy: copy.wait())

            @pl.loop(0, 2)
            def _(side):
                here = rows_at(side * 2 * part, 2 * part)
                for lane in range(0, D, 512):
                    lanes = slice(lane, lane + 512)
                    acc[here, lanes] += matmul(
                        tiles[lax.rem(step, 3), here, :], wt[lax.rem(step, 2), :, lanes]
                    )

            @pl.when(step + 2 < products)
            def _():
                weight_copies(step + 2, lambda copy: copy.start())

        @pl.when(step == products)
        def _():
            @pl.loop(0, LINE)
            def _(shard):
                here = rows_at(shard * part, part)
                parts[here, :] = acc[here, :].astype(bf16)

            @pl.loop(0, LINE)
            def _(chunk):
                gn.ends(chunk)

        @pl.when((step < early) | ((step >= products) & (step < steps)))
        def _():
            job = jnp.where(step < early, step, step - products + early)

            @pl.when(job >= 2)
            def _():
                pl.semaphore_wait(credit, 1)
                swap_copy(job - 2).wait_send()

            for first in range(0, TILE, HALF_TILE):
                lanes = slice(first, first + HALF_TILE)
                product = matmul_tn(tiles[lax.rem(step, 3), :, lanes], y[job // 6, :, theirs])
                here = rows_at(lax.rem(job, 2) * TILE + first, HALF_TILE)
                give_buf[here, :] = product.astype(bf16)
            swap_copy(job).start()

        @pl.when(((step >= 1) & (step <= early)) | (step >= products + 1))
        def _():
            job = jnp.where(step <= early, step - 1, step - products + early - 1)
            swap_copy(job).wait_recv()
            base_row = (job // 3) * hidden + lax.rem(job, 3) * TILE
            for first in range(0, TILE, HALF_TILE):
                lanes = slice(first, first + HALF_TILE)
                product = matmul_tn(tiles[lax.rem(step + 2, 3), :, lanes], y[job // 6, :, ours])
                here = rows_at(lax.rem(job, 2) * TILE + first, HALF_TILE)
                product = product + got_buf[here, :].astype(f32)
                total[rows_at(base_row + first, HALF_TILE), :] = product.astype(bf16)
            pl.semaphore_signal(credit, inc=1, device_id=partner, device_id_type=MESH)

        @pl.when((step >= 1) & (step + 2 < steps))
        def _():
            tile_copy(step + 2).start()

        @pl.when(step == 3)
        def _():
            out.near(0)

        @pl.when(step == 5)
        def _():
            out.near(1)
            out.far(0)

        @pl.when(step == 7)
        def _():
            gn.near(0)
            out.far(1)
            out.finish()
            for chunk in range(2):
                low[:, chunk * width : (chunk + 1) * width] = out.own(chunk).astype(bf16)
            cot_copy.start()

        @pl.when(step == 8)
        def _():
            cot_copy.wait()

        @pl.when(step == 10)
        def _():
            gn.near(1)
            gn.far(0)

        @pl.when(step == 12)
        def _():
            gn.near(2)
            gn.far(1)

        for number, when in enumerate((1, 2, 3, 5, 7, 9, 11)):

            @pl.when(step == when)
            def _():
                reduce.step(number)

    wof_copies = [
        pltpu.make_async_copy(
            wof_in.at[shard],
            wt.at[shard // 2, pl.ds(shard % 2 * width, width)],
            att_sem.at[shard],
        )
        for shard in range(LINE)
    ]
    for copy in wof_copies:
        copy.start()
    own_rows = rows_at(col * part, part)
    rest_copies = [
        pltpu.make_async_copy(
            low.at[:, pl.ds(chunk * width, width)],
            result.at[pl.ds(chunk * (LINE - 1) * part, part)],
            rest_sem.at[chunk],
        )
        for chunk in range(2)
    ]
    for copy in rest_copies:
        copy.start()
    for copy in rest_copies:
        copy.wait()
    low[...] = y[1, own_rows, :]
    n1_copy = pltpu.make_async_copy(n1_in, y.at[1], y_sem.at[1])
    n1_copy.start()
    for copy in loads:
        copy.wait()
    gn.near(3)
    gn.far(2)
    gn.far(3)
    reduce.step(7)
    reduce.step(8)

    gain_sum[...] = jnp.zeros_like(gain_sum)

    @pl.loop(0, LINE)
    def _(chunk):
        gn.wait_own(chunk)
        here = rows_at(chunk * grain, grain)
        squares = jnp.zeros((grain, 1), f32)
        inner = jnp.zeros((grain, 1), f32)
        grads = []
        for shard in range(LINE):
            lanes = slice(shard * width, (shard + 1) * width)
            middle = mid[here, lanes]
            grad = parts[rows_at(col * part + chunk * grain, grain), lanes].astype(f32)
            grad = grad + boxes[col, here, lanes].astype(f32)
            grad = grad + boxes[LINE, here, lanes].astype(f32)
            grads.append(grad)
            squares = squares + jnp.sum(middle * middle, axis=1, keepdims=True)
            inner = inner + jnp.sum(
                grad * aux_all[shard, 1:2, :] * middle, axis=1, keepdims=True
            )
        inverse = lax.rsqrt(squares / D + eps)
        factor = inverse * inverse * inverse * inner / D
        for shard in range(LINE):
            lanes = slice(shard * width, (shard + 1) * width)
            middle, grad = mid[here, lanes], grads[shard]
            gain_sum[1:2, lanes] += jnp.sum(grad * middle * inverse, axis=0, keepdims=True)
            new = inverse * grad * aux_all[shard, 1:2, :] - middle * factor
            new = new + low[here, lanes].astype(f32)
            mid[here, lanes] = new
            low[here, lanes] = new.astype(bf16)

    @pl.when(col > 0)
    def _():
        pl.semaphore_signal(
            free_sem.at[1], inc=1, device_id=(dp, row, col - 1), device_id_type=MESH
        )

    @pl.when(col < LINE - 1)
    def _():
        pl.semaphore_signal(
            free_sem.at[0], inc=1, device_id=(dp, row, col + 1), device_id_type=MESH
        )

    def ga_copy(k):
        to = lax.rem(col + k, LINE)
        return remote(
            ga_send.at[k - 1],
            ga.at[own_rows],
            ga_ssem.at[k - 1],
            ga_rsem.at[k - 1],
            (dp, row, to),
        )

    for copy in wof_copies:
        copy.wait()
    for k in (1, 2, 3, 0):
        shard = lax.rem(col + k, LINE)
        weights = wt[shard // 2, rows_at(lax.rem(shard, 2) * width, width), :]
        block = matmul_nt(low[...], weights).astype(bf16)
        if k:
            ga_send[k - 1] = block
            ga_copy(k).start()
        else:
            ga[own_rows, :] = block
    reduce.step(9)

    held = [att_in.at[h] for h in range(heads)] + [trig_in.at[0], trig_in.at[1], lse_in]
    att_copies = [
        pltpu.make_async_copy(src, acc.at[:, pl.ds(512 + k * HEAD_WIDTH, HEAD_WIDTH)], att_sem.at[k])
        for k, src in enumerate(held)
    ]
    trig_lanes = [
        slice(512 + (heads + k) * HEAD_WIDTH, 512 + (heads + k + 1) * HEAD_WIDTH) for k in range(2)
    ]
    lse_lanes = 512 + (heads + 2) * HEAD_WIDTH
    for copy in att_copies:
        copy.start()
    acc[:, :512] = jnp.zeros((rows, 512), f32)
    gn.finish()
    wall_width = width + 2 * HEAD_WIDTH
    wall_copies = [
        pltpu.make_async_copy(
            wall_in.at[pl.ds(shard * width, width)],
            parts.at[
                pl.ds(shard % 2 * width, width), pl.ds(shard // 2 * wall_width, wall_width)
            ],
            wall_sem.at[shard],
        )
        for shard in range(LINE)
    ]
    for copy in wall_copies:
        copy.start()
    y[0, own_rows, :] = low[...]

    chain = RowChain(place, low, y.at[0], gm_send, gm_recv, LINE, 2)

    @pl.when(col > 0)
    def _():
        pl.semaphore_wait(free_sem.at[0], 1)

    @pl.when(col < LINE - 1)
    def _():
        pl.semaphore_wait(free_sem.at[1], 1)

    for chunk in range(2):
        chain.start_own(chunk)

    span = min(512, rows)
    per_side = rows // span
    for copy in att_copies:
        copy.wait()

    def key_rows(index):
        return rows_at(lax.rem(index, per_side) * span, span)

    def key_lanes(index, which):
        return lanes_at(index // per_side * 2 * HEAD_WIDTH + which * HEAD_WIDTH, HEAD_WIDTH)

    @pl.loop(0, LINE)
    def _(turn):
        block = lax.rem(col + LINE - turn, LINE)
        here = rows_at(block * part, part)
        for k in range(1, LINE):

            @pl.when(turn == k)
            def _():
                ga_copy(k).wait_recv()

        first_query = row * rows + block * part
        query = q[:, here, :].reshape(heads * part, HEAD_WIDTH)
        back = jnp.concatenate(
            [ga[here, h * HEAD_WIDTH : (h + 1) * HEAD_WIDTH] for h in range(heads)], axis=0
        )
        attended = jnp.concatenate(
            [
                acc[here, 512 + h * HEAD_WIDTH : 512 + (h + 1) * HEAD_WIDTH]
                for h in range(heads)
            ],
            axis=0,
        )
        log_total = jnp.concatenate(
            [acc[here, lse_lanes + h : lse_lanes + h + 1] for h in range(heads)], axis=0
        )
        delta = jnp.sum(back.astype(f32) * attended, axis=1, keepdims=True)

        def body(index, grad):
            keys = rows_at(index * span, span)
            key, value = kv[keys, :HEAD_WIDTH], kv[keys, HEAD_WIDTH:]
            scores = matmul_nt(query, key) * SCALE
            allowed = allowed_keys(lengths, first_query, part, index * span, span)
            probs = jnp.exp(scores - log_total).reshape(heads, part, span)
            probs = jnp.where(allowed[None], probs, 0.0).reshape(heads * part, span)
            grads = matmul_nt(back, value)
            grad_scores = (probs * (grads - delta)).astype(bf16)
            acc[key_rows(index), key_lanes(index, 0)] += matmul_tn(grad_scores, query)
            acc[key_rows(index), key_lanes(index, 1)] += matmul_tn(probs.astype(bf16), back)
            return grad + matmul(grad_scores, key)

        blocks = (first_query + part + span - 1) // span
        grad = lax.fori_loop(0, blocks, body, jnp.zeros((heads * part, HEAD_WIDTH), f32))
        cosine, sine = acc[here, trig_lanes[0]], -acc[here, trig_lanes[1]]
        for h in range(heads):
            lanes = slice(h * HEAD_WIDTH, (h + 1) * HEAD_WIDTH)
            turned = rotate(grad[h * part : (h + 1) * part] * SCALE, cosine, sine)
            ga[here, lanes] = turned.astype(bf16)
        @pl.when(turn == LINE - 1)
        def _():
            for chunk in range(2):
                chain.step(1, chunk)

        reduce.step(10 + turn)

    kv_give[...] = acc[:, lanes_at((1 - row) * 2 * HEAD_WIDTH, 2 * HEAD_WIDTH)].astype(bf16)
    kv_copy = remote(kv_give, kv_got, kv_sem.at[0], kv_sem.at[1], partner)
    kv_copy.start()
    reduce.step(14)
    kv_copy.wait()
    lane = lax.broadcasted_iota(jnp.int32, (1, HEAD_WIDTH), 1)
    low_lanes = lane < HEAD_WIDTH // 2
    turn_by = HEAD_WIDTH // 2
    mate_give = kv_give.at[:, pl.ds(0, HEAD_WIDTH)]
    mate_copy = remote(mate_give, mate_got, mate_sem.at[0], mate_sem.at[1], mate)
    own_lanes = lanes_at(row * 2 * HEAD_WIDTH, 2 * HEAD_WIDTH)

    @pl.loop(0, LINE)
    def _(chunk):
        here = rows_at(chunk * part, part)
        both = acc[here, own_lanes] + kv_got[here, :].astype(f32)
        key = rotate(
            both[:, :HEAD_WIDTH] * SCALE, acc[here, trig_lanes[0]], -acc[here, trig_lanes[1]]
        )
        value = both[:, HEAD_WIDTH:]
        first = jnp.where(low_lanes, key, pltpu.roll(value, turn_by, 1))
        second = jnp.where(low_lanes, pltpu.roll(key, turn_by, 1), value)
        is_first = jnp.where(member == 0, 1.0, 0.0)
        kept = first * is_first + second * (1.0 - is_first)
        given = second * is_first + first * (1.0 - is_first)
        acc[here, 512 : 512 + HEAD_WIDTH] = kept
        kv_give[here, :HEAD_WIDTH] = given.astype(bf16)

    mate_copy.start()
    reduce.step(15)
    mate_copy.wait_recv()

    @pl.loop(0, LINE)
    def _(chunk):
        here = rows_at(chunk * part, part)
        kept = acc[here, 512 : 512 + HEAD_WIDTH] + mate_got[here, :].astype(f32)
        gkv[here, :] = kept.astype(bf16)

    n1_copy.wait()
    base = 3 * hidden
    first_kv, first_out = half // 2, half // 2 + HEAD_WIDTH
    first_small = first_out + width

    def projections(side_lanes, store):
        product = matmul_tn(y[1, :, side_lanes], ga[...])
        for k in range(2):
            store(
                0,
                half // 2,
                slice(k * width, (k + 1) * width),
                product[k * half // 2 : (k + 1) * half // 2],
            )
        product = matmul_tn(y[1, :, side_lanes], gkv[...])
        for k in range(half // HEAD_WIDTH):
            store(
                first_kv,
                HEAD_WIDTH,
                slice(k * HEAD_WIDTH, (k + 1) * HEAD_WIDTH),
                product[k * HEAD_WIDTH : (k + 1) * HEAD_WIDTH],
            )

    for k in range(2):
        swap_copy(jobs - 2 + k).wait_send()
    pl.semaphore_wait(credit, 2)

    def store_give(first, count, lanes, value):
        give_buf[first : first + count, lanes] = value.astype(bf16)

    def store_keep(first, count, lanes, value):
        got = got_buf[first : first + count, lanes].astype(f32)
        total[base + first : base + first + count, lanes] = (got + value).astype(bf16)

    projections(theirs, store_give)
    tail = pl.ds(0, first_out)
    tail_copy = remote(give_buf.at[tail], got_buf.at[tail], end_sem.at[0], end_sem.at[1], partner)
    tail_copy.start()
    for chunk in range(2):
        chain.step(2, chunk)
    reduce.step(16)
    tail_copy.wait_recv()
    projections(ours, store_keep)
    x_copy = pltpu.make_async_copy(x_in, y.at[1], y_sem.at[1])
    x_copy.start()

    fin.clear_ends()

    for copy in wall_copies:
        copy.wait()
    x_copy.wait()

    @pl.loop(0, LINE + 2)
    def _(chunk):
        @pl.when(chunk < LINE)
        def _():
            here = rows_at(chunk * part, part)
            squares = jnp.zeros((part, 1), f32)
            inner = jnp.zeros((part, 1), f32)
            for shard in range(LINE):
                lanes = slice(shard * width, (shard + 1) * width)
                there = slice(shard % 2 * width, (shard % 2 + 1) * width)
                first = shard // 2 * wall_width
                kv_lanes = lanes_at(first + width + member * HEAD_WIDTH, HEAD_WIDTH)
                grad = matmul_nt(ga[here, :], parts[there, first : first + width])
                grad = grad + matmul_nt(gkv[here, :], parts[there, kv_lanes])
                acc[:part, lanes] = grad
                value = y[1, here, lanes].astype(f32)
                squares = squares + jnp.sum(value * value, axis=1, keepdims=True)
                scaled = grad * aux_all[shard, 0:1, :]
                inner = inner + jnp.sum(scaled * value, axis=1, keepdims=True)
            inverse = lax.rsqrt(squares / D + eps)
            factor = inverse * inverse * inverse * inner / D
            own = jnp.where(chunk == col, 1.0, 0.0)
            there = rows_at(lax.rem(chunk, 2) * part, part)
            for shard in range(LINE):
                lanes = slice(shard * width, (shard + 1) * width)
                grad, value = acc[:part, lanes], y[1, here, lanes].astype(f32)
                gain_sum[0:1, lanes] += jnp.sum(grad * value * inverse, axis=0, keepdims=True)
                share = inverse * grad * aux_all[shard, 0:1, :] - value * factor
                share = share + mid[:, lanes] * own
                wt[chunk // 2, there, lanes] = share.astype(bf16)
            fin.ends(chunk)

        @pl.when((chunk >= 1) & (chunk <= LINE))
        def _():
            fin.near(chunk - 1)

        @pl.when(chunk >= 2)
        def _():
            fin.far(chunk - 2)

        @pl.when(chunk < LINE)
        def _():
            reduce.step(17 + chunk)

    gains[...] = gain_sum[...]

    def gain_copy(k):
        to = lax.rem(col + k, LINE)
        return remote(
            gains.at[:, lanes_at(to * width, width)],
            gains_got.at[k - 1],
            gain_ssem.at[k - 1],
            gain_rsem.at[k - 1],
            (dp, row, to),
        )

    for k in range(1, LINE):
        gain_copy(k).start()
    reduce.step(21)
    bias = jnp.concatenate(
        [jnp.sum(ref[...].astype(f32), axis=0, keepdims=True) for ref in (ga, gkv)], axis=1
    )
    for k in range(1, LINE):
        gain_copy(k).wait_recv()
    gain_total = gains[:, lanes_at(col * width, width)]
    for k in range(1, LINE):
        gain_total = gain_total + gains_got[k - 1]
    small = jnp.concatenate(
        [
            jnp.concatenate([gain_total, jnp.zeros((8, half - width), f32)], axis=1),
            jnp.concatenate(
                [
                    jnp.broadcast_to(bias, (8, width + HEAD_WIDTH)),
                    jnp.zeros((8, half - width - HEAD_WIDTH), f32),
                ],
                axis=1,
            ),
        ],
        axis=0,
    )
    small_rows = pl.ds(first_out, width + 16)
    for chunk in range(2):
        chain.step(3, chunk)
    product = matmul_tn(att_low[...], y[0, :, theirs])
    give_buf[first_out:first_small, :] = product.astype(bf16)
    give_buf[first_small : first_small + 16, :] = small.astype(bf16)
    small_copy = remote(
        give_buf.at[small_rows], got_buf.at[small_rows], end_sem.at[2], end_sem.at[3], partner
    )
    small_copy.start()
    product = matmul_tn(att_low[...], y[0, :, ours])
    small_copy.wait_recv()
    product = product + got_buf[first_out:first_small, :].astype(f32)
    total[base + first_out : base + first_small, :] = product.astype(bf16)
    small = small + got_buf[first_small : first_small + 16, :].astype(f32)
    total[base + first_small : base + first_small + 16, :] = small.astype(bf16)
    rest = TAIL - first_small - 16
    total[base + first_small + 16 : base + TAIL, :] = jnp.zeros((rest, half), bf16)
    for number in (22, 23):
        reduce.step(number)

    @pl.loop(0, LINE)
    def _(chunk):
        ga[rows_at(chunk * part, part), :] = fin.own(chunk).astype(bf16)

    grad_copy = pltpu.make_async_copy(ga, grad_x, att_sem.at[1])
    grad_copy.start()

    @pl.loop(24, chunks + 4 * LAG)
    def _(number):
        reduce.step(number)

    outs = [
        pltpu.make_async_copy(
            sums_out.at[pl.ds(base, half // 2), pl.ds(k * width, width)],
            gq_out.at[pl.ds(k * half // 2, half // 2)],
            load_sem.at[k],
        )
        for k in range(2)
    ]
    outs += [
        pltpu.make_async_copy(
            sums_out.at[pl.ds(base + first_kv, HEAD_WIDTH), pl.ds(k * HEAD_WIDTH, HEAD_WIDTH)],
            gkv_out.at[pl.ds(k * HEAD_WIDTH, HEAD_WIDTH)],
            load_sem.at[2 + k],
        )
        for k in range(half // HEAD_WIDTH)
    ]
    outs.append(
        pltpu.make_async_copy(
            sums_out.at[pl.ds(base + first_small, 16)], small_out, load_sem.at[8]
        )
    )
    for copy in outs:
        copy.start()

    chain.finish()
    fin.finish()
    for k in range(1, LINE):
        ga_copy(k).wait_send()
        gain_copy(k).wait_send()
    for copy in (mate_copy, tail_copy, small_copy):
        copy.wait_send()
    for copy in outs + [grad_copy]:
        copy.wait()


def back(lefts, n2, cot, hid, rest, result, own, peer, aux_all, wof, wall, n1, x, kv, q, att, lse, trig, att_low, lengths):
    f32, bf16 = jnp.float32, jnp.bfloat16
    shape = jax.ShapeDtypeStruct
    dma = pltpu.SemaphoreType.DMA
    heads, rows, _ = q.shape
    width = heads * HEAD_WIDTH
    part = hid.shape[0]
    hidden = own[0].shape[0]
    total_rows = 3 * hidden + TAIL
    outs = [
        (shape((rows, width), bf16), any_spec()),
        (shape((rows, width), bf16), any_spec()),
        (shape((total_rows, TILE), bf16), any_spec()),
        (shape((TILE, width), bf16), any_spec()),
        (shape((TILE, HEAD_WIDTH), bf16), any_spec()),
        (shape((16, TILE), bf16), vmem_spec()),
    ]
    vmem = pltpu.VMEM
    return pl.pallas_call(
        functools.partial(back_kernel, heads),
        out_shape=[o[0] for o in outs],
        in_specs=[any_spec()] * 9
        + [vmem_spec()]
        + [any_spec()] * 10
        + [pl.BlockSpec(memory_space=pltpu.SMEM), any_spec()],
        out_specs=[o[1] for o in outs],
        scratch_shapes=[
            vmem((total_rows, TILE), bf16),
            vmem((RING * CHUNK * 3 // 4, TILE), bf16),
            vmem((2 * TILE, TILE), bf16),
            vmem((2 * TILE, TILE), bf16),
            vmem((3, rows, TILE), bf16),
            vmem((2, rows, D), bf16),
            vmem((2, TILE, D), bf16),
            vmem((rows, D), f32),
            vmem((rows, D), bf16),
            vmem((LINE + 1, part, D), bf16),
            vmem(kv.shape, bf16),
            vmem(q.shape, bf16),
            vmem(att_low.shape, bf16),
            vmem((part, D), f32),
            vmem((part, D), bf16),
            vmem((LINE - 1, part, width), bf16),
            vmem((rows, width), bf16),
            vmem((rows, 2 * HEAD_WIDTH), bf16),
            vmem((rows, 2 * HEAD_WIDTH), bf16),
            vmem((rows, HEAD_WIDTH), bf16),
            vmem((rows, HEAD_WIDTH), bf16),
            vmem((8, D), f32),
            vmem((8, D), f32),
            vmem((LINE - 1, 8, width), f32),
            dma((9,)),
            dma((2,)),
            dma((3,)),
            dma((2, 2)),
            dma((6,)),
            pltpu.SemaphoreType.REGULAR,
            pltpu.SemaphoreType.REGULAR((2,)),
            dma((2,)),
            dma((2,)),
            dma((RING, 2, 5)),
            dma((RING, 2, 5)),
            dma((RING, 2)),
            dma((LINE, LINE)),
            dma((LINE + 1, LINE)),
            dma((LINE, 2)),
            dma((LINE + 1, 2)),
            dma((LINE - 1,)),
            dma((LINE - 1,)),
            dma((2, LINE - 1, 2)),
            dma((LINE, 2)),
            dma((2,)),
            dma((2,)),
            dma((LINE, LINE)),
            dma((LINE + 1, LINE)),
            dma((LINE - 1,)),
            dma((LINE - 1,)),
            dma((4,)),
            dma((2,)),
            dma((LINE,)),
        ],
        compiler_params=pltpu.CompilerParams(
            collective_id=3, has_side_effects=True, vmem_limit_bytes=63 * 2**20
        ),
        cost_estimate=pl.CostEstimate(
            flops=64 * 10**9, bytes_accessed=60 * 10**6, transcendentals=10**7
        ),
        input_output_aliases={21: 1},
        name="back",
    )(
        lefts, n2, cot, hid, rest, *own[:2], *peer[:2], aux_all, wof, wall, n1, x, kv, q, att, lse, trig, att_low, lengths, result
    )


def per_device(
    inputs,
    seq_lengths,
    gain_one,
    w_query,
    b_query,
    w_key,
    b_key,
    w_value,
    b_value,
    w_out,
    gain_two,
    w_gate,
    w_up,
    w_down,
    cotangent,
):
    f32 = jnp.float32
    planes = lax.axis_size("dp")
    rows, width = inputs.shape
    kv_cols = w_key.shape[1]
    hidden = w_down.shape[0]
    half = HEAD_WIDTH // 2
    freq = theta_base ** (-(jnp.arange(half, dtype=f32) * 2.0) / HEAD_WIDTH)
    freq = jnp.concatenate([freq, freq]).reshape(1, HEAD_WIDTH)
    biases = jnp.concatenate([b_key, b_value]).astype(f32)
    biases = jnp.pad(biases, (0, width - 2 * kv_cols))
    aux = jnp.stack([gain_one, gain_two, b_query.astype(f32), biases])
    aux = jnp.pad(aux, ((0, 4), (0, 0)))
    own_kv = jnp.concatenate([w_key.T, w_value.T], axis=0).T
    own = (w_gate.T, w_up.T, w_down)
    (
        x_full,
        normed_one,
        cot_full,
        queries,
        keys_values,
        attended,
        log_total,
        att_own,
        hidden_mid,
        normed_two,
        trig,
        att_low,
        aux_all,
        wall,
        wof,
        *peer,
    ) = front(
        (LINE, planes),
        aux,
        inputs,
        cotangent,
        w_query,
        own_kv,
        w_out,
        *own,
        seq_lengths,
        freq,
    )
    lefts, normed_full, result, rest = mlp(normed_two, cot_full, hidden_mid, own, peer)
    grad_inputs, result, sums, grad_w_query, grad_kv, small = back(
        lefts,
        normed_full,
        cot_full,
        hidden_mid,
        rest,
        result,
        own,
        peer,
        aux_all,
        wof,
        wall,
        normed_one,
        x_full,
        keys_values,
        queries,
        attended,
        log_total,
        trig,
        att_low.reshape(rows, width),
        seq_lengths,
    )
    grad_w_gate, grad_w_up, grad_w_down = (
        sums[k * hidden : (k + 1) * hidden].astype(f32) for k in range(3)
    )
    first = 3 * hidden + TILE // 2 + HEAD_WIDTH
    grad_w_out = sums[first : first + width].astype(f32)
    grad_kv = grad_kv.astype(f32)
    small = small.astype(f32)
    bias = small[8]
    return (
        result,
        grad_inputs,
        small[0, :width],
        grad_w_query.astype(f32),
        bias[:width],
        grad_kv[:, :kv_cols],
        bias[width : width + kv_cols],
        grad_kv[:, kv_cols:],
        bias[width + kv_cols : width + 2 * kv_cols],
        grad_w_out,
        small[1, :width],
        grad_w_gate.T,
        grad_w_up.T,
        grad_w_down,
    )


def solution(mesh):
    whole_heads = dict(mesh.shape) == {"dp": 4, "row": 2, "col": LINE}
    return jax.shard_map(
        per_device if whole_heads else per_device_any,
        mesh=mesh,
        in_specs=(
            P(("dp", "row"), "col"),
            P("dp", None),
            P("col"),
            P("row", "col"),
            P("col"),
            P("row", "col"),
            P("col"),
            P("row", "col"),
            P("col"),
            P("col", "row"),
            P("col"),
            P("row", "col"),
            P("row", "col"),
            P("col", "row"),
            P(("dp", "row"), "col"),
        ),
        out_specs=(
            P(("dp", "row"), "col"),
            P(("dp", "row"), "col"),
            P("col"),
            P("row", "col"),
            P("col"),
            P("row", "col"),
            P("col"),
            P("row", "col"),
            P("col"),
            P("col", "row"),
            P("col"),
            P("row", "col"),
            P("row", "col"),
            P("col", "row"),
        ),
        check_vma=False,
    )
```
